32 devices in a mesh: pipe: 4 (over y, x), dp: 8 (over z, core).
Axes of the slice: x: 2, y: 2, z: 4, core: 2. Of those that a mesh axis runs over, the one named last changes fastest.
Arguments:
- clips: bfloat16 [32, 4, 7, 7, 512], P('dp'), may hold values from -6 to 6
- boxes: int32 [32, 6], P('dp'), may hold values from 0 to 7, as said below
- spatial_w: bfloat16 [4, 4608, 1152], P('pipe'), may hold values from -0.09375 to 0.09375
- temporal_w: bfloat16 [4, 3456, 512], P('pipe'), may hold values from -0.109375 to 0.109375
- spatial_gain: float32 [4, 1152], P('pipe'), may hold values from 0.5 to 1.5
- spatial_shift: float32 [4, 1152], P('pipe'), may hold values from -3 to 3
- temporal_gain: float32 [4, 512], P('pipe'), may hold values from 0.5 to 1.5
- temporal_shift: float32 [4, 512], P('pipe'), may hold values from -3 to 3
- cotangent: bfloat16 [32, 4, 7, 7, 512], P('dp'), may hold values from -6 to 6
Outputs:
- activations: bfloat16 [4, 32, 4, 7, 7, 512], P('pipe', 'dp')
- input_grads: bfloat16 [4, 32, 4, 7, 7, 512], P('pipe', 'dp')
- spatial_w_grad: float32 [4, 4608, 1152], P('pipe', 'dp')
- temporal_w_grad: float32 [4, 3456, 512], P('pipe', 'dp')
- spatial_gain_grad: float32 [4, 1152], P('pipe')
- spatial_shift_grad: float32 [4, 1152], P('pipe')
- temporal_gain_grad: float32 [4, 512], P('pipe')
- temporal_shift_grad: float32 [4, 512], P('pipe')
The draws below stay inside these ranges and needn't reach their ends.
Inputs may be any that keep to these rules, and one draw needn't show every extreme that they name: `boxes`: row c gives clip c's valid box: first and end frame, first and end row, first and end column, ends exclusive; at least 2 frames, 3 rows and 3 columns are valid.
All inputs are finite; a program needn't handle non-finite values.
Results may differ from the reference program's by a relative error of at most 0.025.
Values may be sent and summed in bfloat16 or wider, within the bound.
A program may use at most 320 MiB of HBM per device.

```python
import jax
import jax.numpy as jnp
from jax import lax

D = 512
M = 1152
FR = 4
HT = 7
WD = 7
MB = 4
CLIP_MB = 1
CLIPS = 32
N_PIPE = 4
N_DP = 8


def draw_boxes(key, part):
    key = jax.random.fold_in(key, 7)
    keys = jax.random.split(key, 6)
    first_frame = jax.random.randint(keys[0], (CLIPS,), 0, FR - 1)
    frame_span = jax.random.randint(keys[1], (CLIPS,), 2, FR + 1)
    first_row = jax.random.randint(keys[2], (CLIPS,), 0, HT - 2)
    row_span = jax.random.randint(keys[3], (CLIPS,), 3, HT + 1)
    first_col = jax.random.randint(keys[4], (CLIPS,), 0, WD - 2)
    col_span = jax.random.randint(keys[5], (CLIPS,), 3, WD + 1)
    leading = jnp.arange(CLIPS, dtype=jnp.int32) == 0
    end_frame = jnp.where(leading, FR, jnp.minimum(first_frame + frame_span, FR))
    end_row = jnp.where(leading, HT, jnp.minimum(first_row + row_span, HT))
    end_col = jnp.where(leading, WD, jnp.minimum(first_col + col_span, WD))
    first_frame = jnp.where(leading, 0, first_frame)
    first_row = jnp.where(leading, 0, first_row)
    first_col = jnp.where(leading, 0, first_col)
    return jnp.stack([first_frame, end_frame, first_row, end_row, first_col, end_col], axis=1).astype(jnp.int32)


def raised(drawn, rng, source, target, parts, factor):
    owner, partner = [(jnp.arange(drawn.shape[position]) // (drawn.shape[position] // parts)).reshape([-1 if axis == position else 1 for axis in range(drawn.ndim)]) for position in (source, target)]
    chosen = jax.random.permutation(rng, parts)[partner]
    strong = (owner == chosen) | (owner == (partner + parts // 2) % parts)
    return jnp.where(strong, factor * drawn, drawn)


def block_scale(rng, shape, shards, smallest, largest):
    factor_of = 1.0
    for dim, parts in shards:
        steps = jax.random.uniform(jax.random.fold_in(jax.random.fold_in(rng, 6), dim), (parts,), jnp.float32, smallest / len(shards), largest / len(shards))
        factor_of = factor_of * jnp.repeat(jnp.exp(steps), shape[dim] // parts).reshape((-1,) + (1,) * (len(shape) - 1 - dim))
    return factor_of


def scatter_about(rng, dims, width, most, cuts=(), held_as=jnp.bfloat16):
    result = width * jax.random.normal(rng, dims, jnp.float32)
    if cuts:
        result = result * block_scale(rng, dims, cuts, -0.22, 0.18)
    return jnp.clip(result, -most, most).astype(held_as)


def gaussian_with(rng, shape, width, bound, cuts, heavy, kind=jnp.bfloat16):
    array = width * jax.random.normal(rng, shape, jnp.float32)
    if cuts:
        array = array * block_scale(rng, shape, cuts, -0.22, 0.18)
    return jnp.clip(raised(array, jax.random.fold_in(rng, 3), *heavy), -bound, bound).astype(kind)


def setup_inputs(seed: int = 0) -> dict:
    seeds = jax.random.split(jax.random.key(seed), 10)
    return {
        "clips": gaussian_with(seeds[0], (CLIPS, FR, HT, WD, D), 1.0, 6.0, ((0, 8),), (0, 4, 8, 2.0)),
        "boxes": draw_boxes(jax.random.fold_in(seeds[9], 71), 0),
        "spatial_w": scatter_about(seeds[2], (N_PIPE, 9 * D, M), (9 * D) ** -0.5, 0.09375, ((0, 4),)),
        "temporal_w": scatter_about(seeds[3], (N_PIPE, 3 * M, D), (3 * M) ** -0.5, 0.109375, ((0, 4),)),
        "spatial_gain": jnp.clip(0.5 + 1.0 * jax.random.uniform(seeds[4], (N_PIPE, M), jnp.float32) ** block_scale(seeds[4], (N_PIPE, M), ((0, 4),), -0.2, 0.2), 0.5, 1.5),
        "spatial_shift": scatter_about(seeds[5], (N_PIPE, M), 0.5, 3.0, ((0, 4),), jnp.float32),
        "temporal_gain": jnp.clip(0.5 + 1.0 * jax.random.uniform(seeds[6], (N_PIPE, D), jnp.float32) ** block_scale(seeds[6], (N_PIPE, D), ((0, 4),), -0.2, 0.2), 0.5, 1.5),
        "temporal_shift": scatter_about(seeds[7], (N_PIPE, D), 0.5, 3.0, ((0, 4),), jnp.float32),
        "cotangent": scatter_about(seeds[8], (CLIPS, FR, HT, WD, D), 1.0, 6.0, ((0, 8),)),
    }


eps_norm = 1e-05
highest = lax.Precision.HIGHEST

@jax.custom_vjp
def low(v):
    return lax.optimization_barrier(v.astype(jnp.bfloat16)).astype(jnp.float32)

@jax.custom_vjp
def low_back(v):
    return v

def low_keep(v):
    return (low(v), None)

def low_pass(kept, grad):
    return (grad,)

def back_keep(v):
    return (v, None)

def back_low(kept, grad):
    return (low(grad),)
low.defvjp(low_keep, low_pass)
low_back.defvjp(back_keep, back_low)

def valid_mask(limits):
    frame_idx = jnp.arange(FR, dtype=jnp.int32)[None, :, None, None]
    row_idx = jnp.arange(HT, dtype=jnp.int32)[None, None, :, None]
    column_idx = jnp.arange(WD, dtype=jnp.int32)[None, None, None, :]
    bounds = limits[:, :, None, None, None]
    inside = (frame_idx >= bounds[:, 0]) & (frame_idx < bounds[:, 1])
    inside = inside & (row_idx >= bounds[:, 2]) & (row_idx < bounds[:, 3])
    inside = inside & (column_idx >= bounds[:, 4]) & (column_idx < bounds[:, 5])
    return inside.astype(jnp.float32)[..., None]

def spatial_columns(activity):
    height, breadth = (activity.shape[2], activity.shape[3])
    padded = jnp.pad(activity, ((0, 0), (0, 0), (1, 1), (1, 1), (0, 0)))
    pieces = [padded[:, :, row_off:row_off + height, col_off:col_off + breadth, :] for row_off in range(3) for col_off in range(3)]
    return jnp.concatenate(pieces, axis=-1)

def temporal_columns(activity):
    frames = activity.shape[1]
    padded = jnp.pad(activity, ((0, 0), (1, 1), (0, 0), (0, 0), (0, 0)))
    return jnp.concatenate([padded[:, offset:offset + frames] for offset in range(3)], axis=-1)

def normalize(values, keep_col):
    counted = jnp.sum(keep_col)
    center = lax.optimization_barrier(jnp.sum(keep_col * values, axis=0)) / counted
    spread = lax.optimization_barrier(jnp.sum(keep_col * (values - center) * (values - center), axis=0)) / counted
    return (values - center) * lax.rsqrt(spread + eps_norm)

def section(activity, skip_in, spatial, temporal, gain_a, shift_a, gain_b, shift_b, keep):
    layout = activity.shape
    pixels = layout[0] * layout[1] * layout[2] * layout[3]
    keep_col = keep.reshape(pixels, 1)
    columns = spatial_columns(activity).reshape(pixels, -1)
    spatial_out = low_back(jnp.dot(columns, spatial, precision=highest))
    hidden = low(keep_col * jax.nn.silu(gain_a * normalize(spatial_out, keep_col) + shift_a))
    stacked = temporal_columns(hidden.reshape(layout[:4] + (hidden.shape[1],))).reshape(pixels, -1)
    temporal_out = low_back(jnp.dot(stacked, temporal, precision=highest))
    preact = gain_b * normalize(temporal_out, keep_col) + shift_b
    if skip_in is not None:
        preact = preact + skip_in.reshape(pixels, -1)
    return low(keep_col * jax.nn.silu(preact)).reshape(layout)

def forward(start_act, perturb, spatial_w, temporal_w, spatial_gain, spatial_shift, temporal_gain, temporal_shift, keep):
    inputs = []
    outputs = []
    current = start_act
    for layer_idx in range(N_PIPE):
        entered = low_back(current + perturb[layer_idx])
        inputs.append(entered)
        skip_in = low_back(inputs[layer_idx - 1]) if layer_idx % 2 == 1 else None
        current = section(entered, skip_in, spatial_w[layer_idx], temporal_w[layer_idx], spatial_gain[layer_idx], spatial_shift[layer_idx], temporal_gain[layer_idx], temporal_shift[layer_idx], keep)
        outputs.append(current)
    return jnp.stack(outputs)

def by_micro(stacked):
    stacked = stacked.reshape((N_DP, MB, CLIP_MB) + stacked.shape[1:])
    stacked = jnp.swapaxes(stacked, 0, 1)
    return stacked.reshape((MB, N_DP * CLIP_MB) + stacked.shape[3:])

def by_clip(stacked):
    stacked = stacked.reshape((MB, N_PIPE, N_DP, CLIP_MB) + stacked.shape[3:])
    stacked = jnp.transpose(stacked, (1, 2, 0, 3) + tuple(range(4, stacked.ndim)))
    return stacked.reshape((N_PIPE, N_DP * MB * CLIP_MB) + stacked.shape[4:])

def reference(clips, boxes, spatial_w, temporal_w, spatial_gain, spatial_shift, temporal_gain, temporal_shift, cotangent):
    clip_parts = by_micro(clips.astype(jnp.float32))
    grad_parts = by_micro(cotangent.astype(jnp.float32))
    box_parts = by_micro(boxes)
    weights_f = tuple((piece.astype(jnp.float32) for piece in (spatial_w, temporal_w, spatial_gain, spatial_shift, temporal_gain, temporal_shift)))

    def micro_step(running, micro_item):
        clip_in, grad_out, box_in = micro_item
        keep = valid_mask(box_in)
        zero_pert = jnp.zeros((N_PIPE,) + clip_in.shape, jnp.float32)

        def run_forward(start_act, perturb, *weights_in):
            return forward(start_act, perturb, *weights_in, keep)
        activations, pullback = jax.vjp(run_forward, clip_in, zero_pert, *weights_f)
        seed_grad = jnp.zeros_like(activations).at[N_PIPE - 1].set(grad_out)
        gradients = pullback(seed_grad)
        running = tuple((total + piece for total, piece in zip(running, gradients[2:])))
        return (running, (activations, gradients[1]))
    start = tuple((jnp.zeros_like(piece) for piece in weights_f))
    totals, (activations, pert_grads) = lax.scan(micro_step, start, (clip_parts, grad_parts, box_parts))
    return (by_clip(activations).astype(jnp.bfloat16), by_clip(pert_grads).astype(jnp.bfloat16), totals[0], totals[1], totals[2], totals[3], totals[4], totals[5])
```

```python
import functools

import jax
import jax.numpy as jnp
from jax import lax
from jax.experimental import pallas as pl
from jax.experimental.pallas import tpu as pltpu
from jax.sharding import PartitionSpec as P

MB = 4
eps_norm = 1e-05
bf16 = jnp.bfloat16
f32 = jnp.float32
MESH = pl.DeviceIdType.MESH


def silu(x):
    return x / (1.0 + jnp.exp(-x))


def silu_slope(x):
    s = 1.0 / (1.0 + jnp.exp(-x))
    return s * (1.0 + x * (1.0 - s))


def lane_chunks(width, body):
    def step(i, carry):
        body(i, pl.ds(pl.multiple_of(i * 128, 128), 128))
        return carry

    lax.fori_loop(0, width // 128, step, 0)


def relay_kernel(
    dims,
    clips,
    boxes,
    w_s_hbm,
    w_t_hbm,
    g_s,
    b_s,
    g_t,
    b_t,
    cotangent,
    o_act,
    o_grad,
    o_in,
    o_hidden,
    o_gu,
    o_gr,
    o_gain_s,
    o_shift_s,
    o_gain_t,
    o_shift_t,
    w_s,
    w_t,
    w_s_back,
    w_t_back,
    cols,
    a_in,
    skip_in,
    a_out,
    ga_in,
    gs_in,
    gs_out,
    ig_out,
    hidden,
    gr,
    gu,
    uh,
    rh,
    gp,
    gq,
    keep,
    fact_s,
    fact_t,
    cnt,
    x_s,
    x_t,
    x_bt,
    x_bs,
    x_send,
    x_recv,
    w_sem,
    load_sem,
    store_sem,
    pipe_send,
    pipe_recv,
):
    cm, frames, height, width = dims
    rows = cm * frames * height * width
    d = a_in.shape[2]
    m_ch = hidden.shape[2]
    section = lax.axis_index("pipe")
    me = lax.axis_index("dp")
    n_pipe = lax.axis_size("pipe")
    n_dp = lax.axis_size("dp")
    first = section == 0
    last = section == n_pipe - 1
    odd = lax.rem(section, 2) == 1
    even_inner = jnp.logical_and(jnp.logical_not(odd), jnp.logical_not(last))
    skipping = odd.astype(f32)

    load_ws = pltpu.make_async_copy(w_s_hbm, w_s, w_sem.at[0])
    load_wt = pltpu.make_async_copy(w_t_hbm, w_t, w_sem.at[1])
    load_ws.start()
    load_wt.start()

    def load_clip(m):
        return pltpu.make_async_copy(clips.at[m], a_in.at[m], load_sem.at[m])

    def load_cot(m):
        return pltpu.make_async_copy(cotangent.at[m], ga_in.at[m], load_sem.at[m])

    @pl.when(first)
    def _():
        for m in range(MB):
            load_clip(m).start()

    @pl.when(last)
    def _():
        for m in range(MB):
            load_cot(m).start()

    for ref in (o_gain_s, o_shift_s, o_gain_t, o_shift_t, skip_in, gs_in):
        ref[...] = jnp.zeros_like(ref)

    barrier = pltpu.get_barrier_semaphore()

    def greet(j, carry):
        pl.semaphore_signal(
            barrier, 1, device_id={"dp": lax.rem(me + j, n_dp)}, device_id_type=MESH
        )
        return carry

    lax.fori_loop(1, n_dp, greet, 0)

    @pl.when(jnp.logical_not(first))
    def _():
        pl.semaphore_signal(barrier, 1, device_id={"pipe": section - 1}, device_id_type=MESH)

    @pl.when(jnp.logical_not(last))
    def _():
        pl.semaphore_signal(barrier, 1, device_id={"pipe": section + 1}, device_id_type=MESH)

    def make_keep(m, carry):
        n_rows = frames * height * width
        pieces = []
        for c in range(cm):
            shape = (frames, height, width, 128)
            t = lax.broadcasted_iota(jnp.int32, shape, 0)
            h = lax.broadcasted_iota(jnp.int32, shape, 1)
            w = lax.broadcasted_iota(jnp.int32, shape, 2)
            box = [boxes[m * cm + c, i] for i in range(6)]
            inside = (t >= box[0]) & (t < box[1]) & (h >= box[2]) & (h < box[3])
            inside = inside & (w >= box[4]) & (w < box[5])
            pieces.append(jnp.where(inside, 1.0, 0.0).astype(f32).reshape(n_rows, 128))
        mask = jnp.concatenate(pieces, axis=0) if cm > 1 else pieces[0]
        keep[m] = mask
        cnt[m] = jnp.sum(mask, axis=0, keepdims=True)
        return carry

    lax.fori_loop(0, MB, make_keep, 0)
    pl.semaphore_wait(barrier, n_dp + 1 - jnp.where(first, 1, 0) - jnp.where(last, 1, 0))

    def share(kind, buf, m):
        def send(j, carry):
            pltpu.make_async_remote_copy(
                src_ref=buf.at[m, me],
                dst_ref=buf.at[m, me],
                send_sem=x_send.at[kind, m],
                recv_sem=x_recv.at[kind, m],
                device_id={"dp": lax.rem(me + j, n_dp)},
                device_id_type=MESH,
            ).start()
            return carry

        lax.fori_loop(1, n_dp, send, 0)

    def shared(kind, buf, m):
        others = buf.at[m, pl.ds(0, n_dp - 1)]
        pltpu.make_async_copy(others, others, x_send.at[kind, m]).wait()
        pltpu.make_async_copy(others, others, x_recv.at[kind, m]).wait()

    def to_pipe(kind, src, dst, m, step):
        return pltpu.make_async_remote_copy(
            src_ref=src.at[m],
            dst_ref=dst.at[m],
            send_sem=pipe_send.at[kind, m],
            recv_sem=pipe_recv.at[kind, m],
            device_id={"pipe": section + step},
            device_id_type=MESH,
        )

    def store(kind, src, dst, m):
        return pltpu.make_async_copy(src.at[m], dst.at[m], store_sem.at[kind, m])

    def shift_space(x, dh, dw):
        if dw:
            x = pltpu.roll(x, (-dw) % rows, 0)
        return shift_rows(x, dh)

    def shift_rows(x, dh):
        if not dh:
            return x
        y = x.reshape(cm * frames, height * width, 128)
        zero = jnp.zeros((cm * frames, width, 128), f32)
        if dh > 0:
            y = jnp.concatenate([y[:, width:], zero], axis=1)
        else:
            y = jnp.concatenate([zero, y[:, :-width]], axis=1)
        return y.reshape(rows, 128)

    def shift_time(x, dt):
        if not dt:
            return x
        y = x.reshape(cm, frames * height * width, 128)
        step = height * width
        zero = jnp.zeros((cm, step, 128), f32)
        if dt > 0:
            y = jnp.concatenate([y[:, step:], zero], axis=1)
        else:
            y = jnp.concatenate([zero, y[:, :-step]], axis=1)
        return y.reshape(rows, 128)

    def local_sums(m, value, buf, c, channels):
        mask = keep[m]
        n_here = cnt[m]
        total = jnp.sum(mask * value, axis=0, keepdims=True)
        dev = mask * (value - total / n_here)
        spread = jnp.sum(dev * dev, axis=0, keepdims=True)
        buf[m, me, :, pl.ds(pl.multiple_of(c * 128, 128), 128)] = total
        buf[m, me, :, pl.ds(pl.multiple_of(channels + c * 128, 128), 128)] = spread

    def merged(m, buf, c, channels):
        counts = buf[m, :, :, 2 * channels :]
        sums = buf[m, :, :, pl.ds(pl.multiple_of(c * 128, 128), 128)]
        spreads = buf[m, :, :, pl.ds(pl.multiple_of(channels + c * 128, 128), 128)]
        n = jnp.sum(counts, axis=0)
        mean = jnp.sum(sums, axis=0) / n
        off = sums / counts - mean[None]
        var = jnp.sum(spreads + counts * off * off, axis=0) / n
        return n, mean, lax.rsqrt(var + eps_norm)

    def forward_spatial(m):
        @pl.when(first)
        def _():
            load_clip(m).wait()

        @pl.when(jnp.logical_not(first))
        def _():
            to_pipe(0, a_out, a_in, m, 1).wait_recv()

        @pl.when(even_inner)
        def _():
            to_pipe(1, a_in, skip_in, m, 1).start()

        store(2, a_in, o_in, m).start()

        def column(i, s):
            x = a_in[m, :, s].astype(f32)
            for dw in (-1, 0, 1):
                y = shift_space(x, 0, dw)
                for dh in (-1, 0, 1):
                    tap = (dh + 1) * 3 + dw + 1
                    at = pl.ds(pl.multiple_of(tap * d + i * 128, 128), 128)
                    cols[:, at] = shift_rows(y, dh).astype(bf16)

        lane_chunks(d, column)

        @pl.when(m == 0)
        def _():
            load_ws.wait()

        uh[m] = jnp.dot(cols[:, : 9 * d], w_s[...], preferred_element_type=f32)
        x_s[m, me, :, 2 * m_ch :] = cnt[m]
        lane_chunks(m_ch, lambda i, s: local_sums(m, uh[m, :, s], x_s, i, m_ch))
        share(0, x_s, m)

    def forward_temporal(m):
        shared(0, x_s, m)

        def column(i, s):
            n, mean, rstd = merged(m, x_s, i, m_ch)
            fact_s[m, :, s] = rstd
            normed = (uh[m, :, s] - mean) * rstd
            uh[m, :, s] = normed
            value = keep[m] * silu(g_s[:, s] * normed + b_s[:, s])
            value = value.astype(bf16)
            hidden[m, :, s] = value
            value = value.astype(f32)
            for dt in (-1, 0, 1):
                at = pl.ds(pl.multiple_of((dt + 1) * m_ch + i * 128, 128), 128)
                cols[:, at] = shift_time(value, dt).astype(bf16)

        lane_chunks(m_ch, column)
        store(3, hidden, o_hidden, m).start()

        @pl.when(m == 0)
        def _():
            load_wt.wait()

        rh[m] = jnp.dot(cols[:, : 3 * m_ch], w_t[...], preferred_element_type=f32)
        x_t[m, me, :, 2 * d :] = cnt[m]
        lane_chunks(d, lambda i, s: local_sums(m, rh[m, :, s], x_t, i, d))
        share(1, x_t, m)

    def preact(m, s, normed):
        return g_t[:, s] * normed + b_t[:, s] + skipping * skip_in[m, :, s].astype(f32)

    def forward_out(m):
        shared(1, x_t, m)

        @pl.when(odd)
        def _():
            to_pipe(1, a_in, skip_in, m, 1).wait_recv()

        def column(i, s):
            n, mean, rstd = merged(m, x_t, i, d)
            fact_t[m, :, s] = rstd
            normed = (rh[m, :, s] - mean) * rstd
            rh[m, :, s] = normed
            a_out[m, :, s] = (keep[m] * silu(preact(m, s, normed))).astype(bf16)

        lane_chunks(d, column)

        @pl.when(jnp.logical_not(last))
        def _():
            to_pipe(0, a_out, a_in, m, 1).start()

        store(0, a_out, o_act, m).start()

    def backward_in(m):
        @pl.when(last)
        def _():
            load_cot(m).wait()

        @pl.when(jnp.logical_not(last))
        def _():
            to_pipe(2, ig_out, ga_in, m, -1).wait_recv()

        def column(i, s):
            normed = rh[m, :, s]
            slope = ga_in[m, :, s].astype(f32) * keep[m] * silu_slope(preact(m, s, normed))
            gp[m, :, s] = slope
            gs_out[m, :, s] = slope.astype(bf16)
            x_bt[m, me, :, s] = jnp.sum(slope, axis=0, keepdims=True)
            at = pl.ds(pl.multiple_of(d + i * 128, 128), 128)
            x_bt[m, me, :, at] = jnp.sum(slope * normed, axis=0, keepdims=True)

        lane_chunks(d, column)
        share(2, x_bt, m)

        @pl.when(odd)
        def _():
            to_pipe(3, gs_out, gs_in, m, -1).start()

    def totals(buf, m, s, i, channels):
        at = pl.ds(pl.multiple_of(channels + i * 128, 128), 128)
        return jnp.sum(buf[m, :, :, s], axis=0), jnp.sum(buf[m, :, :, at], axis=0)

    def backward_temporal(m):
        shared(2, x_bt, m)
        n = jnp.sum(x_t[m, :, :, 2 * d :], axis=0)

        def column(i, s):
            shift_sum, gain_sum = totals(x_bt, m, s, i, d)
            o_shift_t[:, s] += shift_sum
            o_gain_t[:, s] += gain_sum
            scale = g_t[:, s] * fact_t[m, :, s]
            value = keep[m] * scale * (gp[m, :, s] - (shift_sum + rh[m, :, s] * gain_sum) / n)
            value = value.astype(bf16)
            gr[m, :, s] = value
            value = value.astype(f32)
            for dt in (-1, 0, 1):
                at = pl.ds(pl.multiple_of((dt + 1) * d + i * 128, 128), 128)
                cols[:, at] = shift_time(value, -dt).astype(bf16)

        lane_chunks(d, column)
        store(4, gr, o_gr, m).start()
        gq[...] = jnp.dot(cols[:, : 3 * d], w_t_back[...], preferred_element_type=f32)

        def sums(i, s):
            normed = uh[m, :, s]
            slope = keep[m] * gq[:, s] * silu_slope(g_s[:, s] * normed + b_s[:, s])
            gq[:, s] = slope
            x_bs[m, me, :, s] = jnp.sum(slope, axis=0, keepdims=True)
            at = pl.ds(pl.multiple_of(m_ch + i * 128, 128), 128)
            x_bs[m, me, :, at] = jnp.sum(slope * normed, axis=0, keepdims=True)

        lane_chunks(m_ch, sums)
        share(3, x_bs, m)

    def backward_spatial(m):
        shared(3, x_bs, m)
        n = jnp.sum(x_t[m, :, :, 2 * d :], axis=0)

        def column(i, s):
            shift_sum, gain_sum = totals(x_bs, m, s, i, m_ch)
            o_shift_s[:, s] += shift_sum
            o_gain_s[:, s] += gain_sum
            scale = g_s[:, s] * fact_s[m, :, s]
            value = keep[m] * scale * (gq[:, s] - (shift_sum + uh[m, :, s] * gain_sum) / n)
            value = value.astype(bf16)
            gu[m, :, s] = value
            value = value.astype(f32)
            for dw in (-1, 0, 1):
                y = shift_space(value, 0, -dw)
                for dh in (-1, 0, 1):
                    tap = (dh + 1) * 3 + dw + 1
                    at = pl.ds(pl.multiple_of(tap * m_ch + i * 128, 128), 128)
                    cols[:, at] = shift_rows(y, -dh).astype(bf16)

        lane_chunks(m_ch, column)
        store(5, gu, o_gu, m).start()

        @pl.when(even_inner)
        def _():
            to_pipe(3, gs_out, gs_in, m, -1).wait_recv()

        with_skip = even_inner.astype(f32)
        half = d // 2
        for part in range(2):
            s = slice(part * half, (part + 1) * half)
            value = jnp.dot(cols[...], w_s_back[:, s], preferred_element_type=f32)
            ig_out[m, :, s] = (value + with_skip * gs_in[m, :, s].astype(f32)).astype(bf16)

        @pl.when(jnp.logical_not(first))
        def _():
            to_pipe(2, ig_out, ga_in, m, -1).start()

        store(1, ig_out, o_grad, m).start()

    def turn_weights():
        def spatial(tap, carry):
            src = pl.ds(pl.multiple_of(tap * d, 128), d)
            dst = pl.ds(pl.multiple_of(tap * m_ch, 128), m_ch)
            w_s_back[dst, :] = w_s[src, :].T
            return carry

        lax.fori_loop(0, 9, spatial, 0)

        def temporal(tap, carry):
            src = pl.ds(pl.multiple_of(tap * m_ch, 128), m_ch)
            dst = pl.ds(pl.multiple_of(tap * d, 128), d)
            w_t_back[dst, :] = w_t[src, :].T
            return carry

        lax.fori_loop(0, 3, temporal, 0)

    wait_back = jnp.where(last, 1, MB)

    def step(s, carry):
        mf = s
        mb = s - wait_back
        do_f = mf < MB
        do_b = jnp.logical_and(mb >= 0, mb < MB)
        mf = jnp.minimum(mf, MB - 1)
        mb = jnp.clip(mb, 0, MB - 1)

        @pl.when(do_f)
        def _():
            forward_spatial(mf)

        @pl.when(s == wait_back)
        def _():
            turn_weights()

        @pl.when(do_b)
        def _():
            backward_in(mb)

        @pl.when(do_f)
        def _():
            forward_temporal(mf)

        @pl.when(do_b)
        def _():
            backward_temporal(mb)

        @pl.when(do_f)
        def _():
            forward_out(mf)

        @pl.when(do_b)
        def _():
            backward_spatial(mb)

        return carry

    lax.fori_loop(0, 2 * MB, step, 0)

    def finish(m, carry):
        for kind, (src, dst) in enumerate(
            (
                (a_out, o_act),
                (ig_out, o_grad),
                (a_in, o_in),
                (hidden, o_hidden),
                (gr, o_gr),
                (gu, o_gu),
            )
        ):
            store(kind, src, dst, m).wait()

        @pl.when(jnp.logical_not(last))
        def _():
            to_pipe(0, a_out, a_in, m, 1).wait_send()

        @pl.when(even_inner)
        def _():
            to_pipe(1, a_in, skip_in, m, 1).wait_send()

        @pl.when(jnp.logical_not(first))
        def _():
            to_pipe(2, ig_out, ga_in, m, -1).wait_send()

        @pl.when(odd)
        def _():
            to_pipe(3, gs_out, gs_in, m, -1).wait_send()

        return carry

    lax.fori_loop(0, MB, finish, 0)


def relay(dims, n_dp, clips, boxes, w_s, w_t, g_s, b_s, g_t, b_t, cotangent):
    cm, frames, height, width = dims
    rows = cm * frames * height * width
    d, m_ch = w_t.shape[1], w_s.shape[1]
    shape = jax.ShapeDtypeStruct
    vmem = pl.BlockSpec(memory_space=pltpu.VMEM)
    hbm = pl.BlockSpec(memory_space=pl.ANY)
    smem = pl.BlockSpec(memory_space=pltpu.SMEM)
    dma = pltpu.SemaphoreType.DMA
    narrow = pltpu.VMEM((MB, rows, d), bf16)
    wide = pltpu.VMEM((MB, rows, m_ch), bf16)
    return pl.pallas_call(
        functools.partial(relay_kernel, dims),
        out_shape=(
            shape((MB, rows, d), bf16),
            shape((MB, rows, d), bf16),
            shape((MB, rows, d), bf16),
            shape((MB, rows, m_ch), bf16),
            shape((MB, rows, m_ch), bf16),
            shape((MB, rows, d), bf16),
            shape((1, m_ch), f32),
            shape((1, m_ch), f32),
            shape((1, d), f32),
            shape((1, d), f32),
        ),
        in_specs=[hbm, smem, hbm, hbm, vmem, vmem, vmem, vmem, hbm],
        out_specs=[hbm] * 6 + [vmem] * 4,
        scratch_shapes=[
            pltpu.VMEM(w_s.shape, bf16),
            pltpu.VMEM(w_t.shape, bf16),
            pltpu.VMEM((9 * m_ch, d), bf16),
            pltpu.VMEM((3 * d, m_ch), bf16),
            pltpu.VMEM((rows, 9 * m_ch), bf16),
            narrow,
            narrow,
            narrow,
            narrow,
            narrow,
            narrow,
            narrow,
            wide,
            narrow,
            wide,
            pltpu.VMEM((MB, rows, m_ch), f32),
            pltpu.VMEM((MB, rows, d), f32),
            pltpu.VMEM((MB, rows, d), f32),
            pltpu.VMEM((rows, m_ch), f32),
            pltpu.VMEM((MB, rows, 128), f32),
            pltpu.VMEM((MB, 1, m_ch), f32),
            pltpu.VMEM((MB, 1, d), f32),
            pltpu.VMEM((MB, 1, 128), f32),
            pltpu.VMEM((MB, n_dp, 1, 2 * m_ch + 128), f32),
            pltpu.VMEM((MB, n_dp, 1, 2 * d + 128), f32),
            pltpu.VMEM((MB, n_dp, 1, 2 * d), f32),
            pltpu.VMEM((MB, n_dp, 1, 2 * m_ch), f32),
            dma((4, MB)),
            dma((4, MB)),
            dma((2,)),
            dma((MB,)),
            dma((6, MB)),
            dma((4, MB)),
            dma((4, MB)),
        ],
        compiler_params=pltpu.CompilerParams(
            collective_id=0, has_side_effects=True, vmem_limit_bytes=62 * 2**20
        ),
    )(clips, boxes, w_s, w_t, g_s, b_s, g_t, b_t, cotangent)


def spatial_columns(activity):
    height, breadth = (activity.shape[2], activity.shape[3])
    padded = jnp.pad(activity, ((0, 0), (0, 0), (1, 1), (1, 1), (0, 0)))
    pieces = [
        padded[:, :, row_off : row_off + height, col_off : col_off + breadth, :]
        for row_off in range(3)
        for col_off in range(3)
    ]
    return jnp.concatenate(pieces, axis=-1)


def temporal_columns(activity):
    frames = activity.shape[1]
    padded = jnp.pad(activity, ((0, 0), (1, 1), (0, 0), (0, 0), (0, 0)))
    return jnp.concatenate([padded[:, offset : offset + frames] for offset in range(3)], axis=-1)


def left_product(former, latter):
    return lax.dot_general(
        former, latter, (((0,), (0,)), ((), ())), preferred_element_type=jnp.float32
    )


def body(
    clips,
    boxes,
    spatial_w,
    temporal_w,
    spatial_gain,
    spatial_shift,
    temporal_gain,
    temporal_shift,
    cotangent,
):
    n_clips, frames, height, breadth, d = clips.shape
    cm = n_clips // MB
    width = (breadth // 8 + 1) * 8
    rows = cm * frames * height * width
    m_ch = spatial_w.shape[2]

    def padded(x):
        x = jnp.pad(x, ((0, 0), (0, 0), (0, 0), (0, width - breadth), (0, 0)))
        return x.reshape(MB, rows, d)

    act, grad, a_in, hidden, gu, gr, gain_s, shift_s, gain_t, shift_t = relay(
        (cm, frames, height, width),
        lax.axis_size("dp"),
        padded(clips),
        boxes,
        spatial_w[0],
        temporal_w[0],
        spatial_gain,
        spatial_shift,
        temporal_gain,
        temporal_shift,
        padded(cotangent),
    )

    def frames_of(x):
        return x.reshape(n_clips, frames, height, width, x.shape[-1])[:, :, :, :breadth]

    cells = n_clips * frames * height * breadth
    cols = spatial_columns(frames_of(a_in)).reshape(cells, -1)
    grad_s = left_product(cols, frames_of(gu).reshape(cells, -1))
    stacked = temporal_columns(frames_of(hidden)).reshape(cells, -1)
    grad_t = left_product(stacked, frames_of(gr).reshape(cells, -1))
    grad_s = lax.psum_scatter(grad_s, "dp", scatter_dimension=0, tiled=True)
    grad_t = lax.psum_scatter(grad_t, "dp", scatter_dimension=0, tiled=True)
    return (
        frames_of(act)[None],
        frames_of(grad)[None],
        grad_s[None],
        grad_t[None],
        gain_s,
        shift_s,
        gain_t,
        shift_t,
    )


def solution(mesh):
    clip_spec = P("dp", None, None, None, None)
    weight_spec = P("pipe", None, None)
    channel_spec = P("pipe", None)
    return jax.shard_map(
        body,
        mesh=mesh,
        in_specs=(
            clip_spec,
            P("dp", None),
            weight_spec,
            weight_spec,
            channel_spec,
            channel_spec,
            channel_spec,
            channel_spec,
            clip_spec,
        ),
        out_specs=(
            P("pipe", "dp", None, None, None, None),
            P("pipe", "dp", None, None, None, None),
            P("pipe", "dp", None),
            P("pipe", "dp", None),
            channel_spec,
            channel_spec,
            channel_spec,
            channel_spec,
        ),
        check_vma=False,
    )
```

```python
import functools

import jax
import jax.numpy as jnp
from jax import lax
from jax.experimental import pallas as pl
from jax.experimental.pallas import tpu as pltpu
from jax.sharding import PartitionSpec as P

MB = 4
eps_norm = 1e-05
bf16 = jnp.bfloat16
f32 = jnp.float32
MESH = pl.DeviceIdType.MESH


def silu(x):
    return x / (1.0 + jnp.exp(-x))


def silu_slope(x):
    s = 1.0 / (1.0 + jnp.exp(-x))
    return s * (1.0 + x * (1.0 - s))


def lane_chunks(width, body):
    def step(i, carry):
        body(i, pl.ds(pl.multiple_of(i * 128, 128), 128))
        return carry

    lax.fori_loop(0, width // 128, step, 0)


def relay_kernel(
    dims,
    clips,
    boxes,
    w_s_hbm,
    w_t_hbm,
    g_s,
    b_s,
    g_t,
    b_t,
    cotangent,
    o_act,
    o_grad,
    o_in,
    o_hidden,
    o_gu,
    o_gr,
    o_gain_s,
    o_shift_s,
    o_gain_t,
    o_shift_t,
    w_s,
    w_t,
    w_s_back,
    w_t_back,
    cols,
    a_in,
    skip_in,
    a_out,
    ga_in,
    gs_in,
    gs_out,
    ig_out,
    hidden,
    gr,
    gu,
    uh,
    rh,
    gp,
    gq,
    keep,
    fact_s,
    fact_t,
    cnt,
    x_s,
    x_t,
    x_bt,
    x_bs,
    x_send,
    x_recv,
    w_sem,
    load_sem,
    store_sem,
    pipe_send,
    pipe_recv,
    twin_send,
    twin_recv,
):
    cm, frames, height, width = dims
    rows = cm * frames * height * width
    d = a_in.shape[2]
    m_ch = hidden.shape[2]
    section = lax.axis_index("pipe")
    me = lax.axis_index("dp")
    n_pipe = lax.axis_size("pipe")
    n_dp = lax.axis_size("dp")
    first = section == 0
    last = section == n_pipe - 1
    odd = lax.rem(section, 2) == 1
    even_inner = jnp.logical_and(jnp.logical_not(odd), jnp.logical_not(last))
    skipping = odd.astype(f32)

    load_ws = pltpu.make_async_copy(w_s_hbm, w_s, w_sem.at[0])
    load_wt = pltpu.make_async_copy(w_t_hbm, w_t, w_sem.at[1])
    load_ws.start()
    load_wt.start()

    def load_clip(m):
        return pltpu.make_async_copy(clips.at[m], a_in.at[m], load_sem.at[m])

    def load_cot(m):
        return pltpu.make_async_copy(cotangent.at[m], ga_in.at[m], load_sem.at[m])

    @pl.when(first)
    def _():
        for m in range(MB):
            load_clip(m).start()

    @pl.when(last)
    def _():
        for m in range(MB):
            load_cot(m).start()

    for ref in (o_gain_s, o_shift_s, o_gain_t, o_shift_t, skip_in, gs_in):
        ref[...] = jnp.zeros_like(ref)

    barrier = pltpu.get_barrier_semaphore()

    def greet(j, carry):
        pl.semaphore_signal(
            barrier, 1, device_id={"dp": lax.rem(me + j, n_dp)}, device_id_type=MESH
        )
        return carry

    lax.fori_loop(1, n_dp, greet, 0)

    @pl.when(jnp.logical_not(first))
    def _():
        pl.semaphore_signal(barrier, 1, device_id={"pipe": section - 1}, device_id_type=MESH)

    @pl.when(jnp.logical_not(last))
    def _():
        pl.semaphore_signal(barrier, 1, device_id={"pipe": section + 1}, device_id_type=MESH)

    def make_keep(m, carry):
        n_rows = frames * height * width
        pieces = []
        for c in range(cm):
            shape = (frames, height, width, 128)
            t = lax.broadcasted_iota(jnp.int32, shape, 0)
            h = lax.broadcasted_iota(jnp.int32, shape, 1)
            w = lax.broadcasted_iota(jnp.int32, shape, 2)
            box = [boxes[m * cm + c, i] for i in range(6)]
            inside = (t >= box[0]) & (t < box[1]) & (h >= box[2]) & (h < box[3])
            inside = inside & (w >= box[4]) & (w < box[5])
            pieces.append(jnp.where(inside, 1.0, 0.0).astype(f32).reshape(n_rows, 128))
        mask = jnp.concatenate(pieces, axis=0) if cm > 1 else pieces[0]
        keep[m] = mask
        cnt[m] = jnp.sum(mask, axis=0, keepdims=True)
        return carry

    lax.fori_loop(0, MB, make_keep, 0)
    pl.semaphore_wait(barrier, n_dp + 1 - jnp.where(first, 1, 0) - jnp.where(last, 1, 0))

    def share(kind, buf, m):
        def send(j, carry):
            pltpu.make_async_remote_copy(
                src_ref=buf.at[m, me],
                dst_ref=buf.at[m, me],
                send_sem=x_send.at[kind, m],
                recv_sem=x_recv.at[kind, m],
                device_id={"dp": lax.rem(me + j, n_dp)},
                device_id_type=MESH,
            ).start()
            return carry

        lax.fori_loop(1, n_dp, send, 0)

    def shared(kind, buf, m):
        others = buf.at[m, pl.ds(0, n_dp - 1)]
        pltpu.make_async_copy(others, others, x_send.at[kind, m]).wait()
        pltpu.make_async_copy(others, others, x_recv.at[kind, m]).wait()

    def to_pipe(kind, src, dst, m, step):
        return pltpu.make_async_remote_copy(
            src_ref=src.at[m],
            dst_ref=dst.at[m],
            send_sem=pipe_send.at[kind, m],
            recv_sem=pipe_recv.at[kind, m],
            device_id={"pipe": section + step},
            device_id_type=MESH,
        )

    def store(kind, src, dst, m):
        return pltpu.make_async_copy(src.at[m], dst.at[m], store_sem.at[kind, m])

    def keep_operand(kind, src, dst, m):
        return pltpu.make_async_copy(src.at[m], dst.at[0, m], store_sem.at[kind, m])

    def twin_operand(kind, src, dst, m):
        return pltpu.make_async_remote_copy(
            src_ref=src.at[m],
            dst_ref=dst.at[1, m],
            send_sem=twin_send.at[kind - 2, m],
            recv_sem=twin_recv.at[kind - 2, m],
            device_id={"dp": me + 1 - 2 * lax.rem(me, 2)},
            device_id_type=MESH,
        )

    def share_operand(kind, src, dst, m):
        keep_operand(kind, src, dst, m).start()
        twin_operand(kind, src, dst, m).start()

    def shift_space(x, dh, dw):
        if dw:
            x = pltpu.roll(x, (-dw) % rows, 0)
        return shift_rows(x, dh)

    def shift_rows(x, dh):
        if not dh:
            return x
        y = x.reshape(cm * frames, height * width, 128)
        zero = jnp.zeros((cm * frames, width, 128), f32)
        if dh > 0:
            y = jnp.concatenate([y[:, width:], zero], axis=1)
        else:
            y = jnp.concatenate([zero, y[:, :-width]], axis=1)
        return y.reshape(rows, 128)

    def shift_time(x, dt):
        if not dt:
            return x
        y = x.reshape(cm, frames * height * width, 128)
        step = height * width
        zero = jnp.zeros((cm, step, 128), f32)
        if dt > 0:
            y = jnp.concatenate([y[:, step:], zero], axis=1)
        else:
            y = jnp.concatenate([zero, y[:, :-step]], axis=1)
        return y.reshape(rows, 128)

    def local_sums(m, value, buf, c, channels):
        mask = keep[m]
        n_here = cnt[m]
        total = jnp.sum(mask * value, axis=0, keepdims=True)
        dev = mask * (value - total / n_here)
        spread = jnp.sum(dev * dev, axis=0, keepdims=True)
        buf[m, me, :, pl.ds(pl.multiple_of(c * 128, 128), 128)] = total
        buf[m, me, :, pl.ds(pl.multiple_of(channels + c * 128, 128), 128)] = spread

    def merged(m, buf, c, channels):
        counts = buf[m, :, :, 2 * channels :]
        sums = buf[m, :, :, pl.ds(pl.multiple_of(c * 128, 128), 128)]
        spreads = buf[m, :, :, pl.ds(pl.multiple_of(channels + c * 128, 128), 128)]
        n = jnp.sum(counts, axis=0)
        mean = jnp.sum(sums, axis=0) / n
        off = sums / counts - mean[None]
        var = jnp.sum(spreads + counts * off * off, axis=0) / n
        return n, mean, lax.rsqrt(var + eps_norm)

    def forward_spatial(m):
        @pl.when(first)
        def _():
            load_clip(m).wait()

        @pl.when(jnp.logical_not(first))
        def _():
            to_pipe(0, a_out, a_in, m, 1).wait_recv()

        @pl.when(even_inner)
        def _():
            to_pipe(1, a_in, skip_in, m, 1).start()

        share_operand(2, a_in, o_in, m)

        def column(i, s):
            x = a_in[m, :, s].astype(f32)
            for dw in (-1, 0, 1):
                y = shift_space(x, 0, dw)
                for dh in (-1, 0, 1):
                    tap = (dh + 1) * 3 + dw + 1
                    at = pl.ds(pl.multiple_of(tap * d + i * 128, 128), 128)
                    cols[:, at] = shift_rows(y, dh).astype(bf16)

        lane_chunks(d, column)

        @pl.when(m == 0)
        def _():
            load_ws.wait()

        uh[m] = jnp.dot(cols[:, : 9 * d], w_s[...], preferred_element_type=f32)
        x_s[m, me, :, 2 * m_ch :] = cnt[m]
        lane_chunks(m_ch, lambda i, s: local_sums(m, uh[m, :, s], x_s, i, m_ch))
        share(0, x_s, m)

    def forward_temporal(m):
        shared(0, x_s, m)

        def column(i, s):
            n, mean, rstd = merged(m, x_s, i, m_ch)
            fact_s[m, :, s] = rstd
            normed = (uh[m, :, s] - mean) * rstd
            uh[m, :, s] = normed
            value = keep[m] * silu(g_s[:, s] * normed + b_s[:, s])
            value = value.astype(bf16)
            hidden[m, :, s] = value
            value = value.astype(f32)
            for dt in (-1, 0, 1):
                at = pl.ds(pl.multiple_of((dt + 1) * m_ch + i * 128, 128), 128)
                cols[:, at] = shift_time(value, dt).astype(bf16)

        lane_chunks(m_ch, column)
        share_operand(3, hidden, o_hidden, m)

        @pl.when(m == 0)
        def _():
            load_wt.wait()

        rh[m] = jnp.dot(cols[:, : 3 * m_ch], w_t[...], preferred_element_type=f32)
        x_t[m, me, :, 2 * d :] = cnt[m]
        lane_chunks(d, lambda i, s: local_sums(m, rh[m, :, s], x_t, i, d))
        share(1, x_t, m)

    def preact(m, s, normed):
        return g_t[:, s] * normed + b_t[:, s] + skipping * skip_in[m, :, s].astype(f32)

    def forward_out(m):
        shared(1, x_t, m)

        @pl.when(odd)
        def _():
            to_pipe(1, a_in, skip_in, m, 1).wait_recv()

        def column(i, s):
            n, mean, rstd = merged(m, x_t, i, d)
            fact_t[m, :, s] = rstd
            normed = (rh[m, :, s] - mean) * rstd
            rh[m, :, s] = normed
            a_out[m, :, s] = (keep[m] * silu(preact(m, s, normed))).astype(bf16)

        lane_chunks(d, column)

        @pl.when(jnp.logical_not(last))
        def _():
            to_pipe(0, a_out, a_in, m, 1).start()

        store(0, a_out, o_act, m).start()

    def backward_in(m):
        @pl.when(last)
        def _():
            load_cot(m).wait()

        @pl.when(jnp.logical_not(last))
        def _():
            to_pipe(2, ig_out, ga_in, m, -1).wait_recv()

        def column(i, s):
            normed = rh[m, :, s]
            slope = ga_in[m, :, s].astype(f32) * keep[m] * silu_slope(preact(m, s, normed))
            gp[m, :, s] = slope
            gs_out[m, :, s] = slope.astype(bf16)
            x_bt[m, me, :, s] = jnp.sum(slope, axis=0, keepdims=True)
            at = pl.ds(pl.multiple_of(d + i * 128, 128), 128)
            x_bt[m, me, :, at] = jnp.sum(slope * normed, axis=0, keepdims=True)

        lane_chunks(d, column)
        share(2, x_bt, m)

        @pl.when(odd)
        def _():
            to_pipe(3, gs_out, gs_in, m, -1).start()

    def totals(buf, m, s, i, channels):
        at = pl.ds(pl.multiple_of(channels + i * 128, 128), 128)
        return jnp.sum(buf[m, :, :, s], axis=0), jnp.sum(buf[m, :, :, at], axis=0)

    def backward_temporal(m):
        shared(2, x_bt, m)
        n = jnp.sum(x_t[m, :, :, 2 * d :], axis=0)

        def column(i, s):
            shift_sum, gain_sum = totals(x_bt, m, s, i, d)
            o_shift_t[:, s] += shift_sum
            o_gain_t[:, s] += gain_sum
            scale = g_t[:, s] * fact_t[m, :, s]
            value = keep[m] * scale * (gp[m, :, s] - (shift_sum + rh[m, :, s] * gain_sum) / n)
            value = value.astype(bf16)
            gr[m, :, s] = value
            value = value.astype(f32)
            for dt in (-1, 0, 1):
                at = pl.ds(pl.multiple_of((dt + 1) * d + i * 128, 128), 128)
                cols[:, at] = shift_time(value, -dt).astype(bf16)

        lane_chunks(d, column)
        share_operand(4, gr, o_gr, m)
        gq[...] = jnp.dot(cols[:, : 3 * d], w_t_back[...], preferred_element_type=f32)

        def sums(i, s):
            normed = uh[m, :, s]
            slope = keep[m] * gq[:, s] * silu_slope(g_s[:, s] * normed + b_s[:, s])
            gq[:, s] = slope
            x_bs[m, me, :, s] = jnp.sum(slope, axis=0, keepdims=True)
            at = pl.ds(pl.multiple_of(m_ch + i * 128, 128), 128)
            x_bs[m, me, :, at] = jnp.sum(slope * normed, axis=0, keepdims=True)

        lane_chunks(m_ch, sums)
        share(3, x_bs, m)

    def backward_spatial(m):
        shared(3, x_bs, m)
        n = jnp.sum(x_t[m, :, :, 2 * d :], axis=0)

        def column(i, s):
            shift_sum, gain_sum = totals(x_bs, m, s, i, m_ch)
            o_shift_s[:, s] += shift_sum
            o_gain_s[:, s] += gain_sum
            scale = g_s[:, s] * fact_s[m, :, s]
            value = keep[m] * scale * (gq[:, s] - (shift_sum + uh[m, :, s] * gain_sum) / n)
            value = value.astype(bf16)
            gu[m, :, s] = value
            value = value.astype(f32)
            for dw in (-1, 0, 1):
                y = shift_space(value, 0, -dw)
                for dh in (-1, 0, 1):
                    tap = (dh + 1) * 3 + dw + 1
                    at = pl.ds(pl.multiple_of(tap * m_ch + i * 128, 128), 128)
                    cols[:, at] = shift_rows(y, -dh).astype(bf16)

        lane_chunks(m_ch, column)
        share_operand(5, gu, o_gu, m)

        @pl.when(even_inner)
        def _():
            to_pipe(3, gs_out, gs_in, m, -1).wait_recv()

        with_skip = even_inner.astype(f32)
        half = d // 2
        for part in range(2):
            s = slice(part * half, (part + 1) * half)
            value = jnp.dot(cols[...], w_s_back[:, s], preferred_element_type=f32)
            ig_out[m, :, s] = (value + with_skip * gs_in[m, :, s].astype(f32)).astype(bf16)

        @pl.when(jnp.logical_not(first))
        def _():
            to_pipe(2, ig_out, ga_in, m, -1).start()

        store(1, ig_out, o_grad, m).start()

    def turn_weights():
        def spatial(tap, carry):
            src = pl.ds(pl.multiple_of(tap * d, 128), d)
            dst = pl.ds(pl.multiple_of(tap * m_ch, 128), m_ch)
            w_s_back[dst, :] = w_s[src, :].T
            return carry

        lax.fori_loop(0, 9, spatial, 0)

        def temporal(tap, carry):
            src = pl.ds(pl.multiple_of(tap * m_ch, 128), m_ch)
            dst = pl.ds(pl.multiple_of(tap * d, 128), d)
            w_t_back[dst, :] = w_t[src, :].T
            return carry

        lax.fori_loop(0, 3, temporal, 0)

    wait_back = jnp.where(last, 1, MB)

    def step(s, carry):
        mf = s
        mb = s - wait_back
        do_f = mf < MB
        do_b = jnp.logical_and(mb >= 0, mb < MB)
        mf = jnp.minimum(mf, MB - 1)
        mb = jnp.clip(mb, 0, MB - 1)

        @pl.when(do_f)
        def _():
            forward_spatial(mf)

        @pl.when(s == wait_back)
        def _():
            turn_weights()

        @pl.when(do_b)
        def _():
            backward_in(mb)

        @pl.when(do_f)
        def _():
            forward_temporal(mf)

        @pl.when(do_b)
        def _():
            backward_temporal(mb)

        @pl.when(do_f)
        def _():
            forward_out(mf)

        @pl.when(do_b)
        def _():
            backward_spatial(mb)

        return carry

    lax.fori_loop(0, 2 * MB, step, 0)

    def finish(m, carry):
        store(0, a_out, o_act, m).wait()
        store(1, ig_out, o_grad, m).wait()
        for kind, src, dst in (
            (2, a_in, o_in),
            (3, hidden, o_hidden),
            (4, gr, o_gr),
            (5, gu, o_gu),
        ):
            keep_operand(kind, src, dst, m).wait()
            twin_operand(kind, src, dst, m).wait()

        @pl.when(jnp.logical_not(last))
        def _():
            to_pipe(0, a_out, a_in, m, 1).wait_send()

        @pl.when(even_inner)
        def _():
            to_pipe(1, a_in, skip_in, m, 1).wait_send()

        @pl.when(jnp.logical_not(first))
        def _():
            to_pipe(2, ig_out, ga_in, m, -1).wait_send()

        @pl.when(odd)
        def _():
            to_pipe(3, gs_out, gs_in, m, -1).wait_send()

        return carry

    lax.fori_loop(0, MB, finish, 0)


def relay(dims, n_dp, clips, boxes, w_s, w_t, g_s, b_s, g_t, b_t, cotangent):
    cm, frames, height, width = dims
    rows = cm * frames * height * width
    d, m_ch = w_t.shape[1], w_s.shape[1]
    shape = jax.ShapeDtypeStruct
    vmem = pl.BlockSpec(memory_space=pltpu.VMEM)
    hbm = pl.BlockSpec(memory_space=pl.ANY)
    smem = pl.BlockSpec(memory_space=pltpu.SMEM)
    dma = pltpu.SemaphoreType.DMA
    narrow = pltpu.VMEM((MB, rows, d), bf16)
    wide = pltpu.VMEM((MB, rows, m_ch), bf16)
    return pl.pallas_call(
        functools.partial(relay_kernel, dims),
        out_shape=(
            shape((MB, rows, d), bf16),
            shape((MB, rows, d), bf16),
            shape((2, MB, rows, d), bf16),
            shape((2, MB, rows, m_ch), bf16),
            shape((2, MB, rows, m_ch), bf16),
            shape((2, MB, rows, d), bf16),
            shape((1, m_ch), f32),
            shape((1, m_ch), f32),
            shape((1, d), f32),
            shape((1, d), f32),
        ),
        in_specs=[hbm, smem, hbm, hbm, vmem, vmem, vmem, vmem, hbm],
        out_specs=[hbm] * 6 + [vmem] * 4,
        scratch_shapes=[
            pltpu.VMEM(w_s.shape, bf16),
            pltpu.VMEM(w_t.shape, bf16),
            pltpu.VMEM((9 * m_ch, d), bf16),
            pltpu.VMEM((3 * d, m_ch), bf16),
            pltpu.VMEM((rows, 9 * m_ch), bf16),
            narrow,
            narrow,
            narrow,
            narrow,
            narrow,
            narrow,
            narrow,
            wide,
            narrow,
            wide,
            pltpu.VMEM((MB, rows, m_ch), f32),
            pltpu.VMEM((MB, rows, d), f32),
            pltpu.VMEM((MB, rows, d), f32),
            pltpu.VMEM((rows, m_ch), f32),
            pltpu.VMEM((MB, rows, 128), f32),
            pltpu.VMEM((MB, 1, m_ch), f32),
            pltpu.VMEM((MB, 1, d), f32),
            pltpu.VMEM((MB, 1, 128), f32),
            pltpu.VMEM((MB, n_dp, 1, 2 * m_ch + 128), f32),
            pltpu.VMEM((MB, n_dp, 1, 2 * d + 128), f32),
            pltpu.VMEM((MB, n_dp, 1, 2 * d), f32),
            pltpu.VMEM((MB, n_dp, 1, 2 * m_ch), f32),
            dma((4, MB)),
            dma((4, MB)),
            dma((2,)),
            dma((MB,)),
            dma((6, MB)),
            dma((4, MB)),
            dma((4, MB)),
            dma((4, MB)),
            dma((4, MB)),
        ],
        compiler_params=pltpu.CompilerParams(
            collective_id=0, has_side_effects=True, vmem_limit_bytes=62 * 2**20
        ),
    )(clips, boxes, w_s, w_t, g_s, b_s, g_t, b_t, cotangent)


def send_order(n, z, q):
    table = []
    for here in range(n):
        sign = 1 if here < n / 2 else -1
        table.append(sorted(range(n), key=lambda to: (-abs(to - here), -sign * to)))
    dest = 0
    for here in range(n):
        for at in range(n):
            dest = dest + jnp.where((z == here) & (q == at), table[here][at], 0)
    return dest


def gradient_kernel(
    dims,
    a_hbm,
    v_hbm,
    gu_hbm,
    gr_hbm,
    o_s,
    o_t,
    a_raw,
    v_raw,
    a_pad,
    v_pad,
    gu,
    gr,
    edge,
    window,
    acc_s,
    acc_t,
    got_s,
    got_t,
    out_s,
    out_t,
    load_sem,
    send_sem,
    recv_sem,
):
    frames, height, width = dims
    n_clips, rows, d = a_hbm.shape
    m_ch = v_hbm.shape[2]
    step = height * width
    me = lax.axis_index("dp")
    n = lax.axis_size("dp") // 2
    z = lax.div(me, 2)
    core = lax.rem(me, 2)
    rows_s, rows_t = o_s.shape[0], o_t.shape[0]
    piece = got_s.shape[3]
    n_pieces = m_ch // piece
    span = acc_s.shape[0]
    lead = a_pad.shape[2] - rows - 8

    load_gu = [
        pltpu.make_async_copy(gu_hbm.at[i], gu.at[pl.ds(i * rows, rows)], load_sem.at[2, i])
        for i in range(n_clips)
    ]
    load_gr = [
        pltpu.make_async_copy(gr_hbm.at[i], gr.at[pl.ds(i * rows, rows)], load_sem.at[3, i])
        for i in range(n_clips)
    ]
    for copy in load_gu + load_gr:
        copy.start()

    def load_a(i):
        return pltpu.make_async_copy(a_hbm.at[i], a_raw.at[lax.rem(i, 2)], load_sem.at[0, i])

    def load_v(i):
        return pltpu.make_async_copy(v_hbm.at[i], v_raw.at[lax.rem(i, 2)], load_sem.at[1, i])

    load_a(0).start()
    load_v(0).start()

    barrier = pltpu.get_barrier_semaphore()

    @pl.when(z > 0)
    def _():
        pl.semaphore_signal(barrier, 1, device_id={"dp": me - 2}, device_id_type=MESH)

    @pl.when(z < n - 1)
    def _():
        pl.semaphore_signal(barrier, 1, device_id={"dp": me + 2}, device_id_type=MESH)

    h = lax.broadcasted_iota(jnp.int32, (frames, height, width, 128), 1)
    for dh in (-1, 0, 1):
        inside = (h + dh >= 0) & (h + dh < height)
        edge[dh + 1] = jnp.where(inside, 1.0, 0.0).astype(f32).reshape(rows, 128)

    def prepare(i, carry):
        load_a(i).wait()
        load_v(i).wait()

        @pl.when(i + 1 < n_clips)
        def _():
            load_a(i + 1).start()
            load_v(i + 1).start()

        slot = lax.rem(i, 2)
        for c in range(0, d, 128):
            x = a_raw[slot, :, c : c + 128].astype(f32)
            for dw in (-1, 0, 1):
                y = pltpu.roll(x, (-dw) % rows, 0) if dw else x
                a_pad[i, dw + 1, lead : lead + rows, c : c + 128] = y
                a_pad[i, dw + 1, lead - 8 : lead, c : c + 128] = jnp.zeros((8, 128), f32)
                a_pad[i, dw + 1, lead + rows :, c : c + 128] = jnp.zeros((8, 128), f32)
        zero = jnp.zeros((step, 128), f32)
        for c in range(0, m_ch, 128):
            v_pad[i, :step, c : c + 128] = zero
            v_pad[i, step : step + rows, c : c + 128] = v_raw[slot, :, c : c + 128].astype(f32)
            v_pad[i, step + rows :, c : c + 128] = zero
        return carry

    lax.fori_loop(0, n_clips, prepare, 0)
    for copy in load_gu + load_gr:
        copy.wait()
    pl.semaphore_wait(barrier, 2 - jnp.where(z == 0, 1, 0) - jnp.where(z == n - 1, 1, 0))

    def transfer(src, dst, dest, p):
        right = dest > z
        slot = dest + jnp.where(right, 1, 0)
        return pltpu.make_async_remote_copy(
            src_ref=src,
            dst_ref=dst(slot),
            send_sem=send_sem.at[dest, p],
            recv_sem=recv_sem.at[slot, p],
            device_id={"dp": me + jnp.where(right, 2, -2)},
            device_id_type=MESH,
        )

    def settle(dest, acc, start, size, got, out, final, p):
        at = pl.ds(pl.multiple_of(start, 8), size)
        from_left = (z > 0) & (dest >= z)
        from_right = (z < n - 1) & (dest <= z)

        @pl.when(from_left)
        def _():
            ref = got(dest + 1)
            pltpu.make_async_copy(ref, ref, recv_sem.at[dest + 1, p]).wait()
            acc[at, :] += ref[...].astype(f32)

        @pl.when(from_right)
        def _():
            ref = got(dest)
            pltpu.make_async_copy(ref, ref, recv_sem.at[dest, p]).wait()
            acc[at, :] += ref[...].astype(f32)

        @pl.when(dest == z)
        def _():
            final[...] = acc[at, :]

        @pl.when(dest != z)
        def _():
            ref = out(dest)
            ref[...] = acc[at, :].astype(bf16)
            transfer(ref, got, dest, p).start()

    def place(row0):
        low = lax.div(row0, 128)
        return low, row0 - low * 128

    def job(q, carry):
        dest = send_order(n, z, q)
        owner = 2 * dest + core

        low, start = place(owner * rows_s)

        def fill_space(i, c):
            for j in range(span // 128):
                chunk = jnp.minimum(low + j, 9 * d // 128 - 1)
                tap = lax.div(chunk, d // 128)
                lane = chunk - tap * (d // 128)
                dh = lax.div(tap, 3)
                dw = tap - 3 * dh
                x = a_pad[
                    i,
                    dw,
                    pl.ds(pl.multiple_of(lead - 8 + 8 * dh, 8), rows),
                    pl.ds(pl.multiple_of(lane * 128, 128), 128),
                ]
                window[pl.ds(pl.multiple_of(i * rows, 16), rows), j * 128 : (j + 1) * 128] = (
                    x * edge[dh]
                ).astype(bf16)
            return c

        lax.fori_loop(0, n_clips, fill_space, 0)

        def space(p, c):
            s = pl.ds(pl.multiple_of(p * piece, 128), piece)
            acc_s[...] = lax.dot_general(
                window[...], gu[:, s], (((0,), (0,)), ((), ())), preferred_element_type=f32
            )
            settle(
                dest,
                acc_s,
                start,
                rows_s,
                lambda slot: got_s.at[slot, p],
                lambda to: out_s.at[to, p],
                o_s.at[:, s],
                p,
            )
            return c

        lax.fori_loop(0, n_pieces, space, 0)

        low_t, start_t = place(owner * rows_t)

        def fill_time(i, c):
            for j in range(span // 128):
                chunk = jnp.minimum(low_t + j, 3 * m_ch // 128 - 1)
                tap = lax.div(chunk, m_ch // 128)
                lane = chunk - tap * (m_ch // 128)
                x = v_pad[
                    i,
                    pl.ds(pl.multiple_of(tap * step, 8), rows),
                    pl.ds(pl.multiple_of(lane * 128, 128), 128),
                ]
                window[pl.ds(pl.multiple_of(i * rows, 16), rows), j * 128 : (j + 1) * 128] = (
                    x.astype(bf16)
                )
            return c

        lax.fori_loop(0, n_clips, fill_time, 0)
        acc_t[...] = lax.dot_general(
            window[...], gr[...], (((0,), (0,)), ((), ())), preferred_element_type=f32
        )
        settle(
            dest,
            acc_t,
            start_t,
            rows_t,
            lambda slot: got_t.at[slot],
            lambda to: out_t.at[to],
            o_t,
            n_pieces,
        )
        return carry

    lax.fori_loop(0, n, job, 0)

    def finish(q, carry):
        dest = send_order(n, z, q)
        for p in range(n_pieces):
            transfer(out_s.at[dest, p], lambda slot: got_s.at[slot, p], dest, p).wait_send()
        transfer(out_t.at[dest], lambda slot: got_t.at[slot], dest, n_pieces).wait_send()
        return carry

    lax.fori_loop(0, n - 1, finish, 0)


def gradients(dims, n_dp, a, v, gu, gr):
    n_clips, rows, d = a.shape
    m_ch = v.shape[2]
    frames, height, width = dims
    step = height * width
    rows_s, rows_t = 9 * d // n_dp, 3 * m_ch // n_dp
    n = n_dp // 2
    piece = 384
    n_pieces = m_ch // piece
    span = 640
    shape = jax.ShapeDtypeStruct
    dma = pltpu.SemaphoreType.DMA
    return pl.pallas_call(
        functools.partial(gradient_kernel, dims),
        out_shape=(shape((rows_s, m_ch), f32), shape((rows_t, d), f32)),
        in_specs=[pl.BlockSpec(memory_space=pl.ANY)] * 4,
        out_specs=[pl.BlockSpec(memory_space=pltpu.VMEM)] * 2,
        scratch_shapes=[
            pltpu.VMEM((2, rows, d), bf16),
            pltpu.VMEM((2, rows, m_ch), bf16),
            pltpu.VMEM((n_clips, 3, rows + 16, d), f32),
            pltpu.VMEM((n_clips, rows + 2 * step, m_ch), f32),
            pltpu.VMEM((n_clips * rows, m_ch), bf16),
            pltpu.VMEM((n_clips * rows, d), bf16),
            pltpu.VMEM((3, rows, 128), f32),
            pltpu.VMEM((n_clips * rows, span), bf16),
            pltpu.VMEM((span, piece), f32),
            pltpu.VMEM((span, d), f32),
            pltpu.VMEM((n + 1, n_pieces, rows_s, piece), bf16),
            pltpu.VMEM((n + 1, rows_t, d), bf16),
            pltpu.VMEM((n, n_pieces, rows_s, piece), bf16),
            pltpu.VMEM((n, rows_t, d), bf16),
            dma((4, n_clips)),
            dma((n, n_pieces + 1)),
            dma((n + 1, n_pieces + 1)),
        ],
        compiler_params=pltpu.CompilerParams(
            collective_id=1, has_side_effects=True, vmem_limit_bytes=62 * 2**20
        ),
    )(a, v, gu, gr)


def spatial_columns(activity):
    height, breadth = (activity.shape[2], activity.shape[3])
    padded = jnp.pad(activity, ((0, 0), (0, 0), (1, 1), (1, 1), (0, 0)))
    pieces = [
        padded[:, :, row_off : row_off + height, col_off : col_off + breadth, :]
        for row_off in range(3)
        for col_off in range(3)
    ]
    return jnp.concatenate(pieces, axis=-1)


def temporal_columns(activity):
    frames = activity.shape[1]
    padded = jnp.pad(activity, ((0, 0), (1, 1), (0, 0), (0, 0), (0, 0)))
    return jnp.concatenate([padded[:, offset : offset + frames] for offset in range(3)], axis=-1)


def left_product(former, latter):
    return lax.dot_general(
        former, latter, (((0,), (0,)), ((), ())), preferred_element_type=jnp.float32
    )


def body(
    clips,
    boxes,
    spatial_w,
    temporal_w,
    spatial_gain,
    spatial_shift,
    temporal_gain,
    temporal_shift,
    cotangent,
):
    n_clips, frames, height, breadth, d = clips.shape
    cm = n_clips // MB
    width = (breadth // 8 + 1) * 8
    rows = cm * frames * height * width
    m_ch = spatial_w.shape[2]

    def padded(x):
        x = jnp.pad(x, ((0, 0), (0, 0), (0, 0), (0, width - breadth), (0, 0)))
        return x.reshape(MB, rows, d)

    act, grad, a_in, hidden, gu, gr, gain_s, shift_s, gain_t, shift_t = relay(
        (cm, frames, height, width),
        lax.axis_size("dp"),
        padded(clips),
        boxes,
        spatial_w[0],
        temporal_w[0],
        spatial_gain,
        spatial_shift,
        temporal_gain,
        temporal_shift,
        padded(cotangent),
    )

    def frames_of(x):
        return x.reshape(n_clips, frames, height, width, x.shape[-1])[:, :, :, :breadth]

    n_dp = lax.axis_size("dp")
    rows_s, rows_t = 9 * d // n_dp, 3 * m_ch // n_dp
    if rows_s % 64 == 0 and rows_t % 16 == 0 and rows_s <= 576 and rows_t <= 528 and n_dp <= 8:
        clip_rows = frames * height * width
        grad_s, grad_t = gradients(
            (frames, height, width),
            n_dp,
            *[x.reshape(2 * n_clips, clip_rows, x.shape[-1]) for x in (a_in, hidden, gu, gr)],
        )
    else:
        cells = n_clips * frames * height * breadth
        cols = spatial_columns(frames_of(a_in[0])).reshape(cells, -1)
        grad_s = left_product(cols, frames_of(gu[0]).reshape(cells, -1))
        stacked = temporal_columns(frames_of(hidden[0])).reshape(cells, -1)
        grad_t = left_product(stacked, frames_of(gr[0]).reshape(cells, -1))
        grad_s = lax.psum_scatter(grad_s, "dp", scatter_dimension=0, tiled=True)
        grad_t = lax.psum_scatter(grad_t, "dp", scatter_dimension=0, tiled=True)
    return (
        frames_of(act)[None],
        frames_of(grad)[None],
        grad_s[None],
        grad_t[None],
        gain_s,
        shift_s,
        gain_t,
        shift_t,
    )


def solution(mesh):
    clip_spec = P("dp", None, None, None, None)
    weight_spec = P("pipe", None, None)
    channel_spec = P("pipe", None)
    return jax.shard_map(
        body,
        mesh=mesh,
        in_specs=(
            clip_spec,
            P("dp", None),
            weight_spec,
            weight_spec,
            channel_spec,
            channel_spec,
            channel_spec,
            channel_spec,
            clip_spec,
        ),
        out_specs=(
            P("pipe", "dp", None, None, None, None),
            P("pipe", "dp", None, None, None, None),
            P("pipe", "dp", None),
            P("pipe", "dp", None),
            channel_spec,
            channel_spec,
            channel_spec,
            channel_spec,
        ),
        check_vma=False,
    )
```

```python
import functools

import jax
import jax.numpy as jnp
from jax import lax
from jax.experimental import pallas as pl
from jax.experimental.pallas import tpu as pltpu
from jax.sharding import PartitionSpec as P

MB = 4
eps_norm = 1e-05
bf16 = jnp.bfloat16
f32 = jnp.float32
MESH = pl.DeviceIdType.MESH


def silu(x):
    return x / (1.0 + jnp.exp(-x))


def silu_slope(x):
    s = 1.0 / (1.0 + jnp.exp(-x))
    return s * (1.0 + x * (1.0 - s))


def lane_chunks(width, body):
    def step(i, carry):
        body(i, pl.ds(pl.multiple_of(i * 128, 128), 128))
        return carry

    lax.fori_loop(0, width // 128, step, 0)


def relay_kernel(
    dims,
    clips,
    boxes,
    w_s_hbm,
    w_t_hbm,
    g_s,
    b_s,
    g_t,
    b_t,
    cotangent,
    o_act,
    o_grad,
    o_in,
    o_hidden,
    o_gu,
    o_gr,
    o_gain_s,
    o_shift_s,
    o_gain_t,
    o_shift_t,
    w_s,
    w_t,
    w_s_back,
    w_t_back,
    cols,
    a_in,
    skip_in,
    a_out,
    ga_in,
    gs_in,
    gs_out,
    ig_out,
    hidden,
    gr,
    gu,
    uh,
    rh,
    gp,
    gq,
    keep,
    fact_s,
    fact_t,
    cnt,
    x_s,
    x_t,
    x_bt,
    x_bs,
    x_send,
    x_recv,
    w_sem,
    load_sem,
    store_sem,
    pipe_send,
    pipe_recv,
    twin_send,
    twin_recv,
):
    cm, frames, height, width = dims
    rows = cm * frames * height * width
    d = a_in.shape[2]
    m_ch = hidden.shape[2]
    section = lax.axis_index("pipe")
    me = lax.axis_index("dp")
    n_pipe = lax.axis_size("pipe")
    n_dp = lax.axis_size("dp")
    first = section == 0
    last = section == n_pipe - 1
    odd = lax.rem(section, 2) == 1
    even_inner = jnp.logical_and(jnp.logical_not(odd), jnp.logical_not(last))
    skipping = odd.astype(f32)

    def load_ws(part, tap):
        half = d // 2
        src = w_s_hbm.at[pl.ds(tap * d + part * half, half)]
        dst = w_s.at[pl.ds((part * 9 + tap) * half, half)]
        return pltpu.make_async_copy(src, dst, w_sem.at[part * 9 + tap])

    load_wt = pltpu.make_async_copy(w_t_hbm, w_t, w_sem.at[18])

    def load_clip(m):
        return pltpu.make_async_copy(clips.at[m], a_in.at[m], load_sem.at[m])

    def load_cot(m):
        return pltpu.make_async_copy(cotangent.at[m], ga_in.at[m], load_sem.at[m])

    @pl.when(first)
    def _():
        for m in range(MB):
            load_clip(m).start()

    for part in range(2):
        for tap in range(9):
            load_ws(part, tap).start()
    load_wt.start()

    @pl.when(last)
    def _():
        for m in range(MB):
            load_cot(m).start()

    for ref in (o_gain_s, o_shift_s, o_gain_t, o_shift_t, skip_in, gs_in):
        ref[...] = jnp.zeros_like(ref)

    barrier = pltpu.get_barrier_semaphore()

    def greet(j, carry):
        pl.semaphore_signal(
            barrier, 1, device_id={"dp": lax.rem(me + j, n_dp)}, device_id_type=MESH
        )
        return carry

    lax.fori_loop(1, n_dp, greet, 0)

    @pl.when(jnp.logical_not(first))
    def _():
        pl.semaphore_signal(barrier, 1, device_id={"pipe": section - 1}, device_id_type=MESH)

    @pl.when(jnp.logical_not(last))
    def _():
        pl.semaphore_signal(barrier, 1, device_id={"pipe": section + 1}, device_id_type=MESH)

    def make_keep(m, carry):
        n_rows = frames * height * width
        pieces = []
        for c in range(cm):
            shape = (frames, height, width, 128)
            t = lax.broadcasted_iota(jnp.int32, shape, 0)
            h = lax.broadcasted_iota(jnp.int32, shape, 1)
            w = lax.broadcasted_iota(jnp.int32, shape, 2)
            box = [boxes[m * cm + c, i] for i in range(6)]
            inside = (t >= box[0]) & (t < box[1]) & (h >= box[2]) & (h < box[3])
            inside = inside & (w >= box[4]) & (w < box[5])
            pieces.append(jnp.where(inside, 1.0, 0.0).astype(f32).reshape(n_rows, 128))
        mask = jnp.concatenate(pieces, axis=0) if cm > 1 else pieces[0]
        keep[m] = mask
        cnt[m] = jnp.sum(mask, axis=0, keepdims=True)
        return carry

    lax.fori_loop(0, MB, make_keep, 0)
    pl.semaphore_wait(barrier, n_dp + 1 - jnp.where(first, 1, 0) - jnp.where(last, 1, 0))

    def share(kind, buf, m):
        def send(j, carry):
            pltpu.make_async_remote_copy(
                src_ref=buf.at[m, me],
                dst_ref=buf.at[m, me],
                send_sem=x_send.at[kind, m],
                recv_sem=x_recv.at[kind, m],
                device_id={"dp": lax.rem(me + j, n_dp)},
                device_id_type=MESH,
            ).start()
            return carry

        lax.fori_loop(1, n_dp, send, 0)

    def shared(kind, buf, m):
        others = buf.at[m, pl.ds(0, n_dp - 1)]
        pltpu.make_async_copy(others, others, x_send.at[kind, m]).wait()
        pltpu.make_async_copy(others, others, x_recv.at[kind, m]).wait()

    def to_pipe(kind, src, dst, m, step):
        return pltpu.make_async_remote_copy(
            src_ref=src.at[m],
            dst_ref=dst.at[m],
            send_sem=pipe_send.at[kind, m],
            recv_sem=pipe_recv.at[kind, m],
            device_id={"pipe": section + step},
            device_id_type=MESH,
        )

    half = d // 2

    def half_to_pipe(kind, part, src, dst, m, step):
        s = pl.ds(part * half, half)
        return pltpu.make_async_remote_copy(
            src_ref=src.at[m, :, s],
            dst_ref=dst.at[m, :, s],
            send_sem=pipe_send.at[kind + part, m],
            recv_sem=pipe_recv.at[kind + part, m],
            device_id={"pipe": section + step},
            device_id_type=MESH,
        )

    def store(kind, src, dst, m):
        return pltpu.make_async_copy(src.at[m], dst.at[m], store_sem.at[kind, m])

    def keep_operand(kind, src, dst, m):
        return pltpu.make_async_copy(src.at[m], dst.at[0, m], store_sem.at[kind, m])

    def twin_operand(kind, src, dst, m):
        return pltpu.make_async_remote_copy(
            src_ref=src.at[m],
            dst_ref=dst.at[1, m],
            send_sem=twin_send.at[kind - 2, m],
            recv_sem=twin_recv.at[kind - 2, m],
            device_id={"dp": me + 1 - 2 * lax.rem(me, 2)},
            device_id_type=MESH,
        )

    def share_operand(kind, src, dst, m):
        keep_operand(kind, src, dst, m).start()
        twin_operand(kind, src, dst, m).start()

    def shift_space(x, dh, dw):
        if dw:
            x = pltpu.roll(x, (-dw) % rows, 0)
        return shift_rows(x, dh)

    def shift_rows(x, dh):
        if not dh:
            return x
        y = x.reshape(cm * frames, height * width, 128)
        zero = jnp.zeros((cm * frames, width, 128), f32)
        if dh > 0:
            y = jnp.concatenate([y[:, width:], zero], axis=1)
        else:
            y = jnp.concatenate([zero, y[:, :-width]], axis=1)
        return y.reshape(rows, 128)

    def shift_time(x, dt):
        if not dt:
            return x
        y = x.reshape(cm, frames * height * width, 128)
        step = height * width
        zero = jnp.zeros((cm, step, 128), f32)
        if dt > 0:
            y = jnp.concatenate([y[:, step:], zero], axis=1)
        else:
            y = jnp.concatenate([zero, y[:, :-step]], axis=1)
        return y.reshape(rows, 128)

    def local_sums(m, value, buf, c, channels):
        mask = keep[m]
        n_here = cnt[m]
        total = jnp.sum(mask * value, axis=0, keepdims=True)
        dev = mask * (value - total / n_here)
        spread = jnp.sum(dev * dev, axis=0, keepdims=True)
        buf[m, me, :, pl.ds(pl.multiple_of(c * 128, 128), 128)] = total
        buf[m, me, :, pl.ds(pl.multiple_of(channels + c * 128, 128), 128)] = spread

    def merged(m, buf, c, channels):
        counts = buf[m, :, :, 2 * channels :]
        sums = buf[m, :, :, pl.ds(pl.multiple_of(c * 128, 128), 128)]
        spreads = buf[m, :, :, pl.ds(pl.multiple_of(channels + c * 128, 128), 128)]
        n = jnp.sum(counts, axis=0)
        mean = jnp.sum(sums, axis=0) / n
        off = sums / counts - mean[None]
        var = jnp.sum(spreads + counts * off * off, axis=0) / n
        return n, mean, lax.rsqrt(var + eps_norm)

    def forward_spatial(m):
        @pl.when(first)
        def _():
            load_clip(m).wait()

        for part in range(2):

            @pl.when(jnp.logical_not(first))
            def _():
                half_to_pipe(2, part, a_out, a_in, m, 1).wait_recv()

            def column(i, s):
                s = pl.ds(pl.multiple_of(part * half + i * 128, 128), 128)
                x = a_in[m, :, s].astype(f32)
                for dw in (-1, 0, 1):
                    y = shift_space(x, 0, dw)
                    for dh in (-1, 0, 1):
                        tap = (dh + 1) * 3 + dw + 1
                        at = part * 9 * half + tap * half + i * 128
                        cols[:, pl.ds(pl.multiple_of(at, 128), 128)] = shift_rows(y, dh).astype(
                            bf16
                        )

            lane_chunks(half, column)

            @pl.when((m == 0) & first)
            def _():
                for tap in range(9):
                    load_ws(part, tap).wait()

            k = slice(part * 9 * half, (part + 1) * 9 * half)
            value = jnp.dot(cols[:, k], w_s[k, :], preferred_element_type=f32)
            if part == 0:
                uh[m] = value
            else:
                uh[m] += value

        @pl.when(even_inner)
        def _():
            to_pipe(0, a_in, skip_in, m, 1).start()

        x_s[m, me, :, 2 * m_ch :] = cnt[m]
        lane_chunks(m_ch, lambda i, s: local_sums(m, uh[m, :, s], x_s, i, m_ch))
        share(0, x_s, m)
        share_operand(2, a_in, o_in, m)

    def forward_temporal(m):
        shared(0, x_s, m)

        def column(i, s):
            n, mean, rstd = merged(m, x_s, i, m_ch)
            fact_s[m, :, s] = rstd
            normed = (uh[m, :, s] - mean) * rstd
            uh[m, :, s] = normed
            value = keep[m] * silu(g_s[:, s] * normed + b_s[:, s])
            value = value.astype(bf16)
            hidden[m, :, s] = value
            value = value.astype(f32)
            for dt in (-1, 0, 1):
                at = pl.ds(pl.multiple_of((dt + 1) * m_ch + i * 128, 128), 128)
                cols[:, at] = shift_time(value, dt).astype(bf16)

        lane_chunks(m_ch, column)
        share_operand(3, hidden, o_hidden, m)

        @pl.when((m == 0) & first)
        def _():
            load_wt.wait()

        rh[m] = jnp.dot(cols[:, : 3 * m_ch], w_t[...], preferred_element_type=f32)
        x_t[m, me, :, 2 * d :] = cnt[m]
        lane_chunks(d, lambda i, s: local_sums(m, rh[m, :, s], x_t, i, d))
        share(1, x_t, m)

    def preact(m, s, normed):
        return g_t[:, s] * normed + b_t[:, s] + skipping * skip_in[m, :, s].astype(f32)

    def forward_out(m):
        shared(1, x_t, m)

        @pl.when(odd)
        def _():
            to_pipe(0, a_in, skip_in, m, 1).wait_recv()

        def column(i, s):
            n, mean, rstd = merged(m, x_t, i, d)
            fact_t[m, :, s] = rstd
            normed = (rh[m, :, s] - mean) * rstd
            rh[m, :, s] = normed
            a_out[m, :, s] = (keep[m] * silu(preact(m, s, normed))).astype(bf16)

        lane_chunks(d, column)

        @pl.when(jnp.logical_not(last))
        def _():
            for part in range(2):
                half_to_pipe(2, part, a_out, a_in, m, 1).start()

        store(0, a_out, o_act, m).start()

    def backward_in(m):
        @pl.when(last)
        def _():
            load_cot(m).wait()

        @pl.when(jnp.logical_not(last))
        def _():
            for part in range(2):
                half_to_pipe(4, part, ig_out, ga_in, m, -1).wait_recv()

        def column(i, s):
            normed = rh[m, :, s]
            slope = ga_in[m, :, s].astype(f32) * keep[m] * silu_slope(preact(m, s, normed))
            gp[lax.rem(m, 2), :, s] = slope
            gs_out[m, :, s] = slope.astype(bf16)
            x_bt[m, me, :, s] = jnp.sum(slope, axis=0, keepdims=True)
            at = pl.ds(pl.multiple_of(d + i * 128, 128), 128)
            x_bt[m, me, :, at] = jnp.sum(slope * normed, axis=0, keepdims=True)

        lane_chunks(d, column)
        share(2, x_bt, m)

        @pl.when(odd)
        def _():
            to_pipe(1, gs_out, gs_in, m, -1).start()

    def totals(buf, m, s, i, channels):
        at = pl.ds(pl.multiple_of(channels + i * 128, 128), 128)
        return jnp.sum(buf[m, :, :, s], axis=0), jnp.sum(buf[m, :, :, at], axis=0)

    def backward_temporal(m):
        shared(2, x_bt, m)
        n = jnp.sum(x_t[m, :, :, 2 * d :], axis=0)

        def column(i, s):
            shift_sum, gain_sum = totals(x_bt, m, s, i, d)
            o_shift_t[:, s] += shift_sum
            o_gain_t[:, s] += gain_sum
            scale = g_t[:, s] * fact_t[m, :, s]
            value = keep[m] * scale * (gp[lax.rem(m, 2), :, s] - (shift_sum + rh[m, :, s] * gain_sum) / n)
            value = value.astype(bf16)
            gr[m, :, s] = value
            value = value.astype(f32)
            for dt in (-1, 0, 1):
                at = pl.ds(pl.multiple_of((dt + 1) * d + i * 128, 128), 128)
                cols[:, at] = shift_time(value, -dt).astype(bf16)

        lane_chunks(d, column)
        share_operand(4, gr, o_gr, m)
        gq[lax.rem(m, 2)] = jnp.dot(cols[:, : 3 * d], w_t_back[...], preferred_element_type=f32)

        def sums(i, s):
            normed = uh[m, :, s]
            slope = keep[m] * gq[lax.rem(m, 2), :, s] * silu_slope(g_s[:, s] * normed + b_s[:, s])
            gq[lax.rem(m, 2), :, s] = slope
            x_bs[m, me, :, s] = jnp.sum(slope, axis=0, keepdims=True)
            at = pl.ds(pl.multiple_of(m_ch + i * 128, 128), 128)
            x_bs[m, me, :, at] = jnp.sum(slope * normed, axis=0, keepdims=True)

        lane_chunks(m_ch, sums)
        share(3, x_bs, m)

    def backward_spatial(m):
        shared(3, x_bs, m)
        n = jnp.sum(x_t[m, :, :, 2 * d :], axis=0)

        def column(i, s):
            shift_sum, gain_sum = totals(x_bs, m, s, i, m_ch)
            o_shift_s[:, s] += shift_sum
            o_gain_s[:, s] += gain_sum
            scale = g_s[:, s] * fact_s[m, :, s]
            value = keep[m] * scale * (gq[lax.rem(m, 2), :, s] - (shift_sum + uh[m, :, s] * gain_sum) / n)
            value = value.astype(bf16)
            gu[m, :, s] = value
            value = value.astype(f32)
            for dw in (-1, 0, 1):
                y = shift_space(value, 0, -dw)
                for dh in (-1, 0, 1):
                    tap = (dh + 1) * 3 + dw + 1
                    at = pl.ds(pl.multiple_of(tap * m_ch + i * 128, 128), 128)
                    cols[:, at] = shift_rows(y, -dh).astype(bf16)

        lane_chunks(m_ch, column)
        share_operand(5, gu, o_gu, m)

        @pl.when(even_inner)
        def _():
            to_pipe(1, gs_out, gs_in, m, -1).wait_recv()

        with_skip = even_inner.astype(f32)
        for part in range(2):
            s = slice(part * half, (part + 1) * half)
            value = jnp.dot(cols[...], w_s_back[:, s], preferred_element_type=f32)
            ig_out[m, :, s] = (value + with_skip * gs_in[m, :, s].astype(f32)).astype(bf16)

            @pl.when(jnp.logical_not(first))
            def _():
                half_to_pipe(4, part, ig_out, ga_in, m, -1).start()

        store(1, ig_out, o_grad, m).start()

    def turn_weights():
        @pl.when(jnp.logical_not(first))
        def _():
            for part in range(2):
                for tap in range(9):
                    load_ws(part, tap).wait()
            load_wt.wait()

        def spatial(tap, carry):
            dst = pl.ds(pl.multiple_of(tap * m_ch, 128), m_ch)
            for part in range(2):
                src = pl.ds(pl.multiple_of((part * 9 + tap) * half, 128), half)
                w_s_back[dst, part * half : (part + 1) * half] = w_s[src, :].T
            return carry

        lax.fori_loop(0, 9, spatial, 0)

        def temporal(tap, carry):
            src = pl.ds(pl.multiple_of(tap * m_ch, 128), m_ch)
            dst = pl.ds(pl.multiple_of(tap * d, 128), d)
            w_t_back[dst, :] = w_t[src, :].T
            return carry

        lax.fori_loop(0, 3, temporal, 0)

    pairs = MB // 2
    wait_back = jnp.where(last, 1, pairs)

    def step(s, carry):
        do_f = s < pairs
        do_b = jnp.logical_and(s >= wait_back, s < wait_back + pairs)
        mf = 2 * jnp.minimum(s, pairs - 1)
        mb = 2 * jnp.clip(s - wait_back, 0, pairs - 1)

        @pl.when(s == jnp.where(first, wait_back, 0))
        def _():
            turn_weights()

        def both(when, phase, m):
            @pl.when(when)
            def _():
                def one(j, c):
                    phase(m + j)
                    return c

                lax.fori_loop(0, 2, one, 0)

        both(do_b, backward_in, mb)
        both(do_f, forward_spatial, mf)
        both(do_b, backward_temporal, mb)
        both(do_f, forward_temporal, mf)
        both(do_b, backward_spatial, mb)
        both(do_f, forward_out, mf)
        return carry

    lax.fori_loop(0, 2 * pairs, step, 0)

    def finish(m, carry):
        store(0, a_out, o_act, m).wait()
        store(1, ig_out, o_grad, m).wait()
        for kind, src, dst in (
            (2, a_in, o_in),
            (3, hidden, o_hidden),
            (4, gr, o_gr),
            (5, gu, o_gu),
        ):
            keep_operand(kind, src, dst, m).wait()
            twin_operand(kind, src, dst, m).wait()

        @pl.when(jnp.logical_not(last))
        def _():
            for part in range(2):
                half_to_pipe(2, part, a_out, a_in, m, 1).wait_send()

        @pl.when(even_inner)
        def _():
            to_pipe(0, a_in, skip_in, m, 1).wait_send()

        @pl.when(jnp.logical_not(first))
        def _():
            for part in range(2):
                half_to_pipe(4, part, ig_out, ga_in, m, -1).wait_send()

        @pl.when(odd)
        def _():
            to_pipe(1, gs_out, gs_in, m, -1).wait_send()

        return carry

    lax.fori_loop(0, MB, finish, 0)


def relay(dims, n_dp, clips, boxes, w_s, w_t, g_s, b_s, g_t, b_t, cotangent):
    cm, frames, height, width = dims
    rows = cm * frames * height * width
    d, m_ch = w_t.shape[1], w_s.shape[1]
    shape = jax.ShapeDtypeStruct
    vmem = pl.BlockSpec(memory_space=pltpu.VMEM)
    hbm = pl.BlockSpec(memory_space=pl.ANY)
    smem = pl.BlockSpec(memory_space=pltpu.SMEM)
    dma = pltpu.SemaphoreType.DMA
    narrow = pltpu.VMEM((MB, rows, d), bf16)
    wide = pltpu.VMEM((MB, rows, m_ch), bf16)
    return pl.pallas_call(
        functools.partial(relay_kernel, dims),
        out_shape=(
            shape((MB, rows, d), bf16),
            shape((MB, rows, d), bf16),
            shape((2, MB, rows, d), bf16),
            shape((2, MB, rows, m_ch), bf16),
            shape((2, MB, rows, m_ch), bf16),
            shape((2, MB, rows, d), bf16),
            shape((1, m_ch), f32),
            shape((1, m_ch), f32),
            shape((1, d), f32),
            shape((1, d), f32),
        ),
        in_specs=[hbm, smem, hbm, hbm, vmem, vmem, vmem, vmem, hbm],
        out_specs=[hbm] * 6 + [vmem] * 4,
        scratch_shapes=[
            pltpu.VMEM(w_s.shape, bf16),
            pltpu.VMEM(w_t.shape, bf16),
            pltpu.VMEM((9 * m_ch, d), bf16),
            pltpu.VMEM((3 * d, m_ch), bf16),
            pltpu.VMEM((rows, 9 * m_ch), bf16),
            narrow,
            narrow,
            narrow,
            narrow,
            narrow,
            narrow,
            narrow,
            wide,
            narrow,
            wide,
            pltpu.VMEM((MB, rows, m_ch), f32),
            pltpu.VMEM((MB, rows, d), f32),
            pltpu.VMEM((2, rows, d), f32),
            pltpu.VMEM((2, rows, m_ch), f32),
            pltpu.VMEM((MB, rows, 128), f32),
            pltpu.VMEM((MB, 1, m_ch), f32),
            pltpu.VMEM((MB, 1, d), f32),
            pltpu.VMEM((MB, 1, 128), f32),
            pltpu.VMEM((MB, n_dp, 1, 2 * m_ch + 128), f32),
            pltpu.VMEM((MB, n_dp, 1, 2 * d + 128), f32),
            pltpu.VMEM((MB, n_dp, 1, 2 * d), f32),
            pltpu.VMEM((MB, n_dp, 1, 2 * m_ch), f32),
            dma((4, MB)),
            dma((4, MB)),
            dma((19,)),
            dma((MB,)),
            dma((6, MB)),
            dma((6, MB)),
            dma((6, MB)),
            dma((4, MB)),
            dma((4, MB)),
        ],
        compiler_params=pltpu.CompilerParams(
            collective_id=0, has_side_effects=True, vmem_limit_bytes=62 * 2**20
        ),
    )(clips, boxes, w_s, w_t, g_s, b_s, g_t, b_t, cotangent)


def send_order(n, z, q):
    table = []
    for here in range(n):
        sign = 1 if here < n / 2 else -1
        table.append(sorted(range(n), key=lambda to: (-abs(to - here), -sign * to)))
    dest = 0
    for here in range(n):
        for at in range(n):
            dest = dest + jnp.where((z == here) & (q == at), table[here][at], 0)
    return dest


def gradient_kernel(
    dims,
    a_hbm,
    v_hbm,
    gu_hbm,
    gr_hbm,
    o_s,
    o_t,
    a,
    v,
    gu,
    gr,
    window,
    acc_s,
    acc_t,
    got_s,
    got_t,
    out_s,
    out_t,
    load_sem,
    send_sem,
    recv_sem,
):
    frames, height, width = dims
    n_clips, rows, d = a_hbm.shape
    m_ch = v_hbm.shape[2]
    me = lax.axis_index("dp")
    n = lax.axis_size("dp") // 2
    z = lax.div(me, 2)
    core = lax.rem(me, 2)
    rows_s, rows_t = o_s.shape[0], o_t.shape[0]
    piece = got_s.shape[3]
    n_pieces = m_ch // piece
    span = acc_s.shape[0]

    barrier = pltpu.get_barrier_semaphore()

    @pl.when(z > 0)
    def _():
        pl.semaphore_signal(barrier, 1, device_id={"dp": me - 2}, device_id_type=MESH)

    @pl.when(z < n - 1)
    def _():
        pl.semaphore_signal(barrier, 1, device_id={"dp": me + 2}, device_id_type=MESH)

    loads = [
        pltpu.make_async_copy(src, dst, load_sem.at[i])
        for i, (src, dst) in enumerate(((a_hbm, a), (gu_hbm, gu), (v_hbm, v), (gr_hbm, gr)))
    ]
    for copy in loads:
        copy.start()
    pl.semaphore_wait(barrier, 2 - jnp.where(z == 0, 1, 0) - jnp.where(z == n - 1, 1, 0))
    loads[0].wait()

    def moved(x, before, after, dt, step):
        if not dt:
            return x
        y = x.reshape(before, after, 128)
        zero = jnp.zeros((before, step, 128), f32)
        if dt > 0:
            y = jnp.concatenate([y[:, step:], zero], axis=1)
        else:
            y = jnp.concatenate([zero, y[:, :-step]], axis=1)
        return y.reshape(rows, 128)

    def transfer(src, dst, dest, p):
        right = dest > z
        slot = dest + jnp.where(right, 1, 0)
        return pltpu.make_async_remote_copy(
            src_ref=src,
            dst_ref=dst(slot),
            send_sem=send_sem.at[dest, p],
            recv_sem=recv_sem.at[slot, p],
            device_id={"dp": me + jnp.where(right, 2, -2)},
            device_id_type=MESH,
        )

    def settle(dest, acc, start, size, got, out, final, p):
        at = pl.ds(pl.multiple_of(start, 8), size)
        from_left = (z > 0) & (dest >= z)
        from_right = (z < n - 1) & (dest <= z)

        @pl.when(from_left)
        def _():
            ref = got(dest + 1)
            pltpu.make_async_copy(ref, ref, recv_sem.at[dest + 1, p]).wait()
            acc[at, :] += ref[...].astype(f32)

        @pl.when(from_right)
        def _():
            ref = got(dest)
            pltpu.make_async_copy(ref, ref, recv_sem.at[dest, p]).wait()
            acc[at, :] += ref[...].astype(f32)

        @pl.when(dest == z)
        def _():
            final[...] = acc[at, :]

        @pl.when(dest != z)
        def _():
            ref = out(dest)
            ref[...] = acc[at, :].astype(bf16)
            transfer(ref, got, dest, p).start()

    def place(row0):
        low = lax.div(row0, 128)
        return low, row0 - low * 128

    def job(q, carry):
        dest = send_order(n, z, q)
        owner = 2 * dest + core

        low, start = place(owner * rows_s)

        def fill_space(i, c):
            to = pl.ds(pl.multiple_of(i * rows, 16), rows)
            for j in range(span // 128):
                chunk = jnp.minimum(low + j, 9 * d // 128 - 1)
                tap = lax.div(chunk, d // 128)
                lane = pl.ds(pl.multiple_of((chunk - tap * (d // 128)) * 128, 128), 128)

                def fill(dh, dw):
                    x = a[i, :, lane].astype(f32)
                    if dw:
                        x = pltpu.roll(x, (-dw) % rows, 0)
                    x = moved(x, frames, height * width, dh, width)
                    window[to, j * 128 : (j + 1) * 128] = x.astype(bf16)

                lax.switch(
                    tap,
                    [
                        functools.partial(fill, dh, dw)
                        for dh in (-1, 0, 1)
                        for dw in (-1, 0, 1)
                    ],
                )
            return c

        lax.fori_loop(0, n_clips, fill_space, 0)

        @pl.when(q == 0)
        def _():
            loads[1].wait()


        def space(p, c):
            s = pl.ds(pl.multiple_of(p * piece, 128), piece)
            acc_s[...] = lax.dot_general(
                window[...],
                gu[:, :, s].reshape(n_clips * rows, piece),
                (((0,), (0,)), ((), ())), preferred_element_type=f32
            )
            settle(
                dest,
                acc_s,
                start,
                rows_s,
                lambda slot: got_s.at[slot, p],
                lambda to: out_s.at[to, p],
                o_s.at[:, s],
                p,
            )
            return c

        lax.fori_loop(0, n_pieces, space, 0)

        low_t, start_t = place(owner * rows_t)

        def fill_time(i, c):
            to = pl.ds(pl.multiple_of(i * rows, 16), rows)
            for j in range(span // 128):
                chunk = jnp.minimum(low_t + j, 3 * m_ch // 128 - 1)
                tap = lax.div(chunk, m_ch // 128)
                lane = pl.ds(pl.multiple_of((chunk - tap * (m_ch // 128)) * 128, 128), 128)

                def fill(dt):
                    x = v[i, :, lane].astype(f32)
                    x = moved(x, 1, rows, dt, height * width)
                    window[to, j * 128 : (j + 1) * 128] = x.astype(bf16)

                lax.switch(tap, [functools.partial(fill, dt) for dt in (-1, 0, 1)])
            return c

        @pl.when(q == 0)
        def _():
            loads[2].wait()
            loads[3].wait()

        lax.fori_loop(0, n_clips, fill_time, 0)
        acc_t[...] = lax.dot_general(
            window[...],
            gr[...].reshape(n_clips * rows, d),
            (((0,), (0,)), ((), ())), preferred_element_type=f32
        )
        settle(
            dest,
            acc_t,
            start_t,
            rows_t,
            lambda slot: got_t.at[slot],
            lambda to: out_t.at[to],
            o_t,
            n_pieces,
        )
        return carry

    lax.fori_loop(0, n, job, 0)

    def finish(q, carry):
        dest = send_order(n, z, q)
        for p in range(n_pieces):
            transfer(out_s.at[dest, p], lambda slot: got_s.at[slot, p], dest, p).wait_send()
        transfer(out_t.at[dest], lambda slot: got_t.at[slot], dest, n_pieces).wait_send()
        return carry

    lax.fori_loop(0, n - 1, finish, 0)


def gradients(dims, n_dp, a, v, gu, gr):
    n_clips, rows, d = a.shape
    m_ch = v.shape[2]
    rows_s, rows_t = 9 * d // n_dp, 3 * m_ch // n_dp
    n = n_dp // 2
    piece = 384
    n_pieces = m_ch // piece
    span = 640
    shape = jax.ShapeDtypeStruct
    dma = pltpu.SemaphoreType.DMA
    return pl.pallas_call(
        functools.partial(gradient_kernel, dims),
        out_shape=(shape((rows_s, m_ch), f32), shape((rows_t, d), f32)),
        in_specs=[pl.BlockSpec(memory_space=pl.ANY)] * 4,
        out_specs=[pl.BlockSpec(memory_space=pltpu.VMEM)] * 2,
        scratch_shapes=[
            pltpu.VMEM(a.shape, bf16),
            pltpu.VMEM(v.shape, bf16),
            pltpu.VMEM(gu.shape, bf16),
            pltpu.VMEM(gr.shape, bf16),
            pltpu.VMEM((n_clips * rows, span), bf16),
            pltpu.VMEM((span, piece), f32),
            pltpu.VMEM((span, d), f32),
            pltpu.VMEM((n + 1, n_pieces, rows_s, piece), bf16),
            pltpu.VMEM((n + 1, rows_t, d), bf16),
            pltpu.VMEM((n, n_pieces, rows_s, piece), bf16),
            pltpu.VMEM((n, rows_t, d), bf16),
            dma((4,)),
            dma((n, n_pieces + 1)),
            dma((n + 1, n_pieces + 1)),
        ],
        compiler_params=pltpu.CompilerParams(
            collective_id=1, has_side_effects=True, vmem_limit_bytes=40 * 2**20
        ),
    )(a, v, gu, gr)


def spatial_columns(activity):
    height, breadth = (activity.shape[2], activity.shape[3])
    padded = jnp.pad(activity, ((0, 0), (0, 0), (1, 1), (1, 1), (0, 0)))
    pieces = [
        padded[:, :, row_off : row_off + height, col_off : col_off + breadth, :]
        for row_off in range(3)
        for col_off in range(3)
    ]
    return jnp.concatenate(pieces, axis=-1)


def temporal_columns(activity):
    frames = activity.shape[1]
    padded = jnp.pad(activity, ((0, 0), (1, 1), (0, 0), (0, 0), (0, 0)))
    return jnp.concatenate([padded[:, offset : offset + frames] for offset in range(3)], axis=-1)


def left_product(former, latter):
    return lax.dot_general(
        former, latter, (((0,), (0,)), ((), ())), preferred_element_type=jnp.float32
    )


def body(
    clips,
    boxes,
    spatial_w,
    temporal_w,
    spatial_gain,
    spatial_shift,
    temporal_gain,
    temporal_shift,
    cotangent,
):
    n_clips, frames, height, breadth, d = clips.shape
    cm = n_clips // MB
    width = (breadth // 8 + 1) * 8
    rows = cm * frames * height * width
    m_ch = spatial_w.shape[2]

    def padded(x):
        x = jnp.pad(x, ((0, 0), (0, 0), (0, 0), (0, width - breadth), (0, 0)))
        return x.reshape(MB, rows, d)

    act, grad, a_in, hidden, gu, gr, gain_s, shift_s, gain_t, shift_t = relay(
        (cm, frames, height, width),
        lax.axis_size("dp"),
        padded(clips),
        boxes,
        spatial_w[0],
        temporal_w[0],
        spatial_gain,
        spatial_shift,
        temporal_gain,
        temporal_shift,
        padded(cotangent),
    )

    def frames_of(x):
        return x.reshape(n_clips, frames, height, width, x.shape[-1])[:, :, :, :breadth]

    n_dp = lax.axis_size("dp")
    rows_s, rows_t = 9 * d // n_dp, 3 * m_ch // n_dp
    if rows_s % 64 == 0 and rows_t % 16 == 0 and rows_s <= 576 and rows_t <= 528 and n_dp <= 8:
        clip_rows = frames * height * width
        grad_s, grad_t = gradients(
            (frames, height, width),
            n_dp,
            *[x.reshape(2 * n_clips, clip_rows, x.shape[-1]) for x in (a_in, hidden, gu, gr)],
        )
    else:
        cells = n_clips * frames * height * breadth
        cols = spatial_columns(frames_of(a_in[0])).reshape(cells, -1)
        grad_s = left_product(cols, frames_of(gu[0]).reshape(cells, -1))
        stacked = temporal_columns(frames_of(hidden[0])).reshape(cells, -1)
        grad_t = left_product(stacked, frames_of(gr[0]).reshape(cells, -1))
        grad_s = lax.psum_scatter(grad_s, "dp", scatter_dimension=0, tiled=True)
        grad_t = lax.psum_scatter(grad_t, "dp", scatter_dimension=0, tiled=True)
    return (
        frames_of(act)[None],
        frames_of(grad)[None],
        grad_s[None],
        grad_t[None],
        gain_s,
        shift_s,
        gain_t,
        shift_t,
    )


def solution(mesh):
    clip_spec = P("dp", None, None, None, None)
    weight_spec = P("pipe", None, None)
    channel_spec = P("pipe", None)
    return jax.shard_map(
        body,
        mesh=mesh,
        in_specs=(
            clip_spec,
            P("dp", None),
            weight_spec,
            weight_spec,
            channel_spec,
            channel_spec,
            channel_spec,
            channel_spec,
            clip_spec,
        ),
        out_specs=(
            P("pipe", "dp", None, None, None, None),
            P("pipe", "dp", None, None, None, None),
            P("pipe", "dp", None),
            P("pipe", "dp", None),
            channel_spec,
            channel_spec,
            channel_spec,
            channel_spec,
        ),
        check_vma=False,
    )
```

```python
import functools

import jax
import jax.numpy as jnp
from jax import lax
from jax.experimental import pallas as pl
from jax.experimental.pallas import tpu as pltpu
from jax.sharding import PartitionSpec as P

MB = 4
eps_norm = 1e-05
bf16 = jnp.bfloat16
f32 = jnp.float32
MESH = pl.DeviceIdType.MESH


def silu(x):
    return x / (1.0 + jnp.exp(-x))


def silu_slope(x):
    s = 1.0 / (1.0 + jnp.exp(-x))
    return s * (1.0 + x * (1.0 - s))


def lane_chunks(width, body):
    def step(i, carry):
        body(i, pl.ds(pl.multiple_of(i * 128, 128), 128))
        return carry

    lax.fori_loop(0, width // 128, step, 0)


def relay_kernel(
    dims,
    clips,
    boxes,
    w_s_hbm,
    w_t_hbm,
    g_s,
    b_s,
    g_t,
    b_t,
    cotangent,
    o_act,
    o_grad,
    o_in,
    o_hidden,
    o_gu,
    o_gr,
    o_gain_s,
    o_shift_s,
    o_gain_t,
    o_shift_t,
    w_s,
    w_t,
    w_s_back,
    w_t_back,
    cols,
    a_in,
    skip_in,
    a_out,
    r_in,
    r_out,
    ga_in,
    gs_in,
    gs_out,
    ig_out,
    hidden,
    gr,
    gu,
    uh,
    r_sum,
    gq,
    keep,
    fact_s,
    fact_t,
    off_t,
    fact_p,
    off_p,
    cnt,
    scale_out,
    scale_in,
    x_s,
    x_t,
    x_p,
    x_bt,
    x_bs,
    x_bp,
    x_send,
    x_recv,
    w_sem,
    load_sem,
    store_sem,
    pipe_send,
    pipe_recv,
    twin_send,
    twin_recv,
):
    cm, frames, height, width = dims
    rows = cm * frames * height * width
    d = a_in.shape[2]
    m_ch = hidden.shape[2]
    section = lax.axis_index("pipe")
    me = lax.axis_index("dp")
    n_pipe = lax.axis_size("pipe")
    n_dp = lax.axis_size("dp")
    first = section == 0
    last = section == n_pipe - 1
    odd = lax.rem(section, 2) == 1
    even_inner = jnp.logical_and(jnp.logical_not(odd), jnp.logical_not(last))
    early = section < 2
    skip_own = odd.astype(f32)
    skip_prev = jnp.logical_not(jnp.logical_or(odd, first)).astype(f32)

    def load_ws(part, tap):
        half = d // 2
        src = w_s_hbm.at[pl.ds(tap * d + part * half, half)]
        dst = w_s.at[pl.ds((part * 9 + tap) * half, half)]
        return pltpu.make_async_copy(src, dst, w_sem.at[part * 9 + tap])

    load_wt = pltpu.make_async_copy(w_t_hbm, w_t, w_sem.at[18])

    def load_clip(m):
        return pltpu.make_async_copy(clips.at[m], a_in.at[m], load_sem.at[m])

    def load_cot(m):
        return pltpu.make_async_copy(cotangent.at[m], ga_in.at[m], load_sem.at[m])

    def load_skip(m):
        return pltpu.make_async_copy(clips.at[m], skip_in.at[m], load_sem.at[m])

    local_skip = jnp.logical_not(jnp.logical_or(first, last))

    @pl.when(first)
    def _():
        for m in range(MB):
            load_clip(m).start()

    @pl.when(local_skip)
    def _():
        for m in range(MB):
            load_skip(m).start()

    for part in range(2):
        for tap in range(9):
            load_ws(part, tap).start()
    load_wt.start()

    @pl.when(last)
    def _():
        for m in range(MB):
            load_cot(m).start()

    for ref in (o_gain_s, o_shift_s, o_gain_t, o_shift_t, gs_in, scale_in):
        ref[...] = jnp.zeros_like(ref)

    @pl.when(first)
    def _():
        skip_in[...] = jnp.zeros_like(skip_in)

    barrier = pltpu.get_barrier_semaphore()

    def greet(j, carry):
        pl.semaphore_signal(
            barrier, 1, device_id={"dp": lax.rem(me + j, n_dp)}, device_id_type=MESH
        )
        return carry

    lax.fori_loop(1, n_dp, greet, 0)

    def greet_pipe(step):
        def greet_one(j, carry):
            pl.semaphore_signal(
                barrier,
                1,
                device_id={"pipe": section + step, "dp": j},
                device_id_type=MESH,
            )
            return carry

        lax.fori_loop(0, n_dp, greet_one, 0)

    @pl.when(jnp.logical_not(first))
    def _():
        greet_pipe(-1)

    @pl.when(jnp.logical_not(last))
    def _():
        greet_pipe(1)

    pl.semaphore_signal(
        barrier,
        1,
        device_id={"pipe": section + jnp.where(early, 2, -2)},
        device_id_type=MESH,
    )
    scale_out[0] = g_t[...]
    scale_out[1] = b_t[...]

    def make_keep(m, carry):
        n_rows = frames * height * width
        pieces = []
        for c in range(cm):
            shape = (frames, height, width, 128)
            t = lax.broadcasted_iota(jnp.int32, shape, 0)
            h = lax.broadcasted_iota(jnp.int32, shape, 1)
            w = lax.broadcasted_iota(jnp.int32, shape, 2)
            box = [boxes[m * cm + c, i] for i in range(6)]
            inside = (t >= box[0]) & (t < box[1]) & (h >= box[2]) & (h < box[3])
            inside = inside & (w >= box[4]) & (w < box[5])
            pieces.append(jnp.where(inside, 1.0, 0.0).astype(f32).reshape(n_rows, 128))
        mask = jnp.concatenate(pieces, axis=0) if cm > 1 else pieces[0]
        keep[m] = mask
        cnt[m] = jnp.sum(mask, axis=0, keepdims=True)
        return carry

    lax.fori_loop(0, MB, make_keep, 0)
    sides = 3 - jnp.where(first, 1, 0) - jnp.where(last, 1, 0)
    pl.semaphore_wait(barrier, sides * n_dp)

    def send_scale():
        return pltpu.make_async_remote_copy(
            src_ref=scale_out,
            dst_ref=scale_in,
            send_sem=w_sem.at[19],
            recv_sem=w_sem.at[20],
            device_id={"pipe": section + 1},
            device_id_type=MESH,
        )

    @pl.when(jnp.logical_not(last))
    def _():
        send_scale().start()

    def share(kind, buf, m):
        def send(j, carry):
            pltpu.make_async_remote_copy(
                src_ref=buf.at[m, me],
                dst_ref=buf.at[m, me],
                send_sem=x_send.at[kind, m],
                recv_sem=x_recv.at[kind, m],
                device_id={"dp": lax.rem(me + j, n_dp)},
                device_id_type=MESH,
            ).start()
            return carry

        lax.fori_loop(1, n_dp, send, 0)

    def shared(kind, buf, m):
        others = buf.at[m, pl.ds(0, n_dp - 1)]
        pltpu.make_async_copy(others, others, x_send.at[kind, m]).wait()
        pltpu.make_async_copy(others, others, x_recv.at[kind, m]).wait()

    def cross(kind, src, dst, m, step):
        def send(j, carry):
            pltpu.make_async_remote_copy(
                src_ref=src,
                dst_ref=dst.at[m, me],
                send_sem=x_send.at[kind, m],
                recv_sem=x_recv.at[kind, m],
                device_id={"pipe": section + step, "dp": lax.rem(me + j, n_dp)},
                device_id_type=MESH,
            ).start()
            return carry

        lax.fori_loop(0, n_dp, send, 0)

    def crossed(kind, buf, m):
        slots = buf.at[m]
        pltpu.make_async_copy(slots, slots, x_recv.at[kind, m]).wait()

    def cross_sent(kind, buf, m):
        slots = buf.at[m]
        pltpu.make_async_copy(slots, slots, x_send.at[kind, m]).wait()

    def to_pipe(kind, src, dst, m, step):
        return pltpu.make_async_remote_copy(
            src_ref=src.at[m],
            dst_ref=dst.at[m],
            send_sem=pipe_send.at[kind, m],
            recv_sem=pipe_recv.at[kind, m],
            device_id={"pipe": section + step},
            device_id_type=MESH,
        )

    half = d // 2

    def half_to_pipe(kind, part, src, dst, m, step):
        s = pl.ds(part * half, half)
        return pltpu.make_async_remote_copy(
            src_ref=src.at[m, :, s],
            dst_ref=dst.at[m, :, s],
            send_sem=pipe_send.at[kind + part, m],
            recv_sem=pipe_recv.at[kind + part, m],
            device_id={"pipe": section + step},
            device_id_type=MESH,
        )

    def store(kind, src, dst, m):
        return pltpu.make_async_copy(src.at[m], dst.at[m], store_sem.at[kind, m])

    def keep_operand(kind, src, dst, m):
        return pltpu.make_async_copy(src.at[m], dst.at[0, m], store_sem.at[kind, m])

    def twin_operand(kind, src, dst, m):
        return pltpu.make_async_remote_copy(
            src_ref=src.at[m],
            dst_ref=dst.at[1, m],
            send_sem=twin_send.at[kind - 2, m],
            recv_sem=twin_recv.at[kind - 2, m],
            device_id={"dp": me + 1 - 2 * lax.rem(me, 2)},
            device_id_type=MESH,
        )

    def share_operand(kind, src, dst, m):
        keep_operand(kind, src, dst, m).start()
        twin_operand(kind, src, dst, m).start()

    def shift_space(x, dh, dw):
        if dw:
            x = pltpu.roll(x, (-dw) % rows, 0)
        return shift_rows(x, dh)

    def shift_rows(x, dh):
        if not dh:
            return x
        y = x.reshape(cm * frames, height * width, 128)
        zero = jnp.zeros((cm * frames, width, 128), f32)
        if dh > 0:
            y = jnp.concatenate([y[:, width:], zero], axis=1)
        else:
            y = jnp.concatenate([zero, y[:, :-width]], axis=1)
        return y.reshape(rows, 128)

    def shift_time(x, dt):
        if not dt:
            return x
        y = x.reshape(cm, frames * height * width, 128)
        step = height * width
        zero = jnp.zeros((cm, step, 128), f32)
        if dt > 0:
            y = jnp.concatenate([y[:, step:], zero], axis=1)
        else:
            y = jnp.concatenate([zero, y[:, :-step]], axis=1)
        return y.reshape(rows, 128)

    def local_sums(m, value, buf, c, channels):
        mask = keep[m]
        n_here = cnt[m]
        total = jnp.sum(mask * value, axis=0, keepdims=True)
        dev = mask * (value - total / n_here)
        spread = jnp.sum(dev * dev, axis=0, keepdims=True)
        buf[m, me, :, pl.ds(pl.multiple_of(c * 128, 128), 128)] = total
        buf[m, me, :, pl.ds(pl.multiple_of(channels + c * 128, 128), 128)] = spread
        return dev

    def merged(m, buf, c, channels):
        counts = buf[m, :, :, 2 * channels :]
        sums = buf[m, :, :, pl.ds(pl.multiple_of(c * 128, 128), 128)]
        spreads = buf[m, :, :, pl.ds(pl.multiple_of(channels + c * 128, 128), 128)]
        n = jnp.sum(counts, axis=0)
        mean = jnp.sum(sums, axis=0) / n
        off = sums / counts - mean[None]
        var = jnp.sum(spreads + counts * off * off, axis=0) / n
        return n, mean, lax.rsqrt(var + eps_norm)

    def lanes_of(part, i):
        return pl.ds(pl.multiple_of(part * half + i * 128, 128), 128)

    def normed_prev(m, s):
        return (r_in[m, :, s].astype(f32) + off_p[m, :, s]) * fact_p[m, :, s]

    def preact_prev(m, s, normed):
        return scale_in[0, :, s] * normed + scale_in[1, :, s]

    def skipped_prev(m, s, value):
        return value + skip_prev * skip_in[m, :, s].astype(f32)

    def activate(m, part, i, s):
        s = lanes_of(part, i)
        n, mean, rstd = merged(m, x_p, part * (half // 128) + i, d)
        off_p[m, :, s] = x_p[m, me, :, s] / x_p[m, me, :, 2 * d :] - mean
        fact_p[m, :, s] = rstd
        value = preact_prev(m, s, normed_prev(m, s))

        @pl.when(section == 2)
        def _():
            a_in[m, :, s] = (keep[m] * silu(skipped_prev(m, s, value))).astype(bf16)

        @pl.when(section != 2)
        def _():
            a_in[m, :, s] = (keep[m] * silu(value)).astype(bf16)

    def forward_spatial(m):
        @pl.when(first)
        def _():
            load_clip(m).wait()

        @pl.when(jnp.logical_not(first))
        def _():
            @pl.when(m == 0)
            def _():
                send_scale().wait_recv()

            @pl.when(local_skip)
            def _():
                load_skip(m).wait()

            crossed(4, x_p, m)

        for part in range(2):

            @pl.when(jnp.logical_not(first))
            def _():
                half_to_pipe(2, part, r_out, r_in, m, 1).wait_recv()
                lane_chunks(half, functools.partial(activate, m, part))

            def column(i, s):
                s = pl.ds(pl.multiple_of(part * half + i * 128, 128), 128)
                x = a_in[m, :, s].astype(f32)
                for dw in (-1, 0, 1):
                    y = shift_space(x, 0, dw)
                    for dh in (-1, 0, 1):
                        tap = (dh + 1) * 3 + dw + 1
                        at = part * 9 * half + tap * half + i * 128
                        cols[:, pl.ds(pl.multiple_of(at, 128), 128)] = shift_rows(y, dh).astype(
                            bf16
                        )

            lane_chunks(half, column)

            @pl.when((m == 0) & first)
            def _():
                for tap in range(9):
                    load_ws(part, tap).wait()

            k = slice(part * 9 * half, (part + 1) * 9 * half)
            for s in (slice(0, 512), slice(512, m_ch)):
                value = jnp.dot(cols[:, k], w_s[k, s], preferred_element_type=f32)
                if part == 0:
                    uh[m, :, s] = value
                else:
                    uh[m, :, s] += value

        x_s[m, me, :, 2 * m_ch :] = cnt[m]

        def sums(i, s):
            local_sums(m, uh[m, :, s], x_s, i, m_ch)

        lane_chunks(m_ch, sums)
        share(0, x_s, m)
        share_operand(2, a_in, o_in, m)

    def forward_temporal(m):
        shared(0, x_s, m)

        def column(i, s):
            n, mean, rstd = merged(m, x_s, i, m_ch)
            fact_s[m, :, s] = rstd
            normed = (uh[m, :, s] - mean) * rstd
            uh[m, :, s] = normed
            value = keep[m] * silu(g_s[:, s] * normed + b_s[:, s])
            value = value.astype(bf16)
            hidden[m, :, s] = value
            value = value.astype(f32)
            for dt in (-1, 0, 1):
                at = pl.ds(pl.multiple_of((dt + 1) * m_ch + i * 128, 128), 128)
                cols[:, at] = shift_time(value, dt).astype(bf16)

        lane_chunks(m_ch, column)
        share_operand(3, hidden, o_hidden, m)

        @pl.when((m == 0) & first)
        def _():
            load_wt.wait()

        r_sum[...] = jnp.dot(cols[:, : 3 * m_ch], w_t[...], preferred_element_type=f32)
        x_t[m, me, :, 2 * d :] = cnt[m]

        def centre(i, s):
            r_out[m, :, s] = local_sums(m, r_sum[:, s], x_t, i, d).astype(bf16)

        lane_chunks(d, centre)

        @pl.when(jnp.logical_not(last))
        def _():
            cross(4, x_t.at[m, me], x_p, m, 1)
            for part in range(2):
                half_to_pipe(2, part, r_out, r_in, m, 1).start()

        share(1, x_t, m)

    def normed_own(m, s):
        return (r_out[m, :, s].astype(f32) + off_t[m, :, s]) * fact_t[m, :, s]

    def preact_own(m, s, normed):
        return g_t[:, s] * normed + b_t[:, s] + skip_own * skip_in[m, :, s].astype(f32)

    def forward_out(m):
        @pl.when(last)
        def _():
            to_pipe(0, a_out, skip_in, m, 2).wait_recv()

        shared(1, x_t, m)

        def column(i, s):
            n, mean, rstd = merged(m, x_t, i, d)
            off_t[m, :, s] = x_t[m, me, :, s] / cnt[m] - mean
            fact_t[m, :, s] = rstd
            value = keep[m] * silu(preact_own(m, s, normed_own(m, s)))
            a_out[m, :, s] = value.astype(bf16)

        lane_chunks(d, column)
        store(0, a_out, o_act, m).start()

        @pl.when(section == 1)
        def _():
            to_pipe(0, a_out, skip_in, m, 2).start()

    def slope_sums(row, value, normed, i, s):
        row[:, s] = jnp.sum(value, axis=0, keepdims=True)
        at = pl.ds(pl.multiple_of(d + i * 128, 128), 128)
        row[:, at] = jnp.sum(value * normed, axis=0, keepdims=True)

    def own_slope(m, s, normed):
        return ga_in[m, :, s].astype(f32) * keep[m] * silu_slope(preact_own(m, s, normed))

    def backward_in(m):
        load_cot(m).wait()

        def column(i, s):
            normed = normed_own(m, s)
            slope_sums(x_bt.at[m, me], own_slope(m, s, normed), normed, i, s)

        lane_chunks(d, column)
        share(2, x_bt, m)

    def totals(buf, m, s, i, channels):
        at = pl.ds(pl.multiple_of(channels + i * 128, 128), 128)
        return jnp.sum(buf[m, :, :, s], axis=0), jnp.sum(buf[m, :, :, at], axis=0)

    def backward_temporal(m):
        @pl.when(last)
        def _():
            shared(2, x_bt, m)

        @pl.when(jnp.logical_not(last))
        def _():
            crossed(2, x_bt, m)
            for part in range(2):
                half_to_pipe(4, part, ig_out, ga_in, m, -1).wait_recv()

        n = jnp.sum(x_t[m, :, :, 2 * d :], axis=0)

        def column(i, s):
            shift_sum, gain_sum = totals(x_bt, m, s, i, d)
            o_shift_t[:, s] += shift_sum
            o_gain_t[:, s] += gain_sum
            normed = normed_own(m, s)
            slope = own_slope(m, s, normed)

            @pl.when(last)
            def _():
                gs_out[m, :, s] = slope.astype(bf16)

            scale = g_t[:, s] * fact_t[m, :, s]
            value = keep[m] * scale * (slope - (shift_sum + normed * gain_sum) / n)
            value = value.astype(bf16)
            gr[m, :, s] = value
            value = value.astype(f32)
            for dt in (-1, 0, 1):
                at = pl.ds(pl.multiple_of((dt + 1) * d + i * 128, 128), 128)
                cols[:, at] = shift_time(value, -dt).astype(bf16)

        lane_chunks(d, column)
        share_operand(4, gr, o_gr, m)

        gq[lax.rem(m, 2)] = jnp.dot(cols[:, : 3 * d], w_t_back[...], preferred_element_type=f32)

        def sums(i, s):
            normed = uh[m, :, s]
            slope = keep[m] * gq[lax.rem(m, 2), :, s] * silu_slope(g_s[:, s] * normed + b_s[:, s])
            gq[lax.rem(m, 2), :, s] = slope
            x_bs[m, me, :, s] = jnp.sum(slope, axis=0, keepdims=True)
            at = pl.ds(pl.multiple_of(m_ch + i * 128, 128), 128)
            x_bs[m, me, :, at] = jnp.sum(slope * normed, axis=0, keepdims=True)

        lane_chunks(m_ch, sums)
        share(3, x_bs, m)

    def backward_spatial(m):
        shared(3, x_bs, m)
        n = jnp.sum(x_t[m, :, :, 2 * d :], axis=0)

        def column(i, s):
            shift_sum, gain_sum = totals(x_bs, m, s, i, m_ch)
            o_shift_s[:, s] += shift_sum
            o_gain_s[:, s] += gain_sum
            scale = g_s[:, s] * fact_s[m, :, s]
            value = keep[m] * scale * (gq[lax.rem(m, 2), :, s] - (shift_sum + uh[m, :, s] * gain_sum) / n)
            value = value.astype(bf16)
            gu[m, :, s] = value
            value = value.astype(f32)
            for dw in (-1, 0, 1):
                y = shift_space(value, 0, -dw)
                for dh in (-1, 0, 1):
                    tap = (dh + 1) * 3 + dw + 1
                    at = pl.ds(pl.multiple_of(tap * m_ch + i * 128, 128), 128)
                    cols[:, at] = shift_rows(y, -dh).astype(bf16)

        lane_chunks(m_ch, column)
        share_operand(5, gu, o_gu, m)

        @pl.when(even_inner)
        def _():
            to_pipe(1, gs_out, gs_in, m, -1).wait_recv()

        with_skip = even_inner.astype(f32)
        for part in range(2):
            s = slice(part * half, (part + 1) * half)
            value = jnp.dot(cols[...], w_s_back[:, s], preferred_element_type=f32)
            ig_out[m, :, s] = (value + with_skip * gs_in[m, :, s].astype(f32)).astype(bf16)

            @pl.when(jnp.logical_not(first))
            def _():
                def sums(i, s):
                    s = lanes_of(part, i)
                    normed = normed_prev(m, s)
                    slope = silu_slope(skipped_prev(m, s, preact_prev(m, s, normed)))
                    slope = ig_out[m, :, s].astype(f32) * keep[m] * slope

                    @pl.when(section == 2)
                    def _():
                        gs_out[m, :, s] = slope.astype(bf16)

                    slope_sums(x_bp.at[m, 0], slope, normed, part * (half // 128) + i, s)

                if part == 0:
                    half_to_pipe(4, part, ig_out, ga_in, m, -1).start()
                lane_chunks(half, sums)
                if part == 1:
                    cross(2, x_bp.at[m, 0], x_bt, m, -1)
                    half_to_pipe(4, part, ig_out, ga_in, m, -1).start()

        store(1, ig_out, o_grad, m).start()

    def send_skip_grad(m):
        to_pipe(1, gs_out, gs_in, m, jnp.where(last, -1, -2)).start()

    def turn_weights():
        @pl.when(jnp.logical_not(first))
        def _():
            for part in range(2):
                for tap in range(9):
                    load_ws(part, tap).wait()
            load_wt.wait()

        def spatial(tap, carry):
            dst = pl.ds(pl.multiple_of(tap * m_ch, 128), m_ch)
            for part in range(2):
                src = pl.ds(pl.multiple_of((part * 9 + tap) * half, 128), half)
                w_s_back[dst, part * half : (part + 1) * half] = w_s[src, :].T
            return carry

        lax.fori_loop(0, 9, spatial, 0)

        def temporal(tap, carry):
            src = pl.ds(pl.multiple_of(tap * m_ch, 128), m_ch)
            dst = pl.ds(pl.multiple_of(tap * d, 128), d)
            w_t_back[dst, :] = w_t[src, :].T
            return carry

        lax.fori_loop(0, 3, temporal, 0)

    pairs = MB // 2
    wait_back = jnp.where(last, 1, pairs)

    def step(s, carry):
        do_f = s < pairs
        do_b = jnp.logical_and(s >= wait_back, s < wait_back + pairs)
        mf = 2 * jnp.minimum(s, pairs - 1)
        mb = 2 * jnp.clip(s - wait_back, 0, pairs - 1)

        @pl.when(s == jnp.where(first, wait_back, 0))
        def _():
            turn_weights()

        def both(when, phase, m):
            @pl.when(when)
            def _():
                def one(j, c):
                    phase(m + j)
                    return c

                lax.fori_loop(0, 2, one, 0)

        inner = jnp.logical_not(last)
        done_f = jnp.logical_and(s > 0, s <= pairs)
        md = 2 * jnp.clip(s - 1, 0, pairs - 1)
        both(jnp.logical_and(done_f, last), forward_out, md)
        both(jnp.logical_and(do_b, last), backward_in, mb)
        both(do_f, forward_spatial, mf)
        both(jnp.logical_and(done_f, inner), forward_out, md)
        both(do_b, backward_temporal, mb)
        both(do_f, forward_temporal, mf)
        both(do_b, backward_spatial, mb)
        both(jnp.logical_and(do_b, jnp.logical_not(early)), send_skip_grad, mb)
        return carry

    lax.fori_loop(0, 2 * pairs, step, 0)

    def finish(m, carry):
        store(0, a_out, o_act, m).wait()
        store(1, ig_out, o_grad, m).wait()
        for kind, src, dst in (
            (2, a_in, o_in),
            (3, hidden, o_hidden),
            (4, gr, o_gr),
            (5, gu, o_gu),
        ):
            keep_operand(kind, src, dst, m).wait()
            twin_operand(kind, src, dst, m).wait()

        @pl.when(jnp.logical_not(last))
        def _():
            cross_sent(4, x_p, m)
            for part in range(2):
                half_to_pipe(2, part, r_out, r_in, m, 1).wait_send()


        @pl.when(section == 1)
        def _():
            to_pipe(0, a_out, skip_in, m, 2).wait_send()

        @pl.when(jnp.logical_not(first))
        def _():
            cross_sent(2, x_bt, m)
            for part in range(2):
                half_to_pipe(4, part, ig_out, ga_in, m, -1).wait_send()

        @pl.when(jnp.logical_not(early))
        def _():
            to_pipe(1, gs_out, gs_in, m, -1).wait_send()

        return carry

    lax.fori_loop(0, MB, finish, 0)

    @pl.when(jnp.logical_not(last))
    def _():
        send_scale().wait_send()


def relay(dims, n_dp, clips, boxes, w_s, w_t, g_s, b_s, g_t, b_t, cotangent):
    cm, frames, height, width = dims
    rows = cm * frames * height * width
    d, m_ch = w_t.shape[1], w_s.shape[1]
    shape = jax.ShapeDtypeStruct
    vmem = pl.BlockSpec(memory_space=pltpu.VMEM)
    hbm = pl.BlockSpec(memory_space=pl.ANY)
    smem = pl.BlockSpec(memory_space=pltpu.SMEM)
    dma = pltpu.SemaphoreType.DMA
    narrow = pltpu.VMEM((MB, rows, d), bf16)
    wide = pltpu.VMEM((MB, rows, m_ch), bf16)
    return pl.pallas_call(
        functools.partial(relay_kernel, dims),
        out_shape=(
            shape((MB, rows, d), bf16),
            shape((MB, rows, d), bf16),
            shape((2, MB, rows, d), bf16),
            shape((2, MB, rows, m_ch), bf16),
            shape((2, MB, rows, m_ch), bf16),
            shape((2, MB, rows, d), bf16),
            shape((1, m_ch), f32),
            shape((1, m_ch), f32),
            shape((1, d), f32),
            shape((1, d), f32),
        ),
        in_specs=[hbm, smem, hbm, hbm, vmem, vmem, vmem, vmem, hbm],
        out_specs=[hbm] * 6 + [vmem] * 4,
        scratch_shapes=[
            pltpu.VMEM(w_s.shape, bf16),
            pltpu.VMEM(w_t.shape, bf16),
            pltpu.VMEM((9 * m_ch, d), bf16),
            pltpu.VMEM((3 * d, m_ch), bf16),
            pltpu.VMEM((rows, 9 * m_ch), bf16),
            narrow,
            narrow,
            narrow,
            narrow,
            narrow,
            narrow,
            narrow,
            narrow,
            narrow,
            wide,
            narrow,
            wide,
            pltpu.VMEM((MB, rows, m_ch), f32),
            pltpu.VMEM((rows, d), f32),
            pltpu.VMEM((2, rows, m_ch), f32),
            pltpu.VMEM((MB, rows, 128), f32),
            pltpu.VMEM((MB, 1, m_ch), f32),
            pltpu.VMEM((MB, 1, d), f32),
            pltpu.VMEM((MB, 1, d), f32),
            pltpu.VMEM((MB, 1, d), f32),
            pltpu.VMEM((MB, 1, d), f32),
            pltpu.VMEM((MB, 1, 128), f32),
            pltpu.VMEM((2, 1, d), f32),
            pltpu.VMEM((2, 1, d), f32),
            pltpu.VMEM((MB, n_dp, 1, 2 * m_ch + 128), f32),
            pltpu.VMEM((MB, n_dp, 1, 2 * d + 128), f32),
            pltpu.VMEM((MB, n_dp, 1, 2 * d + 128), f32),
            pltpu.VMEM((MB, n_dp, 1, 2 * d), f32),
            pltpu.VMEM((MB, n_dp, 1, 2 * m_ch), f32),
            pltpu.VMEM((MB, 1, 1, 2 * d), f32),
            dma((5, MB)),
            dma((5, MB)),
            dma((21,)),
            dma((MB,)),
            dma((6, MB)),
            dma((6, MB)),
            dma((6, MB)),
            dma((4, MB)),
            dma((4, MB)),
        ],
        compiler_params=pltpu.CompilerParams(
            collective_id=0, has_side_effects=True, vmem_limit_bytes=62 * 2**20
        ),
    )(clips, boxes, w_s, w_t, g_s, b_s, g_t, b_t, cotangent)


def send_order(n, z, q):
    table = []
    for here in range(n):
        sign = 1 if here < n / 2 else -1
        table.append(sorted(range(n), key=lambda to: (-abs(to - here), -sign * to)))
    dest = 0
    for here in range(n):
        for at in range(n):
            dest = dest + jnp.where((z == here) & (q == at), table[here][at], 0)
    return dest


def gradient_kernel(
    dims,
    a_hbm,
    v_hbm,
    gu_hbm,
    gr_hbm,
    o_s,
    o_t,
    a,
    v,
    gu,
    gr,
    window,
    acc_s,
    acc_t,
    got_s,
    got_t,
    out_s,
    out_t,
    load_sem,
    send_sem,
    recv_sem,
):
    frames, height, width = dims
    n_clips, rows, d = a_hbm.shape
    m_ch = v_hbm.shape[2]
    me = lax.axis_index("dp")
    n = lax.axis_size("dp") // 2
    z = lax.div(me, 2)
    core = lax.rem(me, 2)
    rows_s, rows_t = o_s.shape[0], o_t.shape[0]
    piece = got_s.shape[3]
    n_pieces = m_ch // piece
    span = acc_s.shape[0]

    barrier = pltpu.get_barrier_semaphore()

    @pl.when(z > 0)
    def _():
        pl.semaphore_signal(barrier, 1, device_id={"dp": me - 2}, device_id_type=MESH)

    @pl.when(z < n - 1)
    def _():
        pl.semaphore_signal(barrier, 1, device_id={"dp": me + 2}, device_id_type=MESH)

    loads = [
        pltpu.make_async_copy(src, dst, load_sem.at[i])
        for i, (src, dst) in enumerate(((a_hbm, a), (gu_hbm, gu), (v_hbm, v), (gr_hbm, gr)))
    ]
    for copy in loads:
        copy.start()
    loads[0].wait()

    def moved(x, before, after, dt, step):
        if not dt:
            return x
        y = x.reshape(before, after, 128)
        zero = jnp.zeros((before, step, 128), f32)
        if dt > 0:
            y = jnp.concatenate([y[:, step:], zero], axis=1)
        else:
            y = jnp.concatenate([zero, y[:, :-step]], axis=1)
        return y.reshape(rows, 128)

    def transfer(src, dst, dest, p):
        right = dest > z
        slot = dest + jnp.where(right, 1, 0)
        return pltpu.make_async_remote_copy(
            src_ref=src,
            dst_ref=dst(slot),
            send_sem=send_sem.at[dest, p],
            recv_sem=recv_sem.at[slot, p],
            device_id={"dp": me + jnp.where(right, 2, -2)},
            device_id_type=MESH,
        )

    def settle(dest, acc, start, size, got, out, final, p):
        at = pl.ds(pl.multiple_of(start, 8), size)
        from_left = (z > 0) & (dest >= z)
        from_right = (z < n - 1) & (dest <= z)

        @pl.when(from_left)
        def _():
            ref = got(dest + 1)
            pltpu.make_async_copy(ref, ref, recv_sem.at[dest + 1, p]).wait()
            acc[at, :] += ref[...].astype(f32)

        @pl.when(from_right)
        def _():
            ref = got(dest)
            pltpu.make_async_copy(ref, ref, recv_sem.at[dest, p]).wait()
            acc[at, :] += ref[...].astype(f32)

        @pl.when(dest == z)
        def _():
            final[...] = acc[at, :]

        @pl.when(dest != z)
        def _():
            ref = out(dest)
            ref[...] = acc[at, :].astype(bf16)
            transfer(ref, got, dest, p).start()

    def place(row0):
        low = lax.div(row0, 128)
        return low, row0 - low * 128

    def job(q, carry):
        dest = send_order(n, z, q)
        owner = 2 * dest + core

        low, start = place(owner * rows_s)

        def fill_space(i, c):
            to = pl.ds(pl.multiple_of(i * rows, 16), rows)
            for j in range(span // 128):
                chunk = jnp.minimum(low + j, 9 * d // 128 - 1)
                tap = lax.div(chunk, d // 128)
                lane = pl.ds(pl.multiple_of((chunk - tap * (d // 128)) * 128, 128), 128)

                def fill(dh, dw):
                    x = a[i, :, lane].astype(f32)
                    if dw:
                        x = pltpu.roll(x, (-dw) % rows, 0)
                    x = moved(x, frames, height * width, dh, width)
                    window[to, j * 128 : (j + 1) * 128] = x.astype(bf16)

                lax.switch(
                    tap,
                    [
                        functools.partial(fill, dh, dw)
                        for dh in (-1, 0, 1)
                        for dw in (-1, 0, 1)
                    ],
                )
            return c

        lax.fori_loop(0, n_clips, fill_space, 0)

        @pl.when(q == 0)
        def _():
            loads[1].wait()
            sides = 2 - jnp.where(z == 0, 1, 0) - jnp.where(z == n - 1, 1, 0)
            pl.semaphore_wait(barrier, sides)


        def space(p, c):
            s = pl.ds(pl.multiple_of(p * piece, 128), piece)
            acc_s[...] = lax.dot_general(
                window[...],
                gu[:, :, s].reshape(n_clips * rows, piece),
                (((0,), (0,)), ((), ())), preferred_element_type=f32
            )
            settle(
                dest,
                acc_s,
                start,
                rows_s,
                lambda slot: got_s.at[slot, p],
                lambda to: out_s.at[to, p],
                o_s.at[:, s],
                p,
            )
            return c

        lax.fori_loop(0, n_pieces, space, 0)

        low_t, start_t = place(owner * rows_t)

        def fill_time(i, c):
            to = pl.ds(pl.multiple_of(i * rows, 16), rows)
            for j in range(span // 128):
                chunk = jnp.minimum(low_t + j, 3 * m_ch // 128 - 1)
                tap = lax.div(chunk, m_ch // 128)
                lane = pl.ds(pl.multiple_of((chunk - tap * (m_ch // 128)) * 128, 128), 128)

                def fill(dt):
                    x = v[i, :, lane].astype(f32)
                    x = moved(x, 1, rows, dt, height * width)
                    window[to, j * 128 : (j + 1) * 128] = x.astype(bf16)

                lax.switch(tap, [functools.partial(fill, dt) for dt in (-1, 0, 1)])
            return c

        @pl.when(q == 0)
        def _():
            loads[2].wait()
            loads[3].wait()

        lax.fori_loop(0, n_clips, fill_time, 0)
        acc_t[...] = lax.dot_general(
            window[...],
            gr[...].reshape(n_clips * rows, d),
            (((0,), (0,)), ((), ())), preferred_element_type=f32
        )
        settle(
            dest,
            acc_t,
            start_t,
            rows_t,
            lambda slot: got_t.at[slot],
            lambda to: out_t.at[to],
            o_t,
            n_pieces,
        )
        return carry

    lax.fori_loop(0, n, job, 0)

    def finish(q, carry):
        dest = send_order(n, z, q)
        for p in range(n_pieces):
            transfer(out_s.at[dest, p], lambda slot: got_s.at[slot, p], dest, p).wait_send()
        transfer(out_t.at[dest], lambda slot: got_t.at[slot], dest, n_pieces).wait_send()
        return carry

    lax.fori_loop(0, n - 1, finish, 0)


def gradients(dims, n_dp, a, v, gu, gr):
    n_clips, rows, d = a.shape
    m_ch = v.shape[2]
    rows_s, rows_t = 9 * d // n_dp, 3 * m_ch // n_dp
    n = n_dp // 2
    piece = 384
    n_pieces = m_ch // piece
    span = 640
    shape = jax.ShapeDtypeStruct
    dma = pltpu.SemaphoreType.DMA
    return pl.pallas_call(
        functools.partial(gradient_kernel, dims),
        out_shape=(shape((rows_s, m_ch), f32), shape((rows_t, d), f32)),
        in_specs=[pl.BlockSpec(memory_space=pl.ANY)] * 4,
        out_specs=[pl.BlockSpec(memory_space=pltpu.VMEM)] * 2,
        scratch_shapes=[
            pltpu.VMEM(a.shape, bf16),
            pltpu.VMEM(v.shape, bf16),
            pltpu.VMEM(gu.shape, bf16),
            pltpu.VMEM(gr.shape, bf16),
            pltpu.VMEM((n_clips * rows, span), bf16),
            pltpu.VMEM((span, piece), f32),
            pltpu.VMEM((span, d), f32),
            pltpu.VMEM((n + 1, n_pieces, rows_s, piece), bf16),
            pltpu.VMEM((n + 1, rows_t, d), bf16),
            pltpu.VMEM((n, n_pieces, rows_s, piece), bf16),
            pltpu.VMEM((n, rows_t, d), bf16),
            dma((4,)),
            dma((n, n_pieces + 1)),
            dma((n + 1, n_pieces + 1)),
        ],
        compiler_params=pltpu.CompilerParams(
            collective_id=1, has_side_effects=True, vmem_limit_bytes=40 * 2**20
        ),
    )(a, v, gu, gr)


def spatial_columns(activity):
    height, breadth = (activity.shape[2], activity.shape[3])
    padded = jnp.pad(activity, ((0, 0), (0, 0), (1, 1), (1, 1), (0, 0)))
    pieces = [
        padded[:, :, row_off : row_off + height, col_off : col_off + breadth, :]
        for row_off in range(3)
        for col_off in range(3)
    ]
    return jnp.concatenate(pieces, axis=-1)


def temporal_columns(activity):
    frames = activity.shape[1]
    padded = jnp.pad(activity, ((0, 0), (1, 1), (0, 0), (0, 0), (0, 0)))
    return jnp.concatenate([padded[:, offset : offset + frames] for offset in range(3)], axis=-1)


def left_product(former, latter):
    return lax.dot_general(
        former, latter, (((0,), (0,)), ((), ())), preferred_element_type=jnp.float32
    )


def body(
    clips,
    boxes,
    spatial_w,
    temporal_w,
    spatial_gain,
    spatial_shift,
    temporal_gain,
    temporal_shift,
    cotangent,
):
    n_clips, frames, height, breadth, d = clips.shape
    cm = n_clips // MB
    width = (breadth // 8 + 1) * 8
    rows = cm * frames * height * width
    m_ch = spatial_w.shape[2]

    def padded(x):
        x = jnp.pad(x, ((0, 0), (0, 0), (0, 0), (0, width - breadth), (0, 0)))
        return x.reshape(MB, rows, d)

    act, grad, a_in, hidden, gu, gr, gain_s, shift_s, gain_t, shift_t = relay(
        (cm, frames, height, width),
        lax.axis_size("dp"),
        padded(clips),
        boxes,
        spatial_w[0],
        temporal_w[0],
        spatial_gain,
        spatial_shift,
        temporal_gain,
        temporal_shift,
        padded(cotangent),
    )

    def frames_of(x):
        return x.reshape(n_clips, frames, height, width, x.shape[-1])[:, :, :, :breadth]

    n_dp = lax.axis_size("dp")
    rows_s, rows_t = 9 * d // n_dp, 3 * m_ch // n_dp
    if rows_s % 64 == 0 and rows_t % 16 == 0 and rows_s <= 576 and rows_t <= 528 and n_dp <= 8:
        clip_rows = frames * height * width
        grad_s, grad_t = gradients(
            (frames, height, width),
            n_dp,
            *[x.reshape(2 * n_clips, clip_rows, x.shape[-1]) for x in (a_in, hidden, gu, gr)],
        )
    else:
        cells = n_clips * frames * height * breadth
        cols = spatial_columns(frames_of(a_in[0])).reshape(cells, -1)
        grad_s = left_product(cols, frames_of(gu[0]).reshape(cells, -1))
        stacked = temporal_columns(frames_of(hidden[0])).reshape(cells, -1)
        grad_t = left_product(stacked, frames_of(gr[0]).reshape(cells, -1))
        grad_s = lax.psum_scatter(grad_s, "dp", scatter_dimension=0, tiled=True)
        grad_t = lax.psum_scatter(grad_t, "dp", scatter_dimension=0, tiled=True)
    return (
        frames_of(act)[None],
        frames_of(grad)[None],
        grad_s[None],
        grad_t[None],
        gain_s,
        shift_s,
        gain_t,
        shift_t,
    )


def solution(mesh):
    clip_spec = P("dp", None, None, None, None)
    weight_spec = P("pipe", None, None)
    channel_spec = P("pipe", None)
    return jax.shard_map(
        body,
        mesh=mesh,
        in_specs=(
            clip_spec,
            P("dp", None),
            weight_spec,
            weight_spec,
            channel_spec,
            channel_spec,
            channel_spec,
            channel_spec,
            clip_spec,
        ),
        out_specs=(
            P("pipe", "dp", None, None, None, None),
            P("pipe", "dp", None, None, None, None),
            P("pipe", "dp", None),
            P("pipe", "dp", None),
            channel_spec,
            channel_spec,
            channel_spec,
            channel_spec,
        ),
        check_vma=False,
    )
```

```python
import functools

import jax
import jax.numpy as jnp
from jax import lax
from jax.experimental import pallas as pl
from jax.experimental.pallas import tpu as pltpu
from jax.sharding import PartitionSpec as P

MB = 4
eps_norm = 1e-05
bf16 = jnp.bfloat16
f32 = jnp.float32
MESH = pl.DeviceIdType.MESH


def silu(x):
    return x / (1.0 + jnp.exp(-x))


def silu_slope(x):
    s = 1.0 / (1.0 + jnp.exp(-x))
    return s * (1.0 + x * (1.0 - s))


def lane_chunks(width, body):
    def step(i, carry):
        body(i, pl.ds(pl.multiple_of(i * 128, 128), 128))
        return carry

    lax.fori_loop(0, width // 128, step, 0)


def relay_kernel(
    dims,
    clips,
    boxes,
    w_s_hbm,
    w_t_hbm,
    g_s,
    b_s,
    g_t,
    b_t,
    cotangent,
    o_act,
    o_grad,
    o_in,
    o_hidden,
    o_gu,
    o_gr,
    o_gain_s,
    o_shift_s,
    o_gain_t,
    o_shift_t,
    w_s,
    w_t,
    w_s_back,
    w_t_back,
    cols,
    a_in,
    skip_in,
    a_out,
    r_in,
    r_out,
    ga_in,
    gs_in,
    gs_out,
    ig_out,
    hidden,
    gr,
    gu,
    uh,
    r_sum,
    gq,
    keep,
    fact_s,
    fact_t,
    off_t,
    fact_p,
    off_p,
    cnt,
    scale_out,
    scale_in,
    x_s,
    x_t,
    x_p,
    x_bt,
    x_bs,
    x_bp,
    x_send,
    x_recv,
    w_sem,
    load_sem,
    store_sem,
    pipe_send,
    pipe_recv,
    twin_send,
    twin_recv,
    hub_sem,
):
    cm, frames, height, width = dims
    rows = cm * frames * height * width
    d = a_in.shape[2]
    m_ch = hidden.shape[2]
    section = lax.axis_index("pipe")
    me = lax.axis_index("dp")
    n_pipe = lax.axis_size("pipe")
    n_dp = lax.axis_size("dp")
    first = section == 0
    last = section == n_pipe - 1
    odd = lax.rem(section, 2) == 1
    even_inner = jnp.logical_and(jnp.logical_not(odd), jnp.logical_not(last))
    early = section < 2
    skip_own = odd.astype(f32)
    skip_prev = jnp.logical_not(jnp.logical_or(odd, first)).astype(f32)

    def load_ws(part, tap):
        half = d // 2
        src = w_s_hbm.at[pl.ds(tap * d + part * half, half)]
        dst = w_s.at[pl.ds((part * 9 + tap) * half, half)]
        return pltpu.make_async_copy(src, dst, w_sem.at[part * 9 + tap])

    load_wt = pltpu.make_async_copy(w_t_hbm, w_t, w_sem.at[18])

    def load_clip(m):
        return pltpu.make_async_copy(clips.at[m], a_in.at[m], load_sem.at[m])

    def load_cot(m):
        return pltpu.make_async_copy(cotangent.at[m], ga_in.at[m], load_sem.at[m])

    def load_skip(m):
        return pltpu.make_async_copy(clips.at[m], skip_in.at[m], load_sem.at[m])

    local_skip = jnp.logical_not(jnp.logical_or(first, last))

    @pl.when(first)
    def _():
        for m in range(MB):
            load_clip(m).start()

    @pl.when(local_skip)
    def _():
        for m in range(MB):
            load_skip(m).start()

    for part in range(2):
        for tap in range(9):
            load_ws(part, tap).start()
    load_wt.start()

    @pl.when(last)
    def _():
        for m in range(MB):
            load_cot(m).start()

    for ref in (o_gain_s, o_shift_s, o_gain_t, o_shift_t, gs_in, scale_in):
        ref[...] = jnp.zeros_like(ref)

    @pl.when(first)
    def _():
        skip_in[...] = jnp.zeros_like(skip_in)

    barrier = pltpu.get_barrier_semaphore()

    def greet(j, carry):
        pl.semaphore_signal(
            barrier, 1, device_id={"dp": lax.rem(me + j, n_dp)}, device_id_type=MESH
        )
        return carry

    lax.fori_loop(1, n_dp, greet, 0)

    def greet_pipe(step):
        def greet_one(j, carry):
            pl.semaphore_signal(
                barrier,
                1,
                device_id={"pipe": section + step, "dp": j},
                device_id_type=MESH,
            )
            return carry

        lax.fori_loop(0, n_dp, greet_one, 0)

    @pl.when(jnp.logical_not(first))
    def _():
        greet_pipe(-1)

    @pl.when(jnp.logical_not(last))
    def _():
        greet_pipe(1)

    pl.semaphore_signal(
        barrier,
        1,
        device_id={"pipe": section + jnp.where(early, 2, -2)},
        device_id_type=MESH,
    )
    scale_out[0] = g_t[...]
    scale_out[1] = b_t[...]

    def make_keep(m, carry):
        n_rows = frames * height * width
        pieces = []
        for c in range(cm):
            shape = (frames, height, width, 128)
            t = lax.broadcasted_iota(jnp.int32, shape, 0)
            h = lax.broadcasted_iota(jnp.int32, shape, 1)
            w = lax.broadcasted_iota(jnp.int32, shape, 2)
            box = [boxes[m * cm + c, i] for i in range(6)]
            inside = (t >= box[0]) & (t < box[1]) & (h >= box[2]) & (h < box[3])
            inside = inside & (w >= box[4]) & (w < box[5])
            pieces.append(jnp.where(inside, 1.0, 0.0).astype(f32).reshape(n_rows, 128))
        mask = jnp.concatenate(pieces, axis=0) if cm > 1 else pieces[0]
        keep[m] = mask
        cnt[m] = jnp.sum(mask, axis=0, keepdims=True)
        return carry

    lax.fori_loop(0, MB, make_keep, 0)
    sides = 3 - jnp.where(first, 1, 0) - jnp.where(last, 1, 0)
    pl.semaphore_wait(barrier, sides * n_dp)

    def send_scale():
        return pltpu.make_async_remote_copy(
            src_ref=scale_out,
            dst_ref=scale_in,
            send_sem=w_sem.at[19],
            recv_sem=w_sem.at[20],
            device_id={"pipe": section + 1},
            device_id_type=MESH,
        )

    @pl.when(jnp.logical_not(last))
    def _():
        send_scale().start()

    def share(kind, buf, m):
        def send(j, carry):
            pltpu.make_async_remote_copy(
                src_ref=buf.at[m, me],
                dst_ref=buf.at[m, me],
                send_sem=x_send.at[kind, m],
                recv_sem=x_recv.at[kind, m],
                device_id={"dp": lax.rem(me + j, n_dp)},
                device_id_type=MESH,
            ).start()
            return carry

        lax.fori_loop(1, n_dp, send, 0)

    def shared(kind, buf, m):
        others = buf.at[m, pl.ds(0, n_dp - 1)]
        pltpu.make_async_copy(others, others, x_send.at[kind, m]).wait()
        pltpu.make_async_copy(others, others, x_recv.at[kind, m]).wait()

    def cross(kind, src, dst, m, step):
        def send(j, carry):
            pltpu.make_async_remote_copy(
                src_ref=src,
                dst_ref=dst.at[m, me],
                send_sem=x_send.at[kind, m],
                recv_sem=x_recv.at[kind, m],
                device_id={"pipe": section + step, "dp": lax.rem(me + j, n_dp)},
                device_id_type=MESH,
            ).start()
            return carry

        lax.fori_loop(0, n_dp, send, 0)

    def crossed(kind, buf, m):
        slots = buf.at[m]
        pltpu.make_async_copy(slots, slots, x_recv.at[kind, m]).wait()

    def cross_sent(kind, buf, m):
        slots = buf.at[m]
        pltpu.make_async_copy(slots, slots, x_send.at[kind, m]).wait()

    def to_pipe(kind, src, dst, m, step):
        return pltpu.make_async_remote_copy(
            src_ref=src.at[m],
            dst_ref=dst.at[m],
            send_sem=pipe_send.at[kind, m],
            recv_sem=pipe_recv.at[kind, m],
            device_id={"pipe": section + step},
            device_id_type=MESH,
        )

    half = d // 2

    def half_to_pipe(kind, part, src, dst, m, step):
        s = pl.ds(part * half, half)
        return pltpu.make_async_remote_copy(
            src_ref=src.at[m, :, s],
            dst_ref=dst.at[m, :, s],
            send_sem=pipe_send.at[kind + part, m],
            recv_sem=pipe_recv.at[kind + part, m],
            device_id={"pipe": section + step},
            device_id_type=MESH,
        )

    hubs = o_in.shape[0] > 2
    z = lax.div(me, 2)
    outer = jnp.logical_or(z == 0, z == n_dp // 2 - 1)

    def to_hub(m):
        return pltpu.make_async_remote_copy(
            src_ref=a_in.at[m],
            dst_ref=o_in.at[2, m],
            send_sem=hub_sem.at[0, m],
            recv_sem=hub_sem.at[1, m],
            device_id={"dp": me + jnp.where(z == 0, 2, -2)},
            device_id_type=MESH,
        )

    def inputs_to_hub():
        @pl.when(outer)
        def _():
            for m in range(MB):
                to_hub(m).start()

    def gu_to_hub(part):
        m = min(part, 1)
        s = (pl.ds(0, m_ch), pl.ds(0, 640), pl.ds(640, m_ch - 640))[part]
        return pltpu.make_async_remote_copy(
            src_ref=gu.at[m, :, s],
            dst_ref=o_gu.at[2, m, :, s],
            send_sem=hub_sem.at[2, part],
            recv_sem=hub_sem.at[3, part],
            device_id={"dp": me + jnp.where(z == 0, 2, -2)},
            device_id_type=MESH,
        )

    def store(kind, src, dst, m):
        return pltpu.make_async_copy(src.at[m], dst.at[m], store_sem.at[kind, m])

    def keep_operand(kind, src, dst, m):
        return pltpu.make_async_copy(src.at[m], dst.at[0, m], store_sem.at[kind, m])

    def twin_operand(kind, src, dst, m):
        return pltpu.make_async_remote_copy(
            src_ref=src.at[m],
            dst_ref=dst.at[1, m],
            send_sem=twin_send.at[kind - 2, m],
            recv_sem=twin_recv.at[kind - 2, m],
            device_id={"dp": me + 1 - 2 * lax.rem(me, 2)},
            device_id_type=MESH,
        )

    def share_operand(kind, src, dst, m):
        keep_operand(kind, src, dst, m).start()
        twin_operand(kind, src, dst, m).start()

    def shift_space(x, dh, dw):
        if dw:
            x = pltpu.roll(x, (-dw) % rows, 0)
        return shift_rows(x, dh)

    def shift_rows(x, dh):
        if not dh:
            return x
        y = x.reshape(cm * frames, height * width, 128)
        zero = jnp.zeros((cm * frames, width, 128), f32)
        if dh > 0:
            y = jnp.concatenate([y[:, width:], zero], axis=1)
        else:
            y = jnp.concatenate([zero, y[:, :-width]], axis=1)
        return y.reshape(rows, 128)

    def shift_time(x, dt):
        if not dt:
            return x
        y = x.reshape(cm, frames * height * width, 128)
        step = height * width
        zero = jnp.zeros((cm, step, 128), f32)
        if dt > 0:
            y = jnp.concatenate([y[:, step:], zero], axis=1)
        else:
            y = jnp.concatenate([zero, y[:, :-step]], axis=1)
        return y.reshape(rows, 128)

    def local_sums(m, value, buf, c, channels):
        mask = keep[m]
        n_here = cnt[m]
        total = jnp.sum(mask * value, axis=0, keepdims=True)
        dev = mask * (value - total / n_here)
        spread = jnp.sum(dev * dev, axis=0, keepdims=True)
        buf[m, me, :, pl.ds(pl.multiple_of(c * 128, 128), 128)] = total
        buf[m, me, :, pl.ds(pl.multiple_of(channels + c * 128, 128), 128)] = spread
        return dev

    def merged(m, buf, c, channels):
        counts = buf[m, :, :, 2 * channels :]
        sums = buf[m, :, :, pl.ds(pl.multiple_of(c * 128, 128), 128)]
        spreads = buf[m, :, :, pl.ds(pl.multiple_of(channels + c * 128, 128), 128)]
        n = jnp.sum(counts, axis=0)
        mean = jnp.sum(sums, axis=0) / n
        off = sums / counts - mean[None]
        var = jnp.sum(spreads + counts * off * off, axis=0) / n
        return n, mean, lax.rsqrt(var + eps_norm)

    def lanes_of(part, i):
        return pl.ds(pl.multiple_of(part * half + i * 128, 128), 128)

    def normed_prev(m, s):
        return (r_in[m, :, s].astype(f32) + off_p[m, :, s]) * fact_p[m, :, s]

    def preact_prev(m, s, normed):
        return scale_in[0, :, s] * normed + scale_in[1, :, s]

    def skipped_prev(m, s, value):
        return value + skip_prev * skip_in[m, :, s].astype(f32)

    def activate(m, part, i, s):
        s = lanes_of(part, i)
        n, mean, rstd = merged(m, x_p, part * (half // 128) + i, d)
        off_p[m, :, s] = x_p[m, me, :, s] / x_p[m, me, :, 2 * d :] - mean
        fact_p[m, :, s] = rstd
        value = preact_prev(m, s, normed_prev(m, s))

        @pl.when(section == 2)
        def _():
            a_in[m, :, s] = (keep[m] * silu(skipped_prev(m, s, value))).astype(bf16)

        @pl.when(section != 2)
        def _():
            a_in[m, :, s] = (keep[m] * silu(value)).astype(bf16)

    def forward_spatial(m):
        @pl.when(first)
        def _():
            load_clip(m).wait()

        @pl.when(jnp.logical_not(first))
        def _():
            @pl.when(m == 0)
            def _():
                send_scale().wait_recv()

            @pl.when(local_skip)
            def _():
                load_skip(m).wait()

            crossed(4, x_p, m)

        for part in range(2):

            @pl.when(jnp.logical_not(first))
            def _():
                half_to_pipe(2, part, r_out, r_in, m, 1).wait_recv()
                lane_chunks(half, functools.partial(activate, m, part))

            def column(i, s):
                s = pl.ds(pl.multiple_of(part * half + i * 128, 128), 128)
                x = a_in[m, :, s].astype(f32)
                for dw in (-1, 0, 1):
                    y = shift_space(x, 0, dw)
                    for dh in (-1, 0, 1):
                        tap = (dh + 1) * 3 + dw + 1
                        at = part * 9 * half + tap * half + i * 128
                        cols[:, pl.ds(pl.multiple_of(at, 128), 128)] = shift_rows(y, dh).astype(
                            bf16
                        )

            lane_chunks(half, column)

            @pl.when((m == 0) & first)
            def _():
                for tap in range(9):
                    load_ws(part, tap).wait()

            k = slice(part * 9 * half, (part + 1) * 9 * half)
            for s in (slice(0, 512), slice(512, m_ch)):
                value = jnp.dot(cols[:, k], w_s[k, s], preferred_element_type=f32)
                if part == 0:
                    uh[m, :, s] = value
                else:
                    uh[m, :, s] += value

        x_s[m, me, :, 2 * m_ch :] = cnt[m]

        def sums(i, s):
            local_sums(m, uh[m, :, s], x_s, i, m_ch)

        lane_chunks(m_ch, sums)
        share(0, x_s, m)
        share_operand(2, a_in, o_in, m)

    def forward_temporal(m):
        shared(0, x_s, m)

        def column(i, s):
            n, mean, rstd = merged(m, x_s, i, m_ch)
            fact_s[m, :, s] = rstd
            normed = (uh[m, :, s] - mean) * rstd
            uh[m, :, s] = normed
            value = keep[m] * silu(g_s[:, s] * normed + b_s[:, s])
            value = value.astype(bf16)
            hidden[m, :, s] = value
            value = value.astype(f32)
            for dt in (-1, 0, 1):
                at = pl.ds(pl.multiple_of((dt + 1) * m_ch + i * 128, 128), 128)
                cols[:, at] = shift_time(value, dt).astype(bf16)

        lane_chunks(m_ch, column)
        share_operand(3, hidden, o_hidden, m)

        @pl.when((m == 0) & first)
        def _():
            load_wt.wait()

        r_sum[...] = jnp.dot(cols[:, : 3 * m_ch], w_t[...], preferred_element_type=f32)
        x_t[m, me, :, 2 * d :] = cnt[m]

        def centre(i, s):
            r_out[m, :, s] = local_sums(m, r_sum[:, s], x_t, i, d).astype(bf16)

        lane_chunks(d, centre)

        @pl.when(jnp.logical_not(last))
        def _():
            cross(4, x_t.at[m, me], x_p, m, 1)
            for part in range(2):
                half_to_pipe(2, part, r_out, r_in, m, 1).start()

        share(1, x_t, m)

    def normed_own(m, s):
        return (r_out[m, :, s].astype(f32) + off_t[m, :, s]) * fact_t[m, :, s]

    def preact_own(m, s, normed):
        return g_t[:, s] * normed + b_t[:, s] + skip_own * skip_in[m, :, s].astype(f32)

    def forward_out(m):
        @pl.when(last)
        def _():
            to_pipe(0, a_out, skip_in, m, 2).wait_recv()

        shared(1, x_t, m)

        def column(i, s):
            n, mean, rstd = merged(m, x_t, i, d)
            off_t[m, :, s] = x_t[m, me, :, s] / cnt[m] - mean
            fact_t[m, :, s] = rstd
            value = keep[m] * silu(preact_own(m, s, normed_own(m, s)))
            a_out[m, :, s] = value.astype(bf16)

        lane_chunks(d, column)
        store(0, a_out, o_act, m).start()

        @pl.when(section == 1)
        def _():
            to_pipe(0, a_out, skip_in, m, 2).start()

    def slope_sums(row, value, normed, i, s):
        row[:, s] = jnp.sum(value, axis=0, keepdims=True)
        at = pl.ds(pl.multiple_of(d + i * 128, 128), 128)
        row[:, at] = jnp.sum(value * normed, axis=0, keepdims=True)

    def own_slope(m, s, normed):
        return ga_in[m, :, s].astype(f32) * keep[m] * silu_slope(preact_own(m, s, normed))

    def backward_in(m):
        load_cot(m).wait()

        def column(i, s):
            normed = normed_own(m, s)
            slope_sums(x_bt.at[m, me], own_slope(m, s, normed), normed, i, s)

        lane_chunks(d, column)
        share(2, x_bt, m)

    def totals(buf, m, s, i, channels):
        at = pl.ds(pl.multiple_of(channels + i * 128, 128), 128)
        return jnp.sum(buf[m, :, :, s], axis=0), jnp.sum(buf[m, :, :, at], axis=0)

    def backward_temporal(m):
        @pl.when(last)
        def _():
            shared(2, x_bt, m)

        @pl.when(jnp.logical_not(last))
        def _():
            crossed(2, x_bt, m)
            for part in range(2):
                half_to_pipe(4, part, ig_out, ga_in, m, -1).wait_recv()

        n = jnp.sum(x_t[m, :, :, 2 * d :], axis=0)

        def column(i, s):
            shift_sum, gain_sum = totals(x_bt, m, s, i, d)
            o_shift_t[:, s] += shift_sum
            o_gain_t[:, s] += gain_sum
            normed = normed_own(m, s)
            slope = own_slope(m, s, normed)

            @pl.when(last)
            def _():
                gs_out[m, :, s] = slope.astype(bf16)

            scale = g_t[:, s] * fact_t[m, :, s]
            value = keep[m] * scale * (slope - (shift_sum + normed * gain_sum) / n)
            value = value.astype(bf16)
            gr[m, :, s] = value
            value = value.astype(f32)
            for dt in (-1, 0, 1):
                at = pl.ds(pl.multiple_of((dt + 1) * d + i * 128, 128), 128)
                cols[:, at] = shift_time(value, -dt).astype(bf16)

        lane_chunks(d, column)
        share_operand(4, gr, o_gr, m)

        gq[lax.rem(m, 2)] = jnp.dot(cols[:, : 3 * d], w_t_back[...], preferred_element_type=f32)

        def sums(i, s):
            normed = uh[m, :, s]
            slope = keep[m] * gq[lax.rem(m, 2), :, s] * silu_slope(g_s[:, s] * normed + b_s[:, s])
            gq[lax.rem(m, 2), :, s] = slope
            x_bs[m, me, :, s] = jnp.sum(slope, axis=0, keepdims=True)
            at = pl.ds(pl.multiple_of(m_ch + i * 128, 128), 128)
            x_bs[m, me, :, at] = jnp.sum(slope * normed, axis=0, keepdims=True)

        lane_chunks(m_ch, sums)
        share(3, x_bs, m)

    def backward_spatial(m):
        shared(3, x_bs, m)
        n = jnp.sum(x_t[m, :, :, 2 * d :], axis=0)

        def column(i, s):
            shift_sum, gain_sum = totals(x_bs, m, s, i, m_ch)
            o_shift_s[:, s] += shift_sum
            o_gain_s[:, s] += gain_sum
            scale = g_s[:, s] * fact_s[m, :, s]
            value = keep[m] * scale * (gq[lax.rem(m, 2), :, s] - (shift_sum + uh[m, :, s] * gain_sum) / n)
            value = value.astype(bf16)
            gu[m, :, s] = value
            value = value.astype(f32)
            for dw in (-1, 0, 1):
                y = shift_space(value, 0, -dw)
                for dh in (-1, 0, 1):
                    tap = (dh + 1) * 3 + dw + 1
                    at = pl.ds(pl.multiple_of(tap * m_ch + i * 128, 128), 128)
                    cols[:, at] = shift_rows(y, -dh).astype(bf16)

        lane_chunks(m_ch, column)
        share_operand(5, gu, o_gu, m)
        if hubs:
            for part in range(2):

                @pl.when(outer & first & (m == part))
                def _():
                    gu_to_hub(part).start()


        @pl.when(even_inner)
        def _():
            to_pipe(1, gs_out, gs_in, m, -1).wait_recv()

        with_skip = even_inner.astype(f32)
        for part in range(2):
            s = slice(part * half, (part + 1) * half)
            value = jnp.dot(cols[...], w_s_back[:, s], preferred_element_type=f32)
            ig_out[m, :, s] = (value + with_skip * gs_in[m, :, s].astype(f32)).astype(bf16)

            @pl.when(jnp.logical_not(first))
            def _():
                def sums(i, s):
                    s = lanes_of(part, i)
                    normed = normed_prev(m, s)
                    slope = silu_slope(skipped_prev(m, s, preact_prev(m, s, normed)))
                    slope = ig_out[m, :, s].astype(f32) * keep[m] * slope

                    @pl.when(section == 2)
                    def _():
                        gs_out[m, :, s] = slope.astype(bf16)

                    slope_sums(x_bp.at[m, 0], slope, normed, part * (half // 128) + i, s)

                if part == 0:
                    half_to_pipe(4, part, ig_out, ga_in, m, -1).start()
                lane_chunks(half, sums)
                if part == 1:
                    cross(2, x_bp.at[m, 0], x_bt, m, -1)
                    half_to_pipe(4, part, ig_out, ga_in, m, -1).start()

        store(1, ig_out, o_grad, m).start()

    def send_skip_grad(m):
        to_pipe(1, gs_out, gs_in, m, jnp.where(last, -1, -2)).start()

    def turn_weights():
        @pl.when(jnp.logical_not(first))
        def _():
            for part in range(2):
                for tap in range(9):
                    load_ws(part, tap).wait()
            load_wt.wait()

        def spatial(tap, carry):
            dst = pl.ds(pl.multiple_of(tap * m_ch, 128), m_ch)
            for part in range(2):
                src = pl.ds(pl.multiple_of((part * 9 + tap) * half, 128), half)
                w_s_back[dst, part * half : (part + 1) * half] = w_s[src, :].T
            return carry

        lax.fori_loop(0, 9, spatial, 0)

        def temporal(tap, carry):
            src = pl.ds(pl.multiple_of(tap * m_ch, 128), m_ch)
            dst = pl.ds(pl.multiple_of(tap * d, 128), d)
            w_t_back[dst, :] = w_t[src, :].T
            return carry

        lax.fori_loop(0, 3, temporal, 0)

    pairs = MB // 2
    wait_back = jnp.where(last, 1, pairs)

    def step(s, carry):
        do_f = s < pairs
        do_b = jnp.logical_and(s >= wait_back, s < wait_back + pairs)
        mf = 2 * jnp.minimum(s, pairs - 1)
        mb = 2 * jnp.clip(s - wait_back, 0, pairs - 1)

        @pl.when(s == jnp.where(first, wait_back, 0))
        def _():
            turn_weights()

        def both(when, phase, m):
            @pl.when(when)
            def _():
                def one(j, c):
                    phase(m + j)
                    return c

                lax.fori_loop(0, 2, one, 0)

        inner = jnp.logical_not(last)
        done_f = jnp.logical_and(s > 0, s <= pairs)
        md = 2 * jnp.clip(s - 1, 0, pairs - 1)
        both(jnp.logical_and(done_f, last), forward_out, md)
        both(jnp.logical_and(do_b, last), backward_in, mb)
        both(do_f, forward_spatial, mf)
        both(jnp.logical_and(done_f, inner), forward_out, md)
        both(do_b, backward_temporal, mb)
        if hubs:

            @pl.when(outer & (s == wait_back + 1) & first)
            def _():
                gu_to_hub(2).start()

        both(do_f, forward_temporal, mf)
        both(do_b, backward_spatial, mb)
        both(jnp.logical_and(do_b, jnp.logical_not(early)), send_skip_grad, mb)
        if hubs:

            @pl.when(s == jnp.where(last, wait_back + 1, pairs - 1))
            def _():
                inputs_to_hub()

            @pl.when(outer & (s == wait_back + 1) & jnp.logical_not(first))
            def _():
                for part in range(3):
                    gu_to_hub(part).start()

        return carry

    lax.fori_loop(0, 2 * pairs, step, 0)

    def finish(m, carry):
        store(0, a_out, o_act, m).wait()
        store(1, ig_out, o_grad, m).wait()
        for kind, src, dst in (
            (2, a_in, o_in),
            (3, hidden, o_hidden),
            (4, gr, o_gr),
            (5, gu, o_gu),
        ):
            keep_operand(kind, src, dst, m).wait()
            twin_operand(kind, src, dst, m).wait()

        @pl.when(jnp.logical_not(last))
        def _():
            cross_sent(4, x_p, m)
            for part in range(2):
                half_to_pipe(2, part, r_out, r_in, m, 1).wait_send()


        @pl.when(section == 1)
        def _():
            to_pipe(0, a_out, skip_in, m, 2).wait_send()

        @pl.when(jnp.logical_not(first))
        def _():
            cross_sent(2, x_bt, m)
            for part in range(2):
                half_to_pipe(4, part, ig_out, ga_in, m, -1).wait_send()

        @pl.when(jnp.logical_not(early))
        def _():
            to_pipe(1, gs_out, gs_in, m, -1).wait_send()

        return carry

    lax.fori_loop(0, MB, finish, 0)
    if hubs:
        for m in range(MB):

            @pl.when(outer)
            def _():
                to_hub(m).wait_send()
                if m < 3:
                    gu_to_hub(m).wait_send()

            @pl.when(jnp.logical_not(outer))
            def _():
                to_hub(m).wait_recv()
                if m < 3:
                    gu_to_hub(m).wait_recv()

    @pl.when(jnp.logical_not(last))
    def _():
        send_scale().wait_send()


def relay(dims, n_dp, hubs, clips, boxes, w_s, w_t, g_s, b_s, g_t, b_t, cotangent):
    cm, frames, height, width = dims
    rows = cm * frames * height * width
    d, m_ch = w_t.shape[1], w_s.shape[1]
    shape = jax.ShapeDtypeStruct
    vmem = pl.BlockSpec(memory_space=pltpu.VMEM)
    hbm = pl.BlockSpec(memory_space=pl.ANY)
    smem = pl.BlockSpec(memory_space=pltpu.SMEM)
    dma = pltpu.SemaphoreType.DMA
    narrow = pltpu.VMEM((MB, rows, d), bf16)
    wide = pltpu.VMEM((MB, rows, m_ch), bf16)
    return pl.pallas_call(
        functools.partial(relay_kernel, dims),
        out_shape=(
            shape((MB, rows, d), bf16),
            shape((MB, rows, d), bf16),
            shape((3 if hubs else 2, MB, rows, d), bf16),
            shape((2, MB, rows, m_ch), bf16),
            shape((3 if hubs else 2, MB, rows, m_ch), bf16),
            shape((2, MB, rows, d), bf16),
            shape((1, m_ch), f32),
            shape((1, m_ch), f32),
            shape((1, d), f32),
            shape((1, d), f32),
        ),
        in_specs=[hbm, smem, hbm, hbm, vmem, vmem, vmem, vmem, hbm],
        out_specs=[hbm] * 6 + [vmem] * 4,
        scratch_shapes=[
            pltpu.VMEM(w_s.shape, bf16),
            pltpu.VMEM(w_t.shape, bf16),
            pltpu.VMEM((9 * m_ch, d), bf16),
            pltpu.VMEM((3 * d, m_ch), bf16),
            pltpu.VMEM((rows, 9 * m_ch), bf16),
            narrow,
            narrow,
            narrow,
            narrow,
            narrow,
            narrow,
            narrow,
            narrow,
            narrow,
            wide,
            narrow,
            wide,
            pltpu.VMEM((MB, rows, m_ch), f32),
            pltpu.VMEM((rows, d), f32),
            pltpu.VMEM((2, rows, m_ch), f32),
            pltpu.VMEM((MB, rows, 128), f32),
            pltpu.VMEM((MB, 1, m_ch), f32),
            pltpu.VMEM((MB, 1, d), f32),
            pltpu.VMEM((MB, 1, d), f32),
            pltpu.VMEM((MB, 1, d), f32),
            pltpu.VMEM((MB, 1, d), f32),
            pltpu.VMEM((MB, 1, 128), f32),
            pltpu.VMEM((2, 1, d), f32),
            pltpu.VMEM((2, 1, d), f32),
            pltpu.VMEM((MB, n_dp, 1, 2 * m_ch + 128), f32),
            pltpu.VMEM((MB, n_dp, 1, 2 * d + 128), f32),
            pltpu.VMEM((MB, n_dp, 1, 2 * d + 128), f32),
            pltpu.VMEM((MB, n_dp, 1, 2 * d), f32),
            pltpu.VMEM((MB, n_dp, 1, 2 * m_ch), f32),
            pltpu.VMEM((MB, 1, 1, 2 * d), f32),
            dma((5, MB)),
            dma((5, MB)),
            dma((21,)),
            dma((MB,)),
            dma((6, MB)),
            dma((6, MB)),
            dma((6, MB)),
            dma((4, MB)),
            dma((4, MB)),
            dma((4, MB)),
        ],
        compiler_params=pltpu.CompilerParams(
            collective_id=0, has_side_effects=True, vmem_limit_bytes=62 * 2**20
        ),
    )(clips, boxes, w_s, w_t, g_s, b_s, g_t, b_t, cotangent)


def send_order(n, z, q):
    table = []
    for here in range(n):
        up = sorted(range(here + 1, n), reverse=True)
        down = list(range(here))
        table.append((up + down if here < n / 2 else down + up) + [here])
    dest = 0
    for here in range(n):
        for at in range(n):
            dest = dest + jnp.where((z == here) & (q == at), table[here][at], 0)
    return dest


FIRST = 128
PIECE = 256
SPAN = 640


def gradient_kernel(
    dims,
    a_hbm,
    v_hbm,
    gu_hbm,
    gr_hbm,
    o_s,
    o_t,
    a,
    v,
    gu,
    gr,
    window,
    window_t,
    acc_s,
    acc_t,
    got_s,
    got_t,
    out_s,
    out_t,
    load_sem,
    a_sem,
    gu_send,
    gu_recv,
    fwd_send,
    fwd_recv,
    s_send,
    s_recv,
    t_send,
    t_recv,
):
    frames, height, width = dims
    nc, rows, d = a_hbm.shape[0] // 3, a_hbm.shape[1], a_hbm.shape[2]
    m_ch = v_hbm.shape[2]
    me = lax.axis_index("dp")
    n = lax.axis_size("dp") // 2
    z = lax.div(me, 2)
    core = lax.rem(me, 2)
    twin = me + 1 - 2 * core
    inner = jnp.logical_and(z > 0, z < n - 1)
    outer = jnp.logical_not(inner)
    step = jnp.where(z < n / 2, 2, -2)
    rows_s, rows_t = o_s.shape[0], o_t.shape[0]
    n_pieces = 1 + (m_ch - FIRST) // PIECE

    barrier = pltpu.get_barrier_semaphore()

    def greet(device):
        pl.semaphore_signal(barrier, 1, device_id={"dp": device}, device_id_type=MESH)

    greet(twin)

    @pl.when(z > 0)
    def _():
        greet(me - 2)

    @pl.when(z < n - 1)
    def _():
        greet(me + 2)

    load_a = pltpu.make_async_copy(a_hbm, a.at[pl.ds(0, 3 * nc)], load_sem.at[0])
    ready = 2 * nc + nc // 2
    load_gu = pltpu.make_async_copy(
        gu_hbm.at[pl.ds(0, ready)], gu.at[pl.ds(0, ready)], load_sem.at[1]
    )
    load_v = pltpu.make_async_copy(v_hbm, v, load_sem.at[2])
    load_gr = pltpu.make_async_copy(gr_hbm, gr, load_sem.at[3])

    @pl.when(inner)
    def _():
        load_a.start()
        load_gu.start()

    load_v.start()
    load_gr.start()
    pl.semaphore_wait(barrier, 3 - jnp.where(z == 0, 1, 0) - jnp.where(z == n - 1, 1, 0))

    def columns(p):
        if isinstance(p, int) and p == 0:
            return pl.ds(0, FIRST)
        return pl.ds(pl.multiple_of(FIRST + (p - 1) * PIECE, 128), PIECE)

    def remote(src, dst, send, recv, device):
        return pltpu.make_async_remote_copy(
            src_ref=src,
            dst_ref=dst,
            send_sem=send,
            recv_sem=recv,
            device_id={"dp": device},
            device_id_type=MESH,
        )

    def gu_to_hub(p):
        s = columns(p)
        return remote(
            gu_hbm.at[pl.ds(nc // 2, nc // 2), :, s],
            gu.at[pl.ds(ready, nc // 2), :, s],
            gu_send.at[p],
            gu_recv.at[p],
            me + step,
        )

    def gu_to_twin(p):
        s = columns(p)
        return remote(
            gu.at[pl.ds(2 * nc, nc), :, s],
            gu.at[pl.ds(3 * nc, nc), :, s],
            fwd_send.at[p],
            fwd_recv.at[p],
            twin,
        )

    a_to_twin = remote(
        a.at[pl.ds(2 * nc, nc)], a.at[pl.ds(3 * nc, nc)], a_sem.at[0], a_sem.at[1], twin
    )

    def moved(x, before, after, dt, step):
        if not dt:
            return x
        y = x.reshape(before, after, 128)
        zero = jnp.zeros((before, step, 128), f32)
        if dt > 0:
            y = jnp.concatenate([y[:, step:], zero], axis=1)
        else:
            y = jnp.concatenate([zero, y[:, :-step]], axis=1)
        return y.reshape(rows, 128)

    def place(row0):
        low = lax.div(row0, 128)
        return low, row0 - low * 128

    def time_job(q):
        dest = send_order(n, z, q)
        low, start = place((2 * dest + core) * rows_t)

        def fill_time(i, c):
            to = pl.ds(pl.multiple_of(i * rows, 16), rows)
            for j in range(SPAN // 128):
                chunk = jnp.minimum(low + j, 3 * m_ch // 128 - 1)
                tap = lax.div(chunk, m_ch // 128)
                lane = pl.ds(pl.multiple_of((chunk - tap * (m_ch // 128)) * 128, 128), 128)

                def fill(dt):
                    x = v[i, :, lane].astype(f32)
                    x = moved(x, 1, rows, dt, height * width)
                    window_t[to, j * 128 : (j + 1) * 128] = x.astype(bf16)

                lax.switch(tap, [functools.partial(fill, dt) for dt in (-1, 0, 1)])
            return c

        lax.fori_loop(0, 2 * nc, fill_time, 0)
        acc_t[...] = lax.dot_general(
            window_t[...],
            gr[...].reshape(2 * nc * rows, d),
            (((0,), (0,)), ((), ())),
            preferred_element_type=f32,
        )
        at = pl.ds(pl.multiple_of(start, 8), rows_t)

        def add(slot):
            pltpu.make_async_copy(got_t.at[slot], got_t.at[slot], t_recv.at[slot]).wait()
            acc_t[at, :] += got_t[slot].astype(f32)

        @pl.when((z > 0) & (dest >= z))
        def _():
            add(dest + 1)

        @pl.when((z < n - 1) & (dest <= z))
        def _():
            add(dest)

        @pl.when(dest == z)
        def _():
            o_t[...] = acc_t[at, :]

        @pl.when(dest != z)
        def _():
            out_t[dest] = acc_t[at, :].astype(bf16)
            time_send(dest).start()

    def time_send(dest):
        right = dest > z
        slot = dest + jnp.where(right, 1, 0)
        return remote(
            out_t.at[dest],
            got_t.at[slot],
            t_send.at[dest],
            t_recv.at[slot],
            me + jnp.where(right, 2, -2),
        )

    def hub_dest(k):
        near = z < n / 2
        far_out = jnp.where(near, n - 1, 0)
        own_out = n - 1 - far_out
        return jnp.where(
            k == 0, far_out, jnp.where(k == 1, n - 1 - z, jnp.where(k == 2, own_out, z))
        )

    def space_place(k):
        return place((2 * hub_dest(k) + core) * rows_s)

    def fill_window(k, first, count):
        low, start = space_place(k)

        def fill_space(i, c):
            to = pl.ds(pl.multiple_of(i * rows, 16), rows)
            for j in range(SPAN // 128):
                chunk = jnp.minimum(low + j, 9 * d // 128 - 1)
                tap = lax.div(chunk, d // 128)
                lane = pl.ds(pl.multiple_of((chunk - tap * (d // 128)) * 128, 128), 128)

                def fill(dh, dw):
                    x = a[i, :, lane].astype(f32)
                    if dw:
                        x = pltpu.roll(x, (-dw) % rows, 0)
                    x = moved(x, frames, height * width, dh, width)
                    window[k, to, j * 128 : (j + 1) * 128] = x.astype(bf16)

                lax.switch(
                    tap,
                    [
                        functools.partial(fill, dh, dw)
                        for dh in (-1, 0, 1)
                        for dw in (-1, 0, 1)
                    ],
                )
            return c

        lax.fori_loop(first, first + count, fill_space, 0)

    def space_send(k, p):
        s = columns(p)
        return remote(
            out_s.at[k, :, s],
            got_s.at[jnp.where(k == 1, 1, 0), :, s],
            s_send.at[k, p],
            s_recv.at[jnp.where(k == 1, 1, 0), p],
            me + jnp.where(k == 2, -step, step),
        )

    def space_job(k, p):
        s = columns(p)
        size = FIRST if isinstance(p, int) else PIECE
        low, start = space_place(k)
        at = pl.ds(pl.multiple_of(start, 8), rows_s)
        acc_s[:, :size] = lax.dot_general(
            window[k],
            gu[:, :, s].reshape(4 * nc * rows, size),
            (((0,), (0,)), ((), ())),
            preferred_element_type=f32,
        )

        @pl.when(k >= 2)
        def _():
            got = got_s.at[k - 2, :, s]
            pltpu.make_async_copy(got, got, s_recv.at[k - 2, p]).wait()
            acc_s[at, :size] += got[...].astype(f32)

        @pl.when(k == 3)
        def _():
            o_s[:, s] = acc_s[at, :size]

        @pl.when(k < 3)
        def _():
            out_s[k, :, s] = acc_s[at, :size].astype(bf16)
            space_send(k, p).start()

    def take_gu(p):
        gu_to_hub(p).wait_recv()
        gu_to_twin(p).start()
        gu_to_twin(p).wait_recv()

    @pl.when(inner)
    def _():
        load_a.wait()
        a_to_twin.start()

        fill_window(0, 0, 3 * nc)
        a_to_twin.wait_recv()
        fill_window(0, 3 * nc, nc)
        load_gu.wait()

        def pair(first, p):
            def one(k, c):
                space_job(k, p)
                return c

            lax.fori_loop(first, first + 2, one, 0)

        def first_round(k, carry):
            @pl.when(k == 0)
            def _():
                take_gu(0)

            @pl.when(k > 0)
            def _():
                fill_window(k, 0, 4 * nc)

            @pl.when(k < 2)
            def _():
                space_job(k, 0)

            return carry

        lax.fori_loop(0, 4, first_round, 0)
        load_v.wait()
        load_gr.wait()

        def later_round(p, carry):
            take_gu(p)
            pair(0, p)

            @pl.when(p < 3)
            def _():
                time_job(p - 1)

            @pl.when(p == 1)
            def _():
                pair(2, 0)

            @pl.when(p > 1)
            def _():
                pair(2, p - 1)

            @pl.when(p == 3)
            def _():
                time_job(2)

            return carry

        lax.fori_loop(1, n_pieces, later_round, 0)
        pair(2, jnp.int32(n_pieces - 1))
        time_job(3)
        a_to_twin.wait_send()
        gu_to_twin(0).wait_send()

        def sent(p, carry):
            gu_to_twin(p).wait_send()
            for k in range(3):
                space_send(k, p).wait_send()
            return carry

        for k in range(3):
            space_send(k, 0).wait_send()
        lax.fori_loop(1, n_pieces, sent, 0)

    @pl.when(outer)
    def _():
        gu_to_hub(0).start()
        gu_to_hub(1).start()
        load_v.wait()
        load_gr.wait()

        def round_out(q, carry):
            time_job(q)

            @pl.when(q == 0)
            def _():
                gu_to_hub(2).start()

            @pl.when(q == 1)
            def _():
                for p in range(3, n_pieces):
                    gu_to_hub(p).start()

            return carry

        lax.fori_loop(0, n, round_out, 0)

        for p in range(n_pieces):
            s = columns(p)
            got = got_s.at[0, :, s]
            pltpu.make_async_copy(got, got, s_recv.at[0, p]).wait()
            o_s[:, s] = got[...].astype(f32)
            gu_to_hub(p).wait_send()

    def finish(q, carry):
        time_send(send_order(n, z, q)).wait_send()
        return carry

    lax.fori_loop(0, n - 1, finish, 0)


def gradients(dims, n_dp, a, v, gu, gr):
    nc, rows, d = a.shape[0] // 3, a.shape[1], a.shape[2]
    m_ch = v.shape[2]
    rows_s, rows_t = 9 * d // n_dp, 3 * m_ch // n_dp
    n = n_dp // 2
    n_pieces = 1 + (m_ch - FIRST) // PIECE
    shape = jax.ShapeDtypeStruct
    dma = pltpu.SemaphoreType.DMA
    return pl.pallas_call(
        functools.partial(gradient_kernel, dims),
        out_shape=(shape((rows_s, m_ch), f32), shape((rows_t, d), f32)),
        in_specs=[pl.BlockSpec(memory_space=pl.ANY)] * 4,
        out_specs=[pl.BlockSpec(memory_space=pltpu.VMEM)] * 2,
        scratch_shapes=[
            pltpu.VMEM((4 * nc, rows, d), bf16),
            pltpu.VMEM(v.shape, bf16),
            pltpu.VMEM((4 * nc, rows, m_ch), bf16),
            pltpu.VMEM(gr.shape, bf16),
            pltpu.VMEM((4, 4 * nc * rows, SPAN), bf16),
            pltpu.VMEM((2 * nc * rows, SPAN), bf16),
            pltpu.VMEM((SPAN, PIECE), f32),
            pltpu.VMEM((SPAN, d), f32),
            pltpu.VMEM((2, rows_s, m_ch), bf16),
            pltpu.VMEM((n + 1, rows_t, d), bf16),
            pltpu.VMEM((3, rows_s, m_ch), bf16),
            pltpu.VMEM((n, rows_t, d), bf16),
            dma((4,)),
            dma((2,)),
            dma((n_pieces,)),
            dma((n_pieces,)),
            dma((n_pieces,)),
            dma((n_pieces,)),
            dma((3, n_pieces)),
            dma((2, n_pieces)),
            dma((n,)),
            dma((n + 1,)),
        ],
        compiler_params=pltpu.CompilerParams(
            collective_id=1, has_side_effects=True, vmem_limit_bytes=62 * 2**20
        ),
    )(a, v, gu, gr)


def spatial_columns(activity):
    height, breadth = (activity.shape[2], activity.shape[3])
    padded = jnp.pad(activity, ((0, 0), (0, 0), (1, 1), (1, 1), (0, 0)))
    pieces = [
        padded[:, :, row_off : row_off + height, col_off : col_off + breadth, :]
        for row_off in range(3)
        for col_off in range(3)
    ]
    return jnp.concatenate(pieces, axis=-1)


def temporal_columns(activity):
    frames = activity.shape[1]
    padded = jnp.pad(activity, ((0, 0), (1, 1), (0, 0), (0, 0), (0, 0)))
    return jnp.concatenate([padded[:, offset : offset + frames] for offset in range(3)], axis=-1)


def left_product(former, latter):
    return lax.dot_general(
        former, latter, (((0,), (0,)), ((), ())), preferred_element_type=jnp.float32
    )


def body(
    clips,
    boxes,
    spatial_w,
    temporal_w,
    spatial_gain,
    spatial_shift,
    temporal_gain,
    temporal_shift,
    cotangent,
):
    n_clips, frames, height, breadth, d = clips.shape
    cm = n_clips // MB
    width = (breadth // 8 + 1) * 8
    rows = cm * frames * height * width
    m_ch = spatial_w.shape[2]

    def padded(x):
        x = jnp.pad(x, ((0, 0), (0, 0), (0, 0), (0, width - breadth), (0, 0)))
        return x.reshape(MB, rows, d)

    n_dp = lax.axis_size("dp")
    hubs = n_dp == 8 and 9 * d // n_dp == 576 and 3 * m_ch // n_dp == 432 and d % 128 == 0
    act, grad, a_in, hidden, gu, gr, gain_s, shift_s, gain_t, shift_t = relay(
        (cm, frames, height, width),
        n_dp,
        hubs,
        padded(clips),
        boxes,
        spatial_w[0],
        temporal_w[0],
        spatial_gain,
        spatial_shift,
        temporal_gain,
        temporal_shift,
        padded(cotangent),
    )

    def frames_of(x):
        return x.reshape(n_clips, frames, height, width, x.shape[-1])[:, :, :, :breadth]

    if hubs:
        clip_rows = frames * height * width
        grad_s, grad_t = gradients(
            (frames, height, width),
            n_dp,
            *[x.reshape(-1, clip_rows, x.shape[-1]) for x in (a_in, hidden, gu, gr)],
        )
    else:
        cells = n_clips * frames * height * breadth
        cols = spatial_columns(frames_of(a_in[0])).reshape(cells, -1)
        grad_s = left_product(cols, frames_of(gu[0]).reshape(cells, -1))
        stacked = temporal_columns(frames_of(hidden[0])).reshape(cells, -1)
        grad_t = left_product(stacked, frames_of(gr[0]).reshape(cells, -1))
        grad_s = lax.psum_scatter(grad_s, "dp", scatter_dimension=0, tiled=True)
        grad_t = lax.psum_scatter(grad_t, "dp", scatter_dimension=0, tiled=True)
    return (
        frames_of(act)[None],
        frames_of(grad)[None],
        grad_s[None],
        grad_t[None],
        gain_s,
        shift_s,
        gain_t,
        shift_t,
    )


def solution(mesh):
    clip_spec = P("dp", None, None, None, None)
    weight_spec = P("pipe", None, None)
    channel_spec = P("pipe", None)
    return jax.shard_map(
        body,
        mesh=mesh,
        in_specs=(
            clip_spec,
            P("dp", None),
            weight_spec,
            weight_spec,
            channel_spec,
            channel_spec,
            channel_spec,
            channel_spec,
            clip_spec,
        ),
        out_specs=(
            P("pipe", "dp", None, None, None, None),
            P("pipe", "dp", None, None, None, None),
            P("pipe", "dp", None),
            P("pipe", "dp", None),
            channel_spec,
            channel_spec,
            channel_spec,
            channel_spec,
        ),
        check_vma=False,
    )
```

```python
import functools

import jax
import jax.numpy as jnp
from jax import lax
from jax.experimental import pallas as pl
from jax.experimental.pallas import tpu as pltpu
from jax.sharding import PartitionSpec as P

MB = 4
eps_norm = 1e-05
bf16 = jnp.bfloat16
f32 = jnp.float32
MESH = pl.DeviceIdType.MESH


def silu(x):
    return x / (1.0 + jnp.exp(-x))


def silu_slope(x):
    s = 1.0 / (1.0 + jnp.exp(-x))
    return s * (1.0 + x * (1.0 - s))


def lane_chunks(width, body):
    def step(i, carry):
        body(i, pl.ds(pl.multiple_of(i * 128, 128), 128))
        return carry

    lax.fori_loop(0, width // 128, step, 0)


def relay_kernel(
    dims,
    clips,
    boxes,
    w_s_hbm,
    w_t_hbm,
    g_s,
    b_s,
    g_t,
    b_t,
    cotangent,
    o_act,
    o_grad,
    o_in,
    o_hidden,
    o_gu,
    o_gr,
    o_gain_s,
    o_shift_s,
    o_gain_t,
    o_shift_t,
    w_s,
    w_t,
    w_s_back,
    w_t_back,
    cols,
    a_in,
    skip_in,
    a_out,
    r_in,
    r_out,
    ga_in,
    gs_in,
    gs_out,
    ig_out,
    hidden,
    gr,
    gu,
    uh,
    r_sum,
    gq,
    keep,
    fact_s,
    fact_t,
    off_t,
    fact_p,
    off_p,
    cnt,
    scale_out,
    scale_in,
    x_s,
    x_t,
    x_p,
    x_bt,
    x_bs,
    x_bp,
    x_send,
    x_recv,
    w_sem,
    load_sem,
    store_sem,
    pipe_send,
    pipe_recv,
    twin_send,
    twin_recv,
    hub_sem,
):
    cm, frames, height, width = dims
    rows = cm * frames * height * width
    d = a_in.shape[2]
    m_ch = hidden.shape[2]
    section = lax.axis_index("pipe")
    me = lax.axis_index("dp")
    n_pipe = lax.axis_size("pipe")
    n_dp = lax.axis_size("dp")
    first = section == 0
    last = section == n_pipe - 1
    odd = lax.rem(section, 2) == 1
    even_inner = jnp.logical_and(jnp.logical_not(odd), jnp.logical_not(last))
    early = section < 2
    skip_own = odd.astype(f32)
    skip_prev = jnp.logical_not(jnp.logical_or(odd, first)).astype(f32)

    def load_ws(part, tap):
        half = d // 2
        src = w_s_hbm.at[pl.ds(tap * d + part * half, half)]
        dst = w_s.at[pl.ds((part * 9 + tap) * half, half)]
        return pltpu.make_async_copy(src, dst, w_sem.at[part * 9 + tap])

    load_wt = pltpu.make_async_copy(w_t_hbm, w_t, w_sem.at[18])

    def load_clip(m):
        return pltpu.make_async_copy(clips.at[m], a_in.at[m], load_sem.at[m])

    def load_cot(m):
        return pltpu.make_async_copy(cotangent.at[m], ga_in.at[m], load_sem.at[m])

    def load_skip(m):
        return pltpu.make_async_copy(clips.at[m], skip_in.at[m], load_sem.at[m])

    local_skip = jnp.logical_not(jnp.logical_or(first, last))

    @pl.when(first)
    def _():
        for m in range(MB):
            load_clip(m).start()

    @pl.when(local_skip)
    def _():
        for m in range(MB):
            load_skip(m).start()

    for part in range(2):
        for tap in range(9):
            load_ws(part, tap).start()
    load_wt.start()

    @pl.when(last)
    def _():
        for m in range(MB):
            load_cot(m).start()

    for ref in (o_gain_s, o_shift_s, o_gain_t, o_shift_t, gs_in, scale_in):
        ref[...] = jnp.zeros_like(ref)

    @pl.when(first)
    def _():
        skip_in[...] = jnp.zeros_like(skip_in)

    barrier = pltpu.get_barrier_semaphore()

    def greet(j, carry):
        pl.semaphore_signal(
            barrier, 1, device_id={"dp": lax.rem(me + j, n_dp)}, device_id_type=MESH
        )
        return carry

    lax.fori_loop(1, n_dp, greet, 0)

    def greet_pipe(step):
        def greet_one(j, carry):
            pl.semaphore_signal(
                barrier,
                1,
                device_id={"pipe": section + step, "dp": j},
                device_id_type=MESH,
            )
            return carry

        lax.fori_loop(0, n_dp, greet_one, 0)

    @pl.when(jnp.logical_not(first))
    def _():
        greet_pipe(-1)

    @pl.when(jnp.logical_not(last))
    def _():
        greet_pipe(1)

    pl.semaphore_signal(
        barrier,
        1,
        device_id={"pipe": section + jnp.where(early, 2, -2)},
        device_id_type=MESH,
    )
    scale_out[0] = g_t[...]
    scale_out[1] = b_t[...]

    def make_keep(m, carry):
        n_rows = frames * height * width
        pieces = []
        for c in range(cm):
            shape = (frames, height, width, 128)
            t = lax.broadcasted_iota(jnp.int32, shape, 0)
            h = lax.broadcasted_iota(jnp.int32, shape, 1)
            w = lax.broadcasted_iota(jnp.int32, shape, 2)
            box = [boxes[m * cm + c, i] for i in range(6)]
            inside = (t >= box[0]) & (t < box[1]) & (h >= box[2]) & (h < box[3])
            inside = inside & (w >= box[4]) & (w < box[5])
            pieces.append(jnp.where(inside, 1.0, 0.0).astype(f32).reshape(n_rows, 128))
        mask = jnp.concatenate(pieces, axis=0) if cm > 1 else pieces[0]
        keep[m] = mask
        cnt[m] = jnp.sum(mask, axis=0, keepdims=True)
        return carry

    lax.fori_loop(0, MB, make_keep, 0)
    sides = 3 - jnp.where(first, 1, 0) - jnp.where(last, 1, 0)
    pl.semaphore_wait(barrier, sides * n_dp)

    def send_scale():
        return pltpu.make_async_remote_copy(
            src_ref=scale_out,
            dst_ref=scale_in,
            send_sem=w_sem.at[19],
            recv_sem=w_sem.at[20],
            device_id={"pipe": section + 1},
            device_id_type=MESH,
        )

    @pl.when(jnp.logical_not(last))
    def _():
        send_scale().start()

    def share(kind, buf, m):
        def send(j, carry):
            pltpu.make_async_remote_copy(
                src_ref=buf.at[m, me],
                dst_ref=buf.at[m, me],
                send_sem=x_send.at[kind, m],
                recv_sem=x_recv.at[kind, m],
                device_id={"dp": lax.rem(me + j, n_dp)},
                device_id_type=MESH,
            ).start()
            return carry

        lax.fori_loop(1, n_dp, send, 0)

    def shared(kind, buf, m):
        others = buf.at[m, pl.ds(0, n_dp - 1)]
        pltpu.make_async_copy(others, others, x_send.at[kind, m]).wait()
        pltpu.make_async_copy(others, others, x_recv.at[kind, m]).wait()

    def cross(kind, src, dst, m, step):
        def send(j, carry):
            pltpu.make_async_remote_copy(
                src_ref=src,
                dst_ref=dst.at[m, me],
                send_sem=x_send.at[kind, m],
                recv_sem=x_recv.at[kind, m],
                device_id={"pipe": section + step, "dp": lax.rem(me + j, n_dp)},
                device_id_type=MESH,
            ).start()
            return carry

        lax.fori_loop(0, n_dp, send, 0)

    def crossed(kind, buf, m):
        slots = buf.at[m]
        pltpu.make_async_copy(slots, slots, x_recv.at[kind, m]).wait()

    def cross_sent(kind, buf, m):
        slots = buf.at[m]
        pltpu.make_async_copy(slots, slots, x_send.at[kind, m]).wait()

    def to_pipe(kind, src, dst, m, step):
        return pltpu.make_async_remote_copy(
            src_ref=src.at[m],
            dst_ref=dst.at[m],
            send_sem=pipe_send.at[kind, m],
            recv_sem=pipe_recv.at[kind, m],
            device_id={"pipe": section + step},
            device_id_type=MESH,
        )

    half = d // 2

    def half_to_pipe(kind, part, src, dst, m, step):
        s = pl.ds(part * half, half)
        return pltpu.make_async_remote_copy(
            src_ref=src.at[m, :, s],
            dst_ref=dst.at[m, :, s],
            send_sem=pipe_send.at[kind + part, m],
            recv_sem=pipe_recv.at[kind + part, m],
            device_id={"pipe": section + step},
            device_id_type=MESH,
        )

    hubs = o_in.shape[0] > 2
    z = lax.div(me, 2)
    outer = jnp.logical_or(z == 0, z == n_dp // 2 - 1)

    def to_hub(m):
        return pltpu.make_async_remote_copy(
            src_ref=a_in.at[m],
            dst_ref=o_in.at[2, m],
            send_sem=hub_sem.at[0, m],
            recv_sem=hub_sem.at[1, m],
            device_id={"dp": me + jnp.where(z == 0, 2, -2)},
            device_id_type=MESH,
        )

    def inputs_to_hub():
        @pl.when(outer)
        def _():
            for m in range(MB):
                to_hub(m).start()

    def gu_to_hub(part):
        m = min(part, 1)
        s = (pl.ds(0, m_ch), pl.ds(0, 640), pl.ds(640, m_ch - 640))[part]
        return pltpu.make_async_remote_copy(
            src_ref=gu.at[m, :, s],
            dst_ref=o_gu.at[2, m, :, s],
            send_sem=hub_sem.at[2, part],
            recv_sem=hub_sem.at[3, part],
            device_id={"dp": me + jnp.where(z == 0, 2, -2)},
            device_id_type=MESH,
        )

    def store(kind, src, dst, m):
        return pltpu.make_async_copy(src.at[m], dst.at[m], store_sem.at[kind, m])

    def keep_operand(kind, src, dst, m):
        return pltpu.make_async_copy(src.at[m], dst.at[0, m], store_sem.at[kind, m])

    def twin_operand(kind, src, dst, m):
        return pltpu.make_async_remote_copy(
            src_ref=src.at[m],
            dst_ref=dst.at[1, m],
            send_sem=twin_send.at[kind - 2, m],
            recv_sem=twin_recv.at[kind - 2, m],
            device_id={"dp": me + 1 - 2 * lax.rem(me, 2)},
            device_id_type=MESH,
        )

    def share_operand(kind, src, dst, m):
        keep_operand(kind, src, dst, m).start()
        twin_operand(kind, src, dst, m).start()

    def shift_space(x, dh, dw):
        if dw:
            x = pltpu.roll(x, (-dw) % rows, 0)
        return shift_rows(x, dh)

    def shift_rows(x, dh):
        if not dh:
            return x
        y = x.reshape(cm * frames, height * width, 128)
        zero = jnp.zeros((cm * frames, width, 128), f32)
        if dh > 0:
            y = jnp.concatenate([y[:, width:], zero], axis=1)
        else:
            y = jnp.concatenate([zero, y[:, :-width]], axis=1)
        return y.reshape(rows, 128)

    def shift_time(x, dt):
        if not dt:
            return x
        y = x.reshape(cm, frames * height * width, 128)
        step = height * width
        zero = jnp.zeros((cm, step, 128), f32)
        if dt > 0:
            y = jnp.concatenate([y[:, step:], zero], axis=1)
        else:
            y = jnp.concatenate([zero, y[:, :-step]], axis=1)
        return y.reshape(rows, 128)

    def local_sums(m, value, buf, c, channels):
        mask = keep[m]
        n_here = cnt[m]
        total = jnp.sum(mask * value, axis=0, keepdims=True)
        dev = mask * (value - total / n_here)
        spread = jnp.sum(dev * dev, axis=0, keepdims=True)
        buf[m, me, :, pl.ds(pl.multiple_of(c * 128, 128), 128)] = total
        buf[m, me, :, pl.ds(pl.multiple_of(channels + c * 128, 128), 128)] = spread
        return dev

    def merged(m, buf, c, channels):
        counts = buf[m, :, :, 2 * channels :]
        sums = buf[m, :, :, pl.ds(pl.multiple_of(c * 128, 128), 128)]
        spreads = buf[m, :, :, pl.ds(pl.multiple_of(channels + c * 128, 128), 128)]
        n = jnp.sum(counts, axis=0)
        mean = jnp.sum(sums, axis=0) / n
        off = sums / counts - mean[None]
        var = jnp.sum(spreads + counts * off * off, axis=0) / n
        return n, mean, lax.rsqrt(var + eps_norm)

    def lanes_of(part, i):
        return pl.ds(pl.multiple_of(part * half + i * 128, 128), 128)

    def normed_prev(m, s):
        return (r_in[m, :, s].astype(f32) + off_p[m, :, s]) * fact_p[m, :, s]

    def preact_prev(m, s, normed):
        return scale_in[0, :, s] * normed + scale_in[1, :, s]

    def skipped_prev(m, s, value):
        return value + skip_prev * skip_in[m, :, s].astype(f32)

    def activate(m, part, i, s):
        s = lanes_of(part, i)
        n, mean, rstd = merged(m, x_p, part * (half // 128) + i, d)
        off_p[m, :, s] = x_p[m, me, :, s] / x_p[m, me, :, 2 * d :] - mean
        fact_p[m, :, s] = rstd
        value = preact_prev(m, s, normed_prev(m, s))

        @pl.when(section == 2)
        def _():
            a_in[m, :, s] = (keep[m] * silu(skipped_prev(m, s, value))).astype(bf16)

        @pl.when(section != 2)
        def _():
            a_in[m, :, s] = (keep[m] * silu(value)).astype(bf16)

    def forward_spatial(m):
        @pl.when(first)
        def _():
            load_clip(m).wait()

        @pl.when(jnp.logical_not(first))
        def _():
            @pl.when(m == 0)
            def _():
                send_scale().wait_recv()

            @pl.when(local_skip)
            def _():
                load_skip(m).wait()

            crossed(4, x_p, m)

        for part in range(2):

            @pl.when(jnp.logical_not(first))
            def _():
                half_to_pipe(2, part, r_out, r_in, m, 1).wait_recv()
                lane_chunks(half, functools.partial(activate, m, part))

            def column(i, s):
                s = pl.ds(pl.multiple_of(part * half + i * 128, 128), 128)
                x = a_in[m, :, s].astype(f32)
                for dw in (-1, 0, 1):
                    y = shift_space(x, 0, dw)
                    for dh in (-1, 0, 1):
                        tap = (dh + 1) * 3 + dw + 1
                        at = part * 9 * half + tap * half + i * 128
                        cols[:, pl.ds(pl.multiple_of(at, 128), 128)] = shift_rows(y, dh).astype(
                            bf16
                        )

            lane_chunks(half, column)

            @pl.when((m == 0) & first)
            def _():
                for tap in range(9):
                    load_ws(part, tap).wait()

            k = slice(part * 9 * half, (part + 1) * 9 * half)
            for s in (slice(0, 512), slice(512, m_ch)):
                value = jnp.dot(cols[:, k], w_s[k, s], preferred_element_type=f32)
                if part == 0:
                    uh[m, :, s] = value
                else:
                    uh[m, :, s] += value

        x_s[m, me, :, 2 * m_ch :] = cnt[m]

        def sums(i, s):
            local_sums(m, uh[m, :, s], x_s, i, m_ch)

        lane_chunks(m_ch, sums)
        share(0, x_s, m)
        share_operand(2, a_in, o_in, m)

    def forward_temporal(m):
        shared(0, x_s, m)

        def column(i, s):
            n, mean, rstd = merged(m, x_s, i, m_ch)
            fact_s[m, :, s] = rstd
            normed = (uh[m, :, s] - mean) * rstd
            uh[m, :, s] = normed
            value = keep[m] * silu(g_s[:, s] * normed + b_s[:, s])
            value = value.astype(bf16)
            hidden[m, :, s] = value
            value = value.astype(f32)
            for dt in (-1, 0, 1):
                at = pl.ds(pl.multiple_of((dt + 1) * m_ch + i * 128, 128), 128)
                cols[:, at] = shift_time(value, dt).astype(bf16)

        lane_chunks(m_ch, column)
        share_operand(3, hidden, o_hidden, m)

        @pl.when((m == 0) & first)
        def _():
            load_wt.wait()

        r_sum[...] = jnp.dot(cols[:, : 3 * m_ch], w_t[...], preferred_element_type=f32)
        x_t[m, me, :, 2 * d :] = cnt[m]

        def centre(i, s):
            r_out[m, :, s] = local_sums(m, r_sum[:, s], x_t, i, d).astype(bf16)

        lane_chunks(d, centre)

        @pl.when(jnp.logical_not(last))
        def _():
            cross(4, x_t.at[m, me], x_p, m, 1)
            for part in range(2):
                half_to_pipe(2, part, r_out, r_in, m, 1).start()

        share(1, x_t, m)

    def normed_own(m, s):
        return (r_out[m, :, s].astype(f32) + off_t[m, :, s]) * fact_t[m, :, s]

    def preact_own(m, s, normed):
        return g_t[:, s] * normed + b_t[:, s] + skip_own * skip_in[m, :, s].astype(f32)

    def forward_out(m):
        @pl.when(last)
        def _():
            to_pipe(0, a_out, skip_in, m, 2).wait_recv()

        shared(1, x_t, m)

        def column(i, s):
            n, mean, rstd = merged(m, x_t, i, d)
            off_t[m, :, s] = x_t[m, me, :, s] / cnt[m] - mean
            fact_t[m, :, s] = rstd
            value = keep[m] * silu(preact_own(m, s, normed_own(m, s)))
            a_out[m, :, s] = value.astype(bf16)

        lane_chunks(d, column)
        store(0, a_out, o_act, m).start()

        @pl.when(section == 1)
        def _():
            to_pipe(0, a_out, skip_in, m, 2).start()

    def slope_sums(row, value, normed, i, s):
        row[:, s] = jnp.sum(value, axis=0, keepdims=True)
        at = pl.ds(pl.multiple_of(d + i * 128, 128), 128)
        row[:, at] = jnp.sum(value * normed, axis=0, keepdims=True)

    def own_slope(m, s, normed):
        return ga_in[m, :, s].astype(f32) * keep[m] * silu_slope(preact_own(m, s, normed))

    def backward_in(m):
        load_cot(m).wait()

        def column(i, s):
            normed = normed_own(m, s)
            slope_sums(x_bt.at[m, me], own_slope(m, s, normed), normed, i, s)

        lane_chunks(d, column)
        share(2, x_bt, m)

    def totals(buf, m, s, i, channels):
        at = pl.ds(pl.multiple_of(channels + i * 128, 128), 128)
        return jnp.sum(buf[m, :, :, s], axis=0), jnp.sum(buf[m, :, :, at], axis=0)

    def backward_temporal(m):
        @pl.when(last)
        def _():
            shared(2, x_bt, m)

        @pl.when(jnp.logical_not(last))
        def _():
            crossed(2, x_bt, m)
            for part in range(2):
                half_to_pipe(4, part, ig_out, ga_in, m, -1).wait_recv()

        n = jnp.sum(x_t[m, :, :, 2 * d :], axis=0)

        def column(i, s):
            shift_sum, gain_sum = totals(x_bt, m, s, i, d)
            o_shift_t[:, s] += shift_sum
            o_gain_t[:, s] += gain_sum
            normed = normed_own(m, s)
            slope = own_slope(m, s, normed)

            @pl.when(last)
            def _():
                gs_out[m, :, s] = slope.astype(bf16)

            scale = g_t[:, s] * fact_t[m, :, s]
            value = keep[m] * scale * (slope - (shift_sum + normed * gain_sum) / n)
            value = value.astype(bf16)
            gr[m, :, s] = value
            value = value.astype(f32)
            for dt in (-1, 0, 1):
                at = pl.ds(pl.multiple_of((dt + 1) * d + i * 128, 128), 128)
                cols[:, at] = shift_time(value, -dt).astype(bf16)

        lane_chunks(d, column)
        share_operand(4, gr, o_gr, m)

        gq[lax.rem(m, 2)] = jnp.dot(cols[:, : 3 * d], w_t_back[...], preferred_element_type=f32)

        def sums(i, s):
            normed = uh[m, :, s]
            slope = keep[m] * gq[lax.rem(m, 2), :, s] * silu_slope(g_s[:, s] * normed + b_s[:, s])
            gq[lax.rem(m, 2), :, s] = slope
            x_bs[m, me, :, s] = jnp.sum(slope, axis=0, keepdims=True)
            at = pl.ds(pl.multiple_of(m_ch + i * 128, 128), 128)
            x_bs[m, me, :, at] = jnp.sum(slope * normed, axis=0, keepdims=True)

        lane_chunks(m_ch, sums)
        share(3, x_bs, m)

    def backward_spatial(m):
        shared(3, x_bs, m)
        n = jnp.sum(x_t[m, :, :, 2 * d :], axis=0)

        def column(i, s):
            shift_sum, gain_sum = totals(x_bs, m, s, i, m_ch)
            o_shift_s[:, s] += shift_sum
            o_gain_s[:, s] += gain_sum
            scale = g_s[:, s] * fact_s[m, :, s]
            value = keep[m] * scale * (gq[lax.rem(m, 2), :, s] - (shift_sum + uh[m, :, s] * gain_sum) / n)
            value = value.astype(bf16)
            gu[m, :, s] = value
            value = value.astype(f32)
            for dw in (-1, 0, 1):
                y = shift_space(value, 0, -dw)
                for dh in (-1, 0, 1):
                    tap = (dh + 1) * 3 + dw + 1
                    at = pl.ds(pl.multiple_of(tap * m_ch + i * 128, 128), 128)
                    cols[:, at] = shift_rows(y, -dh).astype(bf16)

        lane_chunks(m_ch, column)
        share_operand(5, gu, o_gu, m)
        if hubs:
            for part in range(2):

                @pl.when(outer & first & (m == part))
                def _():
                    gu_to_hub(part).start()


        @pl.when(even_inner)
        def _():
            to_pipe(1, gs_out, gs_in, m, -1).wait_recv()

        with_skip = even_inner.astype(f32)
        for part in range(2):
            s = slice(part * half, (part + 1) * half)
            value = jnp.dot(cols[...], w_s_back[:, s], preferred_element_type=f32)
            ig_out[m, :, s] = (value + with_skip * gs_in[m, :, s].astype(f32)).astype(bf16)

            @pl.when(jnp.logical_not(first))
            def _():
                def sums(i, s):
                    s = lanes_of(part, i)
                    normed = normed_prev(m, s)
                    slope = silu_slope(skipped_prev(m, s, preact_prev(m, s, normed)))
                    slope = ig_out[m, :, s].astype(f32) * keep[m] * slope

                    @pl.when(section == 2)
                    def _():
                        gs_out[m, :, s] = slope.astype(bf16)

                    slope_sums(x_bp.at[m, 0], slope, normed, part * (half // 128) + i, s)

                if part == 0:
                    half_to_pipe(4, part, ig_out, ga_in, m, -1).start()
                lane_chunks(half, sums)
                if part == 1:
                    cross(2, x_bp.at[m, 0], x_bt, m, -1)
                    half_to_pipe(4, part, ig_out, ga_in, m, -1).start()

        store(1, ig_out, o_grad, m).start()

    def send_skip_grad(m):
        to_pipe(1, gs_out, gs_in, m, jnp.where(last, -1, -2)).start()

    def turn_weights():
        @pl.when(jnp.logical_not(first))
        def _():
            for part in range(2):
                for tap in range(9):
                    load_ws(part, tap).wait()
            load_wt.wait()

        def spatial(tap, carry):
            dst = pl.ds(pl.multiple_of(tap * m_ch, 128), m_ch)
            for part in range(2):
                src = pl.ds(pl.multiple_of((part * 9 + tap) * half, 128), half)
                w_s_back[dst, part * half : (part + 1) * half] = w_s[src, :].T
            return carry

        lax.fori_loop(0, 9, spatial, 0)

        def temporal(tap, carry):
            src = pl.ds(pl.multiple_of(tap * m_ch, 128), m_ch)
            dst = pl.ds(pl.multiple_of(tap * d, 128), d)
            w_t_back[dst, :] = w_t[src, :].T
            return carry

        lax.fori_loop(0, 3, temporal, 0)

    pairs = MB // 2
    wait_back = jnp.where(last, 1, pairs)

    def step(s, carry):
        do_f = s < pairs
        do_b = jnp.logical_and(s >= wait_back, s < wait_back + pairs)
        mf = 2 * jnp.minimum(s, pairs - 1)
        mb = 2 * jnp.clip(s - wait_back, 0, pairs - 1)

        @pl.when(s == jnp.where(first, wait_back, 0))
        def _():
            turn_weights()

        def both(when, phase, m):
            @pl.when(when)
            def _():
                def one(j, c):
                    phase(m + j)
                    return c

                lax.fori_loop(0, 2, one, 0)

        inner = jnp.logical_not(last)
        done_f = jnp.logical_and(s > 0, s <= pairs)
        md = 2 * jnp.clip(s - 1, 0, pairs - 1)
        both(jnp.logical_and(done_f, last), forward_out, md)
        both(jnp.logical_and(do_b, last), backward_in, mb)
        both(do_f, forward_spatial, mf)
        both(jnp.logical_and(done_f, inner), forward_out, md)
        both(do_b, backward_temporal, mb)
        if hubs:

            @pl.when(outer & (s == wait_back + 1) & first)
            def _():
                gu_to_hub(2).start()

        both(do_f, forward_temporal, mf)
        both(do_b, backward_spatial, mb)
        both(jnp.logical_and(do_b, jnp.logical_not(early)), send_skip_grad, mb)
        if hubs:

            @pl.when(s == jnp.where(last, wait_back + 1, pairs - 1))
            def _():
                inputs_to_hub()

            @pl.when(outer & (s == wait_back + 1) & jnp.logical_not(first))
            def _():
                for part in range(3):
                    gu_to_hub(part).start()

        return carry

    lax.fori_loop(0, 2 * pairs, step, 0)

    def finish(m, carry):
        store(0, a_out, o_act, m).wait()
        store(1, ig_out, o_grad, m).wait()
        for kind, src, dst in (
            (2, a_in, o_in),
            (3, hidden, o_hidden),
            (4, gr, o_gr),
            (5, gu, o_gu),
        ):
            keep_operand(kind, src, dst, m).wait()
            twin_operand(kind, src, dst, m).wait()

        @pl.when(jnp.logical_not(last))
        def _():
            cross_sent(4, x_p, m)
            for part in range(2):
                half_to_pipe(2, part, r_out, r_in, m, 1).wait_send()


        @pl.when(section == 1)
        def _():
            to_pipe(0, a_out, skip_in, m, 2).wait_send()

        @pl.when(jnp.logical_not(first))
        def _():
            cross_sent(2, x_bt, m)
            for part in range(2):
                half_to_pipe(4, part, ig_out, ga_in, m, -1).wait_send()

        @pl.when(jnp.logical_not(early))
        def _():
            to_pipe(1, gs_out, gs_in, m, -1).wait_send()

        return carry

    lax.fori_loop(0, MB, finish, 0)
    if hubs:
        for m in range(MB):

            @pl.when(outer)
            def _():
                to_hub(m).wait_send()
                if m < 3:
                    gu_to_hub(m).wait_send()

            @pl.when(jnp.logical_not(outer))
            def _():
                to_hub(m).wait_recv()
                if m < 3:
                    gu_to_hub(m).wait_recv()

    @pl.when(jnp.logical_not(last))
    def _():
        send_scale().wait_send()


def relay(dims, n_dp, hubs, clips, boxes, w_s, w_t, g_s, b_s, g_t, b_t, cotangent):
    cm, frames, height, width = dims
    rows = cm * frames * height * width
    d, m_ch = w_t.shape[1], w_s.shape[1]
    shape = jax.ShapeDtypeStruct
    vmem = pl.BlockSpec(memory_space=pltpu.VMEM)
    hbm = pl.BlockSpec(memory_space=pl.ANY)
    smem = pl.BlockSpec(memory_space=pltpu.SMEM)
    dma = pltpu.SemaphoreType.DMA
    narrow = pltpu.VMEM((MB, rows, d), bf16)
    wide = pltpu.VMEM((MB, rows, m_ch), bf16)
    return pl.pallas_call(
        functools.partial(relay_kernel, dims),
        out_shape=(
            shape((MB, rows, d), bf16),
            shape((MB, rows, d), bf16),
            shape((3 if hubs else 2, MB, rows, d), bf16),
            shape((2, MB, rows, m_ch), bf16),
            shape((3 if hubs else 2, MB, rows, m_ch), bf16),
            shape((2, MB, rows, d), bf16),
            shape((1, m_ch), f32),
            shape((1, m_ch), f32),
            shape((1, d), f32),
            shape((1, d), f32),
        ),
        in_specs=[hbm, smem, hbm, hbm, vmem, vmem, vmem, vmem, hbm],
        out_specs=[hbm] * 6 + [vmem] * 4,
        scratch_shapes=[
            pltpu.VMEM(w_s.shape, bf16),
            pltpu.VMEM(w_t.shape, bf16),
            pltpu.VMEM((9 * m_ch, d), bf16),
            pltpu.VMEM((3 * d, m_ch), bf16),
            pltpu.VMEM((rows, 9 * m_ch), bf16),
            narrow,
            narrow,
            narrow,
            narrow,
            narrow,
            narrow,
            narrow,
            narrow,
            narrow,
            wide,
            narrow,
            wide,
            pltpu.VMEM((MB, rows, m_ch), f32),
            pltpu.VMEM((rows, d), f32),
            pltpu.VMEM((2, rows, m_ch), f32),
            pltpu.VMEM((MB, rows, 128), f32),
            pltpu.VMEM((MB, 1, m_ch), f32),
            pltpu.VMEM((MB, 1, d), f32),
            pltpu.VMEM((MB, 1, d), f32),
            pltpu.VMEM((MB, 1, d), f32),
            pltpu.VMEM((MB, 1, d), f32),
            pltpu.VMEM((MB, 1, 128), f32),
            pltpu.VMEM((2, 1, d), f32),
            pltpu.VMEM((2, 1, d), f32),
            pltpu.VMEM((MB, n_dp, 1, 2 * m_ch + 128), f32),
            pltpu.VMEM((MB, n_dp, 1, 2 * d + 128), f32),
            pltpu.VMEM((MB, n_dp, 1, 2 * d + 128), f32),
            pltpu.VMEM((MB, n_dp, 1, 2 * d), f32),
            pltpu.VMEM((MB, n_dp, 1, 2 * m_ch), f32),
            pltpu.VMEM((MB, 1, 1, 2 * d), f32),
            dma((5, MB)),
            dma((5, MB)),
            dma((21,)),
            dma((MB,)),
            dma((6, MB)),
            dma((6, MB)),
            dma((6, MB)),
            dma((4, MB)),
            dma((4, MB)),
            dma((4, MB)),
        ],
        compiler_params=pltpu.CompilerParams(
            collective_id=0, has_side_effects=True, vmem_limit_bytes=62 * 2**20
        ),
    )(clips, boxes, w_s, w_t, g_s, b_s, g_t, b_t, cotangent)


def send_order(n, z, q):
    table = []
    for here in range(n):
        up = sorted(range(here + 1, n), reverse=True)
        down = list(range(here))
        table.append((up + down if here < n / 2 else down + up) + [here])
    dest = 0
    for here in range(n):
        for at in range(n):
            dest = dest + jnp.where((z == here) & (q == at), table[here][at], 0)
    return dest


PIECE = 384
SPAN = 640

HUB_JOBS = (
    (0, 0, -1),
    (0, 1, 0),
    (1, 0, -1),
    (2, 0, -1),
    (0, 2, 1),
    (2, 1, -1),
    (1, 1, -1),
    (1, 2, -1),
    (3, 0, 2),
    (2, 2, 3),
    (3, 1, -1),
    (3, 2, -1),
)


def of_job(j, column):
    return sum(jnp.where(j == i, job[column], 0) for i, job in enumerate(HUB_JOBS))


def is_one_of(j, members):
    found = j < 0
    for i in members:
        found = found | (j == i)
    return found


def gradient_kernel(
    dims,
    a_hbm,
    v_hbm,
    gu_hbm,
    gr_hbm,
    o_s,
    o_t,
    a,
    v,
    gu,
    gr,
    window,
    window_t,
    acc_s,
    acc_t,
    got_s,
    got_t,
    out_s,
    out_t,
    load_sem,
    a_sem,
    gu_send,
    gu_recv,
    fwd_send,
    fwd_recv,
    s_send,
    s_recv,
    t_send,
    t_recv,
):
    frames, height, width = dims
    nc, rows, d = a_hbm.shape[0] // 3, a_hbm.shape[1], a_hbm.shape[2]
    m_ch = v_hbm.shape[2]
    me = lax.axis_index("dp")
    n = lax.axis_size("dp") // 2
    z = lax.div(me, 2)
    core = lax.rem(me, 2)
    twin = me + 1 - 2 * core
    inner = jnp.logical_and(z > 0, z < n - 1)
    outer = jnp.logical_not(inner)
    step = jnp.where(z < n / 2, 2, -2)
    rows_s, rows_t = o_s.shape[0], o_t.shape[0]
    n_pieces = m_ch // PIECE

    barrier = pltpu.get_barrier_semaphore()

    def greet(device):
        pl.semaphore_signal(barrier, 1, device_id={"dp": device}, device_id_type=MESH)

    greet(twin)

    @pl.when(z > 0)
    def _():
        greet(me - 2)

    @pl.when(z < n - 1)
    def _():
        greet(me + 2)

    load_a = pltpu.make_async_copy(a_hbm, a.at[pl.ds(0, 3 * nc)], load_sem.at[0])
    ready = 2 * nc + nc // 2
    load_gu = pltpu.make_async_copy(
        gu_hbm.at[pl.ds(0, ready)], gu.at[pl.ds(0, ready)], load_sem.at[1]
    )
    load_v = pltpu.make_async_copy(v_hbm, v, load_sem.at[2])
    load_gr = pltpu.make_async_copy(gr_hbm, gr, load_sem.at[3])

    @pl.when(inner)
    def _():
        load_a.start()
        load_gu.start()

    load_v.start()
    load_gr.start()
    pl.semaphore_wait(barrier, 3 - jnp.where(z == 0, 1, 0) - jnp.where(z == n - 1, 1, 0))

    def columns(p):
        return pl.ds(pl.multiple_of(p * PIECE, 128), PIECE)

    def remote(src, dst, send, recv, device):
        return pltpu.make_async_remote_copy(
            src_ref=src,
            dst_ref=dst,
            send_sem=send,
            recv_sem=recv,
            device_id={"dp": device},
            device_id_type=MESH,
        )

    def gu_to_hub(p):
        s = columns(p)
        return remote(
            gu_hbm.at[pl.ds(nc // 2, nc // 2), :, s],
            gu.at[pl.ds(ready, nc // 2), :, s],
            gu_send.at[p],
            gu_recv.at[p],
            me + step,
        )

    def gu_to_twin(p):
        s = columns(p)
        return remote(
            gu.at[pl.ds(2 * nc, nc), :, s],
            gu.at[pl.ds(3 * nc, nc), :, s],
            fwd_send.at[p],
            fwd_recv.at[p],
            twin,
        )

    a_to_twin = remote(
        a.at[pl.ds(2 * nc, nc)], a.at[pl.ds(3 * nc, nc)], a_sem.at[0], a_sem.at[1], twin
    )

    def moved(x, before, after, dt, step):
        if not dt:
            return x
        y = x.reshape(before, after, 128)
        zero = jnp.zeros((before, step, 128), f32)
        if dt > 0:
            y = jnp.concatenate([y[:, step:], zero], axis=1)
        else:
            y = jnp.concatenate([zero, y[:, :-step]], axis=1)
        return y.reshape(rows, 128)

    def place(row0):
        low = lax.div(row0, 128)
        return low, row0 - low * 128

    def time_job(q):
        dest = send_order(n, z, q)
        low, start = place((2 * dest + core) * rows_t)

        def fill_time(i, c):
            to = pl.ds(pl.multiple_of(i * rows, 16), rows)
            for j in range(SPAN // 128):
                chunk = jnp.minimum(low + j, 3 * m_ch // 128 - 1)
                tap = lax.div(chunk, m_ch // 128)
                lane = pl.ds(pl.multiple_of((chunk - tap * (m_ch // 128)) * 128, 128), 128)

                def fill(dt):
                    x = v[i, :, lane].astype(f32)
                    x = moved(x, 1, rows, dt, height * width)
                    window_t[to, j * 128 : (j + 1) * 128] = x.astype(bf16)

                lax.switch(tap, [functools.partial(fill, dt) for dt in (-1, 0, 1)])
            return c

        lax.fori_loop(0, 2 * nc, fill_time, 0)
        acc_t[...] = lax.dot_general(
            window_t[...],
            gr[...].reshape(2 * nc * rows, d),
            (((0,), (0,)), ((), ())),
            preferred_element_type=f32,
        )
        at = pl.ds(pl.multiple_of(start, 8), rows_t)

        def add(slot):
            pltpu.make_async_copy(got_t.at[slot], got_t.at[slot], t_recv.at[slot]).wait()
            acc_t[at, :] += got_t[slot].astype(f32)

        @pl.when((z > 0) & (dest >= z))
        def _():
            add(dest + 1)

        @pl.when((z < n - 1) & (dest <= z))
        def _():
            add(dest)

        @pl.when(dest == z)
        def _():
            o_t[...] = acc_t[at, :]

        @pl.when(dest != z)
        def _():
            out_t[dest] = acc_t[at, :].astype(bf16)
            time_send(dest).start()

    def time_send(dest):
        right = dest > z
        slot = dest + jnp.where(right, 1, 0)
        return remote(
            out_t.at[dest],
            got_t.at[slot],
            t_send.at[dest],
            t_recv.at[slot],
            me + jnp.where(right, 2, -2),
        )

    def hub_dest(k):
        near = z < n / 2
        far_out = jnp.where(near, n - 1, 0)
        own_out = n - 1 - far_out
        return jnp.where(
            k == 0, far_out, jnp.where(k == 1, n - 1 - z, jnp.where(k == 2, own_out, z))
        )

    def space_place(k):
        return place((2 * hub_dest(k) + core) * rows_s)

    def fill_window(k, first, count):
        low, start = space_place(k)

        def fill_space(i, c):
            to = pl.ds(pl.multiple_of(i * rows, 16), rows)
            for j in range(SPAN // 128):
                chunk = jnp.minimum(low + j, 9 * d // 128 - 1)
                tap = lax.div(chunk, d // 128)
                lane = pl.ds(pl.multiple_of((chunk - tap * (d // 128)) * 128, 128), 128)

                def fill(dh, dw):
                    x = a[i, :, lane].astype(f32)
                    if dw:
                        x = pltpu.roll(x, (-dw) % rows, 0)
                    x = moved(x, frames, height * width, dh, width)
                    window[k, to, j * 128 : (j + 1) * 128] = x.astype(bf16)

                lax.switch(
                    tap,
                    [
                        functools.partial(fill, dh, dw)
                        for dh in (-1, 0, 1)
                        for dw in (-1, 0, 1)
                    ],
                )
            return c

        lax.fori_loop(first, first + count, fill_space, 0)

    def space_send(k, p):
        s = columns(p)
        return remote(
            out_s.at[k, :, s],
            got_s.at[jnp.where(k == 1, 1, 0), :, s],
            s_send.at[k, p],
            s_recv.at[jnp.where(k == 1, 1, 0), p],
            me + jnp.where(k == 2, -step, step),
        )

    def space_job(k, p):
        s = columns(p)
        low, start = space_place(k)
        at = pl.ds(pl.multiple_of(start, 8), rows_s)
        acc_s[...] = lax.dot_general(
            window[k],
            gu[:, :, s].reshape(4 * nc * rows, PIECE),
            (((0,), (0,)), ((), ())),
            preferred_element_type=f32,
        )

        @pl.when(k >= 2)
        def _():
            got = got_s.at[k - 2, :, s]
            pltpu.make_async_copy(got, got, s_recv.at[k - 2, p]).wait()
            acc_s[at, :] += got[...].astype(f32)

        @pl.when(k == 3)
        def _():
            o_s[:, s] = acc_s[at, :]

        @pl.when(k < 3)
        def _():
            out_s[k, :, s] = acc_s[at, :].astype(bf16)
            space_send(k, p).start()

    def take_gu(p):
        gu_to_hub(p).wait_recv()
        gu_to_twin(p).start()
        gu_to_twin(p).wait_recv()

    @pl.when(inner)
    def _():
        load_a.wait()
        a_to_twin.start()

        a_to_twin.wait_recv()

        new_k = [i for i, job in enumerate(HUB_JOBS) if job[0] not in [x[0] for x in HUB_JOBS[:i]]]
        new_p = [i for i, job in enumerate(HUB_JOBS) if job[1] not in [x[1] for x in HUB_JOBS[:i]]]
        timed = [i for i, job in enumerate(HUB_JOBS) if job[2] >= 0]

        def hub_job(j, carry):
            k, p = of_job(j, 0), of_job(j, 1)

            @pl.when(is_one_of(j, new_k))
            def _():
                fill_window(k, 0, 4 * nc)

            @pl.when(j == 0)
            def _():
                load_gu.wait()

            @pl.when(is_one_of(j, new_p))
            def _():
                take_gu(p)

            space_job(k, p)

            @pl.when(j == timed[0])
            def _():
                load_v.wait()
                load_gr.wait()

            @pl.when(is_one_of(j, timed))
            def _():
                time_job(of_job(j, 2))

            return carry

        lax.fori_loop(0, len(HUB_JOBS), hub_job, 0)
        a_to_twin.wait_send()

        def sent(p, carry):
            gu_to_twin(p).wait_send()
            for k in range(3):
                space_send(k, p).wait_send()
            return carry

        lax.fori_loop(0, n_pieces, sent, 0)

    @pl.when(outer)
    def _():
        gu_to_hub(0).start()
        gu_to_hub(1).start()
        load_v.wait()
        load_gr.wait()

        def round_out(q, carry):
            time_job(q)

            @pl.when(q == 0)
            def _():
                for p in range(2, n_pieces):
                    gu_to_hub(p).start()

            return carry

        lax.fori_loop(0, n, round_out, 0)

        for p in range(n_pieces):
            s = columns(p)
            got = got_s.at[0, :, s]
            pltpu.make_async_copy(got, got, s_recv.at[0, p]).wait()
            o_s[:, s] = got[...].astype(f32)
            gu_to_hub(p).wait_send()

    def finish(q, carry):
        time_send(send_order(n, z, q)).wait_send()
        return carry

    lax.fori_loop(0, n - 1, finish, 0)


def gradients(dims, n_dp, a, v, gu, gr):
    nc, rows, d = a.shape[0] // 3, a.shape[1], a.shape[2]
    m_ch = v.shape[2]
    rows_s, rows_t = 9 * d // n_dp, 3 * m_ch // n_dp
    n = n_dp // 2
    n_pieces = m_ch // PIECE
    shape = jax.ShapeDtypeStruct
    dma = pltpu.SemaphoreType.DMA
    return pl.pallas_call(
        functools.partial(gradient_kernel, dims),
        out_shape=(shape((rows_s, m_ch), f32), shape((rows_t, d), f32)),
        in_specs=[pl.BlockSpec(memory_space=pl.ANY)] * 4,
        out_specs=[pl.BlockSpec(memory_space=pltpu.VMEM)] * 2,
        scratch_shapes=[
            pltpu.VMEM((4 * nc, rows, d), bf16),
            pltpu.VMEM(v.shape, bf16),
            pltpu.VMEM((4 * nc, rows, m_ch), bf16),
            pltpu.VMEM(gr.shape, bf16),
            pltpu.VMEM((4, 4 * nc * rows, SPAN), bf16),
            pltpu.VMEM((2 * nc * rows, SPAN), bf16),
            pltpu.VMEM((SPAN, PIECE), f32),
            pltpu.VMEM((SPAN, d), f32),
            pltpu.VMEM((2, rows_s, m_ch), bf16),
            pltpu.VMEM((n + 1, rows_t, d), bf16),
            pltpu.VMEM((3, rows_s, m_ch), bf16),
            pltpu.VMEM((n, rows_t, d), bf16),
            dma((4,)),
            dma((2,)),
            dma((n_pieces,)),
            dma((n_pieces,)),
            dma((n_pieces,)),
            dma((n_pieces,)),
            dma((3, n_pieces)),
            dma((2, n_pieces)),
            dma((n,)),
            dma((n + 1,)),
        ],
        compiler_params=pltpu.CompilerParams(
            collective_id=1, has_side_effects=True, vmem_limit_bytes=62 * 2**20
        ),
    )(a, v, gu, gr)


def spatial_columns(activity):
    height, breadth = (activity.shape[2], activity.shape[3])
    padded = jnp.pad(activity, ((0, 0), (0, 0), (1, 1), (1, 1), (0, 0)))
    pieces = [
        padded[:, :, row_off : row_off + height, col_off : col_off + breadth, :]
        for row_off in range(3)
        for col_off in range(3)
    ]
    return jnp.concatenate(pieces, axis=-1)


def temporal_columns(activity):
    frames = activity.shape[1]
    padded = jnp.pad(activity, ((0, 0), (1, 1), (0, 0), (0, 0), (0, 0)))
    return jnp.concatenate([padded[:, offset : offset + frames] for offset in range(3)], axis=-1)


def left_product(former, latter):
    return lax.dot_general(
        former, latter, (((0,), (0,)), ((), ())), preferred_element_type=jnp.float32
    )


def body(
    clips,
    boxes,
    spatial_w,
    temporal_w,
    spatial_gain,
    spatial_shift,
    temporal_gain,
    temporal_shift,
    cotangent,
):
    n_clips, frames, height, breadth, d = clips.shape
    cm = n_clips // MB
    width = (breadth // 8 + 1) * 8
    rows = cm * frames * height * width
    m_ch = spatial_w.shape[2]

    def padded(x):
        x = jnp.pad(x, ((0, 0), (0, 0), (0, 0), (0, width - breadth), (0, 0)))
        return x.reshape(MB, rows, d)

    n_dp = lax.axis_size("dp")
    hubs = n_dp == 8 and 9 * d // n_dp == 576 and 3 * m_ch // n_dp == 432 and d % 128 == 0
    act, grad, a_in, hidden, gu, gr, gain_s, shift_s, gain_t, shift_t = relay(
        (cm, frames, height, width),
        n_dp,
        hubs,
        padded(clips),
        boxes,
        spatial_w[0],
        temporal_w[0],
        spatial_gain,
        spatial_shift,
        temporal_gain,
        temporal_shift,
        padded(cotangent),
    )

    def frames_of(x):
        return x.reshape(n_clips, frames, height, width, x.shape[-1])[:, :, :, :breadth]

    if hubs:
        clip_rows = frames * height * width
        grad_s, grad_t = gradients(
            (frames, height, width),
            n_dp,
            *[x.reshape(-1, clip_rows, x.shape[-1]) for x in (a_in, hidden, gu, gr)],
        )
    else:
        cells = n_clips * frames * height * breadth
        cols = spatial_columns(frames_of(a_in[0])).reshape(cells, -1)
        grad_s = left_product(cols, frames_of(gu[0]).reshape(cells, -1))
        stacked = temporal_columns(frames_of(hidden[0])).reshape(cells, -1)
        grad_t = left_product(stacked, frames_of(gr[0]).reshape(cells, -1))
        grad_s = lax.psum_scatter(grad_s, "dp", scatter_dimension=0, tiled=True)
        grad_t = lax.psum_scatter(grad_t, "dp", scatter_dimension=0, tiled=True)
    return (
        frames_of(act)[None],
        frames_of(grad)[None],
        grad_s[None],
        grad_t[None],
        gain_s,
        shift_s,
        gain_t,
        shift_t,
    )


def solution(mesh):
    clip_spec = P("dp", None, None, None, None)
    weight_spec = P("pipe", None, None)
    channel_spec = P("pipe", None)
    return jax.shard_map(
        body,
        mesh=mesh,
        in_specs=(
            clip_spec,
            P("dp", None),
            weight_spec,
            weight_spec,
            channel_spec,
            channel_spec,
            channel_spec,
            channel_spec,
            clip_spec,
        ),
        out_specs=(
            P("pipe", "dp", None, None, None, None),
            P("pipe", "dp", None, None, None, None),
            P("pipe", "dp", None),
            P("pipe", "dp", None),
            channel_spec,
            channel_spec,
            channel_spec,
            channel_spec,
        ),
        check_vma=False,
    )
```

```python
import functools

import jax
import jax.numpy as jnp
from jax import lax
from jax.experimental import pallas as pl
from jax.experimental.pallas import tpu as pltpu
from jax.sharding import PartitionSpec as P

MB = 4
eps_norm = 1e-05
bf16 = jnp.bfloat16
f32 = jnp.float32
MESH = pl.DeviceIdType.MESH


def silu(x):
    return x / (1.0 + jnp.exp(-x))


def silu_slope(x):
    s = 1.0 / (1.0 + jnp.exp(-x))
    return s * (1.0 + x * (1.0 - s))


def lane_chunks(width, body):
    def step(i, carry):
        body(i, pl.ds(pl.multiple_of(i * 128, 128), 128))
        return carry

    lax.fori_loop(0, width // 128, step, 0)


def relay_kernel(
    dims,
    clips,
    boxes,
    w_s_hbm,
    w_t_hbm,
    g_s,
    b_s,
    g_t,
    b_t,
    cotangent,
    o_act,
    o_grad,
    o_in,
    o_hidden,
    o_gu,
    o_gr,
    o_gain_s,
    o_shift_s,
    o_gain_t,
    o_shift_t,
    w_s,
    w_t,
    w_s_back,
    w_t_back,
    cols,
    a_in,
    skip_in,
    a_out,
    r_in,
    r_out,
    ga_in,
    gs_in,
    gs_out,
    ig_out,
    hidden,
    gr,
    gu,
    uh,
    r_sum,
    gq,
    keep,
    fact_s,
    fact_t,
    off_t,
    fact_p,
    off_p,
    cnt,
    scale_out,
    scale_in,
    x_s,
    x_t,
    x_p,
    x_bt,
    x_bs,
    x_bp,
    x_send,
    x_recv,
    w_sem,
    load_sem,
    store_sem,
    pipe_send,
    pipe_recv,
    twin_send,
    twin_recv,
    hub_sem,
):
    cm, frames, height, width = dims
    rows = cm * frames * height * width
    d = a_in.shape[2]
    m_ch = hidden.shape[2]
    section = lax.axis_index("pipe")
    me = lax.axis_index("dp")
    n_pipe = lax.axis_size("pipe")
    n_dp = lax.axis_size("dp")
    first = section == 0
    last = section == n_pipe - 1
    odd = lax.rem(section, 2) == 1
    even_inner = jnp.logical_and(jnp.logical_not(odd), jnp.logical_not(last))
    early = section < 2
    skip_own = odd.astype(f32)
    skip_prev = jnp.logical_not(jnp.logical_or(odd, first)).astype(f32)

    def load_ws(part, tap):
        half = d // 2
        src = w_s_hbm.at[pl.ds(tap * d + part * half, half)]
        dst = w_s.at[pl.ds((part * 9 + tap) * half, half)]
        return pltpu.make_async_copy(src, dst, w_sem.at[part * 9 + tap])

    load_wt = pltpu.make_async_copy(w_t_hbm, w_t, w_sem.at[18])

    def load_clip(m):
        return pltpu.make_async_copy(clips.at[m], a_in.at[m], load_sem.at[m])

    def load_cot(m):
        return pltpu.make_async_copy(cotangent.at[m], ga_in.at[m], load_sem.at[m])

    def load_skip(m):
        return pltpu.make_async_copy(clips.at[m], skip_in.at[m], load_sem.at[m])

    local_skip = jnp.logical_not(jnp.logical_or(first, last))

    @pl.when(first)
    def _():
        for m in range(MB):
            load_clip(m).start()

    @pl.when(local_skip)
    def _():
        for m in range(MB):
            load_skip(m).start()

    for part in range(2):
        for tap in range(9):
            load_ws(part, tap).start()
    load_wt.start()

    @pl.when(last)
    def _():
        for m in range(MB):
            load_cot(m).start()

    for ref in (o_gain_s, o_shift_s, o_gain_t, o_shift_t, gs_in, scale_in):
        ref[...] = jnp.zeros_like(ref)

    @pl.when(first)
    def _():
        skip_in[...] = jnp.zeros_like(skip_in)

    barrier = pltpu.get_barrier_semaphore()

    def greet(j, carry):
        pl.semaphore_signal(
            barrier, 1, device_id={"dp": lax.rem(me + j, n_dp)}, device_id_type=MESH
        )
        return carry

    lax.fori_loop(1, n_dp, greet, 0)

    def greet_pipe(step):
        def greet_one(j, carry):
            pl.semaphore_signal(
                barrier,
                1,
                device_id={"pipe": section + step, "dp": j},
                device_id_type=MESH,
            )
            return carry

        lax.fori_loop(0, n_dp, greet_one, 0)

    @pl.when(jnp.logical_not(first))
    def _():
        greet_pipe(-1)

    @pl.when(jnp.logical_not(last))
    def _():
        greet_pipe(1)

    pl.semaphore_signal(
        barrier,
        1,
        device_id={"pipe": section + jnp.where(early, 2, -2)},
        device_id_type=MESH,
    )
    scale_out[0] = g_t[...]
    scale_out[1] = b_t[...]

    def make_keep(m, carry):
        n_rows = frames * height * width
        pieces = []
        for c in range(cm):
            shape = (frames, height, width, 128)
            t = lax.broadcasted_iota(jnp.int32, shape, 0)
            h = lax.broadcasted_iota(jnp.int32, shape, 1)
            w = lax.broadcasted_iota(jnp.int32, shape, 2)
            box = [boxes[m * cm + c, i] for i in range(6)]
            inside = (t >= box[0]) & (t < box[1]) & (h >= box[2]) & (h < box[3])
            inside = inside & (w >= box[4]) & (w < box[5])
            pieces.append(jnp.where(inside, 1.0, 0.0).astype(f32).reshape(n_rows, 128))
        mask = jnp.concatenate(pieces, axis=0) if cm > 1 else pieces[0]
        keep[m] = mask
        cnt[m] = jnp.sum(mask, axis=0, keepdims=True)
        return carry

    lax.fori_loop(0, MB, make_keep, 0)
    def share(kind, buf, m):
        def send(j, carry):
            pltpu.make_async_remote_copy(
                src_ref=buf.at[m, me],
                dst_ref=buf.at[m, me],
                send_sem=x_send.at[kind, m],
                recv_sem=x_recv.at[kind, m],
                device_id={"dp": lax.rem(me + j, n_dp)},
                device_id_type=MESH,
            ).start()
            return carry

        lax.fori_loop(1, n_dp, send, 0)

    def shared(kind, buf, m):
        others = buf.at[m, pl.ds(0, n_dp - 1)]
        pltpu.make_async_copy(others, others, x_send.at[kind, m]).wait()
        pltpu.make_async_copy(others, others, x_recv.at[kind, m]).wait()

    def cross(kind, src, dst, m, step):
        def send(j, carry):
            pltpu.make_async_remote_copy(
                src_ref=src,
                dst_ref=dst.at[m, me],
                send_sem=x_send.at[kind, m],
                recv_sem=x_recv.at[kind, m],
                device_id={"pipe": section + step, "dp": lax.rem(me + j, n_dp)},
                device_id_type=MESH,
            ).start()
            return carry

        lax.fori_loop(0, n_dp, send, 0)

    def crossed(kind, buf, m):
        slots = buf.at[m]
        pltpu.make_async_copy(slots, slots, x_recv.at[kind, m]).wait()

    def cross_sent(kind, buf, m):
        slots = buf.at[m]
        pltpu.make_async_copy(slots, slots, x_send.at[kind, m]).wait()

    def to_pipe(kind, src, dst, m, step):
        return pltpu.make_async_remote_copy(
            src_ref=src.at[m],
            dst_ref=dst.at[m],
            send_sem=pipe_send.at[kind, m],
            recv_sem=pipe_recv.at[kind, m],
            device_id={"pipe": section + step},
            device_id_type=MESH,
        )

    half = d // 2

    def half_to_pipe(kind, part, src, dst, m, step):
        s = pl.ds(part * half, half)
        return pltpu.make_async_remote_copy(
            src_ref=src.at[m, :, s],
            dst_ref=dst.at[m, :, s],
            send_sem=pipe_send.at[kind + part, m],
            recv_sem=pipe_recv.at[kind + part, m],
            device_id={"pipe": section + step},
            device_id_type=MESH,
        )

    hubs = o_in.shape[0] > 2
    z = lax.div(me, 2)
    outer = jnp.logical_or(z == 0, z == n_dp // 2 - 1)

    def to_hub(m):
        return pltpu.make_async_remote_copy(
            src_ref=a_in.at[m],
            dst_ref=o_in.at[2, m],
            send_sem=hub_sem.at[0, m],
            recv_sem=hub_sem.at[1, m],
            device_id={"dp": me + jnp.where(z == 0, 2, -2)},
            device_id_type=MESH,
        )

    def inputs_to_hub():
        @pl.when(outer)
        def _():
            for m in range(MB):
                to_hub(m).start()

    def gu_to_hub(part):
        m = max(part - 1, 0)
        s = (pl.ds(0, 640), pl.ds(640, m_ch - 640), pl.ds(0, PIECE))[min(part, 2)]
        return pltpu.make_async_remote_copy(
            src_ref=gu.at[m, :, s],
            dst_ref=o_gu.at[2, m, :, s],
            send_sem=hub_sem.at[2, part],
            recv_sem=hub_sem.at[3, part],
            device_id={"dp": me + jnp.where(z == 0, 2, -2)},
            device_id_type=MESH,
        )

    def store(kind, src, dst, m):
        return pltpu.make_async_copy(src.at[m], dst.at[m], store_sem.at[kind, m])

    def keep_operand(kind, src, dst, m):
        return pltpu.make_async_copy(src.at[m], dst.at[0, m], store_sem.at[kind, m])

    def twin_operand(kind, src, dst, m):
        return pltpu.make_async_remote_copy(
            src_ref=src.at[m],
            dst_ref=dst.at[1, m],
            send_sem=twin_send.at[kind - 2, m],
            recv_sem=twin_recv.at[kind - 2, m],
            device_id={"dp": me + 1 - 2 * lax.rem(me, 2)},
            device_id_type=MESH,
        )

    def share_operand(kind, src, dst, m):
        keep_operand(kind, src, dst, m).start()
        twin_operand(kind, src, dst, m).start()

    def shift_space(x, dh, dw):
        if dw:
            x = pltpu.roll(x, (-dw) % rows, 0)
        return shift_rows(x, dh)

    def shift_rows(x, dh):
        if not dh:
            return x
        y = x.reshape(cm * frames, height * width, 128)
        zero = jnp.zeros((cm * frames, width, 128), f32)
        if dh > 0:
            y = jnp.concatenate([y[:, width:], zero], axis=1)
        else:
            y = jnp.concatenate([zero, y[:, :-width]], axis=1)
        return y.reshape(rows, 128)

    def shift_time(x, dt):
        if not dt:
            return x
        y = x.reshape(cm, frames * height * width, 128)
        step = height * width
        zero = jnp.zeros((cm, step, 128), f32)
        if dt > 0:
            y = jnp.concatenate([y[:, step:], zero], axis=1)
        else:
            y = jnp.concatenate([zero, y[:, :-step]], axis=1)
        return y.reshape(rows, 128)

    def local_sums(m, value, buf, c, channels):
        mask = keep[m]
        n_here = cnt[m]
        total = jnp.sum(mask * value, axis=0, keepdims=True)
        dev = mask * (value - total / n_here)
        spread = jnp.sum(dev * dev, axis=0, keepdims=True)
        buf[m, me, :, pl.ds(pl.multiple_of(c * 128, 128), 128)] = total
        buf[m, me, :, pl.ds(pl.multiple_of(channels + c * 128, 128), 128)] = spread
        return dev

    def merged(m, buf, c, channels):
        counts = buf[m, :, :, 2 * channels :]
        sums = buf[m, :, :, pl.ds(pl.multiple_of(c * 128, 128), 128)]
        spreads = buf[m, :, :, pl.ds(pl.multiple_of(channels + c * 128, 128), 128)]
        n = jnp.sum(counts, axis=0)
        mean = jnp.sum(sums, axis=0) / n
        off = sums / counts - mean[None]
        var = jnp.sum(spreads + counts * off * off, axis=0) / n
        return n, mean, lax.rsqrt(var + eps_norm)

    def lanes_of(part, i):
        return pl.ds(pl.multiple_of(part * half + i * 128, 128), 128)

    def normed_prev(m, s):
        return (r_in[m, :, s].astype(f32) + off_p[m, :, s]) * fact_p[m, :, s]

    def preact_prev(m, s, normed):
        return scale_in[0, :, s] * normed + scale_in[1, :, s]

    def skipped_prev(m, s, value):
        return value + skip_prev * skip_in[m, :, s].astype(f32)

    def activate(m, part, i, s):
        s = lanes_of(part, i)
        n, mean, rstd = merged(m, x_p, part * (half // 128) + i, d)
        off_p[m, :, s] = x_p[m, me, :, s] / x_p[m, me, :, 2 * d :] - mean
        fact_p[m, :, s] = rstd
        value = preact_prev(m, s, normed_prev(m, s))

        @pl.when(section == 2)
        def _():
            a_in[m, :, s] = (keep[m] * silu(skipped_prev(m, s, value))).astype(bf16)

        @pl.when(section != 2)
        def _():
            a_in[m, :, s] = (keep[m] * silu(value)).astype(bf16)

    def spatial_conv(m, begins):
        for part in range(2):
            if not begins:

                @pl.when(jnp.logical_not(first))
                def _():
                    half_to_pipe(2, part, r_out, r_in, m, 1).wait_recv()
                    lane_chunks(half, functools.partial(activate, m, part))

            def column(i, s):
                s = lanes_of(part, i)
                x = a_in[m, :, s].astype(f32)
                for dw in (-1, 0, 1):
                    y = shift_space(x, 0, dw)
                    for dh in (-1, 0, 1):
                        tap = (dh + 1) * 3 + dw + 1
                        at = part * 9 * half + tap * half + i * 128
                        cols[:, pl.ds(pl.multiple_of(at, 128), 128)] = shift_rows(y, dh).astype(
                            bf16
                        )

            lane_chunks(half, column)
            if begins:
                for tap in range(9):
                    load_ws(part, tap).wait()

            k = slice(part * 9 * half, (part + 1) * 9 * half)
            for s in (slice(0, 512), slice(512, m_ch)):
                value = jnp.dot(cols[:, k], w_s[k, s], preferred_element_type=f32)
                if part == 0:
                    uh[m, :, s] = value
                else:
                    uh[m, :, s] += value

    @pl.when(first)
    def _():
        load_clip(0).wait()
        spatial_conv(0, True)

    sides = 3 - jnp.where(first, 1, 0) - jnp.where(last, 1, 0)
    pl.semaphore_wait(barrier, sides * n_dp)

    def send_scale():
        return pltpu.make_async_remote_copy(
            src_ref=scale_out,
            dst_ref=scale_in,
            send_sem=w_sem.at[19],
            recv_sem=w_sem.at[20],
            device_id={"pipe": section + 1},
            device_id_type=MESH,
        )

    @pl.when(jnp.logical_not(last))
    def _():
        send_scale().start()

    def forward_spatial(m):
        @pl.when(first & (m > 0))
        def _():
            load_clip(m).wait()

        @pl.when(jnp.logical_not(first))
        def _():
            @pl.when(m == 0)
            def _():
                send_scale().wait_recv()

            @pl.when(local_skip)
            def _():
                load_skip(m).wait()

            crossed(4, x_p, m)

        @pl.when(jnp.logical_not(first & (m == 0)))
        def _():
            spatial_conv(m, False)

        x_s[m, me, :, 2 * m_ch :] = cnt[m]

        def sums(i, s):
            local_sums(m, uh[m, :, s], x_s, i, m_ch)

        lane_chunks(m_ch, sums)
        share(0, x_s, m)
        share_operand(2, a_in, o_in, m)

    def forward_temporal(m):
        shared(0, x_s, m)

        def column(i, s):
            n, mean, rstd = merged(m, x_s, i, m_ch)
            fact_s[m, :, s] = rstd
            normed = (uh[m, :, s] - mean) * rstd
            uh[m, :, s] = normed
            value = keep[m] * silu(g_s[:, s] * normed + b_s[:, s])
            value = value.astype(bf16)
            hidden[m, :, s] = value
            value = value.astype(f32)
            for dt in (-1, 0, 1):
                at = pl.ds(pl.multiple_of((dt + 1) * m_ch + i * 128, 128), 128)
                cols[:, at] = shift_time(value, dt).astype(bf16)

        lane_chunks(m_ch, column)
        share_operand(3, hidden, o_hidden, m)

        @pl.when((m == 0) & first)
        def _():
            load_wt.wait()

        r_sum[...] = jnp.dot(cols[:, : 3 * m_ch], w_t[...], preferred_element_type=f32)
        x_t[m, me, :, 2 * d :] = cnt[m]

        def centre(i, s):
            r_out[m, :, s] = local_sums(m, r_sum[:, s], x_t, i, d).astype(bf16)

        lane_chunks(d, centre)

        @pl.when(jnp.logical_not(last))
        def _():
            cross(4, x_t.at[m, me], x_p, m, 1)
            for part in range(2):
                half_to_pipe(2, part, r_out, r_in, m, 1).start()

        share(1, x_t, m)

    def normed_own(m, s):
        return (r_out[m, :, s].astype(f32) + off_t[m, :, s]) * fact_t[m, :, s]

    def preact_own(m, s, normed):
        return g_t[:, s] * normed + b_t[:, s] + skip_own * skip_in[m, :, s].astype(f32)

    def forward_out(m):
        @pl.when(last)
        def _():
            to_pipe(0, a_out, skip_in, m, 2).wait_recv()

        shared(1, x_t, m)

        def column(i, s):
            n, mean, rstd = merged(m, x_t, i, d)
            off_t[m, :, s] = x_t[m, me, :, s] / cnt[m] - mean
            fact_t[m, :, s] = rstd
            value = keep[m] * silu(preact_own(m, s, normed_own(m, s)))
            a_out[m, :, s] = value.astype(bf16)

        lane_chunks(d, column)
        store(0, a_out, o_act, m).start()

        @pl.when(section == 1)
        def _():
            to_pipe(0, a_out, skip_in, m, 2).start()

    def slope_sums(row, value, normed, i, s):
        row[:, s] = jnp.sum(value, axis=0, keepdims=True)
        at = pl.ds(pl.multiple_of(d + i * 128, 128), 128)
        row[:, at] = jnp.sum(value * normed, axis=0, keepdims=True)

    def own_slope(m, s, normed):
        return ga_in[m, :, s].astype(f32) * keep[m] * silu_slope(preact_own(m, s, normed))

    def backward_in(m):
        load_cot(m).wait()

        def column(i, s):
            normed = normed_own(m, s)
            slope_sums(x_bt.at[m, me], own_slope(m, s, normed), normed, i, s)

        lane_chunks(d, column)
        share(2, x_bt, m)

    def totals(buf, m, s, i, channels):
        at = pl.ds(pl.multiple_of(channels + i * 128, 128), 128)
        return jnp.sum(buf[m, :, :, s], axis=0), jnp.sum(buf[m, :, :, at], axis=0)

    def backward_temporal(m):
        @pl.when(last)
        def _():
            shared(2, x_bt, m)

        @pl.when(jnp.logical_not(last))
        def _():
            crossed(2, x_bt, m)
            for part in range(2):
                half_to_pipe(4, part, ig_out, ga_in, m, -1).wait_recv()

        n = jnp.sum(x_t[m, :, :, 2 * d :], axis=0)

        def column(i, s):
            shift_sum, gain_sum = totals(x_bt, m, s, i, d)
            o_shift_t[:, s] += shift_sum
            o_gain_t[:, s] += gain_sum
            normed = normed_own(m, s)
            slope = own_slope(m, s, normed)

            @pl.when(last)
            def _():
                gs_out[m, :, s] = slope.astype(bf16)

            scale = g_t[:, s] * fact_t[m, :, s]
            value = keep[m] * scale * (slope - (shift_sum + normed * gain_sum) / n)
            value = value.astype(bf16)
            gr[m, :, s] = value
            value = value.astype(f32)
            for dt in (-1, 0, 1):
                at = pl.ds(pl.multiple_of((dt + 1) * d + i * 128, 128), 128)
                cols[:, at] = shift_time(value, -dt).astype(bf16)

        lane_chunks(d, column)
        share_operand(4, gr, o_gr, m)

        gq[lax.rem(m, 2)] = jnp.dot(cols[:, : 3 * d], w_t_back[...], preferred_element_type=f32)

        def sums(i, s):
            normed = uh[m, :, s]
            slope = keep[m] * gq[lax.rem(m, 2), :, s] * silu_slope(g_s[:, s] * normed + b_s[:, s])
            gq[lax.rem(m, 2), :, s] = slope
            x_bs[m, me, :, s] = jnp.sum(slope, axis=0, keepdims=True)
            at = pl.ds(pl.multiple_of(m_ch + i * 128, 128), 128)
            x_bs[m, me, :, at] = jnp.sum(slope * normed, axis=0, keepdims=True)

        lane_chunks(m_ch, sums)
        share(3, x_bs, m)

    def backward_spatial(m):
        shared(3, x_bs, m)
        n = jnp.sum(x_t[m, :, :, 2 * d :], axis=0)

        def column(i, s):
            shift_sum, gain_sum = totals(x_bs, m, s, i, m_ch)
            o_shift_s[:, s] += shift_sum
            o_gain_s[:, s] += gain_sum
            scale = g_s[:, s] * fact_s[m, :, s]
            value = keep[m] * scale * (gq[lax.rem(m, 2), :, s] - (shift_sum + uh[m, :, s] * gain_sum) / n)
            value = value.astype(bf16)
            gu[m, :, s] = value
            value = value.astype(f32)
            for dw in (-1, 0, 1):
                y = shift_space(value, 0, -dw)
                for dh in (-1, 0, 1):
                    tap = (dh + 1) * 3 + dw + 1
                    at = pl.ds(pl.multiple_of(tap * m_ch + i * 128, 128), 128)
                    cols[:, at] = shift_rows(y, -dh).astype(bf16)

        lane_chunks(m_ch, column)
        share_operand(5, gu, o_gu, m)
        if hubs:
            for part, when in ((0, 0), (1, 0), (3, 2)):

                @pl.when(outer & first & (m == when))
                def _():
                    gu_to_hub(part).start()


        @pl.when(even_inner)
        def _():
            to_pipe(1, gs_out, gs_in, m, -1).wait_recv()

        with_skip = even_inner.astype(f32)
        for part in range(2):
            s = slice(part * half, (part + 1) * half)
            value = jnp.dot(cols[...], w_s_back[:, s], preferred_element_type=f32)
            ig_out[m, :, s] = (value + with_skip * gs_in[m, :, s].astype(f32)).astype(bf16)

            @pl.when(jnp.logical_not(first))
            def _():
                def sums(i, s):
                    s = lanes_of(part, i)
                    normed = normed_prev(m, s)
                    slope = silu_slope(skipped_prev(m, s, preact_prev(m, s, normed)))
                    slope = ig_out[m, :, s].astype(f32) * keep[m] * slope

                    @pl.when(section == 2)
                    def _():
                        gs_out[m, :, s] = slope.astype(bf16)

                    slope_sums(x_bp.at[m, 0], slope, normed, part * (half // 128) + i, s)

                if part == 0:
                    half_to_pipe(4, part, ig_out, ga_in, m, -1).start()
                lane_chunks(half, sums)
                if part == 1:
                    cross(2, x_bp.at[m, 0], x_bt, m, -1)
                    half_to_pipe(4, part, ig_out, ga_in, m, -1).start()

        store(1, ig_out, o_grad, m).start()

    def send_skip_grad(m):
        to_pipe(1, gs_out, gs_in, m, jnp.where(last, -1, -2)).start()

    def turn_weights():
        @pl.when(jnp.logical_not(first))
        def _():
            for part in range(2):
                for tap in range(9):
                    load_ws(part, tap).wait()
            load_wt.wait()

        def spatial(tap, carry):
            dst = pl.ds(pl.multiple_of(tap * m_ch, 128), m_ch)
            for part in range(2):
                src = pl.ds(pl.multiple_of((part * 9 + tap) * half, 128), half)
                w_s_back[dst, part * half : (part + 1) * half] = w_s[src, :].T
            return carry

        lax.fori_loop(0, 9, spatial, 0)

        def temporal(tap, carry):
            src = pl.ds(pl.multiple_of(tap * m_ch, 128), m_ch)
            dst = pl.ds(pl.multiple_of(tap * d, 128), d)
            w_t_back[dst, :] = w_t[src, :].T
            return carry

        lax.fori_loop(0, 3, temporal, 0)

    pairs = MB // 2
    wait_back = jnp.where(last, 1, pairs)

    def step(s, carry):
        do_f = s < pairs
        do_b = jnp.logical_and(s >= wait_back, s < wait_back + pairs)
        mf = 2 * jnp.minimum(s, pairs - 1)
        mb = 2 * jnp.clip(s - wait_back, 0, pairs - 1)

        @pl.when(s == jnp.where(first, wait_back, 0))
        def _():
            turn_weights()

        def both(when, phase, m):
            @pl.when(when)
            def _():
                def one(j, c):
                    phase(m + j)
                    return c

                lax.fori_loop(0, 2, one, 0)

        def some(begin, end, m):
            def spatial(j, c):
                backward_spatial(m + j)
                return c

            def skip(j, c):
                send_skip_grad(m + j)
                return c

            lax.fori_loop(begin, end, spatial, 0)

            @pl.when(jnp.logical_not(early))
            def _():
                lax.fori_loop(begin, end, skip, 0)

        inner = jnp.logical_not(last)
        done_f = jnp.logical_and(s > 0, s <= pairs)
        md = 2 * jnp.clip(s - 1, 0, pairs - 1)
        both(jnp.logical_and(done_f, last), forward_out, md)
        both(jnp.logical_and(do_b, last), backward_in, mb)
        some(1, jnp.where(last & do_b & (s > wait_back), 2, 1), mb - 2)
        both(do_f, forward_spatial, mf)
        both(jnp.logical_and(done_f, inner), forward_out, md)
        both(do_b, backward_temporal, mb)
        if hubs:

            @pl.when(outer & first & (s == wait_back + 1))
            def _():
                gu_to_hub(2).start()

        both(do_f, forward_temporal, mf)
        ends = s == wait_back + pairs - 1
        some(0, jnp.where(do_b, jnp.where(last & jnp.logical_not(ends), 1, 2), 0), mb)
        if hubs:

            @pl.when(s == jnp.where(last, wait_back + 1, pairs - 1))
            def _():
                inputs_to_hub()

            @pl.when(outer & (section == 1) & (s == wait_back))
            def _():
                gu_to_hub(0).start()

            @pl.when(outer & (section > 1) & (s == wait_back + 1))
            def _():
                gu_to_hub(0).start()

            @pl.when(outer & jnp.logical_not(first) & (s == wait_back + 1))
            def _():
                for part in range(1, MB):
                    gu_to_hub(part).start()

        return carry

    lax.fori_loop(0, 2 * pairs, step, 0)

    def finish(m, carry):
        store(0, a_out, o_act, m).wait()
        store(1, ig_out, o_grad, m).wait()
        for kind, src, dst in (
            (2, a_in, o_in),
            (3, hidden, o_hidden),
            (4, gr, o_gr),
            (5, gu, o_gu),
        ):
            keep_operand(kind, src, dst, m).wait()
            twin_operand(kind, src, dst, m).wait()

        @pl.when(jnp.logical_not(last))
        def _():
            cross_sent(4, x_p, m)
            for part in range(2):
                half_to_pipe(2, part, r_out, r_in, m, 1).wait_send()


        @pl.when(section == 1)
        def _():
            to_pipe(0, a_out, skip_in, m, 2).wait_send()

        @pl.when(jnp.logical_not(first))
        def _():
            cross_sent(2, x_bt, m)
            for part in range(2):
                half_to_pipe(4, part, ig_out, ga_in, m, -1).wait_send()

        @pl.when(jnp.logical_not(early))
        def _():
            to_pipe(1, gs_out, gs_in, m, -1).wait_send()

        return carry

    lax.fori_loop(0, MB, finish, 0)
    if hubs:


        @pl.when(outer)
        def _():
            for m in range(MB):
                to_hub(m).wait_send()
            for part in range(MB):
                gu_to_hub(part).wait_send()

        @pl.when(jnp.logical_not(outer))
        def _():
            for m in range(MB):
                to_hub(m).wait_recv()
            for part in range(MB):
                gu_to_hub(part).wait_recv()

    @pl.when(jnp.logical_not(last))
    def _():
        send_scale().wait_send()


def relay(dims, n_dp, hubs, clips, boxes, w_s, w_t, g_s, b_s, g_t, b_t, cotangent):
    cm, frames, height, width = dims
    rows = cm * frames * height * width
    d, m_ch = w_t.shape[1], w_s.shape[1]
    shape = jax.ShapeDtypeStruct
    vmem = pl.BlockSpec(memory_space=pltpu.VMEM)
    hbm = pl.BlockSpec(memory_space=pl.ANY)
    smem = pl.BlockSpec(memory_space=pltpu.SMEM)
    dma = pltpu.SemaphoreType.DMA
    narrow = pltpu.VMEM((MB, rows, d), bf16)
    wide = pltpu.VMEM((MB, rows, m_ch), bf16)
    return pl.pallas_call(
        functools.partial(relay_kernel, dims),
        out_shape=(
            shape((MB, rows, d), bf16),
            shape((MB, rows, d), bf16),
            shape((3 if hubs else 2, MB, rows, d), bf16),
            shape((2, MB, rows, m_ch), bf16),
            shape((3 if hubs else 2, MB, rows, m_ch), bf16),
            shape((2, MB, rows, d), bf16),
            shape((1, m_ch), f32),
            shape((1, m_ch), f32),
            shape((1, d), f32),
            shape((1, d), f32),
        ),
        in_specs=[hbm, smem, hbm, hbm, vmem, vmem, vmem, vmem, hbm],
        out_specs=[hbm] * 6 + [vmem] * 4,
        scratch_shapes=[
            pltpu.VMEM(w_s.shape, bf16),
            pltpu.VMEM(w_t.shape, bf16),
            pltpu.VMEM((9 * m_ch, d), bf16),
            pltpu.VMEM((3 * d, m_ch), bf16),
            pltpu.VMEM((rows, 9 * m_ch), bf16),
            narrow,
            narrow,
            narrow,
            narrow,
            narrow,
            narrow,
            narrow,
            narrow,
            narrow,
            wide,
            narrow,
            wide,
            pltpu.VMEM((MB, rows, m_ch), f32),
            pltpu.VMEM((rows, d), f32),
            pltpu.VMEM((2, rows, m_ch), f32),
            pltpu.VMEM((MB, rows, 128), f32),
            pltpu.VMEM((MB, 1, m_ch), f32),
            pltpu.VMEM((MB, 1, d), f32),
            pltpu.VMEM((MB, 1, d), f32),
            pltpu.VMEM((MB, 1, d), f32),
            pltpu.VMEM((MB, 1, d), f32),
            pltpu.VMEM((MB, 1, 128), f32),
            pltpu.VMEM((2, 1, d), f32),
            pltpu.VMEM((2, 1, d), f32),
            pltpu.VMEM((MB, n_dp, 1, 2 * m_ch + 128), f32),
            pltpu.VMEM((MB, n_dp, 1, 2 * d + 128), f32),
            pltpu.VMEM((MB, n_dp, 1, 2 * d + 128), f32),
            pltpu.VMEM((MB, n_dp, 1, 2 * d), f32),
            pltpu.VMEM((MB, n_dp, 1, 2 * m_ch), f32),
            pltpu.VMEM((MB, 1, 1, 2 * d), f32),
            dma((5, MB)),
            dma((5, MB)),
            dma((21,)),
            dma((MB,)),
            dma((6, MB)),
            dma((6, MB)),
            dma((6, MB)),
            dma((4, MB)),
            dma((4, MB)),
            dma((4, MB)),
        ],
        compiler_params=pltpu.CompilerParams(
            collective_id=0, has_side_effects=True, vmem_limit_bytes=62 * 2**20
        ),
    )(clips, boxes, w_s, w_t, g_s, b_s, g_t, b_t, cotangent)


def send_order(n, z, q):
    table = []
    for here in range(n):
        up = sorted(range(here + 1, n), reverse=True)
        down = list(range(here))
        table.append((up + down if here < n / 2 else down + up) + [here])
    dest = 0
    for here in range(n):
        for at in range(n):
            dest = dest + jnp.where((z == here) & (q == at), table[here][at], 0)
    return dest


PIECE = 384
SPAN = 640

HUB_JOBS = (
    (0, 0, -1),
    (0, 1, 0),
    (1, 0, -1),
    (2, 0, -1),
    (0, 2, 1),
    (2, 1, -1),
    (1, 1, -1),
    (1, 2, -1),
    (3, 0, 2),
    (2, 2, 3),
    (3, 1, -1),
    (3, 2, -1),
)


def of_job(j, column):
    return sum(jnp.where(j == i, job[column], 0) for i, job in enumerate(HUB_JOBS))


def is_one_of(j, members):
    found = j < 0
    for i in members:
        found = found | (j == i)
    return found


def gradient_kernel(
    dims,
    a_hbm,
    v_hbm,
    gu_hbm,
    gr_hbm,
    o_s,
    o_t,
    a,
    v,
    gu,
    gr,
    window,
    window_t,
    acc_s,
    acc_t,
    got_s,
    got_t,
    out_s,
    out_t,
    load_sem,
    a_sem,
    gu_send,
    gu_recv,
    fwd_send,
    fwd_recv,
    s_send,
    s_recv,
    t_send,
    t_recv,
):
    frames, height, width = dims
    nc, rows, d = a_hbm.shape[0] // 3, a_hbm.shape[1], a_hbm.shape[2]
    m_ch = v_hbm.shape[2]
    me = lax.axis_index("dp")
    n = lax.axis_size("dp") // 2
    z = lax.div(me, 2)
    core = lax.rem(me, 2)
    twin = me + 1 - 2 * core
    inner = jnp.logical_and(z > 0, z < n - 1)
    outer = jnp.logical_not(inner)
    step = jnp.where(z < n / 2, 2, -2)
    rows_s, rows_t = o_s.shape[0], o_t.shape[0]
    n_pieces = m_ch // PIECE

    barrier = pltpu.get_barrier_semaphore()

    def greet(device):
        pl.semaphore_signal(barrier, 1, device_id={"dp": device}, device_id_type=MESH)

    greet(twin)

    @pl.when(z > 0)
    def _():
        greet(me - 2)

    @pl.when(z < n - 1)
    def _():
        greet(me + 2)

    load_a = pltpu.make_async_copy(a_hbm, a.at[pl.ds(0, 3 * nc)], load_sem.at[0])
    full = 2 * nc + nc // MB
    load_gu = pltpu.make_async_copy(
        gu_hbm.at[pl.ds(0, full)], gu.at[pl.ds(0, full)], load_sem.at[1]
    )
    late = 3 * nc - nc // MB
    early = (pl.ds(full, late - full), slice(None), pl.ds(0, PIECE))
    load_early = pltpu.make_async_copy(gu_hbm.at[early], gu.at[early], load_sem.at[4])
    load_v = pltpu.make_async_copy(v_hbm, v, load_sem.at[2])
    load_gr = pltpu.make_async_copy(gr_hbm, gr, load_sem.at[3])

    @pl.when(inner)
    def _():
        load_a.start()
        load_gu.start()
        load_early.start()

    load_v.start()
    load_gr.start()
    pl.semaphore_wait(barrier, 3 - jnp.where(z == 0, 1, 0) - jnp.where(z == n - 1, 1, 0))

    def columns(p):
        return pl.ds(pl.multiple_of(p * PIECE, 128), PIECE)

    def remote(src, dst, send, recv, device):
        return pltpu.make_async_remote_copy(
            src_ref=src,
            dst_ref=dst,
            send_sem=send,
            recv_sem=recv,
            device_id={"dp": device},
            device_id_type=MESH,
        )

    def gu_to_hub(p):
        s = columns(p)
        return remote(
            gu_hbm.at[pl.ds(nc // MB, nc - nc // MB), :, s],
            gu.at[pl.ds(full, nc - nc // MB), :, s],
            gu_send.at[p],
            gu_recv.at[p],
            me + step,
        )

    def first_to_hub():
        s = pl.ds(0, PIECE)
        return remote(
            gu_hbm.at[pl.ds(late - 2 * nc, nc // MB), :, s],
            gu.at[pl.ds(late, nc // MB), :, s],
            gu_send.at[0],
            gu_recv.at[0],
            me + step,
        )

    def gu_to_twin(p):
        s = columns(p)
        return remote(
            gu.at[pl.ds(2 * nc, nc), :, s],
            gu.at[pl.ds(3 * nc, nc), :, s],
            fwd_send.at[p],
            fwd_recv.at[p],
            twin,
        )

    a_to_twin = remote(
        a.at[pl.ds(2 * nc, nc)], a.at[pl.ds(3 * nc, nc)], a_sem.at[0], a_sem.at[1], twin
    )

    def moved(x, before, after, dt, step):
        if not dt:
            return x
        y = x.reshape(before, after, 128)
        zero = jnp.zeros((before, step, 128), f32)
        if dt > 0:
            y = jnp.concatenate([y[:, step:], zero], axis=1)
        else:
            y = jnp.concatenate([zero, y[:, :-step]], axis=1)
        return y.reshape(rows, 128)

    def place(row0):
        low = lax.div(row0, 128)
        return low, row0 - low * 128

    def time_job(q):
        dest = send_order(n, z, q)
        low, start = place((2 * dest + core) * rows_t)

        def fill_time(i, c):
            to = pl.ds(pl.multiple_of(i * rows, 16), rows)
            for j in range(SPAN // 128):
                chunk = jnp.minimum(low + j, 3 * m_ch // 128 - 1)
                tap = lax.div(chunk, m_ch // 128)
                lane = pl.ds(pl.multiple_of((chunk - tap * (m_ch // 128)) * 128, 128), 128)

                def fill(dt):
                    x = v[i, :, lane].astype(f32)
                    x = moved(x, 1, rows, dt, height * width)
                    window_t[to, j * 128 : (j + 1) * 128] = x.astype(bf16)

                lax.switch(tap, [functools.partial(fill, dt) for dt in (-1, 0, 1)])
            return c

        lax.fori_loop(0, 2 * nc, fill_time, 0)
        acc_t[...] = lax.dot_general(
            window_t[...],
            gr[...].reshape(2 * nc * rows, d),
            (((0,), (0,)), ((), ())),
            preferred_element_type=f32,
        )
        at = pl.ds(pl.multiple_of(start, 8), rows_t)

        def add(slot):
            pltpu.make_async_copy(got_t.at[slot], got_t.at[slot], t_recv.at[slot]).wait()
            acc_t[at, :] += got_t[slot].astype(f32)

        @pl.when((z > 0) & (dest >= z))
        def _():
            add(dest + 1)

        @pl.when((z < n - 1) & (dest <= z))
        def _():
            add(dest)

        @pl.when(dest == z)
        def _():
            o_t[...] = acc_t[at, :]

        @pl.when(dest != z)
        def _():
            out_t[dest] = acc_t[at, :].astype(bf16)
            time_send(dest).start()

    def time_send(dest):
        right = dest > z
        slot = dest + jnp.where(right, 1, 0)
        return remote(
            out_t.at[dest],
            got_t.at[slot],
            t_send.at[dest],
            t_recv.at[slot],
            me + jnp.where(right, 2, -2),
        )

    def hub_dest(k):
        near = z < n / 2
        far_out = jnp.where(near, n - 1, 0)
        own_out = n - 1 - far_out
        return jnp.where(
            k == 0, far_out, jnp.where(k == 1, n - 1 - z, jnp.where(k == 2, own_out, z))
        )

    def space_place(k):
        return place((2 * hub_dest(k) + core) * rows_s)

    def fill_window(k, first, count):
        low, start = space_place(k)

        def fill_space(i, c):
            to = pl.ds(pl.multiple_of(i * rows, 16), rows)
            for j in range(SPAN // 128):
                chunk = jnp.minimum(low + j, 9 * d // 128 - 1)
                tap = lax.div(chunk, d // 128)
                lane = pl.ds(pl.multiple_of((chunk - tap * (d // 128)) * 128, 128), 128)

                def fill(dh, dw):
                    x = a[i, :, lane].astype(f32)
                    if dw:
                        x = pltpu.roll(x, (-dw) % rows, 0)
                    x = moved(x, frames, height * width, dh, width)
                    window[k, to, j * 128 : (j + 1) * 128] = x.astype(bf16)

                lax.switch(
                    tap,
                    [
                        functools.partial(fill, dh, dw)
                        for dh in (-1, 0, 1)
                        for dw in (-1, 0, 1)
                    ],
                )
            return c

        lax.fori_loop(first, first + count, fill_space, 0)

    def space_send(k, p):
        s = columns(p)
        return remote(
            out_s.at[k, :, s],
            got_s.at[jnp.where(k == 1, 1, 0), :, s],
            s_send.at[k, p],
            s_recv.at[jnp.where(k == 1, 1, 0), p],
            me + jnp.where(k == 2, -step, step),
        )

    def space_job(k, p):
        s = columns(p)
        low, start = space_place(k)
        at = pl.ds(pl.multiple_of(start, 8), rows_s)
        acc_s[...] = lax.dot_general(
            window[k],
            gu[:, :, s].reshape(4 * nc * rows, PIECE),
            (((0,), (0,)), ((), ())),
            preferred_element_type=f32,
        )

        @pl.when(k >= 2)
        def _():
            got = got_s.at[k - 2, :, s]
            pltpu.make_async_copy(got, got, s_recv.at[k - 2, p]).wait()
            acc_s[at, :] += got[...].astype(f32)

        @pl.when(k == 3)
        def _():
            o_s[:, s] = acc_s[at, :]

        @pl.when(k < 3)
        def _():
            out_s[k, :, s] = acc_s[at, :].astype(bf16)
            space_send(k, p).start()

    def take_gu(p):
        @pl.when(p == 0)
        def _():
            first_to_hub().wait_recv()

        @pl.when(p > 0)
        def _():
            gu_to_hub(p).wait_recv()

        gu_to_twin(p).start()
        gu_to_twin(p).wait_recv()

    @pl.when(inner)
    def _():
        load_a.wait()
        a_to_twin.start()

        a_to_twin.wait_recv()

        new_k = [i for i, job in enumerate(HUB_JOBS) if job[0] not in [x[0] for x in HUB_JOBS[:i]]]
        new_p = [i for i, job in enumerate(HUB_JOBS) if job[1] not in [x[1] for x in HUB_JOBS[:i]]]
        timed = [i for i, job in enumerate(HUB_JOBS) if job[2] >= 0]

        def hub_job(j, carry):
            k, p = of_job(j, 0), of_job(j, 1)

            @pl.when(is_one_of(j, new_k))
            def _():
                fill_window(k, 0, 4 * nc)

            @pl.when(j == 0)
            def _():
                load_gu.wait()
                load_early.wait()

            @pl.when(is_one_of(j, new_p))
            def _():
                take_gu(p)

            space_job(k, p)

            @pl.when(j == timed[0])
            def _():
                load_v.wait()
                load_gr.wait()

            @pl.when(is_one_of(j, timed))
            def _():
                time_job(of_job(j, 2))

            return carry

        lax.fori_loop(0, len(HUB_JOBS), hub_job, 0)
        a_to_twin.wait_send()

        def sent(p, carry):
            gu_to_twin(p).wait_send()
            for k in range(3):
                space_send(k, p).wait_send()
            return carry

        lax.fori_loop(0, n_pieces, sent, 0)

    @pl.when(outer)
    def _():
        first_to_hub().start()
        gu_to_hub(1).start()
        load_v.wait()
        load_gr.wait()

        def round_out(q, carry):
            time_job(q)

            @pl.when(q == 0)
            def _():
                for p in range(2, n_pieces):
                    gu_to_hub(p).start()

            return carry

        lax.fori_loop(0, n, round_out, 0)

        for p in range(n_pieces):
            s = columns(p)
            got = got_s.at[0, :, s]
            pltpu.make_async_copy(got, got, s_recv.at[0, p]).wait()
            o_s[:, s] = got[...].astype(f32)
            (gu_to_hub(p) if p else first_to_hub()).wait_send()

    def finish(q, carry):
        time_send(send_order(n, z, q)).wait_send()
        return carry

    lax.fori_loop(0, n - 1, finish, 0)


def gradients(dims, n_dp, a, v, gu, gr):
    nc, rows, d = a.shape[0] // 3, a.shape[1], a.shape[2]
    m_ch = v.shape[2]
    rows_s, rows_t = 9 * d // n_dp, 3 * m_ch // n_dp
    n = n_dp // 2
    n_pieces = m_ch // PIECE
    shape = jax.ShapeDtypeStruct
    dma = pltpu.SemaphoreType.DMA
    return pl.pallas_call(
        functools.partial(gradient_kernel, dims),
        out_shape=(shape((rows_s, m_ch), f32), shape((rows_t, d), f32)),
        in_specs=[pl.BlockSpec(memory_space=pl.ANY)] * 4,
        out_specs=[pl.BlockSpec(memory_space=pltpu.VMEM)] * 2,
        scratch_shapes=[
            pltpu.VMEM((4 * nc, rows, d), bf16),
            pltpu.VMEM(v.shape, bf16),
            pltpu.VMEM((4 * nc, rows, m_ch), bf16),
            pltpu.VMEM(gr.shape, bf16),
            pltpu.VMEM((4, 4 * nc * rows, SPAN), bf16),
            pltpu.VMEM((2 * nc * rows, SPAN), bf16),
            pltpu.VMEM((SPAN, PIECE), f32),
            pltpu.VMEM((SPAN, d), f32),
            pltpu.VMEM((2, rows_s, m_ch), bf16),
            pltpu.VMEM((n + 1, rows_t, d), bf16),
            pltpu.VMEM((3, rows_s, m_ch), bf16),
            pltpu.VMEM((n, rows_t, d), bf16),
            dma((5,)),
            dma((2,)),
            dma((n_pieces,)),
            dma((n_pieces,)),
            dma((n_pieces,)),
            dma((n_pieces,)),
            dma((3, n_pieces)),
            dma((2, n_pieces)),
            dma((n,)),
            dma((n + 1,)),
        ],
        compiler_params=pltpu.CompilerParams(
            collective_id=1, has_side_effects=True, vmem_limit_bytes=62 * 2**20
        ),
    )(a, v, gu, gr)


def spatial_columns(activity):
    height, breadth = (activity.shape[2], activity.shape[3])
    padded = jnp.pad(activity, ((0, 0), (0, 0), (1, 1), (1, 1), (0, 0)))
    pieces = [
        padded[:, :, row_off : row_off + height, col_off : col_off + breadth, :]
        for row_off in range(3)
        for col_off in range(3)
    ]
    return jnp.concatenate(pieces, axis=-1)


def temporal_columns(activity):
    frames = activity.shape[1]
    padded = jnp.pad(activity, ((0, 0), (1, 1), (0, 0), (0, 0), (0, 0)))
    return jnp.concatenate([padded[:, offset : offset + frames] for offset in range(3)], axis=-1)


def left_product(former, latter):
    return lax.dot_general(
        former, latter, (((0,), (0,)), ((), ())), preferred_element_type=jnp.float32
    )


def body(
    clips,
    boxes,
    spatial_w,
    temporal_w,
    spatial_gain,
    spatial_shift,
    temporal_gain,
    temporal_shift,
    cotangent,
):
    n_clips, frames, height, breadth, d = clips.shape
    cm = n_clips // MB
    width = (breadth // 8 + 1) * 8
    rows = cm * frames * height * width
    m_ch = spatial_w.shape[2]

    def padded(x):
        x = jnp.pad(x, ((0, 0), (0, 0), (0, 0), (0, width - breadth), (0, 0)))
        return x.reshape(MB, rows, d)

    n_dp = lax.axis_size("dp")
    hubs = n_dp == 8 and 9 * d // n_dp == 576 and 3 * m_ch // n_dp == 432 and d % 128 == 0
    act, grad, a_in, hidden, gu, gr, gain_s, shift_s, gain_t, shift_t = relay(
        (cm, frames, height, width),
        n_dp,
        hubs,
        padded(clips),
        boxes,
        spatial_w[0],
        temporal_w[0],
        spatial_gain,
        spatial_shift,
        temporal_gain,
        temporal_shift,
        padded(cotangent),
    )

    def frames_of(x):
        return x.reshape(n_clips, frames, height, width, x.shape[-1])[:, :, :, :breadth]

    if hubs:
        clip_rows = frames * height * width
        grad_s, grad_t = gradients(
            (frames, height, width),
            n_dp,
            *[x.reshape(-1, clip_rows, x.shape[-1]) for x in (a_in, hidden, gu, gr)],
        )
    else:
        cells = n_clips * frames * height * breadth
        cols = spatial_columns(frames_of(a_in[0])).reshape(cells, -1)
        grad_s = left_product(cols, frames_of(gu[0]).reshape(cells, -1))
        stacked = temporal_columns(frames_of(hidden[0])).reshape(cells, -1)
        grad_t = left_product(stacked, frames_of(gr[0]).reshape(cells, -1))
        grad_s = lax.psum_scatter(grad_s, "dp", scatter_dimension=0, tiled=True)
        grad_t = lax.psum_scatter(grad_t, "dp", scatter_dimension=0, tiled=True)
    return (
        frames_of(act)[None],
        frames_of(grad)[None],
        grad_s[None],
        grad_t[None],
        gain_s,
        shift_s,
        gain_t,
        shift_t,
    )


def solution(mesh):
    clip_spec = P("dp", None, None, None, None)
    weight_spec = P("pipe", None, None)
    channel_spec = P("pipe", None)
    return jax.shard_map(
        body,
        mesh=mesh,
        in_specs=(
            clip_spec,
            P("dp", None),
            weight_spec,
            weight_spec,
            channel_spec,
            channel_spec,
            channel_spec,
            channel_spec,
            clip_spec,
        ),
        out_specs=(
            P("pipe", "dp", None, None, None, None),
            P("pipe", "dp", None, None, None, None),
            P("pipe", "dp", None),
            P("pipe", "dp", None),
            channel_spec,
            channel_spec,
            channel_spec,
            channel_spec,
        ),
        check_vma=False,
    )
```

```python
import functools

import jax
import jax.numpy as jnp
from jax import lax
from jax.experimental import pallas as pl
from jax.experimental.pallas import tpu as pltpu
from jax.sharding import PartitionSpec as P

MB = 4
eps_norm = 1e-05
bf16 = jnp.bfloat16
f32 = jnp.float32
MESH = pl.DeviceIdType.MESH


def silu(x):
    return x / (1.0 + jnp.exp(-x))


def silu_slope(x):
    s = 1.0 / (1.0 + jnp.exp(-x))
    return s * (1.0 + x * (1.0 - s))


def lane_chunks(width, body):
    def step(i, carry):
        body(i, pl.ds(pl.multiple_of(i * 128, 128), 128))
        return carry

    lax.fori_loop(0, width // 128, step, 0)


def relay_kernel(
    dims,
    clips,
    boxes,
    w_s_hbm,
    w_t_hbm,
    g_s,
    b_s,
    g_t,
    b_t,
    cotangent,
    o_act,
    o_grad,
    o_in,
    o_hidden,
    o_gu,
    o_gr,
    o_gain_s,
    o_shift_s,
    o_gain_t,
    o_shift_t,
    w_s,
    w_t,
    w_s_back,
    w_t_back,
    cols,
    raw,
    raw_act,
    raw_grad,
    a_in,
    skip_in,
    a_out,
    r_in,
    r_out,
    ga_in,
    gs_in,
    gs_out,
    ig_out,
    hidden,
    gr,
    gu,
    uh,
    r_sum,
    gq,
    keep,
    fact_s,
    fact_t,
    off_t,
    fact_p,
    off_p,
    cnt,
    scale_out,
    scale_in,
    x_s,
    x_t,
    x_p,
    x_bt,
    x_bs,
    x_bp,
    x_send,
    x_recv,
    w_sem,
    load_sem,
    store_sem,
    pipe_send,
    pipe_recv,
    twin_send,
    twin_recv,
    hub_sem,
):
    cm, frames, height, width = dims
    breadth = clips.shape[2]
    rows = cm * frames * height * width
    d = a_in.shape[2]
    m_ch = hidden.shape[2]
    section = lax.axis_index("pipe")
    me = lax.axis_index("dp")
    n_pipe = lax.axis_size("pipe")
    n_dp = lax.axis_size("dp")
    first = section == 0
    last = section == n_pipe - 1
    odd = lax.rem(section, 2) == 1
    even_inner = jnp.logical_and(jnp.logical_not(odd), jnp.logical_not(last))
    early = section < 2
    skip_own = odd.astype(f32)
    skip_prev = jnp.logical_not(jnp.logical_or(odd, first)).astype(f32)

    def load_ws(part, tap):
        half = d // 2
        src = w_s_hbm.at[pl.ds(tap * d + part * half, half)]
        dst = w_s.at[pl.ds((part * 9 + tap) * half, half)]
        return pltpu.make_async_copy(src, dst, w_sem.at[part * 9 + tap])

    load_wt = pltpu.make_async_copy(w_t_hbm, w_t, w_sem.at[18])

    def load_raw(src, m):
        at = pl.ds(m * cm, cm)
        return pltpu.make_async_copy(src.at[at], raw.at[at], load_sem.at[m])

    def unpack(m, dst):
        pad = jnp.zeros((width - breadth, 128), f32)

        def column(i, s):
            pieces = []
            for c in range(cm):
                x = raw[m * cm + c, :, :, :, s].astype(f32)
                x = jnp.transpose(x.reshape(height * breadth, frames, 128), (1, 0, 2))
                for t in range(frames):
                    for h in range(height):
                        pieces += [x[t, h * breadth : (h + 1) * breadth], pad]
            dst[m, :, s] = jnp.concatenate(pieces, axis=0).astype(bf16)

        lane_chunks(d, column)

    def pack(m, src, dst):
        def column(i, s):
            x = src[m, :, s].astype(f32).reshape(cm * frames * height, width, 128)
            x = x[:, :breadth].reshape(cm, frames, height * breadth, 128)
            for c in range(cm):
                y = jnp.transpose(x[c], (1, 0, 2)).reshape(height, breadth, frames, 128)
                dst[m * cm + c, :, :, :, s] = y.astype(bf16)

        lane_chunks(d, column)

    local_skip = jnp.logical_not(jnp.logical_or(first, last))

    @pl.when(first)
    def _():
        for m in range(MB):
            load_raw(clips, m).start()

    @pl.when(local_skip)
    def _():
        for m in range(MB):
            load_raw(clips, m).start()

    for part in range(2):
        for tap in range(9):
            load_ws(part, tap).start()
    load_wt.start()

    @pl.when(last)
    def _():
        for m in range(MB):
            load_raw(cotangent, m).start()

    for ref in (o_gain_s, o_shift_s, o_gain_t, o_shift_t, gs_in, scale_in):
        ref[...] = jnp.zeros_like(ref)

    @pl.when(first)
    def _():
        skip_in[...] = jnp.zeros_like(skip_in)

    barrier = pltpu.get_barrier_semaphore()

    def greet(j, carry):
        pl.semaphore_signal(
            barrier, 1, device_id={"dp": lax.rem(me + j, n_dp)}, device_id_type=MESH
        )
        return carry

    lax.fori_loop(1, n_dp, greet, 0)

    def greet_pipe(step):
        def greet_one(j, carry):
            pl.semaphore_signal(
                barrier,
                1,
                device_id={"pipe": section + step, "dp": j},
                device_id_type=MESH,
            )
            return carry

        lax.fori_loop(0, n_dp, greet_one, 0)

    @pl.when(jnp.logical_not(first))
    def _():
        greet_pipe(-1)

    @pl.when(jnp.logical_not(last))
    def _():
        greet_pipe(1)

    pl.semaphore_signal(
        barrier,
        1,
        device_id={"pipe": section + jnp.where(early, 2, -2)},
        device_id_type=MESH,
    )
    scale_out[0] = g_t[...]
    scale_out[1] = b_t[...]

    def make_keep(m, carry):
        n_rows = frames * height * width
        pieces = []
        for c in range(cm):
            shape = (frames, height, width, 128)
            t = lax.broadcasted_iota(jnp.int32, shape, 0)
            h = lax.broadcasted_iota(jnp.int32, shape, 1)
            w = lax.broadcasted_iota(jnp.int32, shape, 2)
            box = [boxes[m * cm + c, i] for i in range(6)]
            inside = (t >= box[0]) & (t < box[1]) & (h >= box[2]) & (h < box[3])
            inside = inside & (w >= box[4]) & (w < box[5])
            pieces.append(jnp.where(inside, 1.0, 0.0).astype(f32).reshape(n_rows, 128))
        mask = jnp.concatenate(pieces, axis=0) if cm > 1 else pieces[0]
        keep[m] = mask
        cnt[m] = jnp.sum(mask, axis=0, keepdims=True)
        return carry

    lax.fori_loop(0, MB, make_keep, 0)
    def share(kind, buf, m):
        def send(j, carry):
            pltpu.make_async_remote_copy(
                src_ref=buf.at[m, me],
                dst_ref=buf.at[m, me],
                send_sem=x_send.at[kind, m],
                recv_sem=x_recv.at[kind, m],
                device_id={"dp": lax.rem(me + j, n_dp)},
                device_id_type=MESH,
            ).start()
            return carry

        lax.fori_loop(1, n_dp, send, 0)

    def shared(kind, buf, m):
        others = buf.at[m, pl.ds(0, n_dp - 1)]
        pltpu.make_async_copy(others, others, x_send.at[kind, m]).wait()
        pltpu.make_async_copy(others, others, x_recv.at[kind, m]).wait()

    def cross(kind, src, dst, m, step):
        def send(j, carry):
            pltpu.make_async_remote_copy(
                src_ref=src,
                dst_ref=dst.at[m, me],
                send_sem=x_send.at[kind, m],
                recv_sem=x_recv.at[kind, m],
                device_id={"pipe": section + step, "dp": lax.rem(me + j, n_dp)},
                device_id_type=MESH,
            ).start()
            return carry

        lax.fori_loop(0, n_dp, send, 0)

    def crossed(kind, buf, m):
        slots = buf.at[m]
        pltpu.make_async_copy(slots, slots, x_recv.at[kind, m]).wait()

    def cross_sent(kind, buf, m):
        slots = buf.at[m]
        pltpu.make_async_copy(slots, slots, x_send.at[kind, m]).wait()

    def to_pipe(kind, src, dst, m, step):
        return pltpu.make_async_remote_copy(
            src_ref=src.at[m],
            dst_ref=dst.at[m],
            send_sem=pipe_send.at[kind, m],
            recv_sem=pipe_recv.at[kind, m],
            device_id={"pipe": section + step},
            device_id_type=MESH,
        )

    half = d // 2

    def half_to_pipe(kind, part, src, dst, m, step):
        s = pl.ds(part * half, half)
        return pltpu.make_async_remote_copy(
            src_ref=src.at[m, :, s],
            dst_ref=dst.at[m, :, s],
            send_sem=pipe_send.at[kind + part, m],
            recv_sem=pipe_recv.at[kind + part, m],
            device_id={"pipe": section + step},
            device_id_type=MESH,
        )

    hubs = o_in.shape[0] > 2
    z = lax.div(me, 2)
    outer = jnp.logical_or(z == 0, z == n_dp // 2 - 1)

    def to_hub(m):
        return pltpu.make_async_remote_copy(
            src_ref=a_in.at[m],
            dst_ref=o_in.at[2, m],
            send_sem=hub_sem.at[0, m],
            recv_sem=hub_sem.at[1, m],
            device_id={"dp": me + jnp.where(z == 0, 2, -2)},
            device_id_type=MESH,
        )

    def inputs_to_hub():
        @pl.when(outer)
        def _():
            for m in range(MB):
                to_hub(m).start()

    def gu_to_hub(part):
        m = max(part - 1, 0)
        s = (pl.ds(0, 640), pl.ds(640, m_ch - 640), pl.ds(0, PIECE))[min(part, 2)]
        return pltpu.make_async_remote_copy(
            src_ref=gu.at[m, :, s],
            dst_ref=o_gu.at[2, m, :, s],
            send_sem=hub_sem.at[2, part],
            recv_sem=hub_sem.at[3, part],
            device_id={"dp": me + jnp.where(z == 0, 2, -2)},
            device_id_type=MESH,
        )

    def store(kind, src, dst, m):
        at = pl.ds(m * cm, cm)
        return pltpu.make_async_copy(src.at[at], dst.at[at], store_sem.at[kind, m])

    def keep_operand(kind, src, dst, m):
        return pltpu.make_async_copy(src.at[m], dst.at[0, m], store_sem.at[kind, m])

    def twin_operand(kind, src, dst, m):
        return pltpu.make_async_remote_copy(
            src_ref=src.at[m],
            dst_ref=dst.at[1, m],
            send_sem=twin_send.at[kind - 2, m],
            recv_sem=twin_recv.at[kind - 2, m],
            device_id={"dp": me + 1 - 2 * lax.rem(me, 2)},
            device_id_type=MESH,
        )

    def share_operand(kind, src, dst, m):
        keep_operand(kind, src, dst, m).start()
        twin_operand(kind, src, dst, m).start()

    def shift_space(x, dh, dw):
        if dw:
            x = pltpu.roll(x, (-dw) % rows, 0)
        return shift_rows(x, dh)

    def shift_rows(x, dh):
        if not dh:
            return x
        y = x.reshape(cm * frames, height * width, 128)
        zero = jnp.zeros((cm * frames, width, 128), f32)
        if dh > 0:
            y = jnp.concatenate([y[:, width:], zero], axis=1)
        else:
            y = jnp.concatenate([zero, y[:, :-width]], axis=1)
        return y.reshape(rows, 128)

    def shift_time(x, dt):
        if not dt:
            return x
        y = x.reshape(cm, frames * height * width, 128)
        step = height * width
        zero = jnp.zeros((cm, step, 128), f32)
        if dt > 0:
            y = jnp.concatenate([y[:, step:], zero], axis=1)
        else:
            y = jnp.concatenate([zero, y[:, :-step]], axis=1)
        return y.reshape(rows, 128)

    def local_sums(m, value, buf, c, channels):
        mask = keep[m]
        n_here = cnt[m]
        total = jnp.sum(mask * value, axis=0, keepdims=True)
        dev = mask * (value - total / n_here)
        spread = jnp.sum(dev * dev, axis=0, keepdims=True)
        buf[m, me, :, pl.ds(pl.multiple_of(c * 128, 128), 128)] = total
        buf[m, me, :, pl.ds(pl.multiple_of(channels + c * 128, 128), 128)] = spread
        return dev

    def merged(m, buf, c, channels):
        counts = buf[m, :, :, 2 * channels :]
        sums = buf[m, :, :, pl.ds(pl.multiple_of(c * 128, 128), 128)]
        spreads = buf[m, :, :, pl.ds(pl.multiple_of(channels + c * 128, 128), 128)]
        n = jnp.sum(counts, axis=0)
        mean = jnp.sum(sums, axis=0) / n
        off = sums / counts - mean[None]
        var = jnp.sum(spreads + counts * off * off, axis=0) / n
        return n, mean, lax.rsqrt(var + eps_norm)

    def lanes_of(part, i):
        return pl.ds(pl.multiple_of(part * half + i * 128, 128), 128)

    def normed_prev(m, s):
        return (r_in[m, :, s].astype(f32) + off_p[m, :, s]) * fact_p[m, :, s]

    def preact_prev(m, s, normed):
        return scale_in[0, :, s] * normed + scale_in[1, :, s]

    def skipped_prev(m, s, value):
        return value + skip_prev * skip_in[m, :, s].astype(f32)

    def activate(m, part, i, s):
        s = lanes_of(part, i)
        n, mean, rstd = merged(m, x_p, part * (half // 128) + i, d)
        off_p[m, :, s] = x_p[m, me, :, s] / x_p[m, me, :, 2 * d :] - mean
        fact_p[m, :, s] = rstd
        value = preact_prev(m, s, normed_prev(m, s))

        @pl.when(section == 2)
        def _():
            a_in[m, :, s] = (keep[m] * silu(skipped_prev(m, s, value))).astype(bf16)

        @pl.when(section != 2)
        def _():
            a_in[m, :, s] = (keep[m] * silu(value)).astype(bf16)

    def spatial_conv(m, begins):
        for part in range(2):
            if not begins:

                @pl.when(jnp.logical_not(first))
                def _():
                    half_to_pipe(2, part, r_out, r_in, m, 1).wait_recv()
                    lane_chunks(half, functools.partial(activate, m, part))

            def column(i, s):
                s = lanes_of(part, i)
                x = a_in[m, :, s].astype(f32)
                for dw in (-1, 0, 1):
                    y = shift_space(x, 0, dw)
                    for dh in (-1, 0, 1):
                        tap = (dh + 1) * 3 + dw + 1
                        at = part * 9 * half + tap * half + i * 128
                        cols[:, pl.ds(pl.multiple_of(at, 128), 128)] = shift_rows(y, dh).astype(
                            bf16
                        )

            lane_chunks(half, column)
            if begins:
                for tap in range(9):
                    load_ws(part, tap).wait()

            k = slice(part * 9 * half, (part + 1) * 9 * half)
            for s in (slice(0, 512), slice(512, m_ch)):
                value = jnp.dot(cols[:, k], w_s[k, s], preferred_element_type=f32)
                if part == 0:
                    uh[m, :, s] = value
                else:
                    uh[m, :, s] += value

    @pl.when(first)
    def _():
        load_raw(clips, 0).wait()
        unpack(0, a_in)
        spatial_conv(0, True)

    sides = 3 - jnp.where(first, 1, 0) - jnp.where(last, 1, 0)
    pl.semaphore_wait(barrier, sides * n_dp)

    def send_scale():
        return pltpu.make_async_remote_copy(
            src_ref=scale_out,
            dst_ref=scale_in,
            send_sem=w_sem.at[19],
            recv_sem=w_sem.at[20],
            device_id={"pipe": section + 1},
            device_id_type=MESH,
        )

    @pl.when(jnp.logical_not(last))
    def _():
        send_scale().start()

    @pl.when(local_skip)
    def _():
        for m in range(MB):
            load_raw(clips, m).wait()
        lax.fori_loop(0, MB, lambda m, c: (unpack(m, skip_in), c)[1], 0)

    @pl.when(last)
    def _():
        for m in range(MB):
            load_raw(cotangent, m).wait()
        lax.fori_loop(0, MB, lambda m, c: (unpack(m, ga_in), c)[1], 0)

    def forward_spatial(m):
        @pl.when(first & (m > 0))
        def _():
            load_raw(clips, m).wait()
            unpack(m, a_in)

        @pl.when(jnp.logical_not(first))
        def _():
            @pl.when(m == 0)
            def _():
                send_scale().wait_recv()

            crossed(4, x_p, m)

        @pl.when(jnp.logical_not(first & (m == 0)))
        def _():
            spatial_conv(m, False)

        x_s[m, me, :, 2 * m_ch :] = cnt[m]

        def sums(i, s):
            local_sums(m, uh[m, :, s], x_s, i, m_ch)

        lane_chunks(m_ch, sums)
        share(0, x_s, m)
        share_operand(2, a_in, o_in, m)

    def forward_temporal(m):
        shared(0, x_s, m)

        def column(i, s):
            n, mean, rstd = merged(m, x_s, i, m_ch)
            fact_s[m, :, s] = rstd
            normed = (uh[m, :, s] - mean) * rstd
            uh[m, :, s] = normed
            value = keep[m] * silu(g_s[:, s] * normed + b_s[:, s])
            value = value.astype(bf16)
            hidden[m, :, s] = value
            value = value.astype(f32)
            for dt in (-1, 0, 1):
                at = pl.ds(pl.multiple_of((dt + 1) * m_ch + i * 128, 128), 128)
                cols[:, at] = shift_time(value, dt).astype(bf16)

        lane_chunks(m_ch, column)
        share_operand(3, hidden, o_hidden, m)

        @pl.when((m == 0) & first)
        def _():
            load_wt.wait()

        r_sum[...] = jnp.dot(cols[:, : 3 * m_ch], w_t[...], preferred_element_type=f32)
        x_t[m, me, :, 2 * d :] = cnt[m]

        def centre(i, s):
            r_out[m, :, s] = local_sums(m, r_sum[:, s], x_t, i, d).astype(bf16)

        lane_chunks(d, centre)

        @pl.when(jnp.logical_not(last))
        def _():
            cross(4, x_t.at[m, me], x_p, m, 1)
            for part in range(2):
                half_to_pipe(2, part, r_out, r_in, m, 1).start()

        share(1, x_t, m)

    def normed_own(m, s):
        return (r_out[m, :, s].astype(f32) + off_t[m, :, s]) * fact_t[m, :, s]

    def preact_own(m, s, normed):
        return g_t[:, s] * normed + b_t[:, s] + skip_own * skip_in[m, :, s].astype(f32)

    def forward_out(m):
        @pl.when(last)
        def _():
            to_pipe(0, a_out, skip_in, m, 2).wait_recv()

        shared(1, x_t, m)

        def column(i, s):
            n, mean, rstd = merged(m, x_t, i, d)
            off_t[m, :, s] = x_t[m, me, :, s] / cnt[m] - mean
            fact_t[m, :, s] = rstd
            value = keep[m] * silu(preact_own(m, s, normed_own(m, s)))
            a_out[m, :, s] = value.astype(bf16)

        lane_chunks(d, column)
        pack(m, a_out, raw_act)
        store(0, raw_act, o_act, m).start()

        @pl.when(section == 1)
        def _():
            to_pipe(0, a_out, skip_in, m, 2).start()

    def slope_sums(row, value, normed, i, s):
        row[:, s] = jnp.sum(value, axis=0, keepdims=True)
        at = pl.ds(pl.multiple_of(d + i * 128, 128), 128)
        row[:, at] = jnp.sum(value * normed, axis=0, keepdims=True)

    def own_slope(m, s, normed):
        return ga_in[m, :, s].astype(f32) * keep[m] * silu_slope(preact_own(m, s, normed))

    def backward_in(m):
        def column(i, s):
            normed = normed_own(m, s)
            slope_sums(x_bt.at[m, me], own_slope(m, s, normed), normed, i, s)

        lane_chunks(d, column)
        share(2, x_bt, m)

    def totals(buf, m, s, i, channels):
        at = pl.ds(pl.multiple_of(channels + i * 128, 128), 128)
        return jnp.sum(buf[m, :, :, s], axis=0), jnp.sum(buf[m, :, :, at], axis=0)

    def backward_temporal(m):
        @pl.when(last)
        def _():
            shared(2, x_bt, m)

        @pl.when(jnp.logical_not(last))
        def _():
            crossed(2, x_bt, m)
            for part in range(2):
                half_to_pipe(4, part, ig_out, ga_in, m, -1).wait_recv()

        n = jnp.sum(x_t[m, :, :, 2 * d :], axis=0)

        def column(i, s):
            shift_sum, gain_sum = totals(x_bt, m, s, i, d)
            o_shift_t[:, s] += shift_sum
            o_gain_t[:, s] += gain_sum
            normed = normed_own(m, s)
            slope = own_slope(m, s, normed)

            @pl.when(last)
            def _():
                gs_out[m, :, s] = slope.astype(bf16)

            scale = g_t[:, s] * fact_t[m, :, s]
            value = keep[m] * scale * (slope - (shift_sum + normed * gain_sum) / n)
            value = value.astype(bf16)
            gr[m, :, s] = value
            value = value.astype(f32)
            for dt in (-1, 0, 1):
                at = pl.ds(pl.multiple_of((dt + 1) * d + i * 128, 128), 128)
                cols[:, at] = shift_time(value, -dt).astype(bf16)

        lane_chunks(d, column)
        share_operand(4, gr, o_gr, m)

        gq[lax.rem(m, 2)] = jnp.dot(cols[:, : 3 * d], w_t_back[...], preferred_element_type=f32)

        def sums(i, s):
            normed = uh[m, :, s]
            slope = keep[m] * gq[lax.rem(m, 2), :, s] * silu_slope(g_s[:, s] * normed + b_s[:, s])
            gq[lax.rem(m, 2), :, s] = slope
            x_bs[m, me, :, s] = jnp.sum(slope, axis=0, keepdims=True)
            at = pl.ds(pl.multiple_of(m_ch + i * 128, 128), 128)
            x_bs[m, me, :, at] = jnp.sum(slope * normed, axis=0, keepdims=True)

        lane_chunks(m_ch, sums)
        share(3, x_bs, m)

    def backward_spatial(m):
        shared(3, x_bs, m)
        n = jnp.sum(x_t[m, :, :, 2 * d :], axis=0)

        def column(i, s):
            shift_sum, gain_sum = totals(x_bs, m, s, i, m_ch)
            o_shift_s[:, s] += shift_sum
            o_gain_s[:, s] += gain_sum
            scale = g_s[:, s] * fact_s[m, :, s]
            value = keep[m] * scale * (gq[lax.rem(m, 2), :, s] - (shift_sum + uh[m, :, s] * gain_sum) / n)
            value = value.astype(bf16)
            gu[m, :, s] = value
            value = value.astype(f32)
            for dw in (-1, 0, 1):
                y = shift_space(value, 0, -dw)
                for dh in (-1, 0, 1):
                    tap = (dh + 1) * 3 + dw + 1
                    at = pl.ds(pl.multiple_of(tap * m_ch + i * 128, 128), 128)
                    cols[:, at] = shift_rows(y, -dh).astype(bf16)

        lane_chunks(m_ch, column)
        share_operand(5, gu, o_gu, m)
        if hubs:
            for part, when in ((0, 0), (1, 0), (3, 2)):

                @pl.when(outer & first & (m == when))
                def _():
                    gu_to_hub(part).start()


        @pl.when(even_inner)
        def _():
            to_pipe(1, gs_out, gs_in, m, -1).wait_recv()

        with_skip = even_inner.astype(f32)
        for part in range(2):
            s = slice(part * half, (part + 1) * half)
            value = jnp.dot(cols[...], w_s_back[:, s], preferred_element_type=f32)
            ig_out[m, :, s] = (value + with_skip * gs_in[m, :, s].astype(f32)).astype(bf16)

            @pl.when(jnp.logical_not(first))
            def _():
                def sums(i, s):
                    s = lanes_of(part, i)
                    normed = normed_prev(m, s)
                    slope = silu_slope(skipped_prev(m, s, preact_prev(m, s, normed)))
                    slope = ig_out[m, :, s].astype(f32) * keep[m] * slope

                    @pl.when(section == 2)
                    def _():
                        gs_out[m, :, s] = slope.astype(bf16)

                    slope_sums(x_bp.at[m, 0], slope, normed, part * (half // 128) + i, s)

                if part == 0:
                    half_to_pipe(4, part, ig_out, ga_in, m, -1).start()
                lane_chunks(half, sums)
                if part == 1:
                    cross(2, x_bp.at[m, 0], x_bt, m, -1)
                    half_to_pipe(4, part, ig_out, ga_in, m, -1).start()

        pack(m, ig_out, raw_grad)
        store(1, raw_grad, o_grad, m).start()

    def send_skip_grad(m):
        to_pipe(1, gs_out, gs_in, m, jnp.where(last, -1, -2)).start()

    def turn_weights():
        @pl.when(jnp.logical_not(first))
        def _():
            for part in range(2):
                for tap in range(9):
                    load_ws(part, tap).wait()
            load_wt.wait()

        def spatial(tap, carry):
            dst = pl.ds(pl.multiple_of(tap * m_ch, 128), m_ch)
            for part in range(2):
                src = pl.ds(pl.multiple_of((part * 9 + tap) * half, 128), half)
                w_s_back[dst, part * half : (part + 1) * half] = w_s[src, :].T
            return carry

        lax.fori_loop(0, 9, spatial, 0)

        def temporal(tap, carry):
            src = pl.ds(pl.multiple_of(tap * m_ch, 128), m_ch)
            dst = pl.ds(pl.multiple_of(tap * d, 128), d)
            w_t_back[dst, :] = w_t[src, :].T
            return carry

        lax.fori_loop(0, 3, temporal, 0)

    pairs = MB // 2
    wait_back = jnp.where(last, 1, pairs)

    def step(s, carry):
        do_f = s < pairs
        do_b = jnp.logical_and(s >= wait_back, s < wait_back + pairs)
        mf = 2 * jnp.minimum(s, pairs - 1)
        mb = 2 * jnp.clip(s - wait_back, 0, pairs - 1)

        @pl.when(s == jnp.where(first, wait_back, 0))
        def _():
            turn_weights()

        def both(when, phase, m):
            @pl.when(when)
            def _():
                def one(j, c):
                    phase(m + j)
                    return c

                lax.fori_loop(0, 2, one, 0)

        def some(begin, end, m):
            def spatial(j, c):
                backward_spatial(m + j)
                return c

            def skip(j, c):
                send_skip_grad(m + j)
                return c

            lax.fori_loop(begin, end, spatial, 0)

            @pl.when(jnp.logical_not(early))
            def _():
                lax.fori_loop(begin, end, skip, 0)

        inner = jnp.logical_not(last)
        done_f = jnp.logical_and(s > 0, s <= pairs)
        md = 2 * jnp.clip(s - 1, 0, pairs - 1)
        both(jnp.logical_and(done_f, last), forward_out, md)
        both(jnp.logical_and(do_b, last), backward_in, mb)
        some(1, jnp.where(last & do_b & (s > wait_back), 2, 1), mb - 2)
        both(do_f, forward_spatial, mf)
        both(jnp.logical_and(done_f, inner), forward_out, md)
        both(do_b, backward_temporal, mb)
        if hubs:

            @pl.when(outer & first & (s == wait_back + 1))
            def _():
                gu_to_hub(2).start()

        both(do_f, forward_temporal, mf)
        ends = s == wait_back + pairs - 1
        some(0, jnp.where(do_b, jnp.where(last & jnp.logical_not(ends), 1, 2), 0), mb)
        if hubs:

            @pl.when(s == jnp.where(last, wait_back + 1, pairs - 1))
            def _():
                inputs_to_hub()

            @pl.when(outer & (section == 1) & (s == wait_back))
            def _():
                gu_to_hub(0).start()

            @pl.when(outer & (section > 1) & (s == wait_back + 1))
            def _():
                gu_to_hub(0).start()

            @pl.when(outer & jnp.logical_not(first) & (s == wait_back + 1))
            def _():
                for part in range(1, MB):
                    gu_to_hub(part).start()

        return carry

    lax.fori_loop(0, 2 * pairs, step, 0)

    def finish(m, carry):
        store(0, raw_act, o_act, m).wait()
        store(1, raw_grad, o_grad, m).wait()
        for kind, src, dst in (
            (2, a_in, o_in),
            (3, hidden, o_hidden),
            (4, gr, o_gr),
            (5, gu, o_gu),
        ):
            keep_operand(kind, src, dst, m).wait()
            twin_operand(kind, src, dst, m).wait()

        @pl.when(jnp.logical_not(last))
        def _():
            cross_sent(4, x_p, m)
            for part in range(2):
                half_to_pipe(2, part, r_out, r_in, m, 1).wait_send()


        @pl.when(section == 1)
        def _():
            to_pipe(0, a_out, skip_in, m, 2).wait_send()

        @pl.when(jnp.logical_not(first))
        def _():
            cross_sent(2, x_bt, m)
            for part in range(2):
                half_to_pipe(4, part, ig_out, ga_in, m, -1).wait_send()

        @pl.when(jnp.logical_not(early))
        def _():
            to_pipe(1, gs_out, gs_in, m, -1).wait_send()

        return carry

    lax.fori_loop(0, MB, finish, 0)
    if hubs:


        @pl.when(outer)
        def _():
            for m in range(MB):
                to_hub(m).wait_send()
            for part in range(MB):
                gu_to_hub(part).wait_send()

        @pl.when(jnp.logical_not(outer))
        def _():
            for m in range(MB):
                to_hub(m).wait_recv()
            for part in range(MB):
                gu_to_hub(part).wait_recv()

    @pl.when(jnp.logical_not(last))
    def _():
        send_scale().wait_send()


def relay(dims, n_dp, hubs, clips, boxes, w_s, w_t, g_s, b_s, g_t, b_t, cotangent):
    cm, frames, height, width = dims
    rows = cm * frames * height * width
    d, m_ch = w_t.shape[1], w_s.shape[1]
    shape = jax.ShapeDtypeStruct
    vmem = pl.BlockSpec(memory_space=pltpu.VMEM)
    hbm = pl.BlockSpec(memory_space=pl.ANY)
    smem = pl.BlockSpec(memory_space=pltpu.SMEM)
    dma = pltpu.SemaphoreType.DMA
    narrow = pltpu.VMEM((MB, rows, d), bf16)
    wide = pltpu.VMEM((MB, rows, m_ch), bf16)
    return pl.pallas_call(
        functools.partial(relay_kernel, dims),
        out_shape=(
            shape(clips.shape, bf16),
            shape(clips.shape, bf16),
            shape((3 if hubs else 2, MB, rows, d), bf16),
            shape((2, MB, rows, m_ch), bf16),
            shape((3 if hubs else 2, MB, rows, m_ch), bf16),
            shape((2, MB, rows, d), bf16),
            shape((1, m_ch), f32),
            shape((1, m_ch), f32),
            shape((1, d), f32),
            shape((1, d), f32),
        ),
        in_specs=[hbm, smem, hbm, hbm, vmem, vmem, vmem, vmem, hbm],
        out_specs=[hbm] * 6 + [vmem] * 4,
        scratch_shapes=[
            pltpu.VMEM(w_s.shape, bf16),
            pltpu.VMEM(w_t.shape, bf16),
            pltpu.VMEM((9 * m_ch, d), bf16),
            pltpu.VMEM((3 * d, m_ch), bf16),
            pltpu.VMEM((rows, 9 * m_ch), bf16),
            pltpu.VMEM(clips.shape, bf16),
            pltpu.VMEM(clips.shape, bf16),
            pltpu.VMEM(clips.shape, bf16),
            narrow,
            narrow,
            narrow,
            narrow,
            narrow,
            narrow,
            narrow,
            narrow,
            narrow,
            wide,
            narrow,
            wide,
            pltpu.VMEM((MB, rows, m_ch), f32),
            pltpu.VMEM((rows, d), f32),
            pltpu.VMEM((2, rows, m_ch), f32),
            pltpu.VMEM((MB, rows, 128), f32),
            pltpu.VMEM((MB, 1, m_ch), f32),
            pltpu.VMEM((MB, 1, d), f32),
            pltpu.VMEM((MB, 1, d), f32),
            pltpu.VMEM((MB, 1, d), f32),
            pltpu.VMEM((MB, 1, d), f32),
            pltpu.VMEM((MB, 1, 128), f32),
            pltpu.VMEM((2, 1, d), f32),
            pltpu.VMEM((2, 1, d), f32),
            pltpu.VMEM((MB, n_dp, 1, 2 * m_ch + 128), f32),
            pltpu.VMEM((MB, n_dp, 1, 2 * d + 128), f32),
            pltpu.VMEM((MB, n_dp, 1, 2 * d + 128), f32),
            pltpu.VMEM((MB, n_dp, 1, 2 * d), f32),
            pltpu.VMEM((MB, n_dp, 1, 2 * m_ch), f32),
            pltpu.VMEM((MB, 1, 1, 2 * d), f32),
            dma((5, MB)),
            dma((5, MB)),
            dma((21,)),
            dma((MB,)),
            dma((6, MB)),
            dma((6, MB)),
            dma((6, MB)),
            dma((4, MB)),
            dma((4, MB)),
            dma((4, MB)),
        ],
        compiler_params=pltpu.CompilerParams(
            collective_id=0, has_side_effects=True, vmem_limit_bytes=62 * 2**20
        ),
    )(clips, boxes, w_s, w_t, g_s, b_s, g_t, b_t, cotangent)


def send_order(n, z, q):
    table = []
    for here in range(n):
        up = sorted(range(here + 1, n), reverse=True)
        down = list(range(here))
        table.append((up + down if here < n / 2 else down + up) + [here])
    dest = 0
    for here in range(n):
        for at in range(n):
            dest = dest + jnp.where((z == here) & (q == at), table[here][at], 0)
    return dest


PIECE = 384
SPAN = 640

HUB_JOBS = (
    (0, 0, -1),
    (0, 1, 0),
    (1, 0, -1),
    (2, 0, -1),
    (0, 2, 1),
    (2, 1, -1),
    (1, 1, -1),
    (1, 2, -1),
    (3, 0, 2),
    (2, 2, 3),
    (3, 1, -1),
    (3, 2, -1),
)


def of_job(j, column):
    return sum(jnp.where(j == i, job[column], 0) for i, job in enumerate(HUB_JOBS))


def is_one_of(j, members):
    found = j < 0
    for i in members:
        found = found | (j == i)
    return found


def gradient_kernel(
    dims,
    a_hbm,
    v_hbm,
    gu_hbm,
    gr_hbm,
    o_s,
    o_t,
    a,
    v,
    gu,
    gr,
    window,
    window_t,
    acc_s,
    acc_t,
    got_s,
    got_t,
    out_s,
    out_t,
    load_sem,
    a_sem,
    gu_send,
    gu_recv,
    fwd_send,
    fwd_recv,
    s_send,
    s_recv,
    t_send,
    t_recv,
):
    frames, height, width = dims
    nc, rows, d = a_hbm.shape[0] // 3, a_hbm.shape[1], a_hbm.shape[2]
    m_ch = v_hbm.shape[2]
    me = lax.axis_index("dp")
    n = lax.axis_size("dp") // 2
    z = lax.div(me, 2)
    core = lax.rem(me, 2)
    twin = me + 1 - 2 * core
    inner = jnp.logical_and(z > 0, z < n - 1)
    outer = jnp.logical_not(inner)
    step = jnp.where(z < n / 2, 2, -2)
    rows_s, rows_t = o_s.shape[0], o_t.shape[0]
    n_pieces = m_ch // PIECE

    barrier = pltpu.get_barrier_semaphore()

    def greet(device):
        pl.semaphore_signal(barrier, 1, device_id={"dp": device}, device_id_type=MESH)

    greet(twin)

    @pl.when(z > 0)
    def _():
        greet(me - 2)

    @pl.when(z < n - 1)
    def _():
        greet(me + 2)

    load_a = pltpu.make_async_copy(a_hbm, a.at[pl.ds(0, 3 * nc)], load_sem.at[0])
    full = 2 * nc + nc // MB
    load_gu = pltpu.make_async_copy(
        gu_hbm.at[pl.ds(0, full)], gu.at[pl.ds(0, full)], load_sem.at[1]
    )
    late = 3 * nc - nc // MB
    early = (pl.ds(full, late - full), slice(None), pl.ds(0, PIECE))
    load_early = pltpu.make_async_copy(gu_hbm.at[early], gu.at[early], load_sem.at[4])
    load_v = pltpu.make_async_copy(v_hbm, v, load_sem.at[2])
    load_gr = pltpu.make_async_copy(gr_hbm, gr, load_sem.at[3])

    @pl.when(inner)
    def _():
        load_a.start()
        load_gu.start()
        load_early.start()

    load_v.start()
    load_gr.start()
    pl.semaphore_wait(barrier, 3 - jnp.where(z == 0, 1, 0) - jnp.where(z == n - 1, 1, 0))

    def columns(p):
        return pl.ds(pl.multiple_of(p * PIECE, 128), PIECE)

    def remote(src, dst, send, recv, device):
        return pltpu.make_async_remote_copy(
            src_ref=src,
            dst_ref=dst,
            send_sem=send,
            recv_sem=recv,
            device_id={"dp": device},
            device_id_type=MESH,
        )

    def gu_to_hub(p):
        s = columns(p)
        return remote(
            gu_hbm.at[pl.ds(nc // MB, nc - nc // MB), :, s],
            gu.at[pl.ds(full, nc - nc // MB), :, s],
            gu_send.at[p],
            gu_recv.at[p],
            me + step,
        )

    def first_to_hub():
        s = pl.ds(0, PIECE)
        return remote(
            gu_hbm.at[pl.ds(late - 2 * nc, nc // MB), :, s],
            gu.at[pl.ds(late, nc // MB), :, s],
            gu_send.at[0],
            gu_recv.at[0],
            me + step,
        )

    def gu_to_twin(p):
        s = columns(p)
        return remote(
            gu.at[pl.ds(2 * nc, nc), :, s],
            gu.at[pl.ds(3 * nc, nc), :, s],
            fwd_send.at[p],
            fwd_recv.at[p],
            twin,
        )

    a_to_twin = remote(
        a.at[pl.ds(2 * nc, nc)], a.at[pl.ds(3 * nc, nc)], a_sem.at[0], a_sem.at[1], twin
    )

    def moved(x, before, after, dt, step):
        if not dt:
            return x
        y = x.reshape(before, after, 128)
        zero = jnp.zeros((before, step, 128), f32)
        if dt > 0:
            y = jnp.concatenate([y[:, step:], zero], axis=1)
        else:
            y = jnp.concatenate([zero, y[:, :-step]], axis=1)
        return y.reshape(rows, 128)

    def place(row0):
        low = lax.div(row0, 128)
        return low, row0 - low * 128

    def time_job(q):
        dest = send_order(n, z, q)
        low, start = place((2 * dest + core) * rows_t)

        def fill_time(i, c):
            to = pl.ds(pl.multiple_of(i * rows, 16), rows)
            for j in range(SPAN // 128):
                chunk = jnp.minimum(low + j, 3 * m_ch // 128 - 1)
                tap = lax.div(chunk, m_ch // 128)
                lane = pl.ds(pl.multiple_of((chunk - tap * (m_ch // 128)) * 128, 128), 128)

                def fill(dt):
                    x = v[i, :, lane].astype(f32)
                    x = moved(x, 1, rows, dt, height * width)
                    window_t[to, j * 128 : (j + 1) * 128] = x.astype(bf16)

                lax.switch(tap, [functools.partial(fill, dt) for dt in (-1, 0, 1)])
            return c

        lax.fori_loop(0, 2 * nc, fill_time, 0)
        acc_t[...] = lax.dot_general(
            window_t[...],
            gr[...].reshape(2 * nc * rows, d),
            (((0,), (0,)), ((), ())),
            preferred_element_type=f32,
        )
        at = pl.ds(pl.multiple_of(start, 8), rows_t)

        def add(slot):
            pltpu.make_async_copy(got_t.at[slot], got_t.at[slot], t_recv.at[slot]).wait()
            acc_t[at, :] += got_t[slot].astype(f32)

        @pl.when((z > 0) & (dest >= z))
        def _():
            add(dest + 1)

        @pl.when((z < n - 1) & (dest <= z))
        def _():
            add(dest)

        @pl.when(dest == z)
        def _():
            o_t[...] = acc_t[at, :]

        @pl.when(dest != z)
        def _():
            out_t[dest] = acc_t[at, :].astype(bf16)
            time_send(dest).start()

    def time_send(dest):
        right = dest > z
        slot = dest + jnp.where(right, 1, 0)
        return remote(
            out_t.at[dest],
            got_t.at[slot],
            t_send.at[dest],
            t_recv.at[slot],
            me + jnp.where(right, 2, -2),
        )

    def hub_dest(k):
        near = z < n / 2
        far_out = jnp.where(near, n - 1, 0)
        own_out = n - 1 - far_out
        return jnp.where(
            k == 0, far_out, jnp.where(k == 1, n - 1 - z, jnp.where(k == 2, own_out, z))
        )

    def space_place(k):
        return place((2 * hub_dest(k) + core) * rows_s)

    def fill_window(k, first, count):
        low, start = space_place(k)

        def fill_space(i, c):
            to = pl.ds(pl.multiple_of(i * rows, 16), rows)
            for j in range(SPAN // 128):
                chunk = jnp.minimum(low + j, 9 * d // 128 - 1)
                tap = lax.div(chunk, d // 128)
                lane = pl.ds(pl.multiple_of((chunk - tap * (d // 128)) * 128, 128), 128)

                def fill(dh, dw):
                    x = a[i, :, lane].astype(f32)
                    if dw:
                        x = pltpu.roll(x, (-dw) % rows, 0)
                    x = moved(x, frames, height * width, dh, width)
                    window[k, to, j * 128 : (j + 1) * 128] = x.astype(bf16)

                lax.switch(
                    tap,
                    [
                        functools.partial(fill, dh, dw)
                        for dh in (-1, 0, 1)
                        for dw in (-1, 0, 1)
                    ],
                )
            return c

        lax.fori_loop(first, first + count, fill_space, 0)

    def space_send(k, p):
        s = columns(p)
        return remote(
            out_s.at[k, :, s],
            got_s.at[jnp.where(k == 1, 1, 0), :, s],
            s_send.at[k, p],
            s_recv.at[jnp.where(k == 1, 1, 0), p],
            me + jnp.where(k == 2, -step, step),
        )

    def space_job(k, p):
        s = columns(p)
        low, start = space_place(k)
        at = pl.ds(pl.multiple_of(start, 8), rows_s)
        acc_s[...] = lax.dot_general(
            window[k],
            gu[:, :, s].reshape(4 * nc * rows, PIECE),
            (((0,), (0,)), ((), ())),
            preferred_element_type=f32,
        )

        @pl.when(k >= 2)
        def _():
            got = got_s.at[k - 2, :, s]
            pltpu.make_async_copy(got, got, s_recv.at[k - 2, p]).wait()
            acc_s[at, :] += got[...].astype(f32)

        @pl.when(k == 3)
        def _():
            o_s[:, s] = acc_s[at, :]

        @pl.when(k < 3)
        def _():
            out_s[k, :, s] = acc_s[at, :].astype(bf16)
            space_send(k, p).start()

    def take_gu(p):
        @pl.when(p == 0)
        def _():
            first_to_hub().wait_recv()

        @pl.when(p > 0)
        def _():
            gu_to_hub(p).wait_recv()

        gu_to_twin(p).start()
        gu_to_twin(p).wait_recv()

    @pl.when(inner)
    def _():
        load_a.wait()
        a_to_twin.start()

        a_to_twin.wait_recv()

        new_k = [i for i, job in enumerate(HUB_JOBS) if job[0] not in [x[0] for x in HUB_JOBS[:i]]]
        new_p = [i for i, job in enumerate(HUB_JOBS) if job[1] not in [x[1] for x in HUB_JOBS[:i]]]
        timed = [i for i, job in enumerate(HUB_JOBS) if job[2] >= 0]

        def hub_job(j, carry):
            k, p = of_job(j, 0), of_job(j, 1)

            @pl.when(is_one_of(j, new_k))
            def _():
                fill_window(k, 0, 4 * nc)

            @pl.when(j == 0)
            def _():
                load_gu.wait()
                load_early.wait()

            @pl.when(is_one_of(j, new_p))
            def _():
                take_gu(p)

            space_job(k, p)

            @pl.when(j == timed[0])
            def _():
                load_v.wait()
                load_gr.wait()

            @pl.when(is_one_of(j, timed))
            def _():
                time_job(of_job(j, 2))

            return carry

        lax.fori_loop(0, len(HUB_JOBS), hub_job, 0)
        a_to_twin.wait_send()

        def sent(p, carry):
            gu_to_twin(p).wait_send()
            for k in range(3):
                space_send(k, p).wait_send()
            return carry

        lax.fori_loop(0, n_pieces, sent, 0)

    @pl.when(outer)
    def _():
        first_to_hub().start()
        gu_to_hub(1).start()
        load_v.wait()
        load_gr.wait()

        def round_out(q, carry):
            time_job(q)

            @pl.when(q == 0)
            def _():
                for p in range(2, n_pieces):
                    gu_to_hub(p).start()

            return carry

        lax.fori_loop(0, n, round_out, 0)

        for p in range(n_pieces):
            s = columns(p)
            got = got_s.at[0, :, s]
            pltpu.make_async_copy(got, got, s_recv.at[0, p]).wait()
            o_s[:, s] = got[...].astype(f32)
            (gu_to_hub(p) if p else first_to_hub()).wait_send()

    def finish(q, carry):
        time_send(send_order(n, z, q)).wait_send()
        return carry

    lax.fori_loop(0, n - 1, finish, 0)


def gradients(dims, n_dp, a, v, gu, gr):
    nc, rows, d = a.shape[0] // 3, a.shape[1], a.shape[2]
    m_ch = v.shape[2]
    rows_s, rows_t = 9 * d // n_dp, 3 * m_ch // n_dp
    n = n_dp // 2
    n_pieces = m_ch // PIECE
    shape = jax.ShapeDtypeStruct
    dma = pltpu.SemaphoreType.DMA
    return pl.pallas_call(
        functools.partial(gradient_kernel, dims),
        out_shape=(shape((rows_s, m_ch), f32), shape((rows_t, d), f32)),
        in_specs=[pl.BlockSpec(memory_space=pl.ANY)] * 4,
        out_specs=[pl.BlockSpec(memory_space=pltpu.VMEM)] * 2,
        scratch_shapes=[
            pltpu.VMEM((4 * nc, rows, d), bf16),
            pltpu.VMEM(v.shape, bf16),
            pltpu.VMEM((4 * nc, rows, m_ch), bf16),
            pltpu.VMEM(gr.shape, bf16),
            pltpu.VMEM((4, 4 * nc * rows, SPAN), bf16),
            pltpu.VMEM((2 * nc * rows, SPAN), bf16),
            pltpu.VMEM((SPAN, PIECE), f32),
            pltpu.VMEM((SPAN, d), f32),
            pltpu.VMEM((2, rows_s, m_ch), bf16),
            pltpu.VMEM((n + 1, rows_t, d), bf16),
            pltpu.VMEM((3, rows_s, m_ch), bf16),
            pltpu.VMEM((n, rows_t, d), bf16),
            dma((5,)),
            dma((2,)),
            dma((n_pieces,)),
            dma((n_pieces,)),
            dma((n_pieces,)),
            dma((n_pieces,)),
            dma((3, n_pieces)),
            dma((2, n_pieces)),
            dma((n,)),
            dma((n + 1,)),
        ],
        compiler_params=pltpu.CompilerParams(
            collective_id=1, has_side_effects=True, vmem_limit_bytes=62 * 2**20
        ),
    )(a, v, gu, gr)


def spatial_columns(activity):
    height, breadth = (activity.shape[2], activity.shape[3])
    padded = jnp.pad(activity, ((0, 0), (0, 0), (1, 1), (1, 1), (0, 0)))
    pieces = [
        padded[:, :, row_off : row_off + height, col_off : col_off + breadth, :]
        for row_off in range(3)
        for col_off in range(3)
    ]
    return jnp.concatenate(pieces, axis=-1)


def temporal_columns(activity):
    frames = activity.shape[1]
    padded = jnp.pad(activity, ((0, 0), (1, 1), (0, 0), (0, 0), (0, 0)))
    return jnp.concatenate([padded[:, offset : offset + frames] for offset in range(3)], axis=-1)


def left_product(former, latter):
    return lax.dot_general(
        former, latter, (((0,), (0,)), ((), ())), preferred_element_type=jnp.float32
    )


def body(
    clips,
    boxes,
    spatial_w,
    temporal_w,
    spatial_gain,
    spatial_shift,
    temporal_gain,
    temporal_shift,
    cotangent,
):
    n_clips, frames, height, breadth, d = clips.shape
    cm = n_clips // MB
    width = (breadth // 8 + 1) * 8
    rows = cm * frames * height * width
    m_ch = spatial_w.shape[2]

    def frames_inside(x):
        return x.transpose(0, 2, 3, 1, 4)

    n_dp = lax.axis_size("dp")
    hubs = n_dp == 8 and 9 * d // n_dp == 576 and 3 * m_ch // n_dp == 432 and d % 128 == 0
    act, grad, a_in, hidden, gu, gr, gain_s, shift_s, gain_t, shift_t = relay(
        (cm, frames, height, width),
        n_dp,
        hubs,
        frames_inside(clips),
        boxes,
        spatial_w[0],
        temporal_w[0],
        spatial_gain,
        spatial_shift,
        temporal_gain,
        temporal_shift,
        frames_inside(cotangent),
    )

    def frames_of(x):
        return x.reshape(n_clips, frames, height, width, x.shape[-1])[:, :, :, :breadth]

    if hubs:
        clip_rows = frames * height * width
        grad_s, grad_t = gradients(
            (frames, height, width),
            n_dp,
            *[x.reshape(-1, clip_rows, x.shape[-1]) for x in (a_in, hidden, gu, gr)],
        )
    else:
        cells = n_clips * frames * height * breadth
        cols = spatial_columns(frames_of(a_in[0])).reshape(cells, -1)
        grad_s = left_product(cols, frames_of(gu[0]).reshape(cells, -1))
        stacked = temporal_columns(frames_of(hidden[0])).reshape(cells, -1)
        grad_t = left_product(stacked, frames_of(gr[0]).reshape(cells, -1))
        grad_s = lax.psum_scatter(grad_s, "dp", scatter_dimension=0, tiled=True)
        grad_t = lax.psum_scatter(grad_t, "dp", scatter_dimension=0, tiled=True)
    return (
        act.transpose(0, 3, 1, 2, 4)[None],
        grad.transpose(0, 3, 1, 2, 4)[None],
        grad_s[None],
        grad_t[None],
        gain_s,
        shift_s,
        gain_t,
        shift_t,
    )


def solution(mesh):
    clip_spec = P("dp", None, None, None, None)
    weight_spec = P("pipe", None, None)
    channel_spec = P("pipe", None)
    return jax.shard_map(
        body,
        mesh=mesh,
        in_specs=(
            clip_spec,
            P("dp", None),
            weight_spec,
            weight_spec,
            channel_spec,
            channel_spec,
            channel_spec,
            channel_spec,
            clip_spec,
        ),
        out_specs=(
            P("pipe", "dp", None, None, None, None),
            P("pipe", "dp", None, None, None, None),
            P("pipe", "dp", None),
            P("pipe", "dp", None),
            channel_spec,
            channel_spec,
            channel_spec,
            channel_spec,
        ),
        check_vma=False,
    )
```

```python
import functools

import jax
import jax.numpy as jnp
from jax import lax
from jax.experimental import pallas as pl
from jax.experimental.pallas import tpu as pltpu
from jax.sharding import PartitionSpec as P

MB = 4
eps_norm = 1e-05
bf16 = jnp.bfloat16
f32 = jnp.float32
MESH = pl.DeviceIdType.MESH


def silu(x):
    return x / (1.0 + jnp.exp(-x))


def silu_slope(x):
    s = 1.0 / (1.0 + jnp.exp(-x))
    return s * (1.0 + x * (1.0 - s))


def lane_chunks(width, body):
    def step(i, carry):
        body(i, pl.ds(pl.multiple_of(i * 128, 128), 128))
        return carry

    lax.fori_loop(0, width // 128, step, 0, unroll=True)


def relay_kernel(
    dims,
    clips,
    boxes,
    w_s_hbm,
    w_t_hbm,
    g_s,
    b_s,
    g_t,
    b_t,
    cotangent,
    o_act,
    o_grad,
    o_in,
    o_hidden,
    o_gu,
    o_gr,
    o_gain_s,
    o_shift_s,
    o_gain_t,
    o_shift_t,
    w_s,
    w_t,
    w_s_back,
    w_t_back,
    cols,
    raw,
    raw_act,
    raw_grad,
    a_in,
    skip_in,
    a_out,
    r_in,
    r_out,
    ga_in,
    gs_in,
    gs_out,
    ig_out,
    hidden,
    gr,
    gu,
    uh,
    r_sum,
    gq,
    keep,
    fact_s,
    fact_t,
    off_t,
    fact_p,
    off_p,
    cnt,
    scale_out,
    scale_in,
    x_s,
    x_t,
    x_p,
    x_bt,
    x_bs,
    x_bp,
    x_send,
    x_recv,
    w_sem,
    load_sem,
    store_sem,
    pipe_send,
    pipe_recv,
    twin_send,
    twin_recv,
    hub_sem,
):
    cm, frames, height, width = dims
    breadth = clips.shape[2]
    rows = cm * frames * height * width
    d = a_in.shape[2]
    m_ch = hidden.shape[2]
    section = lax.axis_index("pipe")
    me = lax.axis_index("dp")
    n_pipe = lax.axis_size("pipe")
    n_dp = lax.axis_size("dp")
    first = section == 0
    last = section == n_pipe - 1
    odd = lax.rem(section, 2) == 1
    even_inner = jnp.logical_and(jnp.logical_not(odd), jnp.logical_not(last))
    early = section < 2
    skip_own = odd.astype(f32)
    skip_prev = jnp.logical_not(jnp.logical_or(odd, first)).astype(f32)

    def load_ws(part, tap):
        half = d // 2
        src = w_s_hbm.at[pl.ds(tap * d + part * half, half)]
        dst = w_s.at[pl.ds((part * 9 + tap) * half, half)]
        return pltpu.make_async_copy(src, dst, w_sem.at[part * 9 + tap])

    load_wt = pltpu.make_async_copy(w_t_hbm, w_t, w_sem.at[18])

    def load_raw(src, m):
        at = pl.ds(m * cm, cm)
        return pltpu.make_async_copy(src.at[at], raw.at[at], load_sem.at[m])

    def unpack(m, dst):
        pad = jnp.zeros((width - breadth, 128), f32)

        def column(i, s):
            pieces = []
            for c in range(cm):
                x = raw[m * cm + c, :, :, :, s].astype(f32)
                x = jnp.transpose(x.reshape(height * breadth, frames, 128), (1, 0, 2))
                for t in range(frames):
                    for h in range(height):
                        pieces += [x[t, h * breadth : (h + 1) * breadth], pad]
            dst[m, :, s] = jnp.concatenate(pieces, axis=0).astype(bf16)

        lane_chunks(d, column)

    def pack(m, src, dst):
        def column(i, s):
            x = src[m, :, s].astype(f32).reshape(cm * frames * height, width, 128)
            x = x[:, :breadth].reshape(cm, frames, height * breadth, 128)
            for c in range(cm):
                y = jnp.transpose(x[c], (1, 0, 2)).reshape(height, breadth, frames, 128)
                dst[m * cm + c, :, :, :, s] = y.astype(bf16)

        lane_chunks(d, column)

    local_skip = jnp.logical_not(jnp.logical_or(first, last))

    @pl.when(first)
    def _():
        for m in range(MB):
            load_raw(clips, m).start()

    @pl.when(local_skip)
    def _():
        for m in range(MB):
            load_raw(clips, m).start()

    for part in range(2):
        for tap in range(9):
            load_ws(part, tap).start()
    load_wt.start()

    @pl.when(last)
    def _():
        for m in range(MB):
            load_raw(cotangent, m).start()

    for ref in (o_gain_s, o_shift_s, o_gain_t, o_shift_t, gs_in, scale_in):
        ref[...] = jnp.zeros_like(ref)

    @pl.when(first)
    def _():
        skip_in[...] = jnp.zeros_like(skip_in)

    barrier = pltpu.get_barrier_semaphore()

    def greet(j, carry):
        pl.semaphore_signal(
            barrier, 1, device_id={"dp": lax.rem(me + j, n_dp)}, device_id_type=MESH
        )
        return carry

    lax.fori_loop(1, n_dp, greet, 0)

    def greet_pipe(step):
        def greet_one(j, carry):
            pl.semaphore_signal(
                barrier,
                1,
                device_id={"pipe": section + step, "dp": j},
                device_id_type=MESH,
            )
            return carry

        lax.fori_loop(0, n_dp, greet_one, 0)

    @pl.when(jnp.logical_not(first))
    def _():
        greet_pipe(-1)

    @pl.when(jnp.logical_not(last))
    def _():
        greet_pipe(1)

    pl.semaphore_signal(
        barrier,
        1,
        device_id={"pipe": section + jnp.where(early, 2, -2)},
        device_id_type=MESH,
    )
    scale_out[0] = g_t[...]
    scale_out[1] = b_t[...]

    def make_keep(m, carry):
        n_rows = frames * height * width
        pieces = []
        for c in range(cm):
            shape = (frames, height, width, 128)
            t = lax.broadcasted_iota(jnp.int32, shape, 0)
            h = lax.broadcasted_iota(jnp.int32, shape, 1)
            w = lax.broadcasted_iota(jnp.int32, shape, 2)
            box = [boxes[m * cm + c, i] for i in range(6)]
            inside = (t >= box[0]) & (t < box[1]) & (h >= box[2]) & (h < box[3])
            inside = inside & (w >= box[4]) & (w < box[5])
            pieces.append(jnp.where(inside, 1.0, 0.0).astype(f32).reshape(n_rows, 128))
        mask = jnp.concatenate(pieces, axis=0) if cm > 1 else pieces[0]
        keep[m] = mask
        cnt[m] = jnp.sum(mask, axis=0, keepdims=True)
        return carry

    lax.fori_loop(0, MB, make_keep, 0)
    def share(kind, buf, m):
        def send(j, carry):
            pltpu.make_async_remote_copy(
                src_ref=buf.at[m, me],
                dst_ref=buf.at[m, me],
                send_sem=x_send.at[kind, m],
                recv_sem=x_recv.at[kind, m],
                device_id={"dp": lax.rem(me + j, n_dp)},
                device_id_type=MESH,
            ).start()
            return carry

        lax.fori_loop(1, n_dp, send, 0)

    def shared(kind, buf, m):
        others = buf.at[m, pl.ds(0, n_dp - 1)]
        pltpu.make_async_copy(others, others, x_send.at[kind, m]).wait()
        pltpu.make_async_copy(others, others, x_recv.at[kind, m]).wait()

    def cross(kind, src, dst, m, step):
        def send(j, carry):
            pltpu.make_async_remote_copy(
                src_ref=src,
                dst_ref=dst.at[m, me],
                send_sem=x_send.at[kind, m],
                recv_sem=x_recv.at[kind, m],
                device_id={"pipe": section + step, "dp": lax.rem(me + j, n_dp)},
                device_id_type=MESH,
            ).start()
            return carry

        lax.fori_loop(0, n_dp, send, 0)

    def crossed(kind, buf, m):
        slots = buf.at[m]
        pltpu.make_async_copy(slots, slots, x_recv.at[kind, m]).wait()

    def cross_sent(kind, buf, m):
        slots = buf.at[m]
        pltpu.make_async_copy(slots, slots, x_send.at[kind, m]).wait()

    def to_pipe(kind, src, dst, m, step):
        return pltpu.make_async_remote_copy(
            src_ref=src.at[m],
            dst_ref=dst.at[m],
            send_sem=pipe_send.at[kind, m],
            recv_sem=pipe_recv.at[kind, m],
            device_id={"pipe": section + step},
            device_id_type=MESH,
        )

    half = d // 2

    def half_to_pipe(kind, part, src, dst, m, step):
        s = pl.ds(part * half, half)
        return pltpu.make_async_remote_copy(
            src_ref=src.at[m, :, s],
            dst_ref=dst.at[m, :, s],
            send_sem=pipe_send.at[kind + part, m],
            recv_sem=pipe_recv.at[kind + part, m],
            device_id={"pipe": section + step},
            device_id_type=MESH,
        )

    hubs = o_in.shape[0] > 2
    z = lax.div(me, 2)
    outer = jnp.logical_or(z == 0, z == n_dp // 2 - 1)

    def to_hub(m):
        return pltpu.make_async_remote_copy(
            src_ref=a_in.at[m],
            dst_ref=o_in.at[2, m],
            send_sem=hub_sem.at[0, m],
            recv_sem=hub_sem.at[1, m],
            device_id={"dp": me + jnp.where(z == 0, 2, -2)},
            device_id_type=MESH,
        )

    def inputs_to_hub():
        @pl.when(outer)
        def _():
            for m in range(MB):
                to_hub(m).start()

    def gu_to_hub(part):
        m = max(part - 1, 0)
        s = (pl.ds(0, 640), pl.ds(640, m_ch - 640), pl.ds(0, PIECE))[min(part, 2)]
        return pltpu.make_async_remote_copy(
            src_ref=gu.at[m, :, s],
            dst_ref=o_gu.at[2, m, :, s],
            send_sem=hub_sem.at[2, part],
            recv_sem=hub_sem.at[3, part],
            device_id={"dp": me + jnp.where(z == 0, 2, -2)},
            device_id_type=MESH,
        )

    def store(kind, src, dst, m):
        at = pl.ds(m * cm, cm)
        return pltpu.make_async_copy(src.at[at], dst.at[at], store_sem.at[kind, m])

    def keep_operand(kind, src, dst, m):
        return pltpu.make_async_copy(src.at[m], dst.at[0, m], store_sem.at[kind, m])

    def twin_operand(kind, src, dst, m):
        return pltpu.make_async_remote_copy(
            src_ref=src.at[m],
            dst_ref=dst.at[1, m],
            send_sem=twin_send.at[kind - 2, m],
            recv_sem=twin_recv.at[kind - 2, m],
            device_id={"dp": me + 1 - 2 * lax.rem(me, 2)},
            device_id_type=MESH,
        )

    def share_operand(kind, src, dst, m):
        keep_operand(kind, src, dst, m).start()
        twin_operand(kind, src, dst, m).start()

    def shift_space(x, dh, dw):
        if dw:
            x = pltpu.roll(x, (-dw) % rows, 0)
        return shift_rows(x, dh)

    def shift_rows(x, dh):
        if not dh:
            return x
        y = x.reshape(cm * frames, height * width, 128)
        zero = jnp.zeros((cm * frames, width, 128), f32)
        if dh > 0:
            y = jnp.concatenate([y[:, width:], zero], axis=1)
        else:
            y = jnp.concatenate([zero, y[:, :-width]], axis=1)
        return y.reshape(rows, 128)

    def shift_time(x, dt):
        if not dt:
            return x
        y = x.reshape(cm, frames * height * width, 128)
        step = height * width
        zero = jnp.zeros((cm, step, 128), f32)
        if dt > 0:
            y = jnp.concatenate([y[:, step:], zero], axis=1)
        else:
            y = jnp.concatenate([zero, y[:, :-step]], axis=1)
        return y.reshape(rows, 128)

    def local_sums(m, value, buf, c, channels):
        mask = keep[m]
        n_here = cnt[m]
        total = jnp.sum(mask * value, axis=0, keepdims=True)
        dev = mask * (value - total / n_here)
        spread = jnp.sum(dev * dev, axis=0, keepdims=True)
        buf[m, me, :, pl.ds(pl.multiple_of(c * 128, 128), 128)] = total
        buf[m, me, :, pl.ds(pl.multiple_of(channels + c * 128, 128), 128)] = spread
        return dev

    def merged(m, buf, c, channels):
        counts = buf[m, :, :, 2 * channels :]
        sums = buf[m, :, :, pl.ds(pl.multiple_of(c * 128, 128), 128)]
        spreads = buf[m, :, :, pl.ds(pl.multiple_of(channels + c * 128, 128), 128)]
        n = jnp.sum(counts, axis=0)
        mean = jnp.sum(sums, axis=0) / n
        off = sums / counts - mean[None]
        var = jnp.sum(spreads + counts * off * off, axis=0) / n
        return n, mean, lax.rsqrt(var + eps_norm)

    def lanes_of(part, i):
        return pl.ds(pl.multiple_of(part * half + i * 128, 128), 128)

    def normed_prev(m, s):
        return (r_in[m, :, s].astype(f32) + off_p[m, :, s]) * fact_p[m, :, s]

    def preact_prev(m, s, normed):
        return scale_in[0, :, s] * normed + scale_in[1, :, s]

    def skipped_prev(m, s, value):
        return value + skip_prev * skip_in[m, :, s].astype(f32)

    def activate(m, part, i, s):
        s = lanes_of(part, i)
        n, mean, rstd = merged(m, x_p, part * (half // 128) + i, d)
        off_p[m, :, s] = x_p[m, me, :, s] / x_p[m, me, :, 2 * d :] - mean
        fact_p[m, :, s] = rstd
        value = preact_prev(m, s, normed_prev(m, s))

        @pl.when(section == 2)
        def _():
            a_in[m, :, s] = (keep[m] * silu(skipped_prev(m, s, value))).astype(bf16)

        @pl.when(section != 2)
        def _():
            a_in[m, :, s] = (keep[m] * silu(value)).astype(bf16)

    def spatial_conv(m, begins):
        for part in range(2):
            if not begins:

                @pl.when(jnp.logical_not(first))
                def _():
                    half_to_pipe(2, part, r_out, r_in, m, 1).wait_recv()
                    lane_chunks(half, functools.partial(activate, m, part))

            def column(i, s):
                s = lanes_of(part, i)
                x = a_in[m, :, s].astype(f32)
                for dw in (-1, 0, 1):
                    y = shift_space(x, 0, dw)
                    for dh in (-1, 0, 1):
                        tap = (dh + 1) * 3 + dw + 1
                        at = part * 9 * half + tap * half + i * 128
                        cols[:, pl.ds(pl.multiple_of(at, 128), 128)] = shift_rows(y, dh).astype(
                            bf16
                        )

            lane_chunks(half, column)
            if begins:
                for tap in range(9):
                    load_ws(part, tap).wait()

            k = slice(part * 9 * half, (part + 1) * 9 * half)
            for s in (slice(0, 512), slice(512, m_ch)):
                value = jnp.dot(cols[:, k], w_s[k, s], preferred_element_type=f32)
                if part == 0:
                    uh[m, :, s] = value
                else:
                    uh[m, :, s] += value

    @pl.when(first)
    def _():
        load_raw(clips, 0).wait()
        unpack(0, a_in)
        spatial_conv(0, True)

    sides = 3 - jnp.where(first, 1, 0) - jnp.where(last, 1, 0)
    pl.semaphore_wait(barrier, sides * n_dp)

    def send_scale():
        return pltpu.make_async_remote_copy(
            src_ref=scale_out,
            dst_ref=scale_in,
            send_sem=w_sem.at[19],
            recv_sem=w_sem.at[20],
            device_id={"pipe": section + 1},
            device_id_type=MESH,
        )

    @pl.when(jnp.logical_not(last))
    def _():
        send_scale().start()

    @pl.when(local_skip)
    def _():
        for m in range(MB):
            load_raw(clips, m).wait()
        lax.fori_loop(0, MB, lambda m, c: (unpack(m, skip_in), c)[1], 0)

    @pl.when(last)
    def _():
        for m in range(MB):
            load_raw(cotangent, m).wait()
        lax.fori_loop(0, MB, lambda m, c: (unpack(m, ga_in), c)[1], 0)

    def forward_spatial(m):
        @pl.when(first & (m > 0))
        def _():
            load_raw(clips, m).wait()
            unpack(m, a_in)

        @pl.when(jnp.logical_not(first))
        def _():
            @pl.when(m == 0)
            def _():
                send_scale().wait_recv()

            crossed(4, x_p, m)

        @pl.when(jnp.logical_not(first & (m == 0)))
        def _():
            spatial_conv(m, False)

        x_s[m, me, :, 2 * m_ch :] = cnt[m]

        def sums(i, s):
            local_sums(m, uh[m, :, s], x_s, i, m_ch)

        lane_chunks(m_ch, sums)
        share(0, x_s, m)
        share_operand(2, a_in, o_in, m)

    def forward_temporal(m):
        shared(0, x_s, m)

        def column(i, s):
            n, mean, rstd = merged(m, x_s, i, m_ch)
            fact_s[m, :, s] = rstd
            normed = (uh[m, :, s] - mean) * rstd
            uh[m, :, s] = normed
            value = keep[m] * silu(g_s[:, s] * normed + b_s[:, s])
            value = value.astype(bf16)
            hidden[m, :, s] = value
            value = value.astype(f32)
            for dt in (-1, 0, 1):
                at = pl.ds(pl.multiple_of((dt + 1) * m_ch + i * 128, 128), 128)
                cols[:, at] = shift_time(value, dt).astype(bf16)

        lane_chunks(m_ch, column)
        share_operand(3, hidden, o_hidden, m)

        @pl.when((m == 0) & first)
        def _():
            load_wt.wait()

        r_sum[...] = jnp.dot(cols[:, : 3 * m_ch], w_t[...], preferred_element_type=f32)
        x_t[m, me, :, 2 * d :] = cnt[m]

        def centre(i, s):
            r_out[m, :, s] = local_sums(m, r_sum[:, s], x_t, i, d).astype(bf16)

        lane_chunks(d, centre)

        @pl.when(jnp.logical_not(last))
        def _():
            cross(4, x_t.at[m, me], x_p, m, 1)
            for part in range(2):
                half_to_pipe(2, part, r_out, r_in, m, 1).start()

        share(1, x_t, m)

    def normed_own(m, s):
        return (r_out[m, :, s].astype(f32) + off_t[m, :, s]) * fact_t[m, :, s]

    def preact_own(m, s, normed):
        return g_t[:, s] * normed + b_t[:, s] + skip_own * skip_in[m, :, s].astype(f32)

    def forward_out(m):
        @pl.when(last)
        def _():
            to_pipe(0, a_out, skip_in, m, 2).wait_recv()

        shared(1, x_t, m)

        def column(i, s):
            n, mean, rstd = merged(m, x_t, i, d)
            off_t[m, :, s] = x_t[m, me, :, s] / cnt[m] - mean
            fact_t[m, :, s] = rstd
            value = keep[m] * silu(preact_own(m, s, normed_own(m, s)))
            a_out[m, :, s] = value.astype(bf16)

        lane_chunks(d, column)
        pack(m, a_out, raw_act)
        store(0, raw_act, o_act, m).start()

        @pl.when(section == 1)
        def _():
            to_pipe(0, a_out, skip_in, m, 2).start()

    def slope_sums(row, value, normed, i, s):
        row[:, s] = jnp.sum(value, axis=0, keepdims=True)
        at = pl.ds(pl.multiple_of(d + i * 128, 128), 128)
        row[:, at] = jnp.sum(value * normed, axis=0, keepdims=True)

    def own_slope(m, s, normed):
        return ga_in[m, :, s].astype(f32) * keep[m] * silu_slope(preact_own(m, s, normed))

    def backward_in(m):
        def column(i, s):
            normed = normed_own(m, s)
            slope_sums(x_bt.at[m, me], own_slope(m, s, normed), normed, i, s)

        lane_chunks(d, column)
        share(2, x_bt, m)

    def totals(buf, m, s, i, channels):
        at = pl.ds(pl.multiple_of(channels + i * 128, 128), 128)
        return jnp.sum(buf[m, :, :, s], axis=0), jnp.sum(buf[m, :, :, at], axis=0)

    def backward_temporal(m):
        @pl.when(last)
        def _():
            shared(2, x_bt, m)

        @pl.when(jnp.logical_not(last))
        def _():
            crossed(2, x_bt, m)
            for part in range(2):
                half_to_pipe(4, part, ig_out, ga_in, m, -1).wait_recv()

        n = jnp.sum(x_t[m, :, :, 2 * d :], axis=0)

        def column(i, s):
            shift_sum, gain_sum = totals(x_bt, m, s, i, d)
            o_shift_t[:, s] += shift_sum
            o_gain_t[:, s] += gain_sum
            normed = normed_own(m, s)
            slope = own_slope(m, s, normed)

            @pl.when(last)
            def _():
                gs_out[m, :, s] = slope.astype(bf16)

            scale = g_t[:, s] * fact_t[m, :, s]
            value = keep[m] * scale * (slope - (shift_sum + normed * gain_sum) / n)
            value = value.astype(bf16)
            gr[m, :, s] = value
            value = value.astype(f32)
            for dt in (-1, 0, 1):
                at = pl.ds(pl.multiple_of((dt + 1) * d + i * 128, 128), 128)
                cols[:, at] = shift_time(value, -dt).astype(bf16)

        lane_chunks(d, column)
        share_operand(4, gr, o_gr, m)

        gq[lax.rem(m, 2)] = jnp.dot(cols[:, : 3 * d], w_t_back[...], preferred_element_type=f32)

        def sums(i, s):
            normed = uh[m, :, s]
            slope = keep[m] * gq[lax.rem(m, 2), :, s] * silu_slope(g_s[:, s] * normed + b_s[:, s])
            gq[lax.rem(m, 2), :, s] = slope
            x_bs[m, me, :, s] = jnp.sum(slope, axis=0, keepdims=True)
            at = pl.ds(pl.multiple_of(m_ch + i * 128, 128), 128)
            x_bs[m, me, :, at] = jnp.sum(slope * normed, axis=0, keepdims=True)

        lane_chunks(m_ch, sums)
        share(3, x_bs, m)

    def backward_spatial(m):
        shared(3, x_bs, m)
        n = jnp.sum(x_t[m, :, :, 2 * d :], axis=0)

        def column(i, s):
            shift_sum, gain_sum = totals(x_bs, m, s, i, m_ch)
            o_shift_s[:, s] += shift_sum
            o_gain_s[:, s] += gain_sum
            scale = g_s[:, s] * fact_s[m, :, s]
            value = keep[m] * scale * (gq[lax.rem(m, 2), :, s] - (shift_sum + uh[m, :, s] * gain_sum) / n)
            value = value.astype(bf16)
            gu[m, :, s] = value
            value = value.astype(f32)
            for dw in (-1, 0, 1):
                y = shift_space(value, 0, -dw)
                for dh in (-1, 0, 1):
                    tap = (dh + 1) * 3 + dw + 1
                    at = pl.ds(pl.multiple_of(tap * m_ch + i * 128, 128), 128)
                    cols[:, at] = shift_rows(y, -dh).astype(bf16)

        lane_chunks(m_ch, column)
        share_operand(5, gu, o_gu, m)
        if hubs:
            for part, when in ((0, 0), (1, 0), (3, 2)):

                @pl.when(outer & first & (m == when))
                def _():
                    gu_to_hub(part).start()


        @pl.when(even_inner)
        def _():
            to_pipe(1, gs_out, gs_in, m, -1).wait_recv()

        with_skip = even_inner.astype(f32)
        for part in range(2):
            s = slice(part * half, (part + 1) * half)
            value = jnp.dot(cols[...], w_s_back[:, s], preferred_element_type=f32)
            ig_out[m, :, s] = (value + with_skip * gs_in[m, :, s].astype(f32)).astype(bf16)

            @pl.when(jnp.logical_not(first))
            def _():
                def sums(i, s):
                    s = lanes_of(part, i)
                    normed = normed_prev(m, s)
                    slope = silu_slope(skipped_prev(m, s, preact_prev(m, s, normed)))
                    slope = ig_out[m, :, s].astype(f32) * keep[m] * slope

                    @pl.when(section == 2)
                    def _():
                        gs_out[m, :, s] = slope.astype(bf16)

                    slope_sums(x_bp.at[m, 0], slope, normed, part * (half // 128) + i, s)

                if part == 0:
                    half_to_pipe(4, part, ig_out, ga_in, m, -1).start()
                lane_chunks(half, sums)
                if part == 1:
                    cross(2, x_bp.at[m, 0], x_bt, m, -1)
                    half_to_pipe(4, part, ig_out, ga_in, m, -1).start()

        pack(m, ig_out, raw_grad)
        store(1, raw_grad, o_grad, m).start()

    def send_skip_grad(m):
        to_pipe(1, gs_out, gs_in, m, jnp.where(last, -1, -2)).start()

    def turn_weights():
        @pl.when(jnp.logical_not(first))
        def _():
            for part in range(2):
                for tap in range(9):
                    load_ws(part, tap).wait()
            load_wt.wait()

        def spatial(tap, carry):
            dst = pl.ds(pl.multiple_of(tap * m_ch, 128), m_ch)
            for part in range(2):
                src = pl.ds(pl.multiple_of((part * 9 + tap) * half, 128), half)
                w_s_back[dst, part * half : (part + 1) * half] = w_s[src, :].T
            return carry

        lax.fori_loop(0, 9, spatial, 0)

        def temporal(tap, carry):
            src = pl.ds(pl.multiple_of(tap * m_ch, 128), m_ch)
            dst = pl.ds(pl.multiple_of(tap * d, 128), d)
            w_t_back[dst, :] = w_t[src, :].T
            return carry

        lax.fori_loop(0, 3, temporal, 0)

    pairs = MB // 2
    wait_back = jnp.where(last, 1, pairs)

    def step(s, carry):
        do_f = s < pairs
        do_b = jnp.logical_and(s >= wait_back, s < wait_back + pairs)
        mf = 2 * jnp.minimum(s, pairs - 1)
        mb = 2 * jnp.clip(s - wait_back, 0, pairs - 1)

        @pl.when(s == jnp.where(first, wait_back, 0))
        def _():
            turn_weights()

        def both(when, phase, m):
            @pl.when(when)
            def _():
                def one(j, c):
                    phase(m + j)
                    return c

                lax.fori_loop(0, 2, one, 0)

        def some(begin, end, m):
            def spatial(j, c):
                backward_spatial(m + j)
                return c

            def skip(j, c):
                send_skip_grad(m + j)
                return c

            lax.fori_loop(begin, end, spatial, 0)

            @pl.when(jnp.logical_not(early))
            def _():
                lax.fori_loop(begin, end, skip, 0)

        inner = jnp.logical_not(last)
        done_f = jnp.logical_and(s > 0, s <= pairs)
        md = 2 * jnp.clip(s - 1, 0, pairs - 1)
        both(jnp.logical_and(done_f, last), forward_out, md)
        both(jnp.logical_and(do_b, last), backward_in, mb)
        some(1, jnp.where(last & do_b & (s > wait_back), 2, 1), mb - 2)
        both(do_f, forward_spatial, mf)
        both(jnp.logical_and(done_f, inner), forward_out, md)
        both(do_b, backward_temporal, mb)
        if hubs:

            @pl.when(outer & first & (s == wait_back + 1))
            def _():
                gu_to_hub(2).start()

        both(do_f, forward_temporal, mf)
        ends = s == wait_back + pairs - 1
        some(0, jnp.where(do_b, jnp.where(last & jnp.logical_not(ends), 1, 2), 0), mb)
        if hubs:

            @pl.when(s == jnp.where(last, wait_back + 1, pairs - 1))
            def _():
                inputs_to_hub()

            @pl.when(outer & (section == 1) & (s == wait_back))
            def _():
                gu_to_hub(0).start()

            @pl.when(outer & (section > 1) & (s == wait_back + 1))
            def _():
                gu_to_hub(0).start()

            @pl.when(outer & jnp.logical_not(first) & (s == wait_back + 1))
            def _():
                for part in range(1, MB):
                    gu_to_hub(part).start()

        return carry

    lax.fori_loop(0, 2 * pairs, step, 0)

    def finish(m, carry):
        store(0, raw_act, o_act, m).wait()
        store(1, raw_grad, o_grad, m).wait()
        for kind, src, dst in (
            (2, a_in, o_in),
            (3, hidden, o_hidden),
            (4, gr, o_gr),
            (5, gu, o_gu),
        ):
            keep_operand(kind, src, dst, m).wait()
            twin_operand(kind, src, dst, m).wait()

        @pl.when(jnp.logical_not(last))
        def _():
            cross_sent(4, x_p, m)
            for part in range(2):
                half_to_pipe(2, part, r_out, r_in, m, 1).wait_send()


        @pl.when(section == 1)
        def _():
            to_pipe(0, a_out, skip_in, m, 2).wait_send()

        @pl.when(jnp.logical_not(first))
        def _():
            cross_sent(2, x_bt, m)
            for part in range(2):
                half_to_pipe(4, part, ig_out, ga_in, m, -1).wait_send()

        @pl.when(jnp.logical_not(early))
        def _():
            to_pipe(1, gs_out, gs_in, m, -1).wait_send()

        return carry

    lax.fori_loop(0, MB, finish, 0)
    if hubs:


        @pl.when(outer)
        def _():
            for m in range(MB):
                to_hub(m).wait_send()
            for part in range(MB):
                gu_to_hub(part).wait_send()

        @pl.when(jnp.logical_not(outer))
        def _():
            for m in range(MB):
                to_hub(m).wait_recv()
            for part in range(MB):
                gu_to_hub(part).wait_recv()

    @pl.when(jnp.logical_not(last))
    def _():
        send_scale().wait_send()


def relay(dims, n_dp, hubs, clips, boxes, w_s, w_t, g_s, b_s, g_t, b_t, cotangent):
    cm, frames, height, width = dims
    rows = cm * frames * height * width
    d, m_ch = w_t.shape[1], w_s.shape[1]
    shape = jax.ShapeDtypeStruct
    vmem = pl.BlockSpec(memory_space=pltpu.VMEM)
    hbm = pl.BlockSpec(memory_space=pl.ANY)
    smem = pl.BlockSpec(memory_space=pltpu.SMEM)
    dma = pltpu.SemaphoreType.DMA
    narrow = pltpu.VMEM((MB, rows, d), bf16)
    wide = pltpu.VMEM((MB, rows, m_ch), bf16)
    return pl.pallas_call(
        functools.partial(relay_kernel, dims),
        out_shape=(
            shape(clips.shape, bf16),
            shape(clips.shape, bf16),
            shape((3 if hubs else 2, MB, rows, d), bf16),
            shape((2, MB, rows, m_ch), bf16),
            shape((3 if hubs else 2, MB, rows, m_ch), bf16),
            shape((2, MB, rows, d), bf16),
            shape((1, m_ch), f32),
            shape((1, m_ch), f32),
            shape((1, d), f32),
            shape((1, d), f32),
        ),
        in_specs=[hbm, smem, hbm, hbm, vmem, vmem, vmem, vmem, hbm],
        out_specs=[hbm] * 6 + [vmem] * 4,
        scratch_shapes=[
            pltpu.VMEM(w_s.shape, bf16),
            pltpu.VMEM(w_t.shape, bf16),
            pltpu.VMEM((9 * m_ch, d), bf16),
            pltpu.VMEM((3 * d, m_ch), bf16),
            pltpu.VMEM((rows, 9 * m_ch), bf16),
            pltpu.VMEM(clips.shape, bf16),
            pltpu.VMEM(clips.shape, bf16),
            pltpu.VMEM(clips.shape, bf16),
            narrow,
            narrow,
            narrow,
            narrow,
            narrow,
            narrow,
            narrow,
            narrow,
            narrow,
            wide,
            narrow,
            wide,
            pltpu.VMEM((MB, rows, m_ch), f32),
            pltpu.VMEM((rows, d), f32),
            pltpu.VMEM((2, rows, m_ch), f32),
            pltpu.VMEM((MB, rows, 128), f32),
            pltpu.VMEM((MB, 1, m_ch), f32),
            pltpu.VMEM((MB, 1, d), f32),
            pltpu.VMEM((MB, 1, d), f32),
            pltpu.VMEM((MB, 1, d), f32),
            pltpu.VMEM((MB, 1, d), f32),
            pltpu.VMEM((MB, 1, 128), f32),
            pltpu.VMEM((2, 1, d), f32),
            pltpu.VMEM((2, 1, d), f32),
            pltpu.VMEM((MB, n_dp, 1, 2 * m_ch + 128), f32),
            pltpu.VMEM((MB, n_dp, 1, 2 * d + 128), f32),
            pltpu.VMEM((MB, n_dp, 1, 2 * d + 128), f32),
            pltpu.VMEM((MB, n_dp, 1, 2 * d), f32),
            pltpu.VMEM((MB, n_dp, 1, 2 * m_ch), f32),
            pltpu.VMEM((MB, 1, 1, 2 * d), f32),
            dma((5, MB)),
            dma((5, MB)),
            dma((21,)),
            dma((MB,)),
            dma((6, MB)),
            dma((6, MB)),
            dma((6, MB)),
            dma((4, MB)),
            dma((4, MB)),
            dma((4, MB)),
        ],
        compiler_params=pltpu.CompilerParams(
            collective_id=0, has_side_effects=True, vmem_limit_bytes=62 * 2**20
        ),
    )(clips, boxes, w_s, w_t, g_s, b_s, g_t, b_t, cotangent)


def send_order(n, z, q):
    table = []
    for here in range(n):
        up = sorted(range(here + 1, n), reverse=True)
        down = list(range(here))
        table.append((up + down if here < n / 2 else down + up) + [here])
    dest = 0
    for here in range(n):
        for at in range(n):
            dest = dest + jnp.where((z == here) & (q == at), table[here][at], 0)
    return dest


PIECE = 384
SPAN = 640

HUB_JOBS = (
    (0, 0, -1),
    (0, 1, 0),
    (1, 0, -1),
    (2, 0, -1),
    (0, 2, 1),
    (2, 1, -1),
    (1, 1, -1),
    (1, 2, -1),
    (3, 0, 2),
    (2, 2, 3),
    (3, 1, -1),
    (3, 2, -1),
)


def of_job(j, column):
    return sum(jnp.where(j == i, job[column], 0) for i, job in enumerate(HUB_JOBS))


def is_one_of(j, members):
    found = j < 0
    for i in members:
        found = found | (j == i)
    return found


def gradient_kernel(
    dims,
    a_hbm,
    v_hbm,
    gu_hbm,
    gr_hbm,
    o_s,
    o_t,
    a,
    v,
    gu,
    gr,
    window,
    window_t,
    acc_s,
    acc_t,
    got_s,
    got_t,
    out_s,
    out_t,
    load_sem,
    a_sem,
    gu_send,
    gu_recv,
    fwd_send,
    fwd_recv,
    s_send,
    s_recv,
    t_send,
    t_recv,
):
    frames, height, width = dims
    nc, rows, d = a_hbm.shape[0] // 3, a_hbm.shape[1], a_hbm.shape[2]
    m_ch = v_hbm.shape[2]
    me = lax.axis_index("dp")
    n = lax.axis_size("dp") // 2
    z = lax.div(me, 2)
    core = lax.rem(me, 2)
    twin = me + 1 - 2 * core
    inner = jnp.logical_and(z > 0, z < n - 1)
    outer = jnp.logical_not(inner)
    step = jnp.where(z < n / 2, 2, -2)
    rows_s, rows_t = o_s.shape[0], o_t.shape[0]
    n_pieces = m_ch // PIECE

    barrier = pltpu.get_barrier_semaphore()

    def greet(device):
        pl.semaphore_signal(barrier, 1, device_id={"dp": device}, device_id_type=MESH)

    greet(twin)

    @pl.when(z > 0)
    def _():
        greet(me - 2)

    @pl.when(z < n - 1)
    def _():
        greet(me + 2)

    load_a = pltpu.make_async_copy(a_hbm, a.at[pl.ds(0, 3 * nc)], load_sem.at[0])
    full = 2 * nc + nc // MB
    load_gu = pltpu.make_async_copy(
        gu_hbm.at[pl.ds(0, full)], gu.at[pl.ds(0, full)], load_sem.at[1]
    )
    late = 3 * nc - nc // MB
    early = (pl.ds(full, late - full), slice(None), pl.ds(0, PIECE))
    load_early = pltpu.make_async_copy(gu_hbm.at[early], gu.at[early], load_sem.at[4])
    load_v = pltpu.make_async_copy(v_hbm, v, load_sem.at[2])
    load_gr = pltpu.make_async_copy(gr_hbm, gr, load_sem.at[3])

    @pl.when(inner)
    def _():
        load_a.start()
        load_gu.start()
        load_early.start()

    load_v.start()
    load_gr.start()
    pl.semaphore_wait(barrier, 3 - jnp.where(z == 0, 1, 0) - jnp.where(z == n - 1, 1, 0))

    def columns(p):
        return pl.ds(pl.multiple_of(p * PIECE, 128), PIECE)

    def remote(src, dst, send, recv, device):
        return pltpu.make_async_remote_copy(
            src_ref=src,
            dst_ref=dst,
            send_sem=send,
            recv_sem=recv,
            device_id={"dp": device},
            device_id_type=MESH,
        )

    def gu_to_hub(p):
        s = columns(p)
        return remote(
            gu_hbm.at[pl.ds(nc // MB, nc - nc // MB), :, s],
            gu.at[pl.ds(full, nc - nc // MB), :, s],
            gu_send.at[p],
            gu_recv.at[p],
            me + step,
        )

    def first_to_hub():
        s = pl.ds(0, PIECE)
        return remote(
            gu_hbm.at[pl.ds(late - 2 * nc, nc // MB), :, s],
            gu.at[pl.ds(late, nc // MB), :, s],
            gu_send.at[0],
            gu_recv.at[0],
            me + step,
        )

    def gu_to_twin(p):
        s = columns(p)
        return remote(
            gu.at[pl.ds(2 * nc, nc), :, s],
            gu.at[pl.ds(3 * nc, nc), :, s],
            fwd_send.at[p],
            fwd_recv.at[p],
            twin,
        )

    a_to_twin = remote(
        a.at[pl.ds(2 * nc, nc)], a.at[pl.ds(3 * nc, nc)], a_sem.at[0], a_sem.at[1], twin
    )

    def moved(x, before, after, dt, step):
        if not dt:
            return x
        y = x.reshape(before, after, 128)
        zero = jnp.zeros((before, step, 128), f32)
        if dt > 0:
            y = jnp.concatenate([y[:, step:], zero], axis=1)
        else:
            y = jnp.concatenate([zero, y[:, :-step]], axis=1)
        return y.reshape(rows, 128)

    def place(row0):
        low = lax.div(row0, 128)
        return low, row0 - low * 128

    def time_job(q):
        dest = send_order(n, z, q)
        low, start = place((2 * dest + core) * rows_t)

        def fill_time(i, c):
            to = pl.ds(pl.multiple_of(i * rows, 16), rows)
            for j in range(SPAN // 128):
                chunk = jnp.minimum(low + j, 3 * m_ch // 128 - 1)
                tap = lax.div(chunk, m_ch // 128)
                lane = pl.ds(pl.multiple_of((chunk - tap * (m_ch // 128)) * 128, 128), 128)

                def fill(dt):
                    x = v[i, :, lane].astype(f32)
                    x = moved(x, 1, rows, dt, height * width)
                    window_t[to, j * 128 : (j + 1) * 128] = x.astype(bf16)

                lax.switch(tap, [functools.partial(fill, dt) for dt in (-1, 0, 1)])
            return c

        lax.fori_loop(0, 2 * nc, fill_time, 0)
        acc_t[...] = lax.dot_general(
            window_t[...],
            gr[...].reshape(2 * nc * rows, d),
            (((0,), (0,)), ((), ())),
            preferred_element_type=f32,
        )
        at = pl.ds(pl.multiple_of(start, 8), rows_t)

        def add(slot):
            pltpu.make_async_copy(got_t.at[slot], got_t.at[slot], t_recv.at[slot]).wait()
            acc_t[at, :] += got_t[slot].astype(f32)

        @pl.when((z > 0) & (dest >= z))
        def _():
            add(dest + 1)

        @pl.when((z < n - 1) & (dest <= z))
        def _():
            add(dest)

        @pl.when(dest == z)
        def _():
            o_t[...] = acc_t[at, :]

        @pl.when(dest != z)
        def _():
            out_t[dest] = acc_t[at, :].astype(bf16)
            time_send(dest).start()

    def time_send(dest):
        right = dest > z
        slot = dest + jnp.where(right, 1, 0)
        return remote(
            out_t.at[dest],
            got_t.at[slot],
            t_send.at[dest],
            t_recv.at[slot],
            me + jnp.where(right, 2, -2),
        )

    def hub_dest(k):
        near = z < n / 2
        far_out = jnp.where(near, n - 1, 0)
        own_out = n - 1 - far_out
        return jnp.where(
            k == 0, far_out, jnp.where(k == 1, n - 1 - z, jnp.where(k == 2, own_out, z))
        )

    def space_place(k):
        return place((2 * hub_dest(k) + core) * rows_s)

    def fill_window(k, first, count):
        low, start = space_place(k)

        def fill_space(i, c):
            to = pl.ds(pl.multiple_of(i * rows, 16), rows)
            for j in range(SPAN // 128):
                chunk = jnp.minimum(low + j, 9 * d // 128 - 1)
                tap = lax.div(chunk, d // 128)
                lane = pl.ds(pl.multiple_of((chunk - tap * (d // 128)) * 128, 128), 128)

                def fill(dh, dw):
                    x = a[i, :, lane].astype(f32)
                    if dw:
                        x = pltpu.roll(x, (-dw) % rows, 0)
                    x = moved(x, frames, height * width, dh, width)
                    window[k, to, j * 128 : (j + 1) * 128] = x.astype(bf16)

                lax.switch(
                    tap,
                    [
                        functools.partial(fill, dh, dw)
                        for dh in (-1, 0, 1)
                        for dw in (-1, 0, 1)
                    ],
                )
            return c

        lax.fori_loop(first, first + count, fill_space, 0)

    def space_send(k, p):
        s = columns(p)
        return remote(
            out_s.at[k, :, s],
            got_s.at[jnp.where(k == 1, 1, 0), :, s],
            s_send.at[k, p],
            s_recv.at[jnp.where(k == 1, 1, 0), p],
            me + jnp.where(k == 2, -step, step),
        )

    def space_job(k, p):
        s = columns(p)
        low, start = space_place(k)
        at = pl.ds(pl.multiple_of(start, 8), rows_s)
        acc_s[...] = lax.dot_general(
            window[k],
            gu[:, :, s].reshape(4 * nc * rows, PIECE),
            (((0,), (0,)), ((), ())),
            preferred_element_type=f32,
        )

        @pl.when(k >= 2)
        def _():
            got = got_s.at[k - 2, :, s]
            pltpu.make_async_copy(got, got, s_recv.at[k - 2, p]).wait()
            acc_s[at, :] += got[...].astype(f32)

        @pl.when(k == 3)
        def _():
            o_s[:, s] = acc_s[at, :]

        @pl.when(k < 3)
        def _():
            out_s[k, :, s] = acc_s[at, :].astype(bf16)
            space_send(k, p).start()

    def take_gu(p):
        @pl.when(p == 0)
        def _():
            first_to_hub().wait_recv()

        @pl.when(p > 0)
        def _():
            gu_to_hub(p).wait_recv()

        gu_to_twin(p).start()
        gu_to_twin(p).wait_recv()

    @pl.when(inner)
    def _():
        load_a.wait()
        a_to_twin.start()

        a_to_twin.wait_recv()

        new_k = [i for i, job in enumerate(HUB_JOBS) if job[0] not in [x[0] for x in HUB_JOBS[:i]]]
        new_p = [i for i, job in enumerate(HUB_JOBS) if job[1] not in [x[1] for x in HUB_JOBS[:i]]]
        timed = [i for i, job in enumerate(HUB_JOBS) if job[2] >= 0]

        def hub_job(j, carry):
            k, p = of_job(j, 0), of_job(j, 1)

            @pl.when(is_one_of(j, new_k))
            def _():
                fill_window(k, 0, 4 * nc)

            @pl.when(j == 0)
            def _():
                load_gu.wait()
                load_early.wait()

            @pl.when(is_one_of(j, new_p))
            def _():
                take_gu(p)

            space_job(k, p)

            @pl.when(j == timed[0])
            def _():
                load_v.wait()
                load_gr.wait()

            @pl.when(is_one_of(j, timed))
            def _():
                time_job(of_job(j, 2))

            return carry

        lax.fori_loop(0, len(HUB_JOBS), hub_job, 0)
        a_to_twin.wait_send()

        def sent(p, carry):
            gu_to_twin(p).wait_send()
            for k in range(3):
                space_send(k, p).wait_send()
            return carry

        lax.fori_loop(0, n_pieces, sent, 0)

    @pl.when(outer)
    def _():
        first_to_hub().start()
        gu_to_hub(1).start()
        load_v.wait()
        load_gr.wait()

        def round_out(q, carry):
            time_job(q)

            @pl.when(q == 0)
            def _():
                for p in range(2, n_pieces):
                    gu_to_hub(p).start()

            return carry

        lax.fori_loop(0, n, round_out, 0)

        for p in range(n_pieces):
            s = columns(p)
            got = got_s.at[0, :, s]
            pltpu.make_async_copy(got, got, s_recv.at[0, p]).wait()
            o_s[:, s] = got[...].astype(f32)
            (gu_to_hub(p) if p else first_to_hub()).wait_send()

    def finish(q, carry):
        time_send(send_order(n, z, q)).wait_send()
        return carry

    lax.fori_loop(0, n - 1, finish, 0)


def gradients(dims, n_dp, a, v, gu, gr):
    nc, rows, d = a.shape[0] // 3, a.shape[1], a.shape[2]
    m_ch = v.shape[2]
    rows_s, rows_t = 9 * d // n_dp, 3 * m_ch // n_dp
    n = n_dp // 2
    n_pieces = m_ch // PIECE
    shape = jax.ShapeDtypeStruct
    dma = pltpu.SemaphoreType.DMA
    return pl.pallas_call(
        functools.partial(gradient_kernel, dims),
        out_shape=(shape((rows_s, m_ch), f32), shape((rows_t, d), f32)),
        in_specs=[pl.BlockSpec(memory_space=pl.ANY)] * 4,
        out_specs=[pl.BlockSpec(memory_space=pltpu.VMEM)] * 2,
        scratch_shapes=[
            pltpu.VMEM((4 * nc, rows, d), bf16),
            pltpu.VMEM(v.shape, bf16),
            pltpu.VMEM((4 * nc, rows, m_ch), bf16),
            pltpu.VMEM(gr.shape, bf16),
            pltpu.VMEM((4, 4 * nc * rows, SPAN), bf16),
            pltpu.VMEM((2 * nc * rows, SPAN), bf16),
            pltpu.VMEM((SPAN, PIECE), f32),
            pltpu.VMEM((SPAN, d), f32),
            pltpu.VMEM((2, rows_s, m_ch), bf16),
            pltpu.VMEM((n + 1, rows_t, d), bf16),
            pltpu.VMEM((3, rows_s, m_ch), bf16),
            pltpu.VMEM((n, rows_t, d), bf16),
            dma((5,)),
            dma((2,)),
            dma((n_pieces,)),
            dma((n_pieces,)),
            dma((n_pieces,)),
            dma((n_pieces,)),
            dma((3, n_pieces)),
            dma((2, n_pieces)),
            dma((n,)),
            dma((n + 1,)),
        ],
        compiler_params=pltpu.CompilerParams(
            collective_id=1, has_side_effects=True, vmem_limit_bytes=62 * 2**20
        ),
    )(a, v, gu, gr)


def spatial_columns(activity):
    height, breadth = (activity.shape[2], activity.shape[3])
    padded = jnp.pad(activity, ((0, 0), (0, 0), (1, 1), (1, 1), (0, 0)))
    pieces = [
        padded[:, :, row_off : row_off + height, col_off : col_off + breadth, :]
        for row_off in range(3)
        for col_off in range(3)
    ]
    return jnp.concatenate(pieces, axis=-1)


def temporal_columns(activity):
    frames = activity.shape[1]
    padded = jnp.pad(activity, ((0, 0), (1, 1), (0, 0), (0, 0), (0, 0)))
    return jnp.concatenate([padded[:, offset : offset + frames] for offset in range(3)], axis=-1)


def left_product(former, latter):
    return lax.dot_general(
        former, latter, (((0,), (0,)), ((), ())), preferred_element_type=jnp.float32
    )


def body(
    clips,
    boxes,
    spatial_w,
    temporal_w,
    spatial_gain,
    spatial_shift,
    temporal_gain,
    temporal_shift,
    cotangent,
):
    n_clips, frames, height, breadth, d = clips.shape
    cm = n_clips // MB
    width = (breadth // 8 + 1) * 8
    rows = cm * frames * height * width
    m_ch = spatial_w.shape[2]

    def frames_inside(x):
        return x.transpose(0, 2, 3, 1, 4)

    n_dp = lax.axis_size("dp")
    hubs = n_dp == 8 and 9 * d // n_dp == 576 and 3 * m_ch // n_dp == 432 and d % 128 == 0
    act, grad, a_in, hidden, gu, gr, gain_s, shift_s, gain_t, shift_t = relay(
        (cm, frames, height, width),
        n_dp,
        hubs,
        frames_inside(clips),
        boxes,
        spatial_w[0],
        temporal_w[0],
        spatial_gain,
        spatial_shift,
        temporal_gain,
        temporal_shift,
        frames_inside(cotangent),
    )

    def frames_of(x):
        return x.reshape(n_clips, frames, height, width, x.shape[-1])[:, :, :, :breadth]

    if hubs:
        clip_rows = frames * height * width
        grad_s, grad_t = gradients(
            (frames, height, width),
            n_dp,
            *[x.reshape(-1, clip_rows, x.shape[-1]) for x in (a_in, hidden, gu, gr)],
        )
    else:
        cells = n_clips * frames * height * breadth
        cols = spatial_columns(frames_of(a_in[0])).reshape(cells, -1)
        grad_s = left_product(cols, frames_of(gu[0]).reshape(cells, -1))
        stacked = temporal_columns(frames_of(hidden[0])).reshape(cells, -1)
        grad_t = left_product(stacked, frames_of(gr[0]).reshape(cells, -1))
        grad_s = lax.psum_scatter(grad_s, "dp", scatter_dimension=0, tiled=True)
        grad_t = lax.psum_scatter(grad_t, "dp", scatter_dimension=0, tiled=True)
    return (
        act.transpose(0, 3, 1, 2, 4)[None],
        grad.transpose(0, 3, 1, 2, 4)[None],
        grad_s[None],
        grad_t[None],
        gain_s,
        shift_s,
        gain_t,
        shift_t,
    )


def solution(mesh):
    clip_spec = P("dp", None, None, None, None)
    weight_spec = P("pipe", None, None)
    channel_spec = P("pipe", None)
    return jax.shard_map(
        body,
        mesh=mesh,
        in_specs=(
            clip_spec,
            P("dp", None),
            weight_spec,
            weight_spec,
            channel_spec,
            channel_spec,
            channel_spec,
            channel_spec,
            clip_spec,
        ),
        out_specs=(
            P("pipe", "dp", None, None, None, None),
            P("pipe", "dp", None, None, None, None),
            P("pipe", "dp", None),
            P("pipe", "dp", None),
            channel_spec,
            channel_spec,
            channel_spec,
            channel_spec,
        ),
        check_vma=False,
    )
```

```python
import functools

import jax
import jax.numpy as jnp
from jax import lax
from jax.experimental import pallas as pl
from jax.experimental.pallas import tpu as pltpu
from jax.sharding import PartitionSpec as P

MB = 4
eps_norm = 1e-05
bf16 = jnp.bfloat16
f32 = jnp.float32
MESH = pl.DeviceIdType.MESH


def silu(x):
    return x / (1.0 + jnp.exp(-x))


def silu_slope(x):
    s = 1.0 / (1.0 + jnp.exp(-x))
    return s * (1.0 + x * (1.0 - s))


def lane_chunks(width, body):
    def step(i, carry):
        body(i, pl.ds(pl.multiple_of(i * 128, 128), 128))
        return carry

    lax.fori_loop(0, width // 128, step, 0, unroll=True)


def relay_kernel(
    dims,
    clips,
    boxes,
    w_s_hbm,
    w_t_hbm,
    g_s,
    b_s,
    g_t,
    b_t,
    cotangent,
    o_act,
    o_grad,
    o_in,
    o_hidden,
    o_gu,
    o_gr,
    o_gain_s,
    o_shift_s,
    o_gain_t,
    o_shift_t,
    w_s,
    w_t,
    w_s_back,
    w_t_back,
    cols,
    raw,
    raw_act,
    raw_grad,
    a_in,
    skip_in,
    a_out,
    r_in,
    r_out,
    ga_in,
    gs_in,
    gs_out,
    ig_out,
    hidden,
    gr,
    gu,
    uh,
    r_sum,
    gq,
    keep,
    fact_s,
    fact_t,
    off_t,
    fact_p,
    off_p,
    cnt,
    scale_out,
    scale_in,
    x_s,
    x_t,
    x_p,
    x_bt,
    x_bs,
    x_bp,
    x_send,
    x_recv,
    w_sem,
    load_sem,
    store_sem,
    pipe_send,
    pipe_recv,
    twin_send,
    twin_recv,
    hub_sem,
):
    cm, frames, height, width = dims
    breadth = clips.shape[2]
    rows = cm * frames * height * width
    d = a_in.shape[2]
    m_ch = hidden.shape[2]
    section = lax.axis_index("pipe")
    me = lax.axis_index("dp")
    n_pipe = lax.axis_size("pipe")
    n_dp = lax.axis_size("dp")
    first = section == 0
    last = section == n_pipe - 1
    odd = lax.rem(section, 2) == 1
    even_inner = jnp.logical_and(jnp.logical_not(odd), jnp.logical_not(last))
    early = section < 2
    skip_own = odd.astype(f32)
    skip_prev = jnp.logical_not(jnp.logical_or(odd, first)).astype(f32)

    def load_ws(part, tap):
        half = d // 2
        src = w_s_hbm.at[pl.ds(tap * d + part * half, half)]
        dst = w_s.at[pl.ds((part * 9 + tap) * half, half)]
        return pltpu.make_async_copy(src, dst, w_sem.at[part * 9 + tap])

    load_wt = pltpu.make_async_copy(w_t_hbm, w_t, w_sem.at[18])

    def load_raw(src, m):
        at = pl.ds(m * cm, cm)
        return pltpu.make_async_copy(src.at[at], raw.at[at], load_sem.at[m])

    def unpack(m, dst):
        pad = jnp.zeros((width - breadth, 128), f32)

        def column(i, s):
            pieces = []
            for c in range(cm):
                x = raw[m * cm + c, :, :, :, s].astype(f32)
                x = jnp.transpose(x.reshape(height * breadth, frames, 128), (1, 0, 2))
                for t in range(frames):
                    for h in range(height):
                        pieces += [x[t, h * breadth : (h + 1) * breadth], pad]
            dst[m, :, s] = jnp.concatenate(pieces, axis=0).astype(bf16)

        lane_chunks(d, column)

    def pack(m, src, dst):
        def column(i, s):
            x = src[m, :, s].astype(f32).reshape(cm * frames * height, width, 128)
            x = x[:, :breadth].reshape(cm, frames, height * breadth, 128)
            for c in range(cm):
                y = jnp.transpose(x[c], (1, 0, 2)).reshape(height, breadth, frames, 128)
                dst[m * cm + c, :, :, :, s] = y.astype(bf16)

        lane_chunks(d, column)

    local_skip = jnp.logical_not(jnp.logical_or(first, last))

    @pl.when(first)
    def _():
        for m in range(MB):
            load_raw(clips, m).start()

    @pl.when(local_skip)
    def _():
        for m in range(MB):
            load_raw(clips, m).start()

    for part in range(2):
        for tap in range(9):
            load_ws(part, tap).start()
    load_wt.start()

    @pl.when(last)
    def _():
        for m in range(MB):
            load_raw(cotangent, m).start()

    for ref in (o_gain_s, o_shift_s, o_gain_t, o_shift_t, gs_in, scale_in):
        ref[...] = jnp.zeros_like(ref)

    @pl.when(first)
    def _():
        skip_in[...] = jnp.zeros_like(skip_in)

    barrier = pltpu.get_barrier_semaphore()

    def greet(j, carry):
        pl.semaphore_signal(
            barrier, 1, device_id={"dp": lax.rem(me + j, n_dp)}, device_id_type=MESH
        )
        return carry

    lax.fori_loop(1, n_dp, greet, 0)

    def greet_pipe(step):
        def greet_one(j, carry):
            pl.semaphore_signal(
                barrier,
                1,
                device_id={"pipe": section + step, "dp": j},
                device_id_type=MESH,
            )
            return carry

        lax.fori_loop(0, n_dp, greet_one, 0)

    @pl.when(jnp.logical_not(first))
    def _():
        greet_pipe(-1)

    @pl.when(jnp.logical_not(last))
    def _():
        greet_pipe(1)

    pl.semaphore_signal(
        barrier,
        1,
        device_id={"pipe": section + jnp.where(early, 2, -2)},
        device_id_type=MESH,
    )
    scale_out[0] = g_t[...]
    scale_out[1] = b_t[...]

    def make_keep(m, carry):
        n_rows = frames * height * width
        pieces = []
        for c in range(cm):
            shape = (frames, height, width, 128)
            t = lax.broadcasted_iota(jnp.int32, shape, 0)
            h = lax.broadcasted_iota(jnp.int32, shape, 1)
            w = lax.broadcasted_iota(jnp.int32, shape, 2)
            box = [boxes[m * cm + c, i] for i in range(6)]
            inside = (t >= box[0]) & (t < box[1]) & (h >= box[2]) & (h < box[3])
            inside = inside & (w >= box[4]) & (w < box[5])
            pieces.append(jnp.where(inside, 1.0, 0.0).astype(f32).reshape(n_rows, 128))
        mask = jnp.concatenate(pieces, axis=0) if cm > 1 else pieces[0]
        keep[m] = mask
        cnt[m] = jnp.sum(mask, axis=0, keepdims=True)
        return carry

    lax.fori_loop(0, MB, make_keep, 0)
    def share(kind, buf, m):
        def send(j, carry):
            pltpu.make_async_remote_copy(
                src_ref=buf.at[m, me],
                dst_ref=buf.at[m, me],
                send_sem=x_send.at[kind, m],
                recv_sem=x_recv.at[kind, m],
                device_id={"dp": lax.rem(me + j, n_dp)},
                device_id_type=MESH,
            ).start()
            return carry

        lax.fori_loop(1, n_dp, send, 0, unroll=n_dp <= 8)

    def shared(kind, buf, m):
        others = buf.at[m, pl.ds(0, n_dp - 1)]
        pltpu.make_async_copy(others, others, x_send.at[kind, m]).wait()
        pltpu.make_async_copy(others, others, x_recv.at[kind, m]).wait()

    def cross(kind, src, dst, m, step):
        def send(j, carry):
            pltpu.make_async_remote_copy(
                src_ref=src,
                dst_ref=dst.at[m, me],
                send_sem=x_send.at[kind, m],
                recv_sem=x_recv.at[kind, m],
                device_id={"pipe": section + step, "dp": lax.rem(me + j, n_dp)},
                device_id_type=MESH,
            ).start()
            return carry

        lax.fori_loop(0, n_dp, send, 0, unroll=n_dp <= 8)

    def crossed(kind, buf, m):
        slots = buf.at[m]
        pltpu.make_async_copy(slots, slots, x_recv.at[kind, m]).wait()

    def cross_sent(kind, buf, m):
        slots = buf.at[m]
        pltpu.make_async_copy(slots, slots, x_send.at[kind, m]).wait()

    def to_pipe(kind, src, dst, m, step):
        return pltpu.make_async_remote_copy(
            src_ref=src.at[m],
            dst_ref=dst.at[m],
            send_sem=pipe_send.at[kind, m],
            recv_sem=pipe_recv.at[kind, m],
            device_id={"pipe": section + step},
            device_id_type=MESH,
        )

    half = d // 2

    def half_to_pipe(kind, part, src, dst, m, step):
        s = pl.ds(part * half, half)
        return pltpu.make_async_remote_copy(
            src_ref=src.at[m, :, s],
            dst_ref=dst.at[m, :, s],
            send_sem=pipe_send.at[kind + part, m],
            recv_sem=pipe_recv.at[kind + part, m],
            device_id={"pipe": section + step},
            device_id_type=MESH,
        )

    hubs = o_in.shape[0] > 2
    z = lax.div(me, 2)
    outer = jnp.logical_or(z == 0, z == n_dp // 2 - 1)

    def to_hub(m):
        return pltpu.make_async_remote_copy(
            src_ref=a_in.at[m],
            dst_ref=o_in.at[2, m],
            send_sem=hub_sem.at[0, m],
            recv_sem=hub_sem.at[1, m],
            device_id={"dp": me + jnp.where(z == 0, 2, -2)},
            device_id_type=MESH,
        )

    def inputs_to_hub():
        @pl.when(outer)
        def _():
            for m in range(MB):
                to_hub(m).start()

    def gu_to_hub(part):
        m = max(part - 1, 0)
        s = (pl.ds(0, 640), pl.ds(640, m_ch - 640), pl.ds(0, PIECE))[min(part, 2)]
        return pltpu.make_async_remote_copy(
            src_ref=gu.at[m, :, s],
            dst_ref=o_gu.at[2, m, :, s],
            send_sem=hub_sem.at[2, part],
            recv_sem=hub_sem.at[3, part],
            device_id={"dp": me + jnp.where(z == 0, 2, -2)},
            device_id_type=MESH,
        )

    def store(kind, src, dst, m):
        at = pl.ds(m * cm, cm)
        return pltpu.make_async_copy(src.at[at], dst.at[at], store_sem.at[kind, m])

    def keep_operand(kind, src, dst, m):
        return pltpu.make_async_copy(src.at[m], dst.at[0, m], store_sem.at[kind, m])

    def twin_operand(kind, src, dst, m):
        return pltpu.make_async_remote_copy(
            src_ref=src.at[m],
            dst_ref=dst.at[1, m],
            send_sem=twin_send.at[kind - 2, m],
            recv_sem=twin_recv.at[kind - 2, m],
            device_id={"dp": me + 1 - 2 * lax.rem(me, 2)},
            device_id_type=MESH,
        )

    def share_operand(kind, src, dst, m):
        keep_operand(kind, src, dst, m).start()
        twin_operand(kind, src, dst, m).start()

    def shift_space(x, dh, dw):
        if dw:
            x = pltpu.roll(x, (-dw) % rows, 0)
        return shift_rows(x, dh)

    def shift_rows(x, dh):
        if not dh:
            return x
        y = x.reshape(cm * frames, height * width, 128)
        zero = jnp.zeros((cm * frames, width, 128), f32)
        if dh > 0:
            y = jnp.concatenate([y[:, width:], zero], axis=1)
        else:
            y = jnp.concatenate([zero, y[:, :-width]], axis=1)
        return y.reshape(rows, 128)

    def shift_time(x, dt):
        if not dt:
            return x
        y = x.reshape(cm, frames * height * width, 128)
        step = height * width
        zero = jnp.zeros((cm, step, 128), f32)
        if dt > 0:
            y = jnp.concatenate([y[:, step:], zero], axis=1)
        else:
            y = jnp.concatenate([zero, y[:, :-step]], axis=1)
        return y.reshape(rows, 128)

    def local_sums(m, value, buf, c, channels):
        mask = keep[m]
        n_here = cnt[m]
        total = jnp.sum(mask * value, axis=0, keepdims=True)
        dev = mask * (value - total / n_here)
        spread = jnp.sum(dev * dev, axis=0, keepdims=True)
        buf[m, me, :, pl.ds(pl.multiple_of(c * 128, 128), 128)] = total
        buf[m, me, :, pl.ds(pl.multiple_of(channels + c * 128, 128), 128)] = spread
        return dev

    def merged(m, buf, c, channels):
        counts = buf[m, :, :, 2 * channels :]
        sums = buf[m, :, :, pl.ds(pl.multiple_of(c * 128, 128), 128)]
        spreads = buf[m, :, :, pl.ds(pl.multiple_of(channels + c * 128, 128), 128)]
        n = jnp.sum(counts, axis=0)
        mean = jnp.sum(sums, axis=0) / n
        off = sums / counts - mean[None]
        var = jnp.sum(spreads + counts * off * off, axis=0) / n
        return n, mean, lax.rsqrt(var + eps_norm)

    def lanes_of(part, i):
        return pl.ds(pl.multiple_of(part * half + i * 128, 128), 128)

    def normed_prev(m, s):
        return (r_in[m, :, s].astype(f32) + off_p[m, :, s]) * fact_p[m, :, s]

    def preact_prev(m, s, normed):
        return scale_in[0, :, s] * normed + scale_in[1, :, s]

    def skipped_prev(m, s, value):
        return value + skip_prev * skip_in[m, :, s].astype(f32)

    def activate(m, part, skipped, i, s):
        s = lanes_of(part, i)
        n, mean, rstd = merged(m, x_p, part * (half // 128) + i, d)
        off_p[m, :, s] = x_p[m, me, :, s] / x_p[m, me, :, 2 * d :] - mean
        fact_p[m, :, s] = rstd
        value = preact_prev(m, s, normed_prev(m, s))
        if skipped:
            value = skipped_prev(m, s, value)
        a_in[m, :, s] = (keep[m] * silu(value)).astype(bf16)

    def spatial_conv(m, begins):
        for part in range(2):
            if not begins:

                @pl.when(jnp.logical_not(first))
                def _():
                    half_to_pipe(2, part, r_out, r_in, m, 1).wait_recv()

                @pl.when(section == 2)
                def _():
                    lane_chunks(half, functools.partial(activate, m, part, True))

                @pl.when(odd)
                def _():
                    lane_chunks(half, functools.partial(activate, m, part, False))

            def column(i, s):
                s = lanes_of(part, i)
                x = a_in[m, :, s].astype(f32)
                for dw in (-1, 0, 1):
                    y = shift_space(x, 0, dw)
                    for dh in (-1, 0, 1):
                        tap = (dh + 1) * 3 + dw + 1
                        at = part * 9 * half + tap * half + i * 128
                        cols[:, pl.ds(pl.multiple_of(at, 128), 128)] = shift_rows(y, dh).astype(
                            bf16
                        )

            lane_chunks(half, column)
            if begins:
                for tap in range(9):
                    load_ws(part, tap).wait()

            k = slice(part * 9 * half, (part + 1) * 9 * half)
            for s in (slice(0, 512), slice(512, m_ch)):
                value = jnp.dot(cols[:, k], w_s[k, s], preferred_element_type=f32)
                if part == 0:
                    uh[m, :, s] = value
                else:
                    uh[m, :, s] += value

    @pl.when(first)
    def _():
        load_raw(clips, 0).wait()
        unpack(0, a_in)
        spatial_conv(0, True)

    sides = 3 - jnp.where(first, 1, 0) - jnp.where(last, 1, 0)
    pl.semaphore_wait(barrier, sides * n_dp)

    def send_scale():
        return pltpu.make_async_remote_copy(
            src_ref=scale_out,
            dst_ref=scale_in,
            send_sem=w_sem.at[19],
            recv_sem=w_sem.at[20],
            device_id={"pipe": section + 1},
            device_id_type=MESH,
        )

    @pl.when(jnp.logical_not(last))
    def _():
        send_scale().start()

    @pl.when(local_skip)
    def _():
        for m in range(MB):
            load_raw(clips, m).wait()
        lax.fori_loop(0, MB, lambda m, c: (unpack(m, skip_in), c)[1], 0)

    @pl.when(last)
    def _():
        for m in range(MB):
            load_raw(cotangent, m).wait()
        lax.fori_loop(0, MB, lambda m, c: (unpack(m, ga_in), c)[1], 0)

    def forward_spatial(m):
        @pl.when(first & (m > 0))
        def _():
            load_raw(clips, m).wait()
            unpack(m, a_in)

        @pl.when(jnp.logical_not(first))
        def _():
            @pl.when(m == 0)
            def _():
                send_scale().wait_recv()

            crossed(4, x_p, m)

        @pl.when(jnp.logical_not(first & (m == 0)))
        def _():
            spatial_conv(m, False)

        x_s[m, me, :, 2 * m_ch :] = cnt[m]

        def sums(i, s):
            local_sums(m, uh[m, :, s], x_s, i, m_ch)

        lane_chunks(m_ch, sums)
        share(0, x_s, m)
        share_operand(2, a_in, o_in, m)

    def forward_temporal(m):
        shared(0, x_s, m)

        def column(i, s):
            n, mean, rstd = merged(m, x_s, i, m_ch)
            fact_s[m, :, s] = rstd
            normed = (uh[m, :, s] - mean) * rstd
            uh[m, :, s] = normed
            value = keep[m] * silu(g_s[:, s] * normed + b_s[:, s])
            value = value.astype(bf16)
            hidden[m, :, s] = value
            value = value.astype(f32)
            for dt in (-1, 0, 1):
                at = pl.ds(pl.multiple_of((dt + 1) * m_ch + i * 128, 128), 128)
                cols[:, at] = shift_time(value, dt).astype(bf16)

        lane_chunks(m_ch, column)
        share_operand(3, hidden, o_hidden, m)

        @pl.when((m == 0) & first)
        def _():
            load_wt.wait()

        r_sum[...] = jnp.dot(cols[:, : 3 * m_ch], w_t[...], preferred_element_type=f32)
        x_t[m, me, :, 2 * d :] = cnt[m]

        def centre(i, s):
            r_out[m, :, s] = local_sums(m, r_sum[:, s], x_t, i, d).astype(bf16)

        lane_chunks(d, centre)

        @pl.when(jnp.logical_not(last))
        def _():
            cross(4, x_t.at[m, me], x_p, m, 1)
            for part in range(2):
                half_to_pipe(2, part, r_out, r_in, m, 1).start()

        share(1, x_t, m)

    def normed_own(m, s):
        return (r_out[m, :, s].astype(f32) + off_t[m, :, s]) * fact_t[m, :, s]

    def preact_own(m, s, normed):
        return g_t[:, s] * normed + b_t[:, s] + skip_own * skip_in[m, :, s].astype(f32)

    def forward_out(m):
        @pl.when(last)
        def _():
            to_pipe(0, a_out, skip_in, m, 2).wait_recv()

        shared(1, x_t, m)

        def column(i, s):
            n, mean, rstd = merged(m, x_t, i, d)
            off_t[m, :, s] = x_t[m, me, :, s] / cnt[m] - mean
            fact_t[m, :, s] = rstd
            value = keep[m] * silu(preact_own(m, s, normed_own(m, s)))
            a_out[m, :, s] = value.astype(bf16)

        lane_chunks(d, column)
        pack(m, a_out, raw_act)
        store(0, raw_act, o_act, m).start()

        @pl.when(section == 1)
        def _():
            to_pipe(0, a_out, skip_in, m, 2).start()

    def slope_sums(row, value, normed, i, s):
        row[:, s] = jnp.sum(value, axis=0, keepdims=True)
        at = pl.ds(pl.multiple_of(d + i * 128, 128), 128)
        row[:, at] = jnp.sum(value * normed, axis=0, keepdims=True)

    def own_slope(m, s, normed):
        return ga_in[m, :, s].astype(f32) * keep[m] * silu_slope(preact_own(m, s, normed))

    def backward_in(m):
        def column(i, s):
            normed = normed_own(m, s)
            slope_sums(x_bt.at[m, me], own_slope(m, s, normed), normed, i, s)

        lane_chunks(d, column)
        share(2, x_bt, m)

    def totals(buf, m, s, i, channels):
        at = pl.ds(pl.multiple_of(channels + i * 128, 128), 128)
        return jnp.sum(buf[m, :, :, s], axis=0), jnp.sum(buf[m, :, :, at], axis=0)

    def backward_temporal(m):
        @pl.when(last)
        def _():
            shared(2, x_bt, m)

        @pl.when(jnp.logical_not(last))
        def _():
            crossed(2, x_bt, m)
            for part in range(2):
                half_to_pipe(4, part, ig_out, ga_in, m, -1).wait_recv()

        n = jnp.sum(x_t[m, :, :, 2 * d :], axis=0)

        def column(i, s):
            shift_sum, gain_sum = totals(x_bt, m, s, i, d)
            o_shift_t[:, s] += shift_sum
            o_gain_t[:, s] += gain_sum
            normed = normed_own(m, s)
            slope = own_slope(m, s, normed)
            gs_out[m, :, s] = slope.astype(bf16)
            scale = g_t[:, s] * fact_t[m, :, s]
            value = keep[m] * scale * (slope - (shift_sum + normed * gain_sum) / n)
            value = value.astype(bf16)
            gr[m, :, s] = value
            value = value.astype(f32)
            for dt in (-1, 0, 1):
                at = pl.ds(pl.multiple_of((dt + 1) * d + i * 128, 128), 128)
                cols[:, at] = shift_time(value, -dt).astype(bf16)

        lane_chunks(d, column)
        share_operand(4, gr, o_gr, m)

        gq[lax.rem(m, 2)] = jnp.dot(cols[:, : 3 * d], w_t_back[...], preferred_element_type=f32)

        def sums(i, s):
            normed = uh[m, :, s]
            slope = keep[m] * gq[lax.rem(m, 2), :, s] * silu_slope(g_s[:, s] * normed + b_s[:, s])
            gq[lax.rem(m, 2), :, s] = slope
            x_bs[m, me, :, s] = jnp.sum(slope, axis=0, keepdims=True)
            at = pl.ds(pl.multiple_of(m_ch + i * 128, 128), 128)
            x_bs[m, me, :, at] = jnp.sum(slope * normed, axis=0, keepdims=True)

        lane_chunks(m_ch, sums)
        share(3, x_bs, m)

    def backward_spatial(m):
        shared(3, x_bs, m)
        n = jnp.sum(x_t[m, :, :, 2 * d :], axis=0)

        def column(i, s):
            shift_sum, gain_sum = totals(x_bs, m, s, i, m_ch)
            o_shift_s[:, s] += shift_sum
            o_gain_s[:, s] += gain_sum
            scale = g_s[:, s] * fact_s[m, :, s]
            value = keep[m] * scale * (gq[lax.rem(m, 2), :, s] - (shift_sum + uh[m, :, s] * gain_sum) / n)
            value = value.astype(bf16)
            gu[m, :, s] = value
            value = value.astype(f32)
            for dw in (-1, 0, 1):
                y = shift_space(value, 0, -dw)
                for dh in (-1, 0, 1):
                    tap = (dh + 1) * 3 + dw + 1
                    at = pl.ds(pl.multiple_of(tap * m_ch + i * 128, 128), 128)
                    cols[:, at] = shift_rows(y, -dh).astype(bf16)

        lane_chunks(m_ch, column)
        share_operand(5, gu, o_gu, m)
        if hubs:
            for part, when in ((0, 0), (1, 0), (3, 2)):

                @pl.when(outer & first & (m == when))
                def _():
                    gu_to_hub(part).start()


        @pl.when(even_inner)
        def _():
            to_pipe(1, gs_out, gs_in, m, -1).wait_recv()

        with_skip = even_inner.astype(f32)
        for part in range(2):
            s = slice(part * half, (part + 1) * half)
            value = jnp.dot(cols[...], w_s_back[:, s], preferred_element_type=f32)
            ig_out[m, :, s] = (value + with_skip * gs_in[m, :, s].astype(f32)).astype(bf16)

            @pl.when(jnp.logical_not(first))
            def _():
                keeps = jnp.full((rows, 128), last.astype(f32))

                def sums(i, s):
                    s = lanes_of(part, i)
                    normed = normed_prev(m, s)
                    slope = silu_slope(skipped_prev(m, s, preact_prev(m, s, normed)))
                    slope = ig_out[m, :, s].astype(f32) * keep[m] * slope
                    held = gs_out[m, :, s].astype(f32)
                    gs_out[m, :, s] = jnp.where(keeps > 0, held, slope).astype(bf16)
                    slope_sums(x_bp.at[m, 0], slope, normed, part * (half // 128) + i, s)

                if part == 0:
                    half_to_pipe(4, part, ig_out, ga_in, m, -1).start()
                lane_chunks(half, sums)
                if part == 1:
                    cross(2, x_bp.at[m, 0], x_bt, m, -1)
                    half_to_pipe(4, part, ig_out, ga_in, m, -1).start()

        pack(m, ig_out, raw_grad)
        store(1, raw_grad, o_grad, m).start()

    def send_skip_grad(m):
        to_pipe(1, gs_out, gs_in, m, jnp.where(last, -1, -2)).start()

    def turn_weights():
        @pl.when(jnp.logical_not(first))
        def _():
            for part in range(2):
                for tap in range(9):
                    load_ws(part, tap).wait()
            load_wt.wait()

        def spatial(tap, carry):
            dst = pl.ds(pl.multiple_of(tap * m_ch, 128), m_ch)
            for part in range(2):
                src = pl.ds(pl.multiple_of((part * 9 + tap) * half, 128), half)
                w_s_back[dst, part * half : (part + 1) * half] = w_s[src, :].T
            return carry

        lax.fori_loop(0, 9, spatial, 0)

        def temporal(tap, carry):
            src = pl.ds(pl.multiple_of(tap * m_ch, 128), m_ch)
            dst = pl.ds(pl.multiple_of(tap * d, 128), d)
            w_t_back[dst, :] = w_t[src, :].T
            return carry

        lax.fori_loop(0, 3, temporal, 0)

    pairs = MB // 2
    wait_back = jnp.where(last, 1, pairs)

    def step(s, carry):
        do_f = s < pairs
        do_b = jnp.logical_and(s >= wait_back, s < wait_back + pairs)
        mf = 2 * jnp.minimum(s, pairs - 1)
        mb = 2 * jnp.clip(s - wait_back, 0, pairs - 1)

        @pl.when(s == jnp.where(first, wait_back, 0))
        def _():
            turn_weights()

        def both(when, phase, m):
            @pl.when(when)
            def _():
                def one(j, c):
                    phase(m + j)
                    return c

                lax.fori_loop(0, 2, one, 0)

        def some(begin, end, m):
            def spatial(j, c):
                backward_spatial(m + j)
                return c

            def skip(j, c):
                send_skip_grad(m + j)
                return c

            lax.fori_loop(begin, end, spatial, 0)

            @pl.when(jnp.logical_not(early))
            def _():
                lax.fori_loop(begin, end, skip, 0)

        inner = jnp.logical_not(last)
        done_f = jnp.logical_and(s > 0, s <= pairs)
        md = 2 * jnp.clip(s - 1, 0, pairs - 1)
        both(jnp.logical_and(done_f, last), forward_out, md)
        both(jnp.logical_and(do_b, last), backward_in, mb)
        some(1, jnp.where(last & do_b & (s > wait_back), 2, 1), mb - 2)
        both(do_f, forward_spatial, mf)
        both(jnp.logical_and(done_f, inner), forward_out, md)
        both(do_b, backward_temporal, mb)
        if hubs:

            @pl.when(outer & first & (s == wait_back + 1))
            def _():
                gu_to_hub(2).start()

        both(do_f, forward_temporal, mf)
        ends = s == wait_back + pairs - 1
        some(0, jnp.where(do_b, jnp.where(last & jnp.logical_not(ends), 1, 2), 0), mb)
        if hubs:

            @pl.when(s == jnp.where(last, wait_back + 1, pairs - 1))
            def _():
                inputs_to_hub()

            @pl.when(outer & (section == 1) & (s == wait_back))
            def _():
                gu_to_hub(0).start()

            @pl.when(outer & (section > 1) & (s == wait_back + 1))
            def _():
                gu_to_hub(0).start()

            @pl.when(outer & jnp.logical_not(first) & (s == wait_back + 1))
            def _():
                for part in range(1, MB):
                    gu_to_hub(part).start()

        return carry

    lax.fori_loop(0, 2 * pairs, step, 0)

    def finish(m, carry):
        store(0, raw_act, o_act, m).wait()
        store(1, raw_grad, o_grad, m).wait()
        for kind, src, dst in (
            (2, a_in, o_in),
            (3, hidden, o_hidden),
            (4, gr, o_gr),
            (5, gu, o_gu),
        ):
            keep_operand(kind, src, dst, m).wait()
            twin_operand(kind, src, dst, m).wait()

        @pl.when(jnp.logical_not(last))
        def _():
            cross_sent(4, x_p, m)
            for part in range(2):
                half_to_pipe(2, part, r_out, r_in, m, 1).wait_send()


        @pl.when(section == 1)
        def _():
            to_pipe(0, a_out, skip_in, m, 2).wait_send()

        @pl.when(jnp.logical_not(first))
        def _():
            cross_sent(2, x_bt, m)
            for part in range(2):
                half_to_pipe(4, part, ig_out, ga_in, m, -1).wait_send()

        @pl.when(jnp.logical_not(early))
        def _():
            to_pipe(1, gs_out, gs_in, m, -1).wait_send()

        return carry

    lax.fori_loop(0, MB, finish, 0)
    if hubs:


        @pl.when(outer)
        def _():
            for m in range(MB):
                to_hub(m).wait_send()
            for part in range(MB):
                gu_to_hub(part).wait_send()

        @pl.when(jnp.logical_not(outer))
        def _():
            for m in range(MB):
                to_hub(m).wait_recv()
            for part in range(MB):
                gu_to_hub(part).wait_recv()

    @pl.when(jnp.logical_not(last))
    def _():
        send_scale().wait_send()


def relay(dims, n_dp, hubs, clips, boxes, w_s, w_t, g_s, b_s, g_t, b_t, cotangent):
    cm, frames, height, width = dims
    rows = cm * frames * height * width
    d, m_ch = w_t.shape[1], w_s.shape[1]
    shape = jax.ShapeDtypeStruct
    vmem = pl.BlockSpec(memory_space=pltpu.VMEM)
    hbm = pl.BlockSpec(memory_space=pl.ANY)
    smem = pl.BlockSpec(memory_space=pltpu.SMEM)
    dma = pltpu.SemaphoreType.DMA
    narrow = pltpu.VMEM((MB, rows, d), bf16)
    wide = pltpu.VMEM((MB, rows, m_ch), bf16)
    return pl.pallas_call(
        functools.partial(relay_kernel, dims),
        out_shape=(
            shape(clips.shape, bf16),
            shape(clips.shape, bf16),
            shape((3 if hubs else 2, MB, rows, d), bf16),
            shape((2, MB, rows, m_ch), bf16),
            shape((3 if hubs else 2, MB, rows, m_ch), bf16),
            shape((2, MB, rows, d), bf16),
            shape((1, m_ch), f32),
            shape((1, m_ch), f32),
            shape((1, d), f32),
            shape((1, d), f32),
        ),
        in_specs=[hbm, smem, hbm, hbm, vmem, vmem, vmem, vmem, hbm],
        out_specs=[hbm] * 6 + [vmem] * 4,
        scratch_shapes=[
            pltpu.VMEM(w_s.shape, bf16),
            pltpu.VMEM(w_t.shape, bf16),
            pltpu.VMEM((9 * m_ch, d), bf16),
            pltpu.VMEM((3 * d, m_ch), bf16),
            pltpu.VMEM((rows, 9 * m_ch), bf16),
            pltpu.VMEM(clips.shape, bf16),
            pltpu.VMEM(clips.shape, bf16),
            pltpu.VMEM(clips.shape, bf16),
            narrow,
            narrow,
            narrow,
            narrow,
            narrow,
            narrow,
            narrow,
            narrow,
            narrow,
            wide,
            narrow,
            wide,
            pltpu.VMEM((MB, rows, m_ch), f32),
            pltpu.VMEM((rows, d), f32),
            pltpu.VMEM((2, rows, m_ch), f32),
            pltpu.VMEM((MB, rows, 128), f32),
            pltpu.VMEM((MB, 1, m_ch), f32),
            pltpu.VMEM((MB, 1, d), f32),
            pltpu.VMEM((MB, 1, d), f32),
            pltpu.VMEM((MB, 1, d), f32),
            pltpu.VMEM((MB, 1, d), f32),
            pltpu.VMEM((MB, 1, 128), f32),
            pltpu.VMEM((2, 1, d), f32),
            pltpu.VMEM((2, 1, d), f32),
            pltpu.VMEM((MB, n_dp, 1, 2 * m_ch + 128), f32),
            pltpu.VMEM((MB, n_dp, 1, 2 * d + 128), f32),
            pltpu.VMEM((MB, n_dp, 1, 2 * d + 128), f32),
            pltpu.VMEM((MB, n_dp, 1, 2 * d), f32),
            pltpu.VMEM((MB, n_dp, 1, 2 * m_ch), f32),
            pltpu.VMEM((MB, 1, 1, 2 * d), f32),
            dma((5, MB)),
            dma((5, MB)),
            dma((21,)),
            dma((MB,)),
            dma((6, MB)),
            dma((6, MB)),
            dma((6, MB)),
            dma((4, MB)),
            dma((4, MB)),
            dma((4, MB)),
        ],
        compiler_params=pltpu.CompilerParams(
            collective_id=0, has_side_effects=True, vmem_limit_bytes=62 * 2**20
        ),
    )(clips, boxes, w_s, w_t, g_s, b_s, g_t, b_t, cotangent)


def send_order(n, z, q):
    table = []
    for here in range(n):
        up = sorted(range(here + 1, n), reverse=True)
        down = list(range(here))
        table.append((up + down if here < n / 2 else down + up) + [here])
    dest = 0
    for here in range(n):
        for at in range(n):
            dest = dest + jnp.where((z == here) & (q == at), table[here][at], 0)
    return dest


PIECE = 384
SPAN = 640

HUB_JOBS = (
    (0, 0, -1),
    (1, 0, -1),
    (0, 1, 0),
    (2, 0, -1),
    (0, 2, 1),
    (2, 1, -1),
    (1, 1, -1),
    (1, 2, -1),
    (3, 0, 2),
    (2, 2, 3),
    (3, 1, -1),
    (3, 2, -1),
)


def of_job(j, column):
    return sum(jnp.where(j == i, job[column], 0) for i, job in enumerate(HUB_JOBS))


def is_one_of(j, members):
    found = j < 0
    for i in members:
        found = found | (j == i)
    return found


def gradient_kernel(
    dims,
    a_hbm,
    v_hbm,
    gu_hbm,
    gr_hbm,
    o_s,
    o_t,
    a,
    v,
    gu,
    gr,
    window,
    window_t,
    acc_s,
    acc_t,
    got_s,
    got_t,
    out_s,
    out_t,
    load_sem,
    a_sem,
    gu_send,
    gu_recv,
    fwd_send,
    fwd_recv,
    s_send,
    s_recv,
    t_send,
    t_recv,
):
    frames, height, width = dims
    nc, rows, d = a_hbm.shape[0] // 3, a_hbm.shape[1], a_hbm.shape[2]
    m_ch = v_hbm.shape[2]
    me = lax.axis_index("dp")
    n = lax.axis_size("dp") // 2
    z = lax.div(me, 2)
    core = lax.rem(me, 2)
    twin = me + 1 - 2 * core
    inner = jnp.logical_and(z > 0, z < n - 1)
    outer = jnp.logical_not(inner)
    step = jnp.where(z < n / 2, 2, -2)
    rows_s, rows_t = o_s.shape[0], o_t.shape[0]
    n_pieces = m_ch // PIECE

    barrier = pltpu.get_barrier_semaphore()

    def greet(device):
        pl.semaphore_signal(barrier, 1, device_id={"dp": device}, device_id_type=MESH)

    greet(twin)

    @pl.when(z > 0)
    def _():
        greet(me - 2)

    @pl.when(z < n - 1)
    def _():
        greet(me + 2)

    load_a = pltpu.make_async_copy(a_hbm, a.at[pl.ds(0, 3 * nc)], load_sem.at[0])
    full = 2 * nc + nc // MB
    load_gu = pltpu.make_async_copy(
        gu_hbm.at[pl.ds(0, full)], gu.at[pl.ds(0, full)], load_sem.at[1]
    )
    late = 3 * nc - nc // MB
    early = (pl.ds(full, late - full), slice(None), pl.ds(0, PIECE))
    load_early = pltpu.make_async_copy(gu_hbm.at[early], gu.at[early], load_sem.at[4])
    load_v = pltpu.make_async_copy(v_hbm, v, load_sem.at[2])
    load_gr = pltpu.make_async_copy(gr_hbm, gr, load_sem.at[3])

    @pl.when(inner)
    def _():
        load_a.start()
        load_gu.start()
        load_early.start()

    load_v.start()
    load_gr.start()
    pl.semaphore_wait(barrier, 3 - jnp.where(z == 0, 1, 0) - jnp.where(z == n - 1, 1, 0))

    def columns(p):
        return pl.ds(pl.multiple_of(p * PIECE, 128), PIECE)

    def remote(src, dst, send, recv, device):
        return pltpu.make_async_remote_copy(
            src_ref=src,
            dst_ref=dst,
            send_sem=send,
            recv_sem=recv,
            device_id={"dp": device},
            device_id_type=MESH,
        )

    def gu_to_hub(p):
        s = columns(p)
        return remote(
            gu_hbm.at[pl.ds(nc // MB, nc - nc // MB), :, s],
            gu.at[pl.ds(full, nc - nc // MB), :, s],
            gu_send.at[p],
            gu_recv.at[p],
            me + step,
        )

    def first_to_hub():
        s = pl.ds(0, PIECE)
        return remote(
            gu_hbm.at[pl.ds(late - 2 * nc, nc // MB), :, s],
            gu.at[pl.ds(late, nc // MB), :, s],
            gu_send.at[0],
            gu_recv.at[0],
            me + step,
        )

    def gu_to_twin(p):
        s = columns(p)
        return remote(
            gu.at[pl.ds(2 * nc, nc), :, s],
            gu.at[pl.ds(3 * nc, nc), :, s],
            fwd_send.at[p],
            fwd_recv.at[p],
            twin,
        )

    a_to_twin = remote(
        a.at[pl.ds(2 * nc, nc)], a.at[pl.ds(3 * nc, nc)], a_sem.at[0], a_sem.at[1], twin
    )

    def moved(x, before, after, dt, step):
        if not dt:
            return x
        y = x.reshape(before, after, 128)
        zero = jnp.zeros((before, step, 128), f32)
        if dt > 0:
            y = jnp.concatenate([y[:, step:], zero], axis=1)
        else:
            y = jnp.concatenate([zero, y[:, :-step]], axis=1)
        return y.reshape(rows, 128)

    def place(row0):
        low = lax.div(row0, 128)
        return low, row0 - low * 128

    def time_job(q):
        dest = send_order(n, z, q)
        low, start = place((2 * dest + core) * rows_t)

        def fill_time(i, c):
            to = pl.ds(pl.multiple_of(i * rows, 16), rows)
            for j in range(SPAN // 128):
                chunk = jnp.minimum(low + j, 3 * m_ch // 128 - 1)
                tap = lax.div(chunk, m_ch // 128)
                lane = pl.ds(pl.multiple_of((chunk - tap * (m_ch // 128)) * 128, 128), 128)

                def fill(dt):
                    x = v[i, :, lane].astype(f32)
                    x = moved(x, 1, rows, dt, height * width)
                    window_t[to, j * 128 : (j + 1) * 128] = x.astype(bf16)

                lax.switch(tap, [functools.partial(fill, dt) for dt in (-1, 0, 1)])
            return c

        lax.fori_loop(0, 2 * nc, fill_time, 0)
        acc_t[...] = lax.dot_general(
            window_t[...],
            gr[...].reshape(2 * nc * rows, d),
            (((0,), (0,)), ((), ())),
            preferred_element_type=f32,
        )
        at = pl.ds(pl.multiple_of(start, 8), rows_t)

        def add(slot):
            pltpu.make_async_copy(got_t.at[slot], got_t.at[slot], t_recv.at[slot]).wait()
            acc_t[at, :] += got_t[slot].astype(f32)

        @pl.when((z > 0) & (dest >= z))
        def _():
            add(dest + 1)

        @pl.when((z < n - 1) & (dest <= z))
        def _():
            add(dest)

        @pl.when(dest == z)
        def _():
            o_t[...] = acc_t[at, :]

        @pl.when(dest != z)
        def _():
            out_t[dest] = acc_t[at, :].astype(bf16)
            time_send(dest).start()

    def time_send(dest):
        right = dest > z
        slot = dest + jnp.where(right, 1, 0)
        return remote(
            out_t.at[dest],
            got_t.at[slot],
            t_send.at[dest],
            t_recv.at[slot],
            me + jnp.where(right, 2, -2),
        )

    def hub_dest(k):
        near = z < n / 2
        far_out = jnp.where(near, n - 1, 0)
        own_out = n - 1 - far_out
        return jnp.where(
            k == 0, far_out, jnp.where(k == 1, n - 1 - z, jnp.where(k == 2, own_out, z))
        )

    def space_place(k):
        return place((2 * hub_dest(k) + core) * rows_s)

    def fill_window(k, first, count):
        low, start = space_place(k)

        def fill_space(i, c):
            to = pl.ds(pl.multiple_of(i * rows, 16), rows)
            for j in range(SPAN // 128):
                chunk = jnp.minimum(low + j, 9 * d // 128 - 1)
                tap = lax.div(chunk, d // 128)
                lane = pl.ds(pl.multiple_of((chunk - tap * (d // 128)) * 128, 128), 128)

                def fill(dh, dw):
                    x = a[i, :, lane].astype(f32)
                    if dw:
                        x = pltpu.roll(x, (-dw) % rows, 0)
                    x = moved(x, frames, height * width, dh, width)
                    window[k, to, j * 128 : (j + 1) * 128] = x.astype(bf16)

                lax.switch(
                    tap,
                    [
                        functools.partial(fill, dh, dw)
                        for dh in (-1, 0, 1)
                        for dw in (-1, 0, 1)
                    ],
                )
            return c

        lax.fori_loop(first, first + count, fill_space, 0)

    def space_send(k, p):
        s = columns(p)
        return remote(
            out_s.at[k, :, s],
            got_s.at[jnp.where(k == 1, 1, 0), :, s],
            s_send.at[k, p],
            s_recv.at[jnp.where(k == 1, 1, 0), p],
            me + jnp.where(k == 2, -step, step),
        )

    def space_job(k, p):
        s = columns(p)
        low, start = space_place(k)
        at = pl.ds(pl.multiple_of(start, 8), rows_s)
        acc_s[...] = lax.dot_general(
            window[k],
            gu[:, :, s].reshape(4 * nc * rows, PIECE),
            (((0,), (0,)), ((), ())),
            preferred_element_type=f32,
        )

        @pl.when(k >= 2)
        def _():
            got = got_s.at[k - 2, :, s]
            pltpu.make_async_copy(got, got, s_recv.at[k - 2, p]).wait()
            acc_s[at, :] += got[...].astype(f32)

        @pl.when(k == 3)
        def _():
            o_s[:, s] = acc_s[at, :]

        @pl.when(k < 3)
        def _():
            out_s[k, :, s] = acc_s[at, :].astype(bf16)
            space_send(k, p).start()

    def take_gu(p):
        @pl.when(p == 0)
        def _():
            first_to_hub().wait_recv()

        @pl.when(p > 0)
        def _():
            gu_to_hub(p).wait_recv()

        gu_to_twin(p).start()
        gu_to_twin(p).wait_recv()

    @pl.when(inner)
    def _():
        load_a.wait()
        a_to_twin.start()

        a_to_twin.wait_recv()

        new_k = [i for i, job in enumerate(HUB_JOBS) if job[0] not in [x[0] for x in HUB_JOBS[:i]]]
        new_p = [i for i, job in enumerate(HUB_JOBS) if job[1] not in [x[1] for x in HUB_JOBS[:i]]]
        timed = [i for i, job in enumerate(HUB_JOBS) if job[2] >= 0]

        def hub_job(j, carry):
            k, p = of_job(j, 0), of_job(j, 1)

            @pl.when(is_one_of(j, new_k))
            def _():
                fill_window(k, 0, 4 * nc)

            @pl.when(j == 0)
            def _():
                load_gu.wait()
                load_early.wait()

            @pl.when(is_one_of(j, new_p))
            def _():
                take_gu(p)

            space_job(k, p)

            @pl.when(j == timed[0])
            def _():
                load_v.wait()
                load_gr.wait()

            @pl.when(is_one_of(j, timed))
            def _():
                time_job(of_job(j, 2))

            return carry

        lax.fori_loop(0, len(HUB_JOBS), hub_job, 0)
        a_to_twin.wait_send()

        def sent(p, carry):
            gu_to_twin(p).wait_send()
            for k in range(3):
                space_send(k, p).wait_send()
            return carry

        lax.fori_loop(0, n_pieces, sent, 0)

    @pl.when(outer)
    def _():
        first_to_hub().start()
        gu_to_hub(1).start()
        load_v.wait()
        load_gr.wait()

        def round_out(q, carry):
            time_job(q)

            @pl.when(q == 0)
            def _():
                for p in range(2, n_pieces):
                    gu_to_hub(p).start()

            return carry

        lax.fori_loop(0, n, round_out, 0)

        for p in range(n_pieces):
            s = columns(p)
            got = got_s.at[0, :, s]
            pltpu.make_async_copy(got, got, s_recv.at[0, p]).wait()
            o_s[:, s] = got[...].astype(f32)
            (gu_to_hub(p) if p else first_to_hub()).wait_send()

    def finish(q, carry):
        time_send(send_order(n, z, q)).wait_send()
        return carry

    lax.fori_loop(0, n - 1, finish, 0)


def gradients(dims, n_dp, a, v, gu, gr):
    nc, rows, d = a.shape[0] // 3, a.shape[1], a.shape[2]
    m_ch = v.shape[2]
    rows_s, rows_t = 9 * d // n_dp, 3 * m_ch // n_dp
    n = n_dp // 2
    n_pieces = m_ch // PIECE
    shape = jax.ShapeDtypeStruct
    dma = pltpu.SemaphoreType.DMA
    return pl.pallas_call(
        functools.partial(gradient_kernel, dims),
        out_shape=(shape((rows_s, m_ch), f32), shape((rows_t, d), f32)),
        in_specs=[pl.BlockSpec(memory_space=pl.ANY)] * 4,
        out_specs=[pl.BlockSpec(memory_space=pltpu.VMEM)] * 2,
        scratch_shapes=[
            pltpu.VMEM((4 * nc, rows, d), bf16),
            pltpu.VMEM(v.shape, bf16),
            pltpu.VMEM((4 * nc, rows, m_ch), bf16),
            pltpu.VMEM(gr.shape, bf16),
            pltpu.VMEM((4, 4 * nc * rows, SPAN), bf16),
            pltpu.VMEM((2 * nc * rows, SPAN), bf16),
            pltpu.VMEM((SPAN, PIECE), f32),
            pltpu.VMEM((SPAN, d), f32),
            pltpu.VMEM((2, rows_s, m_ch), bf16),
            pltpu.VMEM((n + 1, rows_t, d), bf16),
            pltpu.VMEM((3, rows_s, m_ch), bf16),
            pltpu.VMEM((n, rows_t, d), bf16),
            dma((5,)),
            dma((2,)),
            dma((n_pieces,)),
            dma((n_pieces,)),
            dma((n_pieces,)),
            dma((n_pieces,)),
            dma((3, n_pieces)),
            dma((2, n_pieces)),
            dma((n,)),
            dma((n + 1,)),
        ],
        compiler_params=pltpu.CompilerParams(
            collective_id=1, has_side_effects=True, vmem_limit_bytes=62 * 2**20
        ),
    )(a, v, gu, gr)


def spatial_columns(activity):
    height, breadth = (activity.shape[2], activity.shape[3])
    padded = jnp.pad(activity, ((0, 0), (0, 0), (1, 1), (1, 1), (0, 0)))
    pieces = [
        padded[:, :, row_off : row_off + height, col_off : col_off + breadth, :]
        for row_off in range(3)
        for col_off in range(3)
    ]
    return jnp.concatenate(pieces, axis=-1)


def temporal_columns(activity):
    frames = activity.shape[1]
    padded = jnp.pad(activity, ((0, 0), (1, 1), (0, 0), (0, 0), (0, 0)))
    return jnp.concatenate([padded[:, offset : offset + frames] for offset in range(3)], axis=-1)


def left_product(former, latter):
    return lax.dot_general(
        former, latter, (((0,), (0,)), ((), ())), preferred_element_type=jnp.float32
    )


def body(
    clips,
    boxes,
    spatial_w,
    temporal_w,
    spatial_gain,
    spatial_shift,
    temporal_gain,
    temporal_shift,
    cotangent,
):
    n_clips, frames, height, breadth, d = clips.shape
    cm = n_clips // MB
    width = (breadth // 8 + 1) * 8
    rows = cm * frames * height * width
    m_ch = spatial_w.shape[2]

    def frames_inside(x):
        return x.transpose(0, 2, 3, 1, 4)

    n_dp = lax.axis_size("dp")
    hubs = n_dp == 8 and 9 * d // n_dp == 576 and 3 * m_ch // n_dp == 432 and d % 128 == 0
    act, grad, a_in, hidden, gu, gr, gain_s, shift_s, gain_t, shift_t = relay(
        (cm, frames, height, width),
        n_dp,
        hubs,
        frames_inside(clips),
        boxes,
        spatial_w[0],
        temporal_w[0],
        spatial_gain,
        spatial_shift,
        temporal_gain,
        temporal_shift,
        frames_inside(cotangent),
    )

    def frames_of(x):
        return x.reshape(n_clips, frames, height, width, x.shape[-1])[:, :, :, :breadth]

    if hubs:
        clip_rows = frames * height * width
        grad_s, grad_t = gradients(
            (frames, height, width),
            n_dp,
            *[x.reshape(-1, clip_rows, x.shape[-1]) for x in (a_in, hidden, gu, gr)],
        )
    else:
        cells = n_clips * frames * height * breadth
        cols = spatial_columns(frames_of(a_in[0])).reshape(cells, -1)
        grad_s = left_product(cols, frames_of(gu[0]).reshape(cells, -1))
        stacked = temporal_columns(frames_of(hidden[0])).reshape(cells, -1)
        grad_t = left_product(stacked, frames_of(gr[0]).reshape(cells, -1))
        grad_s = lax.psum_scatter(grad_s, "dp", scatter_dimension=0, tiled=True)
        grad_t = lax.psum_scatter(grad_t, "dp", scatter_dimension=0, tiled=True)
    return (
        act.transpose(0, 3, 1, 2, 4)[None],
        grad.transpose(0, 3, 1, 2, 4)[None],
        grad_s[None],
        grad_t[None],
        gain_s,
        shift_s,
        gain_t,
        shift_t,
    )


def solution(mesh):
    clip_spec = P("dp", None, None, None, None)
    weight_spec = P("pipe", None, None)
    channel_spec = P("pipe", None)
    return jax.shard_map(
        body,
        mesh=mesh,
        in_specs=(
            clip_spec,
            P("dp", None),
            weight_spec,
            weight_spec,
            channel_spec,
            channel_spec,
            channel_spec,
            channel_spec,
            clip_spec,
        ),
        out_specs=(
            P("pipe", "dp", None, None, None, None),
            P("pipe", "dp", None, None, None, None),
            P("pipe", "dp", None),
            P("pipe", "dp", None),
            channel_spec,
            channel_spec,
            channel_spec,
            channel_spec,
        ),
        check_vma=False,
    )
```

```python
import functools

import jax
import jax.numpy as jnp
from jax import lax
from jax.experimental import pallas as pl
from jax.experimental.pallas import tpu as pltpu
from jax.sharding import PartitionSpec as P

MB = 4
eps_norm = 1e-05
bf16 = jnp.bfloat16
f32 = jnp.float32
MESH = pl.DeviceIdType.MESH


def silu(x):
    return x / (1.0 + jnp.exp(-x))


def silu_slope(x):
    s = 1.0 / (1.0 + jnp.exp(-x))
    return s * (1.0 + x * (1.0 - s))


def lane_chunks(width, body):
    def step(i, carry):
        body(i, pl.ds(pl.multiple_of(i * 128, 128), 128))
        return carry

    lax.fori_loop(0, width // 128, step, 0, unroll=True)


def relay_kernel(
    dims,
    clips,
    boxes,
    w_s_hbm,
    w_t_hbm,
    g_s,
    b_s,
    g_t,
    b_t,
    cotangent,
    o_act,
    o_grad,
    o_in,
    o_hidden,
    o_gu,
    o_gr,
    o_gain_s,
    o_shift_s,
    o_gain_t,
    o_shift_t,
    w_s,
    w_t,
    w_s_back,
    w_t_back,
    cols,
    raw,
    raw_act,
    raw_grad,
    a_in,
    skip_in,
    a_out,
    r_in,
    r_out,
    ga_in,
    gs_in,
    gs_out,
    ig_out,
    hidden,
    gr,
    gu,
    uh,
    r_sum,
    gq,
    keep,
    fact_s,
    fact_t,
    off_t,
    fact_p,
    off_p,
    cnt,
    scale_out,
    scale_in,
    x_s,
    x_t,
    x_p,
    x_bt,
    x_bs,
    x_bp,
    x_send,
    x_recv,
    w_sem,
    load_sem,
    store_sem,
    pipe_send,
    pipe_recv,
    twin_send,
    twin_recv,
    hub_sem,
):
    cm, frames, height, width = dims
    breadth = clips.shape[2]
    rows = cm * frames * height * width
    d = a_in.shape[2]
    m_ch = hidden.shape[2]
    section = lax.axis_index("pipe")
    me = lax.axis_index("dp")
    n_pipe = lax.axis_size("pipe")
    n_dp = lax.axis_size("dp")
    first = section == 0
    last = section == n_pipe - 1
    odd = lax.rem(section, 2) == 1
    even_inner = jnp.logical_and(jnp.logical_not(odd), jnp.logical_not(last))
    early = section < 2
    skip_own = odd.astype(f32)
    skip_prev = jnp.logical_not(jnp.logical_or(odd, first)).astype(f32)

    def load_ws(part, tap):
        half = d // 2
        src = w_s_hbm.at[pl.ds(tap * d + part * half, half)]
        dst = w_s.at[pl.ds((part * 9 + tap) * half, half)]
        return pltpu.make_async_copy(src, dst, w_sem.at[part * 9 + tap])

    load_wt = pltpu.make_async_copy(w_t_hbm, w_t, w_sem.at[18])

    def load_raw(src, m):
        at = pl.ds(m * cm, cm)
        return pltpu.make_async_copy(src.at[at], raw.at[at], load_sem.at[m])

    def unpack(m, dst):
        pad = jnp.zeros((width - breadth, 128), f32)

        def column(i, s):
            pieces = []
            for c in range(cm):
                x = raw[m * cm + c, :, :, :, s].astype(f32)
                x = jnp.transpose(x.reshape(height * breadth, frames, 128), (1, 0, 2))
                for t in range(frames):
                    for h in range(height):
                        pieces += [x[t, h * breadth : (h + 1) * breadth], pad]
            dst[m, :, s] = jnp.concatenate(pieces, axis=0).astype(bf16)

        lane_chunks(d, column)

    def pack(m, src, dst):
        def column(i, s):
            x = src[m, :, s].astype(f32).reshape(cm * frames * height, width, 128)
            x = x[:, :breadth].reshape(cm, frames, height * breadth, 128)
            for c in range(cm):
                y = jnp.transpose(x[c], (1, 0, 2)).reshape(height, breadth, frames, 128)
                dst[m * cm + c, :, :, :, s] = y.astype(bf16)

        lane_chunks(d, column)

    local_skip = jnp.logical_not(jnp.logical_or(first, last))

    @pl.when(first)
    def _():
        for m in range(MB):
            load_raw(clips, m).start()

    @pl.when(local_skip)
    def _():
        for m in range(MB):
            load_raw(clips, m).start()

    for part in range(2):
        for tap in range(9):
            load_ws(part, tap).start()
    load_wt.start()

    @pl.when(last)
    def _():
        for m in range(MB):
            load_raw(cotangent, m).start()

    for ref in (o_gain_s, o_shift_s, o_gain_t, o_shift_t, gs_in, scale_in):
        ref[...] = jnp.zeros_like(ref)

    @pl.when(first)
    def _():
        skip_in[...] = jnp.zeros_like(skip_in)

    barrier = pltpu.get_barrier_semaphore()

    def greet(j, carry):
        pl.semaphore_signal(
            barrier, 1, device_id={"dp": lax.rem(me + j, n_dp)}, device_id_type=MESH
        )
        return carry

    lax.fori_loop(1, n_dp, greet, 0)

    def greet_pipe(step):
        def greet_one(j, carry):
            pl.semaphore_signal(
                barrier,
                1,
                device_id={"pipe": section + step, "dp": j},
                device_id_type=MESH,
            )
            return carry

        lax.fori_loop(0, n_dp, greet_one, 0)

    @pl.when(jnp.logical_not(first))
    def _():
        greet_pipe(-1)

    @pl.when(jnp.logical_not(last))
    def _():
        greet_pipe(1)

    pl.semaphore_signal(
        barrier,
        1,
        device_id={"pipe": section + jnp.where(early, 2, -2)},
        device_id_type=MESH,
    )
    scale_out[0] = g_t[...]
    scale_out[1] = b_t[...]

    def make_keep(m, carry):
        n_rows = frames * height * width
        pieces = []
        for c in range(cm):
            shape = (frames, height, width, 128)
            t = lax.broadcasted_iota(jnp.int32, shape, 0)
            h = lax.broadcasted_iota(jnp.int32, shape, 1)
            w = lax.broadcasted_iota(jnp.int32, shape, 2)
            box = [boxes[m * cm + c, i] for i in range(6)]
            inside = (t >= box[0]) & (t < box[1]) & (h >= box[2]) & (h < box[3])
            inside = inside & (w >= box[4]) & (w < box[5])
            pieces.append(jnp.where(inside, 1.0, 0.0).astype(f32).reshape(n_rows, 128))
        mask = jnp.concatenate(pieces, axis=0) if cm > 1 else pieces[0]
        keep[m] = mask
        cnt[m] = jnp.sum(mask, axis=0, keepdims=True)
        return carry

    lax.fori_loop(0, MB, make_keep, 0)
    def share(kind, buf, m):
        def send(j, carry):
            pltpu.make_async_remote_copy(
                src_ref=buf.at[m, me],
                dst_ref=buf.at[m, me],
                send_sem=x_send.at[kind, m],
                recv_sem=x_recv.at[kind, m],
                device_id={"dp": lax.rem(me + j, n_dp)},
                device_id_type=MESH,
            ).start()
            return carry

        lax.fori_loop(1, n_dp, send, 0, unroll=n_dp <= 8)

    def shared(kind, buf, m):
        others = buf.at[m, pl.ds(0, n_dp - 1)]
        pltpu.make_async_copy(others, others, x_send.at[kind, m]).wait()
        pltpu.make_async_copy(others, others, x_recv.at[kind, m]).wait()

    def cross(kind, src, dst, m, step):
        def send(j, carry):
            pltpu.make_async_remote_copy(
                src_ref=src,
                dst_ref=dst.at[m, me],
                send_sem=x_send.at[kind, m],
                recv_sem=x_recv.at[kind, m],
                device_id={"pipe": section + step, "dp": lax.rem(me + j, n_dp)},
                device_id_type=MESH,
            ).start()
            return carry

        lax.fori_loop(0, n_dp, send, 0, unroll=n_dp <= 8)

    def crossed(kind, buf, m):
        slots = buf.at[m]
        pltpu.make_async_copy(slots, slots, x_recv.at[kind, m]).wait()

    def cross_sent(kind, buf, m):
        slots = buf.at[m]
        pltpu.make_async_copy(slots, slots, x_send.at[kind, m]).wait()

    def to_pipe(kind, src, dst, m, step):
        return pltpu.make_async_remote_copy(
            src_ref=src.at[m],
            dst_ref=dst.at[m],
            send_sem=pipe_send.at[kind, m],
            recv_sem=pipe_recv.at[kind, m],
            device_id={"pipe": section + step},
            device_id_type=MESH,
        )

    half = d // 2

    def half_to_pipe(kind, part, src, dst, m, step):
        s = pl.ds(part * half, half)
        return pltpu.make_async_remote_copy(
            src_ref=src.at[m, :, s],
            dst_ref=dst.at[m, :, s],
            send_sem=pipe_send.at[kind + part, m],
            recv_sem=pipe_recv.at[kind + part, m],
            device_id={"pipe": section + step},
            device_id_type=MESH,
        )

    hubs = o_in.shape[0] > 2
    z = lax.div(me, 2)
    outer = jnp.logical_or(z == 0, z == n_dp // 2 - 1)

    def to_hub(m):
        return pltpu.make_async_remote_copy(
            src_ref=a_in.at[m],
            dst_ref=o_in.at[2, m],
            send_sem=hub_sem.at[0, m],
            recv_sem=hub_sem.at[1, m],
            device_id={"dp": me + jnp.where(z == 0, 2, -2)},
            device_id_type=MESH,
        )

    def inputs_to_hub():
        @pl.when(outer)
        def _():
            for m in range(MB):
                to_hub(m).start()

    def gu_to_hub(part):
        m = max(part - 1, 0)
        s = (pl.ds(0, 640), pl.ds(640, m_ch - 640), pl.ds(0, PIECE))[min(part, 2)]
        return pltpu.make_async_remote_copy(
            src_ref=gu.at[m, :, s],
            dst_ref=o_gu.at[2, m, :, s],
            send_sem=hub_sem.at[2, part],
            recv_sem=hub_sem.at[3, part],
            device_id={"dp": me + jnp.where(z == 0, 2, -2)},
            device_id_type=MESH,
        )

    def store(kind, src, dst, m):
        at = pl.ds(m * cm, cm)
        return pltpu.make_async_copy(src.at[at], dst.at[at], store_sem.at[kind, m])

    def keep_operand(kind, src, dst, m):
        return pltpu.make_async_copy(src.at[m], dst.at[0, m], store_sem.at[kind, m])

    def twin_operand(kind, src, dst, m):
        return pltpu.make_async_remote_copy(
            src_ref=src.at[m],
            dst_ref=dst.at[1, m],
            send_sem=twin_send.at[kind - 2, m],
            recv_sem=twin_recv.at[kind - 2, m],
            device_id={"dp": me + 1 - 2 * lax.rem(me, 2)},
            device_id_type=MESH,
        )

    def share_operand(kind, src, dst, m):
        keep_operand(kind, src, dst, m).start()
        twin_operand(kind, src, dst, m).start()

    def shift_space(x, dh, dw):
        if dw:
            x = pltpu.roll(x, (-dw) % rows, 0)
        return shift_rows(x, dh)

    def shift_rows(x, dh):
        if not dh:
            return x
        y = x.reshape(cm * frames, height * width, 128)
        zero = jnp.zeros((cm * frames, width, 128), f32)
        if dh > 0:
            y = jnp.concatenate([y[:, width:], zero], axis=1)
        else:
            y = jnp.concatenate([zero, y[:, :-width]], axis=1)
        return y.reshape(rows, 128)

    def shift_time(x, dt):
        if not dt:
            return x
        y = x.reshape(cm, frames * height * width, 128)
        step = height * width
        zero = jnp.zeros((cm, step, 128), f32)
        if dt > 0:
            y = jnp.concatenate([y[:, step:], zero], axis=1)
        else:
            y = jnp.concatenate([zero, y[:, :-step]], axis=1)
        return y.reshape(rows, 128)

    def local_sums(m, value, buf, c, channels):
        mask = keep[m]
        n_here = cnt[m]
        total = jnp.sum(mask * value, axis=0, keepdims=True)
        dev = mask * (value - total / n_here)
        spread = jnp.sum(dev * dev, axis=0, keepdims=True)
        buf[m, me, :, pl.ds(pl.multiple_of(c * 128, 128), 128)] = total
        buf[m, me, :, pl.ds(pl.multiple_of(channels + c * 128, 128), 128)] = spread
        return dev

    def merged(m, buf, c, channels):
        counts = buf[m, :, :, 2 * channels :]
        sums = buf[m, :, :, pl.ds(pl.multiple_of(c * 128, 128), 128)]
        spreads = buf[m, :, :, pl.ds(pl.multiple_of(channels + c * 128, 128), 128)]
        n = jnp.sum(counts, axis=0)
        mean = jnp.sum(sums, axis=0) / n
        off = sums / counts - mean[None]
        var = jnp.sum(spreads + counts * off * off, axis=0) / n
        return n, mean, lax.rsqrt(var + eps_norm)

    def lanes_of(part, i):
        return pl.ds(pl.multiple_of(part * half + i * 128, 128), 128)

    def normed_prev(m, s):
        return (r_in[m, :, s].astype(f32) + off_p[m, :, s]) * fact_p[m, :, s]

    def preact_prev(m, s, normed):
        return scale_in[0, :, s] * normed + scale_in[1, :, s]

    def skipped_prev(m, s, value):
        return value + skip_prev * skip_in[m, :, s].astype(f32)

    def activate(m, part, skipped, i, s):
        s = lanes_of(part, i)
        n, mean, rstd = merged(m, x_p, part * (half // 128) + i, d)
        off_p[m, :, s] = x_p[m, me, :, s] / x_p[m, me, :, 2 * d :] - mean
        fact_p[m, :, s] = rstd
        value = preact_prev(m, s, normed_prev(m, s))
        if skipped:
            value = skipped_prev(m, s, value)
        a_in[m, :, s] = (keep[m] * silu(value)).astype(bf16)

    def spatial_conv(m, begins):
        for part in range(2):
            if not begins:

                @pl.when(jnp.logical_not(first))
                def _():
                    half_to_pipe(2, part, r_out, r_in, m, 1).wait_recv()

                @pl.when(section == 2)
                def _():
                    lane_chunks(half, functools.partial(activate, m, part, True))

                @pl.when(odd)
                def _():
                    lane_chunks(half, functools.partial(activate, m, part, False))

            def column(i, s):
                s = lanes_of(part, i)
                x = a_in[m, :, s].astype(f32)
                for dw in (-1, 0, 1):
                    y = shift_space(x, 0, dw)
                    for dh in (-1, 0, 1):
                        tap = (dh + 1) * 3 + dw + 1
                        at = part * 9 * half + tap * half + i * 128
                        cols[:, pl.ds(pl.multiple_of(at, 128), 128)] = shift_rows(y, dh).astype(
                            bf16
                        )

            lane_chunks(half, column)
            if begins:
                for tap in range(9):
                    load_ws(part, tap).wait()

            k = slice(part * 9 * half, (part + 1) * 9 * half)
            for s in (slice(0, 512), slice(512, m_ch)):
                value = jnp.dot(cols[:, k], w_s[k, s], preferred_element_type=f32)
                if part == 0:
                    uh[m, :, s] = value
                else:
                    uh[m, :, s] += value

    @pl.when(first)
    def _():
        load_raw(clips, 0).wait()
        unpack(0, a_in)
        spatial_conv(0, True)

    sides = 3 - jnp.where(first, 1, 0) - jnp.where(last, 1, 0)
    pl.semaphore_wait(barrier, sides * n_dp)

    def send_scale():
        return pltpu.make_async_remote_copy(
            src_ref=scale_out,
            dst_ref=scale_in,
            send_sem=w_sem.at[19],
            recv_sem=w_sem.at[20],
            device_id={"pipe": section + 1},
            device_id_type=MESH,
        )

    @pl.when(jnp.logical_not(last))
    def _():
        send_scale().start()

    @pl.when(local_skip)
    def _():
        for m in range(MB):
            load_raw(clips, m).wait()
        lax.fori_loop(0, MB, lambda m, c: (unpack(m, skip_in), c)[1], 0)

    @pl.when(last)
    def _():
        for m in range(MB):
            load_raw(cotangent, m).wait()
        lax.fori_loop(0, MB, lambda m, c: (unpack(m, ga_in), c)[1], 0)

    def forward_spatial(m):
        @pl.when(first & (m > 0))
        def _():
            load_raw(clips, m).wait()
            unpack(m, a_in)

        @pl.when(jnp.logical_not(first))
        def _():
            @pl.when(m == 0)
            def _():
                send_scale().wait_recv()

            crossed(4, x_p, m)

        @pl.when(jnp.logical_not(first & (m == 0)))
        def _():
            spatial_conv(m, False)

        x_s[m, me, :, 2 * m_ch :] = cnt[m]

        def sums(i, s):
            local_sums(m, uh[m, :, s], x_s, i, m_ch)

        lane_chunks(m_ch, sums)
        share(0, x_s, m)
        share_operand(2, a_in, o_in, m)

    def forward_temporal(m):
        shared(0, x_s, m)

        def column(i, s):
            n, mean, rstd = merged(m, x_s, i, m_ch)
            fact_s[m, :, s] = rstd
            normed = (uh[m, :, s] - mean) * rstd
            uh[m, :, s] = normed
            value = keep[m] * silu(g_s[:, s] * normed + b_s[:, s])
            value = value.astype(bf16)
            hidden[m, :, s] = value
            value = value.astype(f32)
            for dt in (-1, 0, 1):
                at = pl.ds(pl.multiple_of((dt + 1) * m_ch + i * 128, 128), 128)
                cols[:, at] = shift_time(value, dt).astype(bf16)

        lane_chunks(m_ch, column)
        share_operand(3, hidden, o_hidden, m)

        @pl.when((m == 0) & first)
        def _():
            load_wt.wait()

        r_sum[...] = jnp.dot(cols[:, : 3 * m_ch], w_t[...], preferred_element_type=f32)
        x_t[m, me, :, 2 * d :] = cnt[m]

        def centre(i, s):
            r_out[m, :, s] = local_sums(m, r_sum[:, s], x_t, i, d).astype(bf16)

        lane_chunks(d, centre)

        @pl.when(jnp.logical_not(last))
        def _():
            cross(4, x_t.at[m, me], x_p, m, 1)
            for part in range(2):
                half_to_pipe(2, part, r_out, r_in, m, 1).start()

        share(1, x_t, m)

    def normed_own(m, s):
        return (r_out[m, :, s].astype(f32) + off_t[m, :, s]) * fact_t[m, :, s]

    def preact_own(m, s, normed):
        return g_t[:, s] * normed + b_t[:, s] + skip_own * skip_in[m, :, s].astype(f32)

    def forward_out(m):
        @pl.when(last)
        def _():
            to_pipe(0, a_out, skip_in, m, 2).wait_recv()

        shared(1, x_t, m)

        def column(i, s):
            n, mean, rstd = merged(m, x_t, i, d)
            off_t[m, :, s] = x_t[m, me, :, s] / cnt[m] - mean
            fact_t[m, :, s] = rstd
            value = keep[m] * silu(preact_own(m, s, normed_own(m, s)))
            a_out[m, :, s] = value.astype(bf16)

        lane_chunks(d, column)
        pack(m, a_out, raw_act)
        store(0, raw_act, o_act, m).start()

        @pl.when(section == 1)
        def _():
            to_pipe(0, a_out, skip_in, m, 2).start()

    def slope_sums(row, value, normed, i, s):
        row[:, s] = jnp.sum(value, axis=0, keepdims=True)
        at = pl.ds(pl.multiple_of(d + i * 128, 128), 128)
        row[:, at] = jnp.sum(value * normed, axis=0, keepdims=True)

    def own_slope(m, s, normed):
        return ga_in[m, :, s].astype(f32) * keep[m] * silu_slope(preact_own(m, s, normed))

    def backward_in(m):
        def column(i, s):
            normed = normed_own(m, s)
            slope_sums(x_bt.at[m, me], own_slope(m, s, normed), normed, i, s)

        lane_chunks(d, column)
        share(2, x_bt, m)

    def totals(buf, m, s, i, channels):
        at = pl.ds(pl.multiple_of(channels + i * 128, 128), 128)
        return jnp.sum(buf[m, :, :, s], axis=0), jnp.sum(buf[m, :, :, at], axis=0)

    def backward_temporal(m):
        @pl.when(last)
        def _():
            shared(2, x_bt, m)

        @pl.when(jnp.logical_not(last))
        def _():
            crossed(2, x_bt, m)
            for part in range(2):
                half_to_pipe(4, part, ig_out, ga_in, m, -1).wait_recv()

        n = jnp.sum(x_t[m, :, :, 2 * d :], axis=0)

        def column(i, s):
            shift_sum, gain_sum = totals(x_bt, m, s, i, d)
            o_shift_t[:, s] += shift_sum
            o_gain_t[:, s] += gain_sum
            normed = normed_own(m, s)
            slope = own_slope(m, s, normed)
            gs_out[m, :, s] = slope.astype(bf16)
            scale = g_t[:, s] * fact_t[m, :, s]
            value = keep[m] * scale * (slope - (shift_sum + normed * gain_sum) / n)
            value = value.astype(bf16)
            gr[m, :, s] = value
            value = value.astype(f32)
            for dt in (-1, 0, 1):
                at = pl.ds(pl.multiple_of((dt + 1) * d + i * 128, 128), 128)
                cols[:, at] = shift_time(value, -dt).astype(bf16)

        lane_chunks(d, column)
        share_operand(4, gr, o_gr, m)

        gq[lax.rem(m, 2)] = jnp.dot(cols[:, : 3 * d], w_t_back[...], preferred_element_type=f32)

        def sums(i, s):
            normed = uh[m, :, s]
            slope = keep[m] * gq[lax.rem(m, 2), :, s] * silu_slope(g_s[:, s] * normed + b_s[:, s])
            gq[lax.rem(m, 2), :, s] = slope
            x_bs[m, me, :, s] = jnp.sum(slope, axis=0, keepdims=True)
            at = pl.ds(pl.multiple_of(m_ch + i * 128, 128), 128)
            x_bs[m, me, :, at] = jnp.sum(slope * normed, axis=0, keepdims=True)

        lane_chunks(m_ch, sums)
        share(3, x_bs, m)

    def backward_spatial(m):
        shared(3, x_bs, m)
        n = jnp.sum(x_t[m, :, :, 2 * d :], axis=0)

        def column(i, s):
            shift_sum, gain_sum = totals(x_bs, m, s, i, m_ch)
            o_shift_s[:, s] += shift_sum
            o_gain_s[:, s] += gain_sum
            scale = g_s[:, s] * fact_s[m, :, s]
            value = keep[m] * scale * (gq[lax.rem(m, 2), :, s] - (shift_sum + uh[m, :, s] * gain_sum) / n)
            value = value.astype(bf16)
            gu[m, :, s] = value
            value = value.astype(f32)
            for dw in (-1, 0, 1):
                y = shift_space(value, 0, -dw)
                for dh in (-1, 0, 1):
                    tap = (dh + 1) * 3 + dw + 1
                    at = pl.ds(pl.multiple_of(tap * m_ch + i * 128, 128), 128)
                    cols[:, at] = shift_rows(y, -dh).astype(bf16)

        lane_chunks(m_ch, column)
        share_operand(5, gu, o_gu, m)
        if hubs:
            for part, when in ((0, 0), (1, 0), (3, 2)):

                @pl.when(outer & first & (m == when))
                def _():
                    gu_to_hub(part).start()


        @pl.when(even_inner)
        def _():
            to_pipe(1, gs_out, gs_in, m, -1).wait_recv()

        with_skip = even_inner.astype(f32)
        keeps = jnp.full((rows, 128), last.astype(f32))

        def sums(part, i, s):
            s = lanes_of(part, i)
            normed = normed_prev(m, s)
            slope = silu_slope(skipped_prev(m, s, preact_prev(m, s, normed)))
            slope = ig_out[m, :, s].astype(f32) * keep[m] * slope
            held = gs_out[m, :, s].astype(f32)
            gs_out[m, :, s] = jnp.where(keeps > 0, held, slope).astype(bf16)
            slope_sums(x_bp.at[m, 0], slope, normed, part * (half // 128) + i, s)

        for part in range(2):
            s = slice(part * half, (part + 1) * half)
            value = jnp.dot(cols[...], w_s_back[:, s], preferred_element_type=f32)
            if part == 1:
                lane_chunks(half, functools.partial(sums, 0))
            ig_out[m, :, s] = (value + with_skip * gs_in[m, :, s].astype(f32)).astype(bf16)

            @pl.when(jnp.logical_not(first))
            def _():
                if part == 1:
                    lane_chunks(half, functools.partial(sums, 1))
                    cross(2, x_bp.at[m, 0], x_bt, m, -1)
                half_to_pipe(4, part, ig_out, ga_in, m, -1).start()

        pack(m, ig_out, raw_grad)
        store(1, raw_grad, o_grad, m).start()

    def send_skip_grad(m):
        to_pipe(1, gs_out, gs_in, m, jnp.where(last, -1, -2)).start()

    def turn_weights():
        @pl.when(jnp.logical_not(first))
        def _():
            for part in range(2):
                for tap in range(9):
                    load_ws(part, tap).wait()
            load_wt.wait()

        def spatial(tap, carry):
            dst = pl.ds(pl.multiple_of(tap * m_ch, 128), m_ch)
            for part in range(2):
                src = pl.ds(pl.multiple_of((part * 9 + tap) * half, 128), half)
                w_s_back[dst, part * half : (part + 1) * half] = w_s[src, :].T
            return carry

        lax.fori_loop(0, 9, spatial, 0)

        def temporal(tap, carry):
            src = pl.ds(pl.multiple_of(tap * m_ch, 128), m_ch)
            dst = pl.ds(pl.multiple_of(tap * d, 128), d)
            w_t_back[dst, :] = w_t[src, :].T
            return carry

        lax.fori_loop(0, 3, temporal, 0)

    pairs = MB // 2
    wait_back = jnp.where(last, 1, pairs)

    def step(s, carry):
        do_f = s < pairs
        do_b = jnp.logical_and(s >= wait_back, s < wait_back + pairs)
        mf = 2 * jnp.minimum(s, pairs - 1)
        mb = 2 * jnp.clip(s - wait_back, 0, pairs - 1)

        @pl.when(s == jnp.where(first, wait_back, 0))
        def _():
            turn_weights()

        def both(when, phase, m):
            @pl.when(when)
            def _():
                def one(j, c):
                    phase(m + j)
                    return c

                lax.fori_loop(0, 2, one, 0)

        def some(begin, end, m):
            def spatial(j, c):
                backward_spatial(m + j)
                return c

            def skip(j, c):
                send_skip_grad(m + j)
                return c

            lax.fori_loop(begin, end, spatial, 0)

            @pl.when(jnp.logical_not(early))
            def _():
                lax.fori_loop(begin, end, skip, 0)

        inner = jnp.logical_not(last)
        done_f = jnp.logical_and(s > 0, s <= pairs)
        md = 2 * jnp.clip(s - 1, 0, pairs - 1)
        both(jnp.logical_and(done_f, last), forward_out, md)
        both(jnp.logical_and(do_b, last), backward_in, mb)
        some(1, jnp.where(last & do_b & (s > wait_back), 2, 1), mb - 2)
        both(do_f, forward_spatial, mf)
        both(jnp.logical_and(done_f, inner), forward_out, md)
        both(do_b, backward_temporal, mb)
        if hubs:

            @pl.when(outer & first & (s == wait_back + 1))
            def _():
                gu_to_hub(2).start()

        both(do_f, forward_temporal, mf)
        ends = s == wait_back + pairs - 1
        some(0, jnp.where(do_b, jnp.where(last & jnp.logical_not(ends), 1, 2), 0), mb)
        if hubs:

            @pl.when(s == jnp.where(last, wait_back + 1, pairs - 1))
            def _():
                inputs_to_hub()

            @pl.when(outer & (section == 1) & (s == wait_back))
            def _():
                gu_to_hub(0).start()

            @pl.when(outer & (section > 1) & (s == wait_back + 1))
            def _():
                gu_to_hub(0).start()

            @pl.when(outer & jnp.logical_not(first) & (s == wait_back + 1))
            def _():
                for part in range(1, MB):
                    gu_to_hub(part).start()

        return carry

    lax.fori_loop(0, 2 * pairs, step, 0)

    def finish(m, carry):
        store(0, raw_act, o_act, m).wait()
        store(1, raw_grad, o_grad, m).wait()
        for kind, src, dst in (
            (2, a_in, o_in),
            (3, hidden, o_hidden),
            (4, gr, o_gr),
            (5, gu, o_gu),
        ):
            keep_operand(kind, src, dst, m).wait()
            twin_operand(kind, src, dst, m).wait()

        @pl.when(jnp.logical_not(last))
        def _():
            cross_sent(4, x_p, m)
            for part in range(2):
                half_to_pipe(2, part, r_out, r_in, m, 1).wait_send()


        @pl.when(section == 1)
        def _():
            to_pipe(0, a_out, skip_in, m, 2).wait_send()

        @pl.when(jnp.logical_not(first))
        def _():
            cross_sent(2, x_bt, m)
            for part in range(2):
                half_to_pipe(4, part, ig_out, ga_in, m, -1).wait_send()

        @pl.when(jnp.logical_not(early))
        def _():
            to_pipe(1, gs_out, gs_in, m, -1).wait_send()

        return carry

    lax.fori_loop(0, MB, finish, 0)
    if hubs:


        @pl.when(outer)
        def _():
            for m in range(MB):
                to_hub(m).wait_send()
            for part in range(MB):
                gu_to_hub(part).wait_send()

        @pl.when(jnp.logical_not(outer))
        def _():
            for m in range(MB):
                to_hub(m).wait_recv()
            for part in range(MB):
                gu_to_hub(part).wait_recv()

    @pl.when(jnp.logical_not(last))
    def _():
        send_scale().wait_send()


def relay(dims, n_dp, hubs, clips, boxes, w_s, w_t, g_s, b_s, g_t, b_t, cotangent):
    cm, frames, height, width = dims
    rows = cm * frames * height * width
    d, m_ch = w_t.shape[1], w_s.shape[1]
    shape = jax.ShapeDtypeStruct
    vmem = pl.BlockSpec(memory_space=pltpu.VMEM)
    hbm = pl.BlockSpec(memory_space=pl.ANY)
    smem = pl.BlockSpec(memory_space=pltpu.SMEM)
    dma = pltpu.SemaphoreType.DMA
    narrow = pltpu.VMEM((MB, rows, d), bf16)
    wide = pltpu.VMEM((MB, rows, m_ch), bf16)
    return pl.pallas_call(
        functools.partial(relay_kernel, dims),
        out_shape=(
            shape(clips.shape, bf16),
            shape(clips.shape, bf16),
            shape((3 if hubs else 2, MB, rows, d), bf16),
            shape((2, MB, rows, m_ch), bf16),
            shape((3 if hubs else 2, MB, rows, m_ch), bf16),
            shape((2, MB, rows, d), bf16),
            shape((1, m_ch), f32),
            shape((1, m_ch), f32),
            shape((1, d), f32),
            shape((1, d), f32),
        ),
        in_specs=[hbm, smem, hbm, hbm, vmem, vmem, vmem, vmem, hbm],
        out_specs=[hbm] * 6 + [vmem] * 4,
        scratch_shapes=[
            pltpu.VMEM(w_s.shape, bf16),
            pltpu.VMEM(w_t.shape, bf16),
            pltpu.VMEM((9 * m_ch, d), bf16),
            pltpu.VMEM((3 * d, m_ch), bf16),
            pltpu.VMEM((rows, 9 * m_ch), bf16),
            pltpu.VMEM(clips.shape, bf16),
            pltpu.VMEM(clips.shape, bf16),
            pltpu.VMEM(clips.shape, bf16),
            narrow,
            narrow,
            narrow,
            narrow,
            narrow,
            narrow,
            narrow,
            narrow,
            narrow,
            wide,
            narrow,
            wide,
            pltpu.VMEM((MB, rows, m_ch), f32),
            pltpu.VMEM((rows, d), f32),
            pltpu.VMEM((2, rows, m_ch), f32),
            pltpu.VMEM((MB, rows, 128), f32),
            pltpu.VMEM((MB, 1, m_ch), f32),
            pltpu.VMEM((MB, 1, d), f32),
            pltpu.VMEM((MB, 1, d), f32),
            pltpu.VMEM((MB, 1, d), f32),
            pltpu.VMEM((MB, 1, d), f32),
            pltpu.VMEM((MB, 1, 128), f32),
            pltpu.VMEM((2, 1, d), f32),
            pltpu.VMEM((2, 1, d), f32),
            pltpu.VMEM((MB, n_dp, 1, 2 * m_ch + 128), f32),
            pltpu.VMEM((MB, n_dp, 1, 2 * d + 128), f32),
            pltpu.VMEM((MB, n_dp, 1, 2 * d + 128), f32),
            pltpu.VMEM((MB, n_dp, 1, 2 * d), f32),
            pltpu.VMEM((MB, n_dp, 1, 2 * m_ch), f32),
            pltpu.VMEM((MB, 1, 1, 2 * d), f32),
            dma((5, MB)),
            dma((5, MB)),
            dma((21,)),
            dma((MB,)),
            dma((6, MB)),
            dma((6, MB)),
            dma((6, MB)),
            dma((4, MB)),
            dma((4, MB)),
            dma((4, MB)),
        ],
        compiler_params=pltpu.CompilerParams(
            collective_id=0, has_side_effects=True, vmem_limit_bytes=62 * 2**20
        ),
    )(clips, boxes, w_s, w_t, g_s, b_s, g_t, b_t, cotangent)


def send_order(n, z, q):
    table = []
    for here in range(n):
        up = sorted(range(here + 1, n), reverse=True)
        down = list(range(here))
        table.append((up + down if here < n / 2 else down + up) + [here])
    dest = 0
    for here in range(n):
        for at in range(n):
            dest = dest + jnp.where((z == here) & (q == at), table[here][at], 0)
    return dest


PIECE = 384
SPAN = 640

HUB_JOBS = (
    (0, 0, -1),
    (1, 0, -1),
    (0, 1, 0),
    (2, 0, -1),
    (0, 2, 1),
    (2, 1, -1),
    (1, 1, -1),
    (1, 2, -1),
    (3, 0, 2),
    (2, 2, 3),
    (3, 1, -1),
    (3, 2, -1),
)


def of_job(j, column):
    return sum(jnp.where(j == i, job[column], 0) for i, job in enumerate(HUB_JOBS))


def is_one_of(j, members):
    found = j < 0
    for i in members:
        found = found | (j == i)
    return found


def gradient_kernel(
    dims,
    a_hbm,
    v_hbm,
    gu_hbm,
    gr_hbm,
    o_s,
    o_t,
    a,
    v,
    gu,
    gr,
    window,
    window_t,
    acc_s,
    acc_t,
    got_s,
    got_t,
    out_s,
    out_t,
    load_sem,
    a_sem,
    gu_send,
    gu_recv,
    fwd_send,
    fwd_recv,
    s_send,
    s_recv,
    t_send,
    t_recv,
):
    frames, height, width = dims
    nc, rows, d = a_hbm.shape[0] // 3, a_hbm.shape[1], a_hbm.shape[2]
    m_ch = v_hbm.shape[2]
    me = lax.axis_index("dp")
    n = lax.axis_size("dp") // 2
    z = lax.div(me, 2)
    core = lax.rem(me, 2)
    twin = me + 1 - 2 * core
    inner = jnp.logical_and(z > 0, z < n - 1)
    outer = jnp.logical_not(inner)
    step = jnp.where(z < n / 2, 2, -2)
    rows_s, rows_t = o_s.shape[0], o_t.shape[0]
    n_pieces = m_ch // PIECE

    barrier = pltpu.get_barrier_semaphore()

    def greet(device):
        pl.semaphore_signal(barrier, 1, device_id={"dp": device}, device_id_type=MESH)

    greet(twin)

    @pl.when(z > 0)
    def _():
        greet(me - 2)

    @pl.when(z < n - 1)
    def _():
        greet(me + 2)

    load_a = pltpu.make_async_copy(a_hbm, a.at[pl.ds(0, 3 * nc)], load_sem.at[0])
    full = 2 * nc + nc // MB
    load_gu = pltpu.make_async_copy(
        gu_hbm.at[pl.ds(0, full)], gu.at[pl.ds(0, full)], load_sem.at[1]
    )
    late = 3 * nc - nc // MB
    early = (pl.ds(full, late - full), slice(None), pl.ds(0, PIECE))
    load_early = pltpu.make_async_copy(gu_hbm.at[early], gu.at[early], load_sem.at[4])
    load_v = pltpu.make_async_copy(v_hbm, v, load_sem.at[2])
    load_gr = pltpu.make_async_copy(gr_hbm, gr, load_sem.at[3])

    @pl.when(inner)
    def _():
        load_a.start()
        load_gu.start()
        load_early.start()

    load_v.start()
    load_gr.start()
    pl.semaphore_wait(barrier, 3 - jnp.where(z == 0, 1, 0) - jnp.where(z == n - 1, 1, 0))

    def columns(p):
        return pl.ds(pl.multiple_of(p * PIECE, 128), PIECE)

    def remote(src, dst, send, recv, device):
        return pltpu.make_async_remote_copy(
            src_ref=src,
            dst_ref=dst,
            send_sem=send,
            recv_sem=recv,
            device_id={"dp": device},
            device_id_type=MESH,
        )

    def gu_to_hub(p):
        s = columns(p)
        return remote(
            gu_hbm.at[pl.ds(nc // MB, nc - nc // MB), :, s],
            gu.at[pl.ds(full, nc - nc // MB), :, s],
            gu_send.at[p],
            gu_recv.at[p],
            me + step,
        )

    def first_to_hub():
        s = pl.ds(0, PIECE)
        return remote(
            gu_hbm.at[pl.ds(late - 2 * nc, nc // MB), :, s],
            gu.at[pl.ds(late, nc // MB), :, s],
            gu_send.at[0],
            gu_recv.at[0],
            me + step,
        )

    def gu_to_twin(p):
        s = columns(p)
        return remote(
            gu.at[pl.ds(2 * nc, nc), :, s],
            gu.at[pl.ds(3 * nc, nc), :, s],
            fwd_send.at[p],
            fwd_recv.at[p],
            twin,
        )

    a_to_twin = remote(
        a.at[pl.ds(2 * nc, nc)], a.at[pl.ds(3 * nc, nc)], a_sem.at[0], a_sem.at[1], twin
    )

    def moved(x, before, after, dt, step):
        if not dt:
            return x
        y = x.reshape(before, after, 128)
        zero = jnp.zeros((before, step, 128), f32)
        if dt > 0:
            y = jnp.concatenate([y[:, step:], zero], axis=1)
        else:
            y = jnp.concatenate([zero, y[:, :-step]], axis=1)
        return y.reshape(rows, 128)

    def place(row0):
        low = lax.div(row0, 128)
        return low, row0 - low * 128

    def time_job(q):
        dest = send_order(n, z, q)
        low, start = place((2 * dest + core) * rows_t)

        def fill_time(i, c):
            to = pl.ds(pl.multiple_of(i * rows, 16), rows)
            for j in range(SPAN // 128):
                chunk = jnp.minimum(low + j, 3 * m_ch // 128 - 1)
                tap = lax.div(chunk, m_ch // 128)
                lane = pl.ds(pl.multiple_of((chunk - tap * (m_ch // 128)) * 128, 128), 128)

                def fill(dt):
                    x = v[i, :, lane].astype(f32)
                    x = moved(x, 1, rows, dt, height * width)
                    window_t[to, j * 128 : (j + 1) * 128] = x.astype(bf16)

                lax.switch(tap, [functools.partial(fill, dt) for dt in (-1, 0, 1)])
            return c

        lax.fori_loop(0, 2 * nc, fill_time, 0)
        acc_t[...] = lax.dot_general(
            window_t[...],
            gr[...].reshape(2 * nc * rows, d),
            (((0,), (0,)), ((), ())),
            preferred_element_type=f32,
        )
        at = pl.ds(pl.multiple_of(start, 8), rows_t)

        def add(slot):
            pltpu.make_async_copy(got_t.at[slot], got_t.at[slot], t_recv.at[slot]).wait()
            acc_t[at, :] += got_t[slot].astype(f32)

        @pl.when((z > 0) & (dest >= z))
        def _():
            add(dest + 1)

        @pl.when((z < n - 1) & (dest <= z))
        def _():
            add(dest)

        @pl.when(dest == z)
        def _():
            o_t[...] = acc_t[at, :]

        @pl.when(dest != z)
        def _():
            out_t[dest] = acc_t[at, :].astype(bf16)
            time_send(dest).start()

    def time_send(dest):
        right = dest > z
        slot = dest + jnp.where(right, 1, 0)
        return remote(
            out_t.at[dest],
            got_t.at[slot],
            t_send.at[dest],
            t_recv.at[slot],
            me + jnp.where(right, 2, -2),
        )

    def hub_dest(k):
        near = z < n / 2
        far_out = jnp.where(near, n - 1, 0)
        own_out = n - 1 - far_out
        return jnp.where(
            k == 0, far_out, jnp.where(k == 1, n - 1 - z, jnp.where(k == 2, own_out, z))
        )

    def space_place(k):
        return place((2 * hub_dest(k) + core) * rows_s)

    def fill_window(k, first, count):
        low, start = space_place(k)

        def fill_space(i, c):
            to = pl.ds(pl.multiple_of(i * rows, 16), rows)
            for j in range(SPAN // 128):
                chunk = jnp.minimum(low + j, 9 * d // 128 - 1)
                tap = lax.div(chunk, d // 128)
                lane = pl.ds(pl.multiple_of((chunk - tap * (d // 128)) * 128, 128), 128)

                def fill(dh, dw):
                    x = a[i, :, lane].astype(f32)
                    if dw:
                        x = pltpu.roll(x, (-dw) % rows, 0)
                    x = moved(x, frames, height * width, dh, width)
                    window[k, to, j * 128 : (j + 1) * 128] = x.astype(bf16)

                lax.switch(
                    tap,
                    [
                        functools.partial(fill, dh, dw)
                        for dh in (-1, 0, 1)
                        for dw in (-1, 0, 1)
                    ],
                )
            return c

        lax.fori_loop(first, first + count, fill_space, 0)

    def space_send(k, p):
        s = columns(p)
        return remote(
            out_s.at[k, :, s],
            got_s.at[jnp.where(k == 1, 1, 0), :, s],
            s_send.at[k, p],
            s_recv.at[jnp.where(k == 1, 1, 0), p],
            me + jnp.where(k == 2, -step, step),
        )

    def space_job(k, p):
        s = columns(p)
        low, start = space_place(k)
        at = pl.ds(pl.multiple_of(start, 8), rows_s)
        acc_s[...] = lax.dot_general(
            window[k],
            gu[:, :, s].reshape(4 * nc * rows, PIECE),
            (((0,), (0,)), ((), ())),
            preferred_element_type=f32,
        )

        @pl.when(k >= 2)
        def _():
            got = got_s.at[k - 2, :, s]
            pltpu.make_async_copy(got, got, s_recv.at[k - 2, p]).wait()
            acc_s[at, :] += got[...].astype(f32)

        @pl.when(k == 3)
        def _():
            o_s[:, s] = acc_s[at, :]

        @pl.when(k < 3)
        def _():
            out_s[k, :, s] = acc_s[at, :].astype(bf16)
            space_send(k, p).start()

    def take_gu(p):
        @pl.when(p == 0)
        def _():
            first_to_hub().wait_recv()

        @pl.when(p > 0)
        def _():
            gu_to_hub(p).wait_recv()

        gu_to_twin(p).start()
        gu_to_twin(p).wait_recv()

    @pl.when(inner)
    def _():
        load_a.wait()
        a_to_twin.start()

        a_to_twin.wait_recv()

        new_k = [i for i, job in enumerate(HUB_JOBS) if job[0] not in [x[0] for x in HUB_JOBS[:i]]]
        new_p = [i for i, job in enumerate(HUB_JOBS) if job[1] not in [x[1] for x in HUB_JOBS[:i]]]
        timed = [i for i, job in enumerate(HUB_JOBS) if job[2] >= 0]

        def hub_job(j, carry):
            k, p = of_job(j, 0), of_job(j, 1)

            @pl.when(is_one_of(j, new_k))
            def _():
                fill_window(k, 0, 4 * nc)

            @pl.when(j == 0)
            def _():
                load_gu.wait()
                load_early.wait()

            @pl.when(is_one_of(j, new_p))
            def _():
                take_gu(p)

            space_job(k, p)

            @pl.when(j == timed[0])
            def _():
                load_v.wait()
                load_gr.wait()

            @pl.when(is_one_of(j, timed))
            def _():
                time_job(of_job(j, 2))

            return carry

        lax.fori_loop(0, len(HUB_JOBS), hub_job, 0)
        a_to_twin.wait_send()

        def sent(p, carry):
            gu_to_twin(p).wait_send()
            for k in range(3):
                space_send(k, p).wait_send()
            return carry

        lax.fori_loop(0, n_pieces, sent, 0)

    @pl.when(outer)
    def _():
        first_to_hub().start()
        gu_to_hub(1).start()
        load_v.wait()
        load_gr.wait()

        def round_out(q, carry):
            time_job(q)

            @pl.when(q == 0)
            def _():
                for p in range(2, n_pieces):
                    gu_to_hub(p).start()

            return carry

        lax.fori_loop(0, n, round_out, 0)

        for p in range(n_pieces):
            s = columns(p)
            got = got_s.at[0, :, s]
            pltpu.make_async_copy(got, got, s_recv.at[0, p]).wait()
            o_s[:, s] = got[...].astype(f32)
            (gu_to_hub(p) if p else first_to_hub()).wait_send()

    def finish(q, carry):
        time_send(send_order(n, z, q)).wait_send()
        return carry

    lax.fori_loop(0, n - 1, finish, 0)


def gradients(dims, n_dp, a, v, gu, gr):
    nc, rows, d = a.shape[0] // 3, a.shape[1], a.shape[2]
    m_ch = v.shape[2]
    rows_s, rows_t = 9 * d // n_dp, 3 * m_ch // n_dp
    n = n_dp // 2
    n_pieces = m_ch // PIECE
    shape = jax.ShapeDtypeStruct
    dma = pltpu.SemaphoreType.DMA
    return pl.pallas_call(
        functools.partial(gradient_kernel, dims),
        out_shape=(shape((rows_s, m_ch), f32), shape((rows_t, d), f32)),
        in_specs=[pl.BlockSpec(memory_space=pl.ANY)] * 4,
        out_specs=[pl.BlockSpec(memory_space=pltpu.VMEM)] * 2,
        scratch_shapes=[
            pltpu.VMEM((4 * nc, rows, d), bf16),
            pltpu.VMEM(v.shape, bf16),
            pltpu.VMEM((4 * nc, rows, m_ch), bf16),
            pltpu.VMEM(gr.shape, bf16),
            pltpu.VMEM((4, 4 * nc * rows, SPAN), bf16),
            pltpu.VMEM((2 * nc * rows, SPAN), bf16),
            pltpu.VMEM((SPAN, PIECE), f32),
            pltpu.VMEM((SPAN, d), f32),
            pltpu.VMEM((2, rows_s, m_ch), bf16),
            pltpu.VMEM((n + 1, rows_t, d), bf16),
            pltpu.VMEM((3, rows_s, m_ch), bf16),
            pltpu.VMEM((n, rows_t, d), bf16),
            dma((5,)),
            dma((2,)),
            dma((n_pieces,)),
            dma((n_pieces,)),
            dma((n_pieces,)),
            dma((n_pieces,)),
            dma((3, n_pieces)),
            dma((2, n_pieces)),
            dma((n,)),
            dma((n + 1,)),
        ],
        compiler_params=pltpu.CompilerParams(
            collective_id=1, has_side_effects=True, vmem_limit_bytes=62 * 2**20
        ),
    )(a, v, gu, gr)


def spatial_columns(activity):
    height, breadth = (activity.shape[2], activity.shape[3])
    padded = jnp.pad(activity, ((0, 0), (0, 0), (1, 1), (1, 1), (0, 0)))
    pieces = [
        padded[:, :, row_off : row_off + height, col_off : col_off + breadth, :]
        for row_off in range(3)
        for col_off in range(3)
    ]
    return jnp.concatenate(pieces, axis=-1)


def temporal_columns(activity):
    frames = activity.shape[1]
    padded = jnp.pad(activity, ((0, 0), (1, 1), (0, 0), (0, 0), (0, 0)))
    return jnp.concatenate([padded[:, offset : offset + frames] for offset in range(3)], axis=-1)


def left_product(former, latter):
    return lax.dot_general(
        former, latter, (((0,), (0,)), ((), ())), preferred_element_type=jnp.float32
    )


def body(
    clips,
    boxes,
    spatial_w,
    temporal_w,
    spatial_gain,
    spatial_shift,
    temporal_gain,
    temporal_shift,
    cotangent,
):
    n_clips, frames, height, breadth, d = clips.shape
    cm = n_clips // MB
    width = (breadth // 8 + 1) * 8
    rows = cm * frames * height * width
    m_ch = spatial_w.shape[2]

    def frames_inside(x):
        return x.transpose(0, 2, 3, 1, 4)

    n_dp = lax.axis_size("dp")
    hubs = n_dp == 8 and 9 * d // n_dp == 576 and 3 * m_ch // n_dp == 432 and d % 128 == 0
    act, grad, a_in, hidden, gu, gr, gain_s, shift_s, gain_t, shift_t = relay(
        (cm, frames, height, width),
        n_dp,
        hubs,
        frames_inside(clips),
        boxes,
        spatial_w[0],
        temporal_w[0],
        spatial_gain,
        spatial_shift,
        temporal_gain,
        temporal_shift,
        frames_inside(cotangent),
    )

    def frames_of(x):
        return x.reshape(n_clips, frames, height, width, x.shape[-1])[:, :, :, :breadth]

    if hubs:
        clip_rows = frames * height * width
        grad_s, grad_t = gradients(
            (frames, height, width),
            n_dp,
            *[x.reshape(-1, clip_rows, x.shape[-1]) for x in (a_in, hidden, gu, gr)],
        )
    else:
        cells = n_clips * frames * height * breadth
        cols = spatial_columns(frames_of(a_in[0])).reshape(cells, -1)
        grad_s = left_product(cols, frames_of(gu[0]).reshape(cells, -1))
        stacked = temporal_columns(frames_of(hidden[0])).reshape(cells, -1)
        grad_t = left_product(stacked, frames_of(gr[0]).reshape(cells, -1))
        grad_s = lax.psum_scatter(grad_s, "dp", scatter_dimension=0, tiled=True)
        grad_t = lax.psum_scatter(grad_t, "dp", scatter_dimension=0, tiled=True)
    return (
        act.transpose(0, 3, 1, 2, 4)[None],
        grad.transpose(0, 3, 1, 2, 4)[None],
        grad_s[None],
        grad_t[None],
        gain_s,
        shift_s,
        gain_t,
        shift_t,
    )


def solution(mesh):
    clip_spec = P("dp", None, None, None, None)
    weight_spec = P("pipe", None, None)
    channel_spec = P("pipe", None)
    return jax.shard_map(
        body,
        mesh=mesh,
        in_specs=(
            clip_spec,
            P("dp", None),
            weight_spec,
            weight_spec,
            channel_spec,
            channel_spec,
            channel_spec,
            channel_spec,
            clip_spec,
        ),
        out_specs=(
            P("pipe", "dp", None, None, None, None),
            P("pipe", "dp", None, None, None, None),
            P("pipe", "dp", None),
            P("pipe", "dp", None),
            channel_spec,
            channel_spec,
            channel_spec,
            channel_spec,
        ),
        check_vma=False,
    )
```
